128 devices in a mesh: dp: 64 (over z, y, x_lo, core), owner: 2 (over x_hi).
Axes of the slice: x: 4 (x_hi: 2, x_lo: 2; x = x_hi * 2 + x_lo), y: 4, z: 4, core: 2. Of those that a mesh axis runs over, the one named last changes fastest.
Arguments:
- hidden: bfloat16 [49152, 2560], P('dp'), may hold values from -16 to 16
- out_grad: bfloat16 [49152, 2560], P('dp'), may hold values from -0.078125 to 0.078125
- left_inverse: bfloat16 [2560, 2560], P(None, 'owner'), as said below
- right_inverse: bfloat16 [2560, 2560], P(None, 'owner'), as said below
Outputs:
- factors: float32 [2, 2560, 2560], P('owner', 'dp')
- update: float32 [2560, 2560], P('dp', 'owner')
The draws below stay inside these ranges and needn't reach their ends.
Inputs may be any that keep to these rules, and one draw needn't show every extreme that they name: `left_inverse`: symmetric and positive definite. `right_inverse`: symmetric and positive definite.
All inputs are finite; a program needn't handle non-finite values.
Results may differ from the reference program's by a relative error of at most 0.004.
Values may be sent and summed in bfloat16 or wider, within the bound.
No kernel may reach another device: no remote copies, remote signals or barrier semaphores. Data moves between devices by JAX's collectives and lax.ppermute only.
A program may use at most 192 MiB of HBM per device.

```python
import math
import jax
import jax.numpy as jnp

D = 2560
TOKENS = 49152


def symmetric_matrix(raw, diagonal):
    spread = 0.35 / math.sqrt(2.0 * D)
    off_part = (raw + raw.T) * spread
    return off_part + jnp.eye(D, dtype=jnp.float32) * diagonal[None, :]


def draw_left_inverse(key, part):
    key = jax.random.fold_in(key, 11)
    noise_key, diag_key = jax.random.split(key)
    raw = jax.random.normal(noise_key, (D, D), jnp.float32)
    diagonal = jnp.exp(jax.random.uniform(diag_key, (D,), jnp.float32, 0.0, 0.4))
    return symmetric_matrix(raw, diagonal).astype(jnp.bfloat16)


def draw_right_inverse(key, part):
    key = jax.random.fold_in(key, 23)
    noise_key, diag_key = jax.random.split(key)
    raw = jax.random.normal(noise_key, (D, D), jnp.float32)
    diagonal = jnp.exp(jax.random.uniform(diag_key, (D,), jnp.float32, 0.0, 0.4))
    return symmetric_matrix(raw, diagonal).astype(jnp.bfloat16)


def strengthened(entries, own_key, source, target, parts, factor):
    def block_of(dim):
        return (jnp.arange(entries.shape[dim]) // (entries.shape[dim] // parts)).reshape((-1,) + (1,) * (entries.ndim - 1 - dim))

    near = jax.random.permutation(own_key, parts)[block_of(target)]
    far = (block_of(target) + parts // 2) % parts
    return jnp.where((block_of(source) == near) | (block_of(source) == far), factor * entries, entries)


def shard_levels(stream_key, extent, cuts, low, high):
    loudness = 1.0
    for position, parts in cuts:
        draws = jax.random.uniform(jax.random.fold_in(jax.random.fold_in(stream_key, 6), position), (parts,), jnp.float32, low / len(cuts), high / len(cuts))
        loudness = loudness * jnp.repeat(jnp.exp(draws), extent[position] // parts).reshape((-1,) + (1,) * (len(extent) - 1 - position))
    return loudness


def bell_draw_with(key, extent, deviation, bound, shards, heavy, kind=jnp.bfloat16):
    entries = deviation * jax.random.normal(key, extent, jnp.float32)
    if shards:
        entries = entries * shard_levels(key, extent, shards, -0.22, 0.18)
    return jnp.clip(strengthened(entries, jax.random.fold_in(key, 3), *heavy), -bound, bound).astype(kind)


def setup_inputs(seed: int = 0) -> dict:
    seeds = jax.random.split(jax.random.key(seed), 5)
    return {
        "hidden": bell_draw_with(seeds[0], (TOKENS, D), 1.0, 16.0, ((0, 64),), (0, 1, 64, 4.0)),
        "out_grad": bell_draw_with(seeds[1], (TOKENS, D), TOKENS ** -0.5, 0.078125, ((0, 64),), (0, 1, 64, 4.0)),
        "left_inverse": draw_left_inverse(jax.random.fold_in(seeds[4], 71), 0),
        "right_inverse": draw_right_inverse(jax.random.fold_in(seeds[4], 71), 0),
    }


def reference(hidden, out_grad, left_inverse, right_inverse):
    inputs_cov = jnp.dot(hidden.T, hidden, preferred_element_type=jnp.float32) / TOKENS
    grads_cov = jnp.dot(out_grad.T, out_grad, preferred_element_type=jnp.float32)
    factors = jnp.stack([inputs_cov, grads_cov])
    left_side = jnp.dot(hidden, left_inverse, preferred_element_type=jnp.float32).astype(jnp.bfloat16)
    right_side = jnp.dot(out_grad, right_inverse, preferred_element_type=jnp.float32).astype(jnp.bfloat16)
    update = jnp.dot(left_side.T, right_side, preferred_element_type=jnp.float32)
    return factors, update
```

```python
import jax
import jax.numpy as jnp
from jax import lax
from jax.sharding import Mesh, PartitionSpec as P

BF = jnp.bfloat16
F32 = jnp.float32


def contract(first_rows, second_rows, out=F32):
    return lax.dot_general(
        first_rows, second_rows, (((0,), (0,)), ((), ())), preferred_element_type=F32
    ).astype(out)


def shift(x, axis, step):
    size = lax.axis_size(axis)
    return lax.ppermute(x, axis, [(i, (i + step) % size) for i in range(size)])


def pick(x, dim, index):
    return lax.dynamic_index_in_dim(x, index, dim, keepdims=False)


def direct_sum(x, dim, axis):
    size = lax.axis_size(axis)
    me = lax.axis_index(axis)
    received = [
        shift(pick(x, dim, (me + step) % size).astype(BF), axis, step)
        for step in range(1, size)
    ]
    total = pick(x, dim, me).astype(F32)
    for block in received:
        total = total + block.astype(F32)
    return total


def ring_sum(x, dim, axis):
    me = lax.axis_index(axis)
    far = pick(x, dim, (me + 2) % 4)
    half = far.shape[0] // 2
    from_left = shift(far[:half], axis, 1)
    from_right = shift(far[half:], axis, -1)
    right = pick(x, dim, (me + 1) % 4).astype(F32)
    left = pick(x, dim, (me + 3) % 4).astype(F32)
    right = jnp.concatenate([right[:half] + from_left.astype(F32), right[half:]])
    left = jnp.concatenate([left[:half], left[half:] + from_right.astype(F32)])
    a = shift(right.astype(BF), axis, 1)
    b = shift(left.astype(BF), axis, -1)
    return pick(x, dim, me).astype(F32) + a.astype(F32) + b.astype(F32)


def split_pair(x):
    high = lax.reduce_precision(x, 8, 7)
    return high.astype(BF), (x - high).astype(BF)


def per_device(hidden, out_grad, left_inverse, right_inverse):
    z, y, xl, c, o = (lax.axis_index(n) for n in ("z", "y", "xl", "c", "o"))
    tokens, width = hidden.shape
    half = width // 2
    token_total = tokens * 64
    first = o == 0

    x = jnp.where(first, hidden, out_grad)
    keep, send = c ^ o, (1 - c) ^ o

    def other_half(index):
        at = index * half
        return jnp.where(
            first,
            lax.dynamic_slice_in_dim(out_grad, at, half, 1),
            lax.dynamic_slice_in_dim(hidden, at, half, 1),
        )

    x2 = jnp.concatenate([x, shift(x, "c", 1)])
    y2 = jnp.concatenate([other_half(keep), shift(other_half(send), "c", 1)])
    xc = lax.dynamic_slice_in_dim(x2, c * half, half, 1)

    grads = jnp.where(first, y2, xc)
    acts = jnp.where(first, xc, y2)
    mt = contract(grads, acts, BF).reshape(4, 4, half // 16, half)
    q = half // 2
    mz = direct_sum(direct_sum(mt[..., :q], 0, "z"), 0, "y")
    my = direct_sum(direct_sum(mt[..., q:], 1, "y"), 0, "z")
    m = jnp.concatenate([mz, my], axis=1).reshape(2, half // 32, half)
    mine, theirs = pick(m, 0, xl), pick(m, 0, 1 - xl)
    own = mine + shift(theirs, "xl", 1)
    partner = shift(mine, "o", 1) + lax.ppermute(
        theirs, ("xl", "o"), [(i, 3 - i) for i in range(4)]
    )
    swap = (c ^ o) == 0
    mrow = jnp.concatenate(
        [jnp.where(swap, own, partner), jnp.where(swap, partner, own)], axis=1
    )
    rows = mrow.shape[0]
    stacked = jnp.concatenate(split_pair(mrow))
    pt = jnp.dot(stacked, left_inverse, preferred_element_type=F32)
    pt = pt[:rows] + pt[rows:]
    pt_other = shift(pt, "o", 1)
    pt = jnp.concatenate(
        [jnp.where(first, pt, pt_other), jnp.where(first, pt_other, pt)], axis=1
    )
    blocks = pt.reshape(rows, 64, rows).transpose(1, 0, 2)
    blocks = lax.all_to_all(blocks, ("z", "y", "xl", "c"), 0, 0, tiled=True)
    blocks = blocks.reshape(32, 2, rows, rows).transpose(1, 0, 2, 3).reshape(width, rows)
    stacked = jnp.concatenate(split_pair(blocks), axis=1)
    update = contract(stacked, right_inverse)
    update = update[:rows] + update[rows:]

    f = contract(x2, xc, BF).reshape(4, 4, width // 16, half)
    fz = direct_sum(ring_sum(f[..., :q], 0, "z"), 0, "y")
    fy = direct_sum(ring_sum(f[..., q:], 1, "y"), 0, "z")
    f = jnp.concatenate([fz, fy], axis=1).reshape(2, width // 32, half)
    f = direct_sum(f, 0, "xl") * jnp.where(first, 1.0 / token_total, 1.0).astype(F32)
    f = f.reshape(2, width // 64, half)
    mine = pick(f, 0, c)
    theirs = shift(pick(f, 0, 1 - c), "c", 1)
    factors = jnp.concatenate(
        [jnp.where(c == 0, mine, theirs), jnp.where(c == 0, theirs, mine)], axis=1
    )[None]
    return factors, update


def solution(mesh):
    fine = Mesh(mesh.devices.reshape(4, 4, 2, 2, 2), ("z", "y", "xl", "c", "o"))
    dp = ("z", "y", "xl", "c")
    in_specs = (P(dp, None), P(dp, None), P(None, "o"), P(None, "o"))
    out_specs = (P("o", dp, None), P(dp, "o"))
    return jax.shard_map(
        per_device, mesh=fine, in_specs=in_specs, out_specs=out_specs, check_vma=False
    )
```

```python
import functools

import jax
import jax.numpy as jnp
from jax import lax
from jax.experimental import pallas as pl
from jax.experimental.pallas import tpu as pltpu
from jax.sharding import Mesh, PartitionSpec as P

BF = jnp.bfloat16
F32 = jnp.float32
TILE = 640


def contract(first_rows, second_rows):
    return lax.dot_general(
        first_rows, second_rows, (((0,), (0,)), ((), ())), preferred_element_type=F32
    )


def shift(x, axis, step):
    size = lax.axis_size(axis)
    return lax.ppermute(x, axis, [(i, (i + step) % size) for i in range(size)])


def turn(x, step, stage):
    pairs = []
    for z in range(4):
        for y in range(4):
            for c in range(2):
                along_z = (c == 0) == (stage == 0)
                there = ((z + step) % 4, y) if along_z else (z, (y + step) % 4)
                pairs.append(((z * 4 + y) * 2 + c, (there[0] * 4 + there[1]) * 2 + c))
    return lax.ppermute(x, ("z", "y", "c"), pairs)


def pick(x, dim, index):
    return lax.dynamic_index_in_dim(x, index, dim, keepdims=False)


def split_pair(x):
    high = lax.reduce_precision(x, 8, 7)
    return high.astype(BF), (x - high).astype(BF)


def place_blocks(place, buffer, sems, outs, step, zs, finish):
    core, z_me, y_me = place[1], place[2], place[3]
    rows = buffer.shape[1] // (zs * 4)
    for a in range(zs):
        for k in range(4):
            z = step * zs + a
            ahead = jnp.where(core == 0, z - z_me + 4, k - y_me + 4) & 3
            slot = jnp.where(core == 0, k, z)
            part = a * 4 + k
            block = buffer.at[step, pl.ds(part * rows, rows), :]

            def move(target):
                copy = pltpu.make_async_copy(block, target, sems.at[step, part])
                if finish:
                    copy.wait()
                else:
                    copy.start()

            for r, out in enumerate(outs):
                if isinstance(out, (list, tuple)):
                    for side, ref in enumerate(out):
                        pl.when((ahead == r) & ((slot >> 1) == side))(
                            functools.partial(lambda ref: move(ref.at[slot & 1]), ref)
                        )
                else:
                    pl.when(ahead == r)(functools.partial(lambda ref: move(ref.at[slot]), out))


def finish_blocks(place, buffer, sems, outs, steps, zs):
    for step in range(steps):
        place_blocks(place, buffer, sems, outs, step, zs, True)


def cross_kernel(place, a0, a1, b0, b1, own, ahead1, ahead2, ahead3, buffer, sems):
    step = pl.program_id(0)
    outs = [own, ahead1, ahead2, ahead3]
    buffer[step] = (contract(a0[...], b0[...]) + contract(a1[...], b1[...])).astype(BF)
    place_blocks(place, buffer, sems, outs, step, 2, False)

    @pl.when(step == 1)
    def _():
        finish_blocks(place, buffer, sems, outs, 2, 2)


def cross_term(place, grads, grads_next, acts, acts_next):
    tokens, width = grads.shape
    half = width // 2
    left = pl.BlockSpec((tokens, TILE), lambda m, p: (0, p[1] * 2 + m))
    right = pl.BlockSpec((tokens, half), lambda m, p: (0, p[1] ^ p[0]))
    out = jax.ShapeDtypeStruct((4, half // 16, half), BF)
    return pl.pallas_call(
        cross_kernel,
        out_shape=[out] * 4,
        grid_spec=pltpu.PrefetchScalarGridSpec(
            num_scalar_prefetch=1,
            grid=(2,),
            in_specs=[left, left, right, right],
            out_specs=[pl.BlockSpec(memory_space=pl.ANY)] * 4,
            scratch_shapes=[pltpu.VMEM((2, TILE, half), BF), pltpu.SemaphoreType.DMA((2, 8))],
        ),
        compiler_params=pltpu.CompilerParams(vmem_limit_bytes=48 * 2**20),
        cost_estimate=pl.CostEstimate(
            flops=4 * tokens * half * half, bytes_accessed=10 * tokens * half, transcendentals=0
        ),
        name="cross_term",
    )(place, grads, grads_next, acts, acts_next)


def factor_kernel(
    place, ha0, ha1, ga0, ga1, hb0, hb1, gb0, gb1, own, right, far_a, far_b, left, buffer, sems
):
    step = pl.program_id(0)
    outs = [own, right, (far_a, far_b), left]

    def term(a0, a1, b0, b1):
        buffer[step] = (contract(a0[...], b0[...]) + contract(a1[...], b1[...])).astype(BF)

    pl.when(place[0] == 0)(lambda: term(ha0, ha1, hb0, hb1))
    pl.when(place[0] == 1)(lambda: term(ga0, ga1, gb0, gb1))
    place_blocks(place, buffer, sems, outs, step, 1, False)

    @pl.when(step == 3)
    def _():
        finish_blocks(place, buffer, sems, outs, 4, 1)


def factor_term(place, acts, acts_next, grads, grads_next):
    tokens, width = acts.shape
    half = width // 2
    a_acts = pl.BlockSpec((tokens, TILE), lambda m, p: (0, m * (1 - p[0])))
    a_grads = pl.BlockSpec((tokens, TILE), lambda m, p: (0, m * p[0]))
    b = pl.BlockSpec((tokens, half), lambda m, p: (0, p[1]))
    out = jax.ShapeDtypeStruct((4, width // 16, half), BF)
    side = jax.ShapeDtypeStruct((2, width // 16, half), BF)
    return pl.pallas_call(
        factor_kernel,
        out_shape=[out, out, side, side, out],
        grid_spec=pltpu.PrefetchScalarGridSpec(
            num_scalar_prefetch=1,
            grid=(4,),
            in_specs=[a_acts, a_acts, a_grads, a_grads, b, b, b, b],
            out_specs=[pl.BlockSpec(memory_space=pl.ANY)] * 5,
            scratch_shapes=[pltpu.VMEM((4, TILE, half), BF), pltpu.SemaphoreType.DMA((4, 4))],
        ),
        compiler_params=pltpu.CompilerParams(vmem_limit_bytes=56 * 2**20),
        cost_estimate=pl.CostEstimate(
            flops=4 * tokens * width * half, bytes_accessed=16 * tokens * half, transcendentals=0
        ),
        name="factor_term",
    )(place, acts, acts_next, grads, grads_next, acts, acts_next, grads, grads_next)


def add(first, *rest):
    total = first.astype(F32)
    for x in rest:
        total = total + x.astype(F32)
    return total


def second_sum(x, me):
    received = [turn(pick(x, 0, (me + step) & 3).astype(BF), step, 1) for step in (1, 2, 3)]
    return add(pick(x, 0, me), *received)


def per_device(hidden, out_grad, left_inverse, right_inverse):
    z, y, xl, c, o = (lax.axis_index(n) for n in ("z", "y", "xl", "c", "o"))
    tokens, width = hidden.shape
    half = width // 2
    token_total = tokens * 64
    first = o == 0
    place = jnp.stack([o, c, z, y]).astype(jnp.int32)
    second_me = jnp.where(c == 0, y, z)

    grads_next = shift(out_grad, "c", 1)
    acts_next = shift(hidden, "c", 1)

    own, m1, m2, m3 = cross_term(place, out_grad, grads_next, hidden, acts_next)
    m = add(own, turn(m1, 1, 0), turn(m2, 2, 0), turn(m3, 3, 0))
    m = second_sum(m, second_me).reshape(2, half // 32, half)
    mine, theirs = pick(m, 0, xl), pick(m, 0, 1 - xl)
    own = mine + shift(theirs, "xl", 1)
    partner = shift(mine, "o", 1) + lax.ppermute(
        theirs, ("xl", "o"), [(i, 3 - i) for i in range(4)]
    )
    swap = (c ^ o) == 0
    mrow = jnp.concatenate(
        [jnp.where(swap, own, partner), jnp.where(swap, partner, own)], axis=1
    )
    rows = mrow.shape[0]
    stacked = jnp.concatenate(split_pair(mrow))
    pt = jnp.dot(stacked, left_inverse, preferred_element_type=F32)
    pt = pt[:rows] + pt[rows:]
    pt_other = shift(pt, "o", 1)
    pt = jnp.concatenate(
        [jnp.where(first, pt, pt_other), jnp.where(first, pt_other, pt)], axis=1
    )
    blocks = pt.reshape(rows, 64, rows).transpose(1, 0, 2)
    blocks = lax.all_to_all(blocks, ("z", "y", "xl", "c"), 0, 0, tiled=True)
    blocks = blocks.reshape(32, 2, rows, rows).transpose(1, 0, 2, 3).reshape(width, rows)
    stacked = jnp.concatenate(split_pair(blocks), axis=1)
    update = contract(stacked, right_inverse)
    update = update[:rows] + update[rows:]

    own, right, far_a, far_b, left = factor_term(place, hidden, acts_next, out_grad, grads_next)
    from_left, from_right = turn(far_a, 1, 0), turn(far_b, -1, 0)
    right = jnp.concatenate([add(right[:2], from_left).astype(BF), right[2:]])
    left = jnp.concatenate([left[:2], add(left[2:], from_right).astype(BF)])
    f = add(own, turn(right, 1, 0), turn(left, -1, 0))
    f = second_sum(f, second_me).reshape(2, width // 32, half)
    f = pick(f, 0, xl) + shift(pick(f, 0, 1 - xl).astype(BF), "xl", 1).astype(F32)
    f = f * jnp.where(first, 1.0 / token_total, 1.0).astype(F32)
    f = f.reshape(2, width // 64, half)
    mine = pick(f, 0, c)
    theirs = shift(pick(f, 0, 1 - c), "c", 1)
    factors = jnp.concatenate(
        [jnp.where(c == 0, mine, theirs), jnp.where(c == 0, theirs, mine)], axis=1
    )[None]
    return factors, update


def solution(mesh):
    fine = Mesh(mesh.devices.reshape(4, 4, 2, 2, 2), ("z", "y", "xl", "c", "o"))
    dp = ("z", "y", "xl", "c")
    in_specs = (P(dp, None), P(dp, None), P(None, "o"), P(None, "o"))
    out_specs = (P("o", dp, None), P(dp, "o"))
    return jax.shard_map(
        per_device, mesh=fine, in_specs=in_specs, out_specs=out_specs, check_vma=False
    )
```

```python
import functools

import jax
import jax.numpy as jnp
from jax import lax
from jax.experimental import pallas as pl
from jax.experimental.pallas import tpu as pltpu
from jax.sharding import Mesh, PartitionSpec as P

BF = jnp.bfloat16
F32 = jnp.float32
TILE = 640


def contract(first_rows, second_rows):
    return lax.dot_general(
        first_rows, second_rows, (((0,), (0,)), ((), ())), preferred_element_type=F32
    )


def shift(x, axis, step):
    size = lax.axis_size(axis)
    return lax.ppermute(x, axis, [(i, (i + step) % size) for i in range(size)])


def turn(x, step, stage):
    pairs = []
    for z in range(4):
        for y in range(4):
            for c in range(2):
                along_z = (c == 0) == (stage == 0)
                there = ((z + step) % 4, y) if along_z else (z, (y + step) % 4)
                pairs.append(((z * 4 + y) * 2 + c, (there[0] * 4 + there[1]) * 2 + c))
    return lax.ppermute(x, ("z", "y", "c"), pairs)


def pick(x, dim, index):
    return lax.dynamic_index_in_dim(x, index, dim, keepdims=False)


def split_pair(x):
    high = lax.reduce_precision(x, 8, 7)
    return high.astype(BF), (x - high).astype(BF)


def place_blocks(place, buffer, sems, outs, m, n, zs, finish):
    core, z_me, y_me = place[1], place[2], place[3]
    rows = TILE // (zs * 4)
    lanes = pl.ds(pl.multiple_of(n * TILE, TILE), TILE)
    for a in range(zs):
        for k in range(4):
            z = m * zs + a
            ahead = jnp.where(core == 0, z - z_me + 4, k - y_me + 4) & 3
            slot = jnp.where(core == 0, k, z)
            part = a * 4 + k
            block = buffer.at[m, pl.ds(part * rows, rows), lanes]

            def move(out):
                copy = pltpu.make_async_copy(block, out.at[slot, :, lanes], sems.at[m, n, part])
                if finish:
                    copy.wait()
                else:
                    copy.start()

            for r, out in enumerate(outs):
                pl.when(ahead == r)(functools.partial(move, out))


def store_tile(place, buffer, sems, outs, tile, steps, zs):
    m, n = pl.program_id(0), pl.program_id(1)
    for lane in range(2):

        @pl.when(n == lane)
        def _():
            buffer[m, :, lane * TILE : (lane + 1) * TILE] = tile()

    place_blocks(place, buffer, sems, outs, m, n, zs, False)

    @pl.when((m == steps - 1) & (n == 1))
    def _():
        for i in range(steps):
            for j in range(2):
                place_blocks(place, buffer, sems, outs, i, j, zs, True)


def cross_kernel(place, a0, a1, b0, b1, own, ahead1, ahead2, ahead3, buffer, sems):
    def tile():
        return (contract(a0[...], b0[...]) + contract(a1[...], b1[...])).astype(BF)

    store_tile(place, buffer, sems, [own, ahead1, ahead2, ahead3], tile, 2, 2)


def cross_term(place, grads, grads_next, acts, acts_next):
    tokens, width = grads.shape
    half = width // 2
    left = pl.BlockSpec((tokens, TILE), lambda m, n, p: (0, p[1] * 2 + m))
    right = pl.BlockSpec((tokens, TILE), lambda m, n, p: (0, (p[1] ^ p[0]) * 2 + n))
    out = jax.ShapeDtypeStruct((4, half // 16, half), BF)
    return pl.pallas_call(
        cross_kernel,
        out_shape=[out] * 4,
        grid_spec=pltpu.PrefetchScalarGridSpec(
            num_scalar_prefetch=1,
            grid=(2, 2),
            in_specs=[left, left, right, right],
            out_specs=[pl.BlockSpec(memory_space=pl.ANY)] * 4,
            scratch_shapes=[pltpu.VMEM((2, TILE, half), BF), pltpu.SemaphoreType.DMA((2, 2, 8))],
        ),
        compiler_params=pltpu.CompilerParams(vmem_limit_bytes=48 * 2**20),
        cost_estimate=pl.CostEstimate(
            flops=4 * tokens * half * half, bytes_accessed=10 * tokens * half, transcendentals=0
        ),
        name="cross_term",
    )(place, grads, grads_next, acts, acts_next)


def factor_kernel(
    place, ha0, ha1, ga0, ga1, hb0, hb1, gb0, gb1, own, ahead1, ahead2, ahead3, buffer, sems
):
    def tile():
        def term(a0, a1, b0, b1):
            return (contract(a0[...], b0[...]) + contract(a1[...], b1[...])).astype(BF)

        return lax.cond(
            place[0] == 0,
            lambda: term(ha0, ha1, hb0, hb1),
            lambda: term(ga0, ga1, gb0, gb1),
        )

    store_tile(place, buffer, sems, [own, ahead1, ahead2, ahead3], tile, 4, 1)


def factor_term(place, acts, acts_next, grads, grads_next):
    tokens, width = acts.shape
    half = width // 2
    a_acts = pl.BlockSpec((tokens, TILE), lambda m, n, p: (0, m * (1 - p[0])))
    a_grads = pl.BlockSpec((tokens, TILE), lambda m, n, p: (0, m * p[0]))
    b_acts = pl.BlockSpec((tokens, TILE), lambda m, n, p: (0, (p[1] * 2 + n) * (1 - p[0])))
    b_grads = pl.BlockSpec((tokens, TILE), lambda m, n, p: (0, (p[1] * 2 + n) * p[0]))
    out = jax.ShapeDtypeStruct((4, width // 16, half), BF)
    return pl.pallas_call(
        factor_kernel,
        out_shape=[out] * 4,
        grid_spec=pltpu.PrefetchScalarGridSpec(
            num_scalar_prefetch=1,
            grid=(4, 2),
            in_specs=[a_acts, a_acts, a_grads, a_grads, b_acts, b_acts, b_grads, b_grads],
            out_specs=[pl.BlockSpec(memory_space=pl.ANY)] * 4,
            scratch_shapes=[pltpu.VMEM((4, TILE, half), BF), pltpu.SemaphoreType.DMA((4, 2, 4))],
        ),
        compiler_params=pltpu.CompilerParams(vmem_limit_bytes=56 * 2**20),
        cost_estimate=pl.CostEstimate(
            flops=4 * tokens * width * half, bytes_accessed=16 * tokens * half, transcendentals=0
        ),
        name="factor_term",
    )(place, acts, acts_next, grads, grads_next, acts, acts_next, grads, grads_next)


def add(first, *rest):
    total = first.astype(F32)
    for x in rest:
        total = total + x.astype(F32)
    return total


def send_second(x, me):
    pieces = [pick(x, 0, (me + step) & 3).astype(BF) for step in (1, 2, 3)]
    return pieces, [turn(piece, step, 1) for step, piece in zip((1, 2, 3), pieces)]


def per_device(hidden, out_grad, left_inverse, right_inverse):
    z, y, xl, c, o = (lax.axis_index(n) for n in ("z", "y", "xl", "c", "o"))
    tokens, width = hidden.shape
    half = width // 2
    token_total = tokens * 64
    first = o == 0
    place = jnp.stack([o, c, z, y]).astype(jnp.int32)
    second_me = jnp.where(c == 0, y, z)

    grads_next = shift(out_grad, "c", 1)
    acts_next = shift(hidden, "c", 1)

    own, m1, m2, m3 = cross_term(place, out_grad, grads_next, hidden, acts_next)
    m_parts = [own, turn(m1, 1, 0), turn(m2, 2, 0), turn(m3, 3, 0)]

    piece = lax.dynamic_slice_in_dim(left_inverse, o * half + c * TILE, TILE, 0)
    piece = shift(piece, "o", 1)
    piece_next = shift(piece, "c", 1)

    own, f1, f2, f3 = factor_term(place, hidden, acts_next, out_grad, grads_next)

    m = add(*m_parts)
    _, received = send_second(m, second_me)
    f_parts = [own, turn(f1, 1, 0), turn(f2, 2, 0), turn(f3, 3, 0)]
    m = add(pick(m, 0, second_me), *received).reshape(2, half // 32, half)
    mine, theirs = pick(m, 0, xl), pick(m, 0, 1 - xl)
    m_own = mine + shift(theirs, "xl", 1)
    partner = shift(mine, "o", 1) + lax.ppermute(
        theirs, ("xl", "o"), [(i, 3 - i) for i in range(4)]
    )
    swap = (c ^ o) == 0
    mrow = jnp.concatenate(
        [jnp.where(swap, m_own, partner), jnp.where(swap, partner, m_own)], axis=1
    )
    rows = mrow.shape[0]
    stacked = jnp.concatenate(split_pair(mrow))
    pt = jnp.dot(stacked, left_inverse, preferred_element_type=F32)
    beside = lax.dynamic_slice_in_dim(left_inverse, (1 - o) * half, half, 0)
    at_own = lax.dynamic_slice_in_dim(stacked, o * half, half, 1)
    at_piece = lax.dynamic_slice_in_dim(stacked, (1 - o) * half + c * TILE, TILE, 1)
    at_next = lax.dynamic_slice_in_dim(stacked, (1 - o) * half + (1 - c) * TILE, TILE, 1)
    pt_other = (
        lax.dot_general(at_own, beside, (((1,), (1,)), ((), ())), preferred_element_type=F32)
        + jnp.dot(at_piece, piece, preferred_element_type=F32)
        + jnp.dot(at_next, piece_next, preferred_element_type=F32)
    )
    pt = pt[:rows] + pt[rows:]
    pt_other = pt_other[:rows] + pt_other[rows:]
    pt = jnp.concatenate(
        [jnp.where(first, pt, pt_other), jnp.where(first, pt_other, pt)], axis=1
    )
    blocks = pt.reshape(rows, 32, 2, rows).transpose(2, 1, 0, 3).reshape(64, rows, rows)
    blocks = lax.all_to_all(blocks, ("c", "z", "y", "xl"), 0, 0, tiled=True)

    f = add(*f_parts)
    pieces, received = send_second(f, second_me)
    blocks = lax.optimization_barrier((blocks, pieces))[0].reshape(width, rows)
    stacked = jnp.concatenate(split_pair(blocks), axis=1)
    update = contract(stacked, right_inverse)
    update = update[:rows] + update[rows:]

    f = add(pick(f, 0, second_me), *received).reshape(2, width // 32, half)
    f = pick(f, 0, xl) + shift(pick(f, 0, 1 - xl).astype(BF), "xl", 1).astype(F32)
    f = f * jnp.where(first, 1.0 / token_total, 1.0).astype(F32)
    f = f.reshape(2, width // 64, half)
    mine = pick(f, 0, c)
    theirs = shift(pick(f, 0, 1 - c), "c", 1)
    factors = jnp.concatenate(
        [jnp.where(c == 0, mine, theirs), jnp.where(c == 0, theirs, mine)], axis=1
    )[None]
    return factors, update


def solution(mesh):
    fine = Mesh(mesh.devices.reshape(4, 4, 2, 2, 2), ("z", "y", "xl", "c", "o"))
    dp = ("z", "y", "xl", "c")
    in_specs = (P(dp, None), P(dp, None), P(None, "o"), P(None, "o"))
    out_specs = (P("o", dp, None), P(dp, "o"))
    return jax.shard_map(
        per_device, mesh=fine, in_specs=in_specs, out_specs=out_specs, check_vma=False
    )
```

```python
import functools

import jax
import jax.numpy as jnp
from jax import lax
from jax.experimental import pallas as pl
from jax.experimental.pallas import tpu as pltpu
from jax.sharding import Mesh, PartitionSpec as P

BF = jnp.bfloat16
F32 = jnp.float32
TILE = 640


def contract(first_rows, second_rows):
    return lax.dot_general(
        first_rows, second_rows, (((0,), (0,)), ((), ())), preferred_element_type=F32
    )


def shift(x, axis, step):
    size = lax.axis_size(axis)
    return lax.ppermute(x, axis, [(i, (i + step) % size) for i in range(size)])


def turn(x, step, stage):
    pairs = []
    for z in range(4):
        for y in range(4):
            for c in range(2):
                along_z = (c == 0) == (stage == 0)
                there = ((z + step) % 4, y) if along_z else (z, (y + step) % 4)
                pairs.append(((z * 4 + y) * 2 + c, (there[0] * 4 + there[1]) * 2 + c))
    return lax.ppermute(x, ("z", "y", "c"), pairs)


def pick(x, dim, index):
    return lax.dynamic_index_in_dim(x, index, dim, keepdims=False)


def split_pair(x):
    high = lax.reduce_precision(x, 8, 7)
    return high.astype(BF), (x - high).astype(BF)


def place_blocks(place, buffer, sems, outs, m, n, zs, finish):
    core, z_me, y_me = place[1], place[2], place[3]
    rows = TILE // (zs * 4)
    wide = buffer.shape[2] // sems.shape[1]
    lanes = pl.ds(pl.multiple_of(n * wide, wide), wide)
    for a in range(zs):
        for k in range(4):
            z = m * zs + a
            ahead = jnp.where(core == 0, z - z_me + 4, k - y_me + 4) & 3
            slot = jnp.where(core == 0, k, z)
            part = a * 4 + k
            block = buffer.at[m, pl.ds(part * rows, rows), lanes]

            def move(out):
                copy = pltpu.make_async_copy(block, out.at[slot, :, lanes], sems.at[m, n, part])
                if finish:
                    copy.wait()
                else:
                    copy.start()

            for r, out in enumerate(outs):
                pl.when(ahead == r)(functools.partial(move, out))


def store_tile(place, buffer, sems, outs, m, n, steps, lanes, zs):
    place_blocks(place, buffer, sems, outs, m, n, zs, False)

    @pl.when((m == steps - 1) & (n == lanes - 1))
    def _():
        for i in range(steps):
            for j in range(lanes):
                place_blocks(place, buffer, sems, outs, i, j, zs, True)


def cross_kernel(place, a0, a1, b0, b1, own, ahead1, ahead2, ahead3, buffer, sems):
    m, n = pl.program_id(0), pl.program_id(1)
    tile = (contract(a0[...], b0[...]) + contract(a1[...], b1[...])).astype(BF)
    for lane in range(2):

        @pl.when(n == lane)
        def _():
            buffer[m, :, lane * TILE : (lane + 1) * TILE] = tile

    store_tile(place, buffer, sems, [own, ahead1, ahead2, ahead3], m, n, 2, 2, 2)


def cross_term(place, grads, grads_next, acts, acts_next):
    tokens, width = grads.shape
    half = width // 2
    left = pl.BlockSpec((tokens, TILE), lambda m, n, p: (0, p[1] * 2 + m))
    right = pl.BlockSpec((tokens, TILE), lambda m, n, p: (0, (p[1] ^ p[0]) * 2 + n))
    out = jax.ShapeDtypeStruct((4, half // 16, half), BF)
    return pl.pallas_call(
        cross_kernel,
        out_shape=[out] * 4,
        grid_spec=pltpu.PrefetchScalarGridSpec(
            num_scalar_prefetch=1,
            grid=(2, 2),
            in_specs=[left, left, right, right],
            out_specs=[pl.BlockSpec(memory_space=pl.ANY)] * 4,
            scratch_shapes=[pltpu.VMEM((2, TILE, half), BF), pltpu.SemaphoreType.DMA((2, 2, 8))],
        ),
        compiler_params=pltpu.CompilerParams(vmem_limit_bytes=48 * 2**20),
        cost_estimate=pl.CostEstimate(
            flops=4 * tokens * half * half, bytes_accessed=10 * tokens * half, transcendentals=0
        ),
        name="cross_term",
    )(place, grads, grads_next, acts, acts_next)


def factor_kernel(
    place, ha0, ha1, ga0, ga1, hb0, hb1, gb0, gb1, own, ahead1, ahead2, ahead3, buffer, sems
):
    m = pl.program_id(0)

    def tile(a0, a1, b0, b1):
        buffer[m] = (contract(a0[...], b0[...]) + contract(a1[...], b1[...])).astype(BF)

    pl.when(place[0] == 0)(lambda: tile(ha0, ha1, hb0, hb1))
    pl.when(place[0] == 1)(lambda: tile(ga0, ga1, gb0, gb1))
    store_tile(place, buffer, sems, [own, ahead1, ahead2, ahead3], m, 0, 4, 1, 1)


def factor_term(place, acts, acts_next, grads, grads_next):
    tokens, width = acts.shape
    half = width // 2
    a_acts = pl.BlockSpec((tokens, TILE), lambda m, p: (0, m * (1 - p[0])))
    a_grads = pl.BlockSpec((tokens, TILE), lambda m, p: (0, m * p[0]))
    b = pl.BlockSpec((tokens, half), lambda m, p: (0, p[1]))
    out = jax.ShapeDtypeStruct((4, width // 16, half), BF)
    return pl.pallas_call(
        factor_kernel,
        out_shape=[out] * 4,
        grid_spec=pltpu.PrefetchScalarGridSpec(
            num_scalar_prefetch=1,
            grid=(4,),
            in_specs=[a_acts, a_acts, a_grads, a_grads, b, b, b, b],
            out_specs=[pl.BlockSpec(memory_space=pl.ANY)] * 4,
            scratch_shapes=[pltpu.VMEM((4, TILE, half), BF), pltpu.SemaphoreType.DMA((4, 1, 4))],
        ),
        compiler_params=pltpu.CompilerParams(vmem_limit_bytes=56 * 2**20),
        cost_estimate=pl.CostEstimate(
            flops=4 * tokens * width * half, bytes_accessed=16 * tokens * half, transcendentals=0
        ),
        name="factor_term",
    )(place, acts, acts_next, grads, grads_next, acts, acts_next, grads, grads_next)


def add(first, *rest):
    total = first.astype(F32)
    for x in rest:
        total = total + x.astype(F32)
    return total


def gate(x, *others):
    anywhere = pl.BlockSpec(memory_space=pl.ANY)
    return pl.pallas_call(
        lambda *refs: None,
        out_shape=jax.ShapeDtypeStruct(x.shape, x.dtype),
        in_specs=[anywhere] * (1 + len(others)),
        out_specs=anywhere,
        input_output_aliases={0: 0},
        name="gate",
    )(x, *others)


def send_second(x, me):
    pieces = [pick(x, 0, (me + step) & 3).astype(BF) for step in (1, 2, 3)]
    return pieces, [turn(piece, step, 1) for step, piece in zip((1, 2, 3), pieces)]


def per_device(hidden, out_grad, left_inverse, right_inverse):
    z, y, xl, c, o = (lax.axis_index(n) for n in ("z", "y", "xl", "c", "o"))
    tokens, width = hidden.shape
    half = width // 2
    token_total = tokens * 64
    first = o == 0
    place = jnp.stack([o, c, z, y]).astype(jnp.int32)
    second_me = jnp.where(c == 0, y, z)

    grads_next = shift(out_grad, "c", 1)
    acts_next = shift(hidden, "c", 1)

    own, m1, m2, m3 = cross_term(place, out_grad, grads_next, hidden, acts_next)
    m_parts = [own, turn(m1, 1, 0), turn(m2, 2, 0), turn(m3, 3, 0)]

    own, f1, f2, f3 = factor_term(place, hidden, acts_next, out_grad, grads_next)

    m_parts[0] = gate(m_parts[0], own)
    m = add(*m_parts)
    _, received = send_second(m, second_me)
    f_parts = [own, turn(f1, 1, 0), turn(f2, 2, 0), turn(f3, 3, 0)]
    m = add(pick(m, 0, second_me), *received).reshape(2, half // 32, half)
    mine, theirs = pick(m, 0, xl), pick(m, 0, 1 - xl)
    m_own = mine + shift(theirs, "xl", 1)
    partner = shift(mine, "o", 1) + lax.ppermute(
        theirs, ("xl", "o"), [(i, 3 - i) for i in range(4)]
    )
    swap = (c ^ o) == 0
    mrow = jnp.concatenate(
        [jnp.where(swap, m_own, partner), jnp.where(swap, partner, m_own)], axis=1
    )
    rows = mrow.shape[0]
    stacked = jnp.concatenate(split_pair(mrow))
    pt = jnp.dot(stacked, left_inverse, preferred_element_type=F32)
    pt = pt[:rows] + pt[rows:]
    pt_other = shift(pt, "o", 1)
    pt = jnp.concatenate(
        [jnp.where(first, pt, pt_other), jnp.where(first, pt_other, pt)], axis=1
    )
    blocks = pt.reshape(rows, 32, 2, rows).transpose(2, 1, 0, 3).reshape(64, rows, rows)
    blocks = lax.all_to_all(blocks, ("c", "z", "y", "xl"), 0, 0, tiled=True)

    f = add(*f_parts)
    pieces, received = send_second(f, second_me)
    blocks = gate(blocks, pieces[0]).reshape(width, rows)
    stacked = jnp.concatenate(split_pair(blocks), axis=1)
    update = contract(stacked, right_inverse)
    update = update[:rows] + update[rows:]

    f = add(pick(f, 0, second_me), *received).reshape(2, width // 32, half)
    f = pick(f, 0, xl) + shift(pick(f, 0, 1 - xl).astype(BF), "xl", 1).astype(F32)
    f = f * jnp.where(first, 1.0 / token_total, 1.0).astype(F32)
    f = f.reshape(2, width // 64, half)
    mine = pick(f, 0, c)
    theirs = shift(pick(f, 0, 1 - c), "c", 1)
    factors = jnp.concatenate(
        [jnp.where(c == 0, mine, theirs), jnp.where(c == 0, theirs, mine)], axis=1
    )[None]
    return factors, update


def solution(mesh):
    fine = Mesh(mesh.devices.reshape(4, 4, 2, 2, 2), ("z", "y", "xl", "c", "o"))
    dp = ("z", "y", "xl", "c")
    in_specs = (P(dp, None), P(dp, None), P(None, "o"), P(None, "o"))
    out_specs = (P("o", dp, None), P(dp, "o"))
    return jax.shard_map(
        per_device, mesh=fine, in_specs=in_specs, out_specs=out_specs, check_vma=False
    )
```

```python
import functools

import jax
import jax.numpy as jnp
from jax import lax
from jax.experimental import pallas as pl
from jax.experimental.pallas import tpu as pltpu
from jax.sharding import Mesh, PartitionSpec as P

BF = jnp.bfloat16
F32 = jnp.float32
TILE = 640


def contract(first_rows, second_rows):
    return lax.dot_general(
        first_rows, second_rows, (((0,), (0,)), ((), ())), preferred_element_type=F32
    )


def shift(x, axis, step):
    size = lax.axis_size(axis)
    return lax.ppermute(x, axis, [(i, (i + step) % size) for i in range(size)])


def turn(x, step, stage):
    pairs = []
    for z in range(4):
        for y in range(4):
            for h in range(2):
                along_z = (h == 0) == (stage == 0)
                z2, y2 = ((z + step) % 4, y) if along_z else (z, (y + step) % 4)
                core, core2 = h ^ ((z + y) & 1), h ^ ((z2 + y2) & 1)
                pairs.append(((z * 4 + y) * 2 + core, (z2 * 4 + y2) * 2 + core2))
    return lax.ppermute(x, ("z", "y", "c"), pairs)


def pick(x, dim, index):
    return lax.dynamic_index_in_dim(x, index, dim, keepdims=False)


def split_pair(x):
    high = lax.reduce_precision(x, 8, 7)
    return high.astype(BF), (x - high).astype(BF)


def place_blocks(place, buffer, sems, outs, m, n, zs, finish):
    part_me, z_me, y_me = place[1], place[2], place[3]
    rows = TILE // (zs * 4)
    wide = buffer.shape[2] // sems.shape[1]
    lanes = pl.ds(pl.multiple_of(n * wide, wide), wide)
    for a in range(zs):
        for k in range(4):
            z = m * zs + a
            ahead = jnp.where(part_me == 0, z - z_me + 4, k - y_me + 4) & 3
            slot = jnp.where(part_me == 0, k, z)
            part = a * 4 + k
            block = buffer.at[m, pl.ds(part * rows, rows), lanes]

            def move(out):
                copy = pltpu.make_async_copy(block, out.at[slot, :, lanes], sems.at[m, n, part])
                if finish:
                    copy.wait()
                else:
                    copy.start()

            for r, out in enumerate(outs):
                pl.when(ahead == r)(functools.partial(move, out))


def store_tile(place, buffer, sems, outs, m, n, steps, lanes, zs):
    place_blocks(place, buffer, sems, outs, m, n, zs, False)

    @pl.when((m == steps - 1) & (n == lanes - 1))
    def _():
        for i in range(steps):
            for j in range(lanes):
                place_blocks(place, buffer, sems, outs, i, j, zs, True)


def own_kernel(place, a, b, out):
    out[...] = contract(a[...], b[...])


def cross_kernel(place, a, b, partial, own, ahead1, ahead2, ahead3, buffer, sems):
    m, n = pl.program_id(0), pl.program_id(1)
    tile = (partial[...] + contract(a[...], b[...])).astype(BF)
    for lane in range(2):

        @pl.when(n == lane)
        def _():
            buffer[m, :, lane * TILE : (lane + 1) * TILE] = tile

    store_tile(place, buffer, sems, [own, ahead1, ahead2, ahead3], m, n, 2, 2, 2)


def cross_term(place, grads, grads_next, acts, acts_next):
    tokens, width = grads.shape
    half = width // 2
    left = pl.BlockSpec((tokens, TILE), lambda m, n, p: (0, p[1] * 2 + m))
    right = pl.BlockSpec((tokens, TILE), lambda m, n, p: (0, (p[1] ^ p[0]) * 2 + n))
    middle = pl.BlockSpec((TILE, TILE), lambda m, n, p: (m, n))
    params = pltpu.CompilerParams(vmem_limit_bytes=48 * 2**20)
    cost = pl.CostEstimate(
        flops=2 * tokens * half * half, bytes_accessed=10 * tokens * half, transcendentals=0
    )
    partial = pl.pallas_call(
        own_kernel,
        out_shape=jax.ShapeDtypeStruct((half, half), F32),
        grid_spec=pltpu.PrefetchScalarGridSpec(
            num_scalar_prefetch=1, grid=(2, 2), in_specs=[left, right], out_specs=middle
        ),
        compiler_params=params,
        cost_estimate=cost,
        name="cross_own",
    )(place, grads, acts)
    out = jax.ShapeDtypeStruct((4, half // 16, half), BF)
    return pl.pallas_call(
        cross_kernel,
        out_shape=[out] * 4,
        grid_spec=pltpu.PrefetchScalarGridSpec(
            num_scalar_prefetch=1,
            grid=(2, 2),
            in_specs=[left, right, middle],
            out_specs=[pl.BlockSpec(memory_space=pl.ANY)] * 4,
            scratch_shapes=[pltpu.VMEM((2, TILE, half), BF), pltpu.SemaphoreType.DMA((2, 2, 8))],
        ),
        compiler_params=params,
        cost_estimate=cost,
        name="cross_term",
    )(place, grads_next, acts_next, partial)


def factor_kernel(
    place, ha0, ha1, ga0, ga1, hb0, hb1, gb0, gb1, own, ahead1, ahead2, ahead3, buffer, sems
):
    m = pl.program_id(0)

    def tile(a0, a1, b0, b1):
        buffer[m] = (contract(a0[...], b0[...]) + contract(a1[...], b1[...])).astype(BF)

    pl.when(place[0] == 0)(lambda: tile(ha0, ha1, hb0, hb1))
    pl.when(place[0] == 1)(lambda: tile(ga0, ga1, gb0, gb1))
    store_tile(place, buffer, sems, [own, ahead1, ahead2, ahead3], m, 0, 4, 1, 1)


def factor_term(place, acts, acts_next, grads, grads_next):
    tokens, width = acts.shape
    half = width // 2
    a_acts = pl.BlockSpec((tokens, TILE), lambda m, p: (0, m * (1 - p[0])))
    a_grads = pl.BlockSpec((tokens, TILE), lambda m, p: (0, m * p[0]))
    b = pl.BlockSpec((tokens, half), lambda m, p: (0, p[1]))
    out = jax.ShapeDtypeStruct((4, width // 16, half), BF)
    return pl.pallas_call(
        factor_kernel,
        out_shape=[out] * 4,
        grid_spec=pltpu.PrefetchScalarGridSpec(
            num_scalar_prefetch=1,
            grid=(4,),
            in_specs=[a_acts, a_acts, a_grads, a_grads, b, b, b, b],
            out_specs=[pl.BlockSpec(memory_space=pl.ANY)] * 4,
            scratch_shapes=[pltpu.VMEM((4, TILE, half), BF), pltpu.SemaphoreType.DMA((4, 1, 4))],
        ),
        compiler_params=pltpu.CompilerParams(vmem_limit_bytes=56 * 2**20),
        cost_estimate=pl.CostEstimate(
            flops=4 * tokens * width * half, bytes_accessed=16 * tokens * half, transcendentals=0
        ),
        name="factor_term",
    )(place, acts, acts_next, grads, grads_next, acts, acts_next, grads, grads_next)


def add(first, *rest):
    total = first.astype(F32)
    for x in rest:
        total = total + x.astype(F32)
    return total


def gate(x, *others):
    anywhere = pl.BlockSpec(memory_space=pl.ANY)
    return pl.pallas_call(
        lambda *refs: None,
        out_shape=jax.ShapeDtypeStruct(x.shape, x.dtype),
        in_specs=[anywhere] * (1 + len(others)),
        out_specs=anywhere,
        input_output_aliases={0: 0},
        name="gate",
    )(x, *others)


def fold_kernel(me, a0, a1, a2, a3, own, ahead1, ahead2, ahead3):
    step = pl.program_id(0)
    total = add(a0[0], a1[0], a2[0], a3[0])

    @pl.when(step == 0)
    def _():
        own[...] = total

    for r, out in enumerate((ahead1, ahead2, ahead3)):

        @pl.when(step == r + 1)
        def _():
            out[...] = total.astype(BF)


def fold(me, parts):
    _, rows, width = parts[0].shape
    block = pl.BlockSpec((1, rows, width), lambda s, m: ((m[0] + s) & 3, 0, 0))
    whole = pl.BlockSpec((rows, width), lambda s, m: (0, 0))
    return pl.pallas_call(
        fold_kernel,
        out_shape=[jax.ShapeDtypeStruct((rows, width), t) for t in (F32, BF, BF, BF)],
        grid_spec=pltpu.PrefetchScalarGridSpec(
            num_scalar_prefetch=1, grid=(4,), in_specs=[block] * 4, out_specs=[whole] * 4
        ),
        compiler_params=pltpu.CompilerParams(vmem_limit_bytes=32 * 2**20),
        cost_estimate=pl.CostEstimate(
            flops=16 * rows * width, bytes_accessed=42 * rows * width, transcendentals=0
        ),
        name="fold",
    )(me, *parts)


def per_device(hidden, out_grad, left_inverse, right_inverse):
    z, y, xl, c, o = (lax.axis_index(n) for n in ("z", "y", "xl", "c", "o"))
    tokens, width = hidden.shape
    half = width // 2
    token_total = tokens * 64
    first = o == 0
    h = c ^ ((z + y) & 1)
    place = jnp.stack([o, h, z, y]).astype(jnp.int32)
    second_me = jnp.where(h == 0, y, z).astype(jnp.int32)[None]

    grads_next = shift(out_grad, "c", 1)
    acts_next = shift(hidden, "c", 1)

    own, m1, m2, m3 = cross_term(place, out_grad, grads_next, hidden, acts_next)
    m_parts = [own, turn(m1, 1, 0), turn(m2, 2, 0), turn(m3, 3, 0)]

    own, f1, f2, f3 = factor_term(place, hidden, acts_next, out_grad, grads_next)
    f_parts = [own, turn(f1, 1, 0), turn(f2, 2, 0), turn(f3, 3, 0)]

    m_parts[0] = gate(m_parts[0], own)
    m, *pieces = fold(second_me, m_parts)
    m = add(m, *[turn(piece, s, 1) for s, piece in enumerate(pieces, 1)])
    m = m.reshape(2, half // 32, half)
    mine, theirs = pick(m, 0, xl), pick(m, 0, 1 - xl)
    m_own = mine + shift(theirs, "xl", 1)
    partner = shift(mine, "o", 1) + lax.ppermute(
        theirs, ("xl", "o"), [(i, 3 - i) for i in range(4)]
    )
    swap = (h ^ o) == 0
    mrow = jnp.concatenate(
        [jnp.where(swap, m_own, partner), jnp.where(swap, partner, m_own)], axis=1
    )
    rows = mrow.shape[0]
    stacked = jnp.concatenate(split_pair(mrow))
    pt = jnp.dot(stacked, left_inverse, preferred_element_type=F32)
    pt = pt[:rows] + pt[rows:]
    pt_other = shift(pt, "o", 1)
    pt = jnp.concatenate(
        [jnp.where(first, pt, pt_other), jnp.where(first, pt_other, pt)], axis=1
    )
    blocks = pt.reshape(rows, 32, 2, rows).transpose(2, 1, 0, 3).reshape(64, rows * rows)

    f, *pieces = fold(second_me, f_parts)
    f = add(f, *[turn(piece, s, 1) for s, piece in enumerate(pieces, 1)])

    blocks = gate(blocks, pieces[0])
    blocks = lax.all_to_all(blocks, ("c", "z", "y", "xl"), 0, 0, tiled=True)
    blocks = blocks.reshape(2, 4, 4, 2, rows, rows)
    odd = ((jnp.arange(4)[:, None] + jnp.arange(4)) & 1).reshape(1, 4, 4, 1, 1, 1) == 1
    blocks = jnp.where(odd, blocks[::-1], blocks).reshape(width, rows)
    stacked = jnp.concatenate(split_pair(blocks), axis=1)
    update = contract(stacked, right_inverse)
    update = update[:rows] + update[rows:]

    f = f.reshape(2, width // 32, half)
    f = pick(f, 0, xl) + shift(pick(f, 0, 1 - xl).astype(BF), "xl", 1).astype(F32)
    f = f * jnp.where(first, 1.0 / token_total, 1.0).astype(F32)
    f = f.reshape(2, width // 64, half)
    mine = pick(f, 0, c)
    theirs = shift(pick(f, 0, 1 - c), "c", 1)
    factors = jnp.concatenate(
        [jnp.where(h == 0, mine, theirs), jnp.where(h == 0, theirs, mine)], axis=1
    )[None]
    return factors, update


def solution(mesh):
    fine = Mesh(mesh.devices.reshape(4, 4, 2, 2, 2), ("z", "y", "xl", "c", "o"))
    dp = ("z", "y", "xl", "c")
    in_specs = (P(dp, None), P(dp, None), P(None, "o"), P(None, "o"))
    out_specs = (P("o", dp, None), P(dp, "o"))
    return jax.shard_map(
        per_device, mesh=fine, in_specs=in_specs, out_specs=out_specs, check_vma=False
    )
```

```python
import functools

import jax
import jax.numpy as jnp
from jax import lax
from jax.experimental import pallas as pl
from jax.experimental.pallas import tpu as pltpu
from jax.sharding import Mesh, PartitionSpec as P

BF = jnp.bfloat16
F32 = jnp.float32
TILE = 640


def contract(first_rows, second_rows):
    return lax.dot_general(
        first_rows, second_rows, (((0,), (0,)), ((), ())), preferred_element_type=F32
    )


def shift(x, axis, step):
    size = lax.axis_size(axis)
    return lax.ppermute(x, axis, [(i, (i + step) % size) for i in range(size)])


def turn(x, step, stage):
    pairs = []
    for z in range(4):
        for y in range(4):
            for h in range(2):
                along_z = (h == 0) == (stage == 0)
                z2, y2 = ((z + step) % 4, y) if along_z else (z, (y + step) % 4)
                core, core2 = h ^ ((z + y) & 1), h ^ ((z2 + y2) & 1)
                pairs.append(((z * 4 + y) * 2 + core, (z2 * 4 + y2) * 2 + core2))
    return lax.ppermute(x, ("z", "y", "c"), pairs)


def pick(x, dim, index):
    return lax.dynamic_index_in_dim(x, index, dim, keepdims=False)


def split_pair(x):
    high = lax.reduce_precision(x, 8, 7)
    return high.astype(BF), (x - high).astype(BF)


def place_tile(place, buffer, sem, outs, m, zs, lanes):
    rows = TILE // (zs * 4)
    for a in range(zs):
        z = m * zs + a

        @pl.when(place[1] == 0)
        def _():
            for r, out in enumerate(outs):

                @pl.when(((z - place[2] + 4) & 3) == r)
                def _():
                    for k in range(4):
                        block = buffer.at[m, pl.ds((a * 4 + k) * rows, rows), lanes]
                        pltpu.make_async_copy(block, out.at[k], sem).start()

        @pl.when(place[1] == 1)
        def _():
            for r, out in enumerate(outs):
                at = pl.multiple_of((a * 4 + ((place[3] + r) & 3)) * rows, 16)
                block = buffer.at[m, pl.ds(at, rows), lanes]
                pltpu.make_async_copy(block, out.at[z], sem).start()


def wait_tiles(buffer, sem):
    pltpu.make_async_copy(buffer, buffer, sem).wait()


def own_kernel(place, a, b, out):
    out[...] = contract(a[...], b[...])


def cross_kernel(place, a, b, partial, own, ahead1, ahead2, ahead3, buffer, sem):
    m, n = pl.program_id(0), pl.program_id(1)
    tile = (partial[...] + contract(a[...], b[...])).astype(BF)
    for lane in range(2):

        @pl.when(n == lane)
        def _():
            buffer[m, :, lane * TILE : (lane + 1) * TILE] = tile

    @pl.when(n == 1)
    def _():
        place_tile(place, buffer, sem, [own, ahead1, ahead2, ahead3], m, 2, slice(None))

    @pl.when((m == 1) & (n == 1))
    def _():
        wait_tiles(buffer, sem)


def cross_term(place, grads, grads_next, acts, acts_next):
    tokens, width = grads.shape
    half = width // 2
    left = pl.BlockSpec((tokens, TILE), lambda m, n, p: (0, p[1] * 2 + m))
    right = pl.BlockSpec((tokens, TILE), lambda m, n, p: (0, (p[1] ^ p[0]) * 2 + n))
    middle = pl.BlockSpec((TILE, TILE), lambda m, n, p: (m, n))
    params = pltpu.CompilerParams(vmem_limit_bytes=48 * 2**20)
    cost = pl.CostEstimate(
        flops=2 * tokens * half * half, bytes_accessed=10 * tokens * half, transcendentals=0
    )
    partial = pl.pallas_call(
        own_kernel,
        out_shape=jax.ShapeDtypeStruct((half, half), F32),
        grid_spec=pltpu.PrefetchScalarGridSpec(
            num_scalar_prefetch=1, grid=(2, 2), in_specs=[left, right], out_specs=middle
        ),
        compiler_params=params,
        cost_estimate=cost,
        name="cross_own",
    )(place, grads, acts)
    out = jax.ShapeDtypeStruct((4, half // 16, half), BF)
    return pl.pallas_call(
        cross_kernel,
        out_shape=[out] * 4,
        grid_spec=pltpu.PrefetchScalarGridSpec(
            num_scalar_prefetch=1,
            grid=(2, 2),
            in_specs=[left, right, middle],
            out_specs=[pl.BlockSpec(memory_space=pl.ANY)] * 4,
            scratch_shapes=[pltpu.VMEM((2, TILE, half), BF), pltpu.SemaphoreType.DMA],
        ),
        compiler_params=params,
        cost_estimate=cost,
        name="cross_term",
    )(place, grads_next, acts_next, partial)


def factor_kernel(place, h0, h1, g0, g1, *rest):
    outs, (lhs, rhs, buffer, lhs_sems, rhs_sem, sem) = rest[:8], rest[8:]
    m = pl.program_id(0)
    half = rhs.shape[2]

    def fetch(step, first):
        at = pl.ds(pl.multiple_of(step * TILE, TILE), TILE)
        right = pl.ds(pl.multiple_of(place[1] * half, half), half)
        for owner, refs in enumerate(((h0, h1), (g0, g1))):

            @pl.when(place[0] == owner)
            def _():
                for k, ref in enumerate(refs):
                    if first:
                        pltpu.make_async_copy(ref.at[:, right], rhs.at[k], rhs_sem).start()
                    slot = step & 1
                    pltpu.make_async_copy(ref.at[:, at], lhs.at[slot, k], lhs_sems.at[slot]).start()

    pl.when(m == 0)(lambda: fetch(0, True))
    pl.when(m < 3)(lambda: fetch(m + 1, False))
    slot = m & 1
    pltpu.make_async_copy(lhs.at[slot], lhs.at[slot], lhs_sems.at[slot]).wait()
    pl.when(m == 0)(lambda: pltpu.make_async_copy(rhs, rhs, rhs_sem).wait())

    buffer[m] = (contract(lhs[slot, 0], rhs[0]) + contract(lhs[slot, 1], rhs[1])).astype(BF)
    for part in range(2):
        lanes = slice(part * TILE, (part + 1) * TILE)
        place_tile(place, buffer, sem, outs[part * 4 : part * 4 + 4], m, 1, lanes)
    pl.when(m == 3)(lambda: wait_tiles(buffer, sem))


def factor_term(place, acts, acts_next, grads, grads_next):
    tokens, width = acts.shape
    half = width // 2
    anywhere = pl.BlockSpec(memory_space=pl.ANY)
    out = jax.ShapeDtypeStruct((4, width // 16, TILE), BF)
    outs = pl.pallas_call(
        factor_kernel,
        out_shape=[out] * 8,
        grid_spec=pltpu.PrefetchScalarGridSpec(
            num_scalar_prefetch=1,
            grid=(4,),
            in_specs=[anywhere] * 4,
            out_specs=[anywhere] * 8,
            scratch_shapes=[
                pltpu.VMEM((2, 2, tokens, TILE), BF),
                pltpu.VMEM((2, tokens, half), BF),
                pltpu.VMEM((4, TILE, half), BF),
                pltpu.SemaphoreType.DMA((2,)),
                pltpu.SemaphoreType.DMA,
                pltpu.SemaphoreType.DMA,
            ],
        ),
        compiler_params=pltpu.CompilerParams(vmem_limit_bytes=40 * 2**20),
        cost_estimate=pl.CostEstimate(
            flops=4 * tokens * width * half, bytes_accessed=16 * tokens * half, transcendentals=0
        ),
        name="factor_term",
    )(place, acts, acts_next, grads, grads_next)
    return outs[:4], outs[4:]


def add(first, *rest):
    total = first.astype(F32)
    for x in rest:
        total = total + x.astype(F32)
    return total


def gate(x, *others):
    anywhere = pl.BlockSpec(memory_space=pl.ANY)
    return pl.pallas_call(
        lambda *refs: None,
        out_shape=jax.ShapeDtypeStruct(x.shape, x.dtype),
        in_specs=[anywhere] * (1 + len(others)),
        out_specs=anywhere,
        input_output_aliases={0: 0},
        name="gate",
    )(x, *others)


def fold_kernel(me, a0, a1, a2, a3, own, ahead1, ahead2, ahead3):
    step = pl.program_id(0)
    total = add(a0[0], a1[0], a2[0], a3[0])

    @pl.when(step == 0)
    def _():
        own[...] = total

    for r, out in enumerate((ahead1, ahead2, ahead3)):

        @pl.when(step == r + 1)
        def _():
            out[...] = total.astype(BF)


def fold(me, parts):
    _, rows, width = parts[0].shape
    block = pl.BlockSpec((1, rows, width), lambda s, m: ((m[0] + s) & 3, 0, 0))
    whole = pl.BlockSpec((rows, width), lambda s, m: (0, 0))
    return pl.pallas_call(
        fold_kernel,
        out_shape=[jax.ShapeDtypeStruct((rows, width), t) for t in (F32, BF, BF, BF)],
        grid_spec=pltpu.PrefetchScalarGridSpec(
            num_scalar_prefetch=1, grid=(4,), in_specs=[block] * 4, out_specs=[whole] * 4
        ),
        compiler_params=pltpu.CompilerParams(vmem_limit_bytes=32 * 2**20),
        cost_estimate=pl.CostEstimate(
            flops=16 * rows * width, bytes_accessed=42 * rows * width, transcendentals=0
        ),
        name="fold",
    )(me, *parts)


def per_device(hidden, out_grad, left_inverse, right_inverse):
    z, y, xl, c, o = (lax.axis_index(n) for n in ("z", "y", "xl", "c", "o"))
    tokens, width = hidden.shape
    half = width // 2
    token_total = tokens * 64
    first = o == 0
    h = c ^ ((z + y) & 1)
    place = jnp.stack([o, h, z, y]).astype(jnp.int32)
    second_me = jnp.where(h == 0, y, z).astype(jnp.int32)[None]

    grads_next = shift(out_grad, "c", 1)
    acts_next = shift(hidden, "c", 1)

    own, m1, m2, m3 = cross_term(place, out_grad, grads_next, hidden, acts_next)
    m_parts = [own, turn(m1, 1, 0), turn(m2, 2, 0), turn(m3, 3, 0)]

    f_terms = factor_term(place, hidden, acts_next, out_grad, grads_next)
    f_parts = [[term[0]] + [turn(term[s], s, 0) for s in (1, 2, 3)] for term in f_terms]

    def second_round(parts):
        total, *pieces = fold(second_me, parts)
        return pieces[0], add(total, *[turn(piece, s, 1) for s, piece in enumerate(pieces, 1)])

    m_parts[0] = gate(m_parts[0], f_terms[0][0])
    _, m = second_round(m_parts)
    early, f_early = second_round(f_parts[0])
    m = m.reshape(2, half // 32, half)
    mine, theirs = pick(m, 0, xl), pick(m, 0, 1 - xl)
    m_own = mine + shift(theirs, "xl", 1)
    partner = shift(mine, "o", 1) + lax.ppermute(
        theirs, ("xl", "o"), [(i, 3 - i) for i in range(4)]
    )
    swap = (h ^ o) == 0
    mrow = jnp.concatenate(
        [jnp.where(swap, m_own, partner), jnp.where(swap, partner, m_own)], axis=1
    )
    rows = mrow.shape[0]
    stacked = jnp.concatenate(split_pair(gate(mrow, early)))
    pt = jnp.dot(stacked, left_inverse, preferred_element_type=F32)
    pt = pt[:rows] + pt[rows:]
    pt_other = shift(pt, "o", 1)
    pt = jnp.concatenate(
        [jnp.where(first, pt, pt_other), jnp.where(first, pt_other, pt)], axis=1
    )
    blocks = pt.reshape(rows, 32, 2, rows).transpose(2, 1, 0, 3).reshape(64, rows, rows)

    late, f_late = second_round(f_parts[1])
    blocks = gate(blocks, late)
    blocks = lax.all_to_all(blocks, ("c", "z", "y", "xl"), 0, 0, tiled=True)
    blocks = blocks.reshape(2, 4, 4, 2, rows, rows)
    odd = ((jnp.arange(4)[:, None] + jnp.arange(4)) & 1).reshape(1, 4, 4, 1, 1, 1) == 1
    blocks = jnp.where(odd, blocks[::-1], blocks).reshape(width, rows)
    stacked = jnp.concatenate(split_pair(blocks), axis=1)
    update = contract(stacked, right_inverse)
    update = update[:rows] + update[rows:]

    f = jnp.concatenate([f_early, f_late], axis=1).reshape(2, width // 32, half)
    f = pick(f, 0, xl) + shift(pick(f, 0, 1 - xl).astype(BF), "xl", 1).astype(F32)
    f = f * jnp.where(first, 1.0 / token_total, 1.0).astype(F32)
    f = f.reshape(2, width // 64, half)
    mine = pick(f, 0, c)
    theirs = shift(pick(f, 0, 1 - c), "c", 1)
    factors = jnp.concatenate(
        [jnp.where(h == 0, mine, theirs), jnp.where(h == 0, theirs, mine)], axis=1
    )[None]
    return factors, update


def solution(mesh):
    fine = Mesh(mesh.devices.reshape(4, 4, 2, 2, 2), ("z", "y", "xl", "c", "o"))
    dp = ("z", "y", "xl", "c")
    in_specs = (P(dp, None), P(dp, None), P(None, "o"), P(None, "o"))
    out_specs = (P("o", dp, None), P(dp, "o"))
    return jax.shard_map(
        per_device, mesh=fine, in_specs=in_specs, out_specs=out_specs, check_vma=False
    )
```

```python
import functools

import jax
import jax.numpy as jnp
from jax import lax
from jax.experimental import pallas as pl
from jax.experimental.pallas import tpu as pltpu
from jax.sharding import Mesh, PartitionSpec as P

BF = jnp.bfloat16
F32 = jnp.float32
TILE = 640


def contract(first_rows, second_rows):
    return lax.dot_general(
        first_rows, second_rows, (((0,), (0,)), ((), ())), preferred_element_type=F32
    )


def shift(x, axis, step):
    size = lax.axis_size(axis)
    return lax.ppermute(x, axis, [(i, (i + step) % size) for i in range(size)])


def turn(x, step, stage):
    pairs = []
    for z in range(4):
        for y in range(4):
            for h in range(2):
                along_z = (h == 0) == (stage == 0)
                z2, y2 = ((z + step) % 4, y) if along_z else (z, (y + step) % 4)
                core, core2 = h ^ ((z + y) & 1), h ^ ((z2 + y2) & 1)
                pairs.append(((z * 4 + y) * 2 + core, (z2 * 4 + y2) * 2 + core2))
    return lax.ppermute(x, ("z", "y", "c"), pairs)


def pick(x, dim, index):
    return lax.dynamic_index_in_dim(x, index, dim, keepdims=False)


def split_pair(x):
    high = lax.reduce_precision(x, 8, 7)
    return high.astype(BF), (x - high).astype(BF)


def place_tile(place, buffer, sem, outs, m, zs):
    rows = TILE // (zs * 4)

    def start(at, out, slot):
        block = buffer.at[m, pl.ds(at, rows)]
        pltpu.make_async_copy(block, out.at[slot], sem).start()

    for a in range(zs):
        z = m * zs + a

        @pl.when(place[1] == 0)
        def _():
            for r, out in enumerate(outs):

                @pl.when(((z - place[2] + 4) & 3) == r)
                def _():
                    for k in range(4):
                        if isinstance(out, tuple):
                            start((a * 4 + k) * rows, out[k // 2], k % 2)
                        else:
                            start((a * 4 + k) * rows, out, k)

        @pl.when(place[1] == 1)
        def _():
            for r, out in enumerate(outs):
                at = pl.multiple_of((a * 4 + ((place[3] + r) & 3)) * rows, 16)
                if isinstance(out, tuple):
                    pl.when(z < 2)(functools.partial(start, at, out[0], z & 1))
                    pl.when(z >= 2)(functools.partial(start, at, out[1], z & 1))
                else:
                    start(at, out, z)


def wait_all(buffer, sem):
    pltpu.make_async_copy(buffer, buffer, sem).wait()


def own_kernel(place, a, b, out):
    out[...] = contract(a[...], b[...])


def cross_kernel(place, a, b, partial, own, ahead1, ahead2, ahead3, held, buffer, held_sems, sem):
    m = pl.program_id(0)

    @pl.when(m == 0)
    def _():
        for k in range(2):
            rows = partial.at[pl.ds(k * TILE, TILE)]
            pltpu.make_async_copy(rows, held.at[k], held_sems.at[k]).start()

    tile = contract(a[...], b[...])
    wait_all(held.at[m], held_sems.at[m])
    buffer[m] = (held[m] + tile).astype(BF)
    place_tile(place, buffer, sem, [own, ahead1, ahead2, ahead3], m, 2)
    pl.when(m == 1)(lambda: wait_all(buffer, sem))


def cross_term(place, grads, grads_next, acts, acts_next):
    tokens, half = grads_next.shape
    anywhere = pl.BlockSpec(memory_space=pl.ANY)
    cost = pl.CostEstimate(
        flops=2 * tokens * half * half, bytes_accessed=10 * tokens * half, transcendentals=0
    )
    partial = pl.pallas_call(
        own_kernel,
        out_shape=jax.ShapeDtypeStruct((half, half), F32),
        grid_spec=pltpu.PrefetchScalarGridSpec(
            num_scalar_prefetch=1,
            grid=(2,),
            in_specs=[
                pl.BlockSpec((tokens, TILE), lambda m, p: (0, p[1] * 2 + m)),
                pl.BlockSpec((tokens, half), lambda m, p: (0, p[1] ^ p[0])),
            ],
            out_specs=pl.BlockSpec((TILE, half), lambda m, p: (m, 0)),
        ),
        compiler_params=pltpu.CompilerParams(vmem_limit_bytes=32 * 2**20),
        cost_estimate=cost,
        name="cross_own",
    )(place, grads, acts)
    out = jax.ShapeDtypeStruct((4, half // 16, half), BF)
    return pl.pallas_call(
        cross_kernel,
        out_shape=[out] * 4,
        grid_spec=pltpu.PrefetchScalarGridSpec(
            num_scalar_prefetch=1,
            grid=(2,),
            in_specs=[
                pl.BlockSpec((tokens, TILE), lambda m, p: (0, m)),
                pl.BlockSpec((tokens, half), lambda m, p: (0, 0)),
                anywhere,
            ],
            out_specs=[anywhere] * 4,
            scratch_shapes=[
                pltpu.VMEM((2, TILE, half), F32),
                pltpu.VMEM((2, TILE, half), BF),
                pltpu.SemaphoreType.DMA((2,)),
                pltpu.SemaphoreType.DMA,
            ],
        ),
        compiler_params=pltpu.CompilerParams(vmem_limit_bytes=32 * 2**20),
        cost_estimate=cost,
        name="cross_term",
    )(place, grads_next, acts_next, partial)


def factor_kernel(place, h_own, g_own, h_next, g_next, x_next, *rest):
    own, right, far_a, far_b, left, lhs, rhs, buffer, lhs_sems, rhs_sem, sem = rest
    m = pl.program_id(0)
    half = rhs.shape[2]

    def lanes(step, wide):
        return pl.ds(pl.multiple_of(step * wide, wide), wide)

    def fetch(step, with_rhs):
        slot = step & 1

        def left_block(ref, k, at):
            pltpu.make_async_copy(ref.at[:, lanes(at, TILE)], lhs.at[slot, k], lhs_sems.at[slot]).start()

        for owner, (mine, theirs) in enumerate(((h_own, h_next), (g_own, g_next))):

            @pl.when(place[0] == owner)
            def _():
                left_block(mine, 0, step)
                pl.when((step >> 1) == place[1])(lambda: left_block(theirs, 1, step & 1))
                if with_rhs:
                    at = lanes(place[1], half)
                    pltpu.make_async_copy(mine.at[:, at], rhs.at[0], rhs_sem).start()
                    pltpu.make_async_copy(theirs, rhs.at[1], rhs_sem).start()

        pl.when((step >> 1) != place[1])(lambda: left_block(x_next, 1, step & 1))

    pl.when(m == 0)(lambda: fetch(0, True))
    pl.when(m < 3)(lambda: fetch(m + 1, False))
    slot = m & 1
    wait_all(lhs.at[slot], lhs_sems.at[slot])
    pl.when(m == 0)(lambda: wait_all(rhs, rhs_sem))

    buffer[m] = (contract(lhs[slot, 0], rhs[0]) + contract(lhs[slot, 1], rhs[1])).astype(BF)
    place_tile(place, buffer, sem, [own, right, (far_a, far_b), left], m, 1)
    pl.when(m == 3)(lambda: wait_all(buffer, sem))


def factor_term(place, acts, grads, acts_next, grads_next, rest_next):
    tokens, width = acts.shape
    half = width // 2
    anywhere = pl.BlockSpec(memory_space=pl.ANY)
    out = jax.ShapeDtypeStruct((4, width // 16, half), BF)
    side = jax.ShapeDtypeStruct((2, width // 16, half), BF)
    return pl.pallas_call(
        factor_kernel,
        out_shape=[out, out, side, side, out],
        grid_spec=pltpu.PrefetchScalarGridSpec(
            num_scalar_prefetch=1,
            grid=(4,),
            in_specs=[anywhere] * 5,
            out_specs=[anywhere] * 5,
            scratch_shapes=[
                pltpu.VMEM((2, 2, tokens, TILE), BF),
                pltpu.VMEM((2, tokens, half), BF),
                pltpu.VMEM((4, TILE, half), BF),
                pltpu.SemaphoreType.DMA((2,)),
                pltpu.SemaphoreType.DMA,
                pltpu.SemaphoreType.DMA,
            ],
        ),
        compiler_params=pltpu.CompilerParams(vmem_limit_bytes=40 * 2**20),
        cost_estimate=pl.CostEstimate(
            flops=4 * tokens * width * half, bytes_accessed=16 * tokens * half, transcendentals=0
        ),
        name="factor_term",
    )(place, acts, grads, acts_next, grads_next, rest_next)


def add(first, *rest):
    total = first.astype(F32)
    for x in rest:
        total = total + x.astype(F32)
    return total


def gate(x, *others):
    anywhere = pl.BlockSpec(memory_space=pl.ANY)
    return pl.pallas_call(
        lambda *refs: None,
        out_shape=jax.ShapeDtypeStruct(x.shape, x.dtype),
        in_specs=[anywhere] * (1 + len(others)),
        out_specs=anywhere,
        input_output_aliases={0: 0},
        name="gate",
    )(x, *others)


def fold_kernel(me, *refs):
    parts, (own, *others) = refs[:-4], refs[-4:]
    step = pl.program_id(0)
    total = add(*[part[0] for part in parts])

    @pl.when(step == 0)
    def _():
        own[...] = total

    for r, out in enumerate(others):

        @pl.when(step == r + 1)
        def _():
            out[...] = total.astype(BF)


def fold(me, parts):
    _, rows, width = parts[0].shape
    block = pl.BlockSpec((1, rows, width), lambda s, m: ((m[0] + s) & 3, 0, 0))
    whole = pl.BlockSpec((rows, width), lambda s, m: (0, 0))
    return pl.pallas_call(
        fold_kernel,
        out_shape=[jax.ShapeDtypeStruct((rows, width), t) for t in (F32, BF, BF, BF)],
        grid_spec=pltpu.PrefetchScalarGridSpec(
            num_scalar_prefetch=1, grid=(4,), in_specs=[block] * len(parts), out_specs=[whole] * 4
        ),
        compiler_params=pltpu.CompilerParams(vmem_limit_bytes=32 * 2**20),
        cost_estimate=pl.CostEstimate(
            flops=16 * rows * width, bytes_accessed=42 * rows * width, transcendentals=0
        ),
        name="fold",
    )(me, *parts)


def per_device(hidden, out_grad, left_inverse, right_inverse):
    z, y, xl, c, o = (lax.axis_index(n) for n in ("z", "y", "xl", "c", "o"))
    tokens, width = hidden.shape
    half = width // 2
    token_total = tokens * 64
    first = o == 0
    h = c ^ ((z + y) & 1)
    place = jnp.stack([o, h, z, y]).astype(jnp.int32)
    second_me = jnp.where(h == 0, y, z).astype(jnp.int32)[None]

    def columns(x, index):
        return lax.dynamic_slice_in_dim(x, index * half, half, 1)

    grads_next = shift(columns(out_grad, 1 - h), "c", 1)
    acts_next = shift(columns(hidden, (1 - h) ^ o), "c", 1)
    rest_next = shift(jnp.where(first, columns(hidden, h), columns(out_grad, h)), "c", 1)

    own, m1, m2, m3 = cross_term(place, out_grad, grads_next, hidden, acts_next)
    m_parts = [own, turn(m1, 1, 0), turn(m2, 2, 0), turn(m3, 3, 0)]

    f_own, right, far_a, far_b, left = factor_term(
        place, hidden, out_grad, acts_next, grads_next, rest_next
    )

    def second_round(parts):
        total, *pieces = fold(second_me, parts)
        return pieces[0], add(total, *[turn(piece, s, 1) for s, piece in enumerate(pieces, 1)])

    m_parts[0] = gate(m_parts[0], f_own)
    from_left, from_right = turn(far_a, 1, 0), turn(far_b, -1, 0)
    right = jnp.concatenate([add(right[:2], from_left).astype(BF), right[2:]])
    left = jnp.concatenate([left[:2], add(left[2:], from_right).astype(BF)])
    f_parts = [f_own, turn(right, 1, 0), turn(left, -1, 0)]

    _, m = second_round(m_parts)
    m = m.reshape(2, half // 32, half)
    mine, theirs = pick(m, 0, xl), pick(m, 0, 1 - xl)
    m_own = mine + shift(theirs, "xl", 1)
    partner = shift(mine, "o", 1) + lax.ppermute(
        theirs, ("xl", "o"), [(i, 3 - i) for i in range(4)]
    )
    swap = (h ^ o) == 0
    mrow = jnp.concatenate(
        [jnp.where(swap, m_own, partner), jnp.where(swap, partner, m_own)], axis=1
    )
    rows = mrow.shape[0]
    stacked = jnp.concatenate(split_pair(mrow))
    pt = jnp.dot(stacked, left_inverse, preferred_element_type=F32)
    pt = pt[:rows] + pt[rows:]
    blocks = pt.reshape(rows, 2, 4, 2, 2, rows).transpose(4, 1, 2, 3, 0, 5)
    blocks = jnp.broadcast_to(blocks[None, :, None], (2, 2, 2, 2, 4, 2, rows, rows))
    blocks = lax.all_to_all(
        blocks.reshape(128, rows, rows), ("o", "c", "z", "y", "xl"), 0, 0, tiled=True
    )

    late, f = second_round(f_parts)
    blocks = pick(blocks.reshape(2, 64, rows, rows), 0, z >> 1)
    blocks = gate(blocks, late)
    blocks = blocks.reshape(2, 4, 4, 2, rows, rows)
    odd = ((jnp.arange(4)[:, None] + jnp.arange(4)) & 1).reshape(1, 4, 4, 1, 1, 1) == 1
    blocks = jnp.where(odd, blocks[::-1], blocks).reshape(width, rows)
    stacked = jnp.concatenate(split_pair(blocks), axis=1)
    update = contract(stacked, right_inverse)
    update = update[:rows] + update[rows:]

    f = f.reshape(2, width // 32, half)
    f = pick(f, 0, xl) + shift(pick(f, 0, 1 - xl).astype(BF), "xl", 1).astype(F32)
    f = f * jnp.where(first, 1.0 / token_total, 1.0).astype(F32)
    f = f.reshape(2, width // 64, half)
    mine = pick(f, 0, c)
    theirs = shift(pick(f, 0, 1 - c), "c", 1)
    factors = jnp.concatenate(
        [jnp.where(h == 0, mine, theirs), jnp.where(h == 0, theirs, mine)], axis=1
    )[None]
    return factors, update


def solution(mesh):
    fine = Mesh(mesh.devices.reshape(4, 4, 2, 2, 2), ("z", "y", "xl", "c", "o"))
    dp = ("z", "y", "xl", "c")
    in_specs = (P(dp, None), P(dp, None), P(None, "o"), P(None, "o"))
    out_specs = (P("o", dp, None), P(dp, "o"))
    return jax.shard_map(
        per_device, mesh=fine, in_specs=in_specs, out_specs=out_specs, check_vma=False
    )
```

```python
import functools

import jax
import jax.numpy as jnp
from jax import lax
from jax.experimental import pallas as pl
from jax.experimental.pallas import tpu as pltpu
from jax.sharding import Mesh, PartitionSpec as P

BF = jnp.bfloat16
F32 = jnp.float32
TILE = 640


def contract(first_rows, second_rows):
    return lax.dot_general(
        first_rows, second_rows, (((0,), (0,)), ((), ())), preferred_element_type=F32
    )


def shift(x, axis, step):
    size = lax.axis_size(axis)
    return lax.ppermute(x, axis, [(i, (i + step) % size) for i in range(size)])


def turn(x, step, stage):
    pairs = []
    for z in range(4):
        for y in range(4):
            for h in range(2):
                along_z = (h == 0) == (stage == 0)
                z2, y2 = ((z + step) % 4, y) if along_z else (z, (y + step) % 4)
                core, core2 = h ^ ((z + y) & 1), h ^ ((z2 + y2) & 1)
                pairs.append(((z * 4 + y) * 2 + core, (z2 * 4 + y2) * 2 + core2))
    return lax.ppermute(x, ("z", "y", "c"), pairs)


def pick(x, dim, index):
    return lax.dynamic_index_in_dim(x, index, dim, keepdims=False)


def split_pair(x):
    high = x.astype(BF)
    return high, (x - high.astype(F32)).astype(BF)


def place_tile(place, buffer, sem, outs, m, zs):
    rows = TILE // (zs * 4)

    def start(at, out, slot):
        block = buffer.at[m, pl.ds(at, rows)]
        pltpu.make_async_copy(block, out.at[slot], sem).start()

    for a in range(zs):
        z = m * zs + a

        @pl.when(place[1] == 0)
        def _():
            for r, out in enumerate(outs):

                @pl.when(((z - place[2] + 4) & 3) == r)
                def _():
                    for k in range(4):
                        if isinstance(out, tuple):
                            start((a * 4 + k) * rows, out[k // 2], k % 2)
                        else:
                            start((a * 4 + k) * rows, out, k)

        @pl.when(place[1] == 1)
        def _():
            for r, out in enumerate(outs):
                at = pl.multiple_of((a * 4 + ((place[3] + r) & 3)) * rows, 16)
                if isinstance(out, tuple):
                    pl.when(z < 2)(functools.partial(start, at, out[0], z & 1))
                    pl.when(z >= 2)(functools.partial(start, at, out[1], z & 1))
                else:
                    start(at, out, z)


def wait_all(buffer, sem):
    pltpu.make_async_copy(buffer, buffer, sem).wait()


def own_kernel(place, a, b, out):
    out[...] = contract(a[...], b[...])


def cross_kernel(place, a, b, partial, own, ahead1, ahead2, ahead3, held, buffer, held_sems, sem):
    m = pl.program_id(0)

    @pl.when(m == 0)
    def _():
        for k in range(2):
            rows = partial.at[pl.ds(k * TILE, TILE)]
            pltpu.make_async_copy(rows, held.at[k], held_sems.at[k]).start()

    tile = contract(a[...], b[...])
    wait_all(held.at[m], held_sems.at[m])
    buffer[m] = (held[m] + tile).astype(BF)
    place_tile(place, buffer, sem, [own, ahead1, ahead2, ahead3], m, 2)
    pl.when(m == 1)(lambda: wait_all(buffer, sem))


def cross_term(place, grads, grads_next, acts, acts_next):
    tokens, half = grads_next.shape
    anywhere = pl.BlockSpec(memory_space=pl.ANY)
    cost = pl.CostEstimate(
        flops=2 * tokens * half * half, bytes_accessed=10 * tokens * half, transcendentals=0
    )
    partial = pl.pallas_call(
        own_kernel,
        out_shape=jax.ShapeDtypeStruct((half, half), F32),
        grid_spec=pltpu.PrefetchScalarGridSpec(
            num_scalar_prefetch=1,
            grid=(2,),
            in_specs=[
                pl.BlockSpec((tokens, TILE), lambda m, p: (0, p[1] * 2 + m)),
                pl.BlockSpec((tokens, half), lambda m, p: (0, p[1] ^ p[0])),
            ],
            out_specs=pl.BlockSpec((TILE, half), lambda m, p: (m, 0)),
        ),
        compiler_params=pltpu.CompilerParams(vmem_limit_bytes=28 * 2**20),
        cost_estimate=cost,
        name="cross_own",
    )(place, grads, acts)
    out = jax.ShapeDtypeStruct((4, half // 16, half), BF)
    return pl.pallas_call(
        cross_kernel,
        out_shape=[out] * 4,
        grid_spec=pltpu.PrefetchScalarGridSpec(
            num_scalar_prefetch=1,
            grid=(2,),
            in_specs=[
                pl.BlockSpec((tokens, TILE), lambda m, p: (0, m)),
                pl.BlockSpec((tokens, half), lambda m, p: (0, 0)),
                anywhere,
            ],
            out_specs=[anywhere] * 4,
            scratch_shapes=[
                pltpu.VMEM((2, TILE, half), F32),
                pltpu.VMEM((2, TILE, half), BF),
                pltpu.SemaphoreType.DMA((2,)),
                pltpu.SemaphoreType.DMA,
            ],
        ),
        compiler_params=pltpu.CompilerParams(vmem_limit_bytes=28 * 2**20),
        cost_estimate=cost,
        name="cross_term",
    )(place, grads_next, acts_next, partial)


def factor_kernel(place, h_own, g_own, h_next, g_next, x_next, after, *rest):
    del after
    own, right, far_a, far_b, left, lhs, rhs, buffer, lhs_sems, rhs_sem, sem = rest
    m = pl.program_id(0)
    half = rhs.shape[2]

    def lanes(step, wide):
        return pl.ds(pl.multiple_of(step * wide, wide), wide)

    def fetch(step, with_rhs):
        slot = step & 1

        def left_block(ref, k, at):
            pltpu.make_async_copy(ref.at[:, lanes(at, TILE)], lhs.at[slot, k], lhs_sems.at[slot]).start()

        for owner, (mine, theirs) in enumerate(((h_own, h_next), (g_own, g_next))):

            @pl.when(place[0] == owner)
            def _():
                left_block(mine, 0, step)
                pl.when((step >> 1) == place[1])(lambda: left_block(theirs, 1, step & 1))
                if with_rhs:
                    at = lanes(place[1], half)
                    pltpu.make_async_copy(mine.at[:, at], rhs.at[0], rhs_sem).start()
                    pltpu.make_async_copy(theirs, rhs.at[1], rhs_sem).start()

        pl.when((step >> 1) != place[1])(lambda: left_block(x_next, 1, step & 1))

    pl.when(m == 0)(lambda: fetch(0, True))
    pl.when(m < 3)(lambda: fetch(m + 1, False))
    slot = m & 1
    wait_all(lhs.at[slot], lhs_sems.at[slot])
    pl.when(m == 0)(lambda: wait_all(rhs, rhs_sem))

    buffer[m] = (contract(lhs[slot, 0], rhs[0]) + contract(lhs[slot, 1], rhs[1])).astype(BF)
    place_tile(place, buffer, sem, [own, right, (far_a, far_b), left], m, 1)
    pl.when(m == 3)(lambda: wait_all(buffer, sem))


def factor_term(place, acts, grads, acts_next, grads_next, rest_next, after):
    tokens, width = acts.shape
    half = width // 2
    anywhere = pl.BlockSpec(memory_space=pl.ANY)
    out = jax.ShapeDtypeStruct((4, width // 16, half), BF)
    side = jax.ShapeDtypeStruct((2, width // 16, half), BF)
    return pl.pallas_call(
        factor_kernel,
        out_shape=[out, out, side, side, out],
        grid_spec=pltpu.PrefetchScalarGridSpec(
            num_scalar_prefetch=1,
            grid=(4,),
            in_specs=[anywhere] * 6,
            out_specs=[anywhere] * 5,
            scratch_shapes=[
                pltpu.VMEM((2, 2, tokens, TILE), BF),
                pltpu.VMEM((2, tokens, half), BF),
                pltpu.VMEM((4, TILE, half), BF),
                pltpu.SemaphoreType.DMA((2,)),
                pltpu.SemaphoreType.DMA,
                pltpu.SemaphoreType.DMA,
            ],
        ),
        compiler_params=pltpu.CompilerParams(vmem_limit_bytes=30 * 2**20),
        cost_estimate=pl.CostEstimate(
            flops=4 * tokens * width * half, bytes_accessed=16 * tokens * half, transcendentals=0
        ),
        name="factor_term",
    )(place, acts, grads, acts_next, grads_next, rest_next, after)


def add(first, *rest):
    total = first.astype(F32)
    for x in rest:
        total = total + x.astype(F32)
    return total


def gate(x, *others):
    anywhere = pl.BlockSpec(memory_space=pl.ANY)
    return pl.pallas_call(
        lambda *refs: None,
        out_shape=jax.ShapeDtypeStruct(x.shape, x.dtype),
        in_specs=[anywhere] * (1 + len(others)),
        out_specs=anywhere,
        input_output_aliases={0: 0},
        compiler_params=pltpu.CompilerParams(vmem_limit_bytes=2**20),
        cost_estimate=pl.CostEstimate(flops=0, bytes_accessed=0, transcendentals=0),
        name="gate",
    )(x, *others)


def fold_kernel(me, *refs):
    parts, (own, *others) = refs[:-4], refs[-4:]
    step = pl.program_id(0)
    total = add(*[part[0] for part in parts])

    @pl.when(step == 0)
    def _():
        own[...] = total

    for r, out in enumerate(others):

        @pl.when(step == r + 1)
        def _():
            out[...] = total.astype(BF)


def fold(me, parts):
    _, rows, width = parts[0].shape
    block = pl.BlockSpec((1, rows, width), lambda s, m: ((m[0] + s) & 3, 0, 0))
    whole = pl.BlockSpec((rows, width), lambda s, m: (0, 0))
    return pl.pallas_call(
        fold_kernel,
        out_shape=[jax.ShapeDtypeStruct((rows, width), t) for t in (F32, BF, BF, BF)],
        grid_spec=pltpu.PrefetchScalarGridSpec(
            num_scalar_prefetch=1, grid=(4,), in_specs=[block] * len(parts), out_specs=[whole] * 4
        ),
        compiler_params=pltpu.CompilerParams(vmem_limit_bytes=14 * 2**20),
        cost_estimate=pl.CostEstimate(
            flops=16 * rows * width, bytes_accessed=42 * rows * width, transcendentals=0
        ),
        name="fold",
    )(me, *parts)


def cut_kernel(place, a, b, out):
    pl.when(place[0] == 0)(lambda: out.__setitem__(..., a[...]))
    pl.when(place[0] == 1)(lambda: out.__setitem__(..., b[...]))


def cut(place, a, b, index):
    tokens, width = a.shape
    block = (tokens // 4, width // 2)
    return pl.pallas_call(
        cut_kernel,
        out_shape=jax.ShapeDtypeStruct((tokens, width // 2), a.dtype),
        grid_spec=pltpu.PrefetchScalarGridSpec(
            num_scalar_prefetch=1,
            grid=(4,),
            in_specs=[
                pl.BlockSpec(block, lambda m, p: (m * (1 - p[0]), index(p))),
                pl.BlockSpec(block, lambda m, p: (m * p[0], index(p))),
            ],
            out_specs=pl.BlockSpec(block, lambda m, p: (m, 0)),
        ),
        compiler_params=pltpu.CompilerParams(vmem_limit_bytes=8 * 2**20),
        cost_estimate=pl.CostEstimate(flops=0, bytes_accessed=2 * tokens * width, transcendentals=0),
        name="cut",
    )(place, a, b)


def grow_kernel(x, received, out):
    out[...] = add(x[...], received[...]).astype(BF)


def grow(x, received, side):
    block = pl.BlockSpec((1,) + x.shape[1:], lambda s: (side * 2 + s, 0, 0))
    return pl.pallas_call(
        grow_kernel,
        out_shape=jax.ShapeDtypeStruct(x.shape, x.dtype),
        grid=(2,),
        in_specs=[block, pl.BlockSpec((1,) + x.shape[1:], lambda s: (s, 0, 0))],
        out_specs=block,
        input_output_aliases={0: 0},
        compiler_params=pltpu.CompilerParams(vmem_limit_bytes=8 * 2**20),
        cost_estimate=pl.CostEstimate(flops=x.size // 2, bytes_accessed=3 * x.size, transcendentals=0),
        name="grow",
    )(x, received)


def left_kernel(place, mine, other, partner, partner_other, left, out, total):
    step = pl.program_id(0)
    at = pl.ds(pl.multiple_of((step & 1) * TILE, TILE), TILE)
    rows = mine.shape[0]

    def term(a, b):
        stacked = jnp.concatenate(split_pair(a[:, at] + b[:, at]), axis=0)
        value = jnp.dot(stacked, left[...], preferred_element_type=F32)
        total[...] = jnp.where(step == 0, value, total[...] + value)

    own = (step >> 1) == (place[1] ^ place[0])
    pl.when(own)(lambda: term(mine, other))
    pl.when(jnp.logical_not(own))(lambda: term(partner, partner_other))

    @pl.when(step == 3)
    def _():
        value = total[:rows] + total[rows:]
        for z in range(2):
            for y in range(4):
                for xl in range(2):
                    for c in range(2):
                        at = (((z * 4 + y) * 2 + xl) * 2 + c) * rows
                        block = value[:, at : at + rows]
                        for there in (0, 2):
                            d = c * 32 + (there + z) * 8 + y * 2 + xl
                            for owner in (0, 64):
                                out[owner + d, 0:16, 0:rows] = block[0:16]
                                out[owner + d, 0:16, rows : 2 * rows] = block[16:32]
                                out[owner + d, 0:8, 2 * rows : 3 * rows] = block[32:40]


def left_product(place, mine, other, partner, partner_other, left):
    rows, half = mine.shape
    whole = pl.BlockSpec((rows, half), lambda k, p: (0, 0))
    return pl.pallas_call(
        left_kernel,
        out_shape=jax.ShapeDtypeStruct((128, 16, 128), F32),
        grid_spec=pltpu.PrefetchScalarGridSpec(
            num_scalar_prefetch=1,
            grid=(4,),
            in_specs=[whole] * 4 + [pl.BlockSpec((TILE, half), lambda k, p: (k, 0))],
            out_specs=pl.BlockSpec((128, 16, 128), lambda k, p: (0, 0, 0)),
            scratch_shapes=[pltpu.VMEM((2 * rows, half), F32)],
        ),
        compiler_params=pltpu.CompilerParams(vmem_limit_bytes=16 * 2**20),
        cost_estimate=pl.CostEstimate(
            flops=8 * rows * half * half, bytes_accessed=4 * half * half, transcendentals=0
        ),
        name="left_product",
    )(place, mine, other, partner, partner_other, left)


def right_kernel(place, blocks, right, late, out, rows_in):
    del late
    step = pl.program_id(0)
    rows = out.shape[0]
    for near in range(2):
        for y in range(4):
            core = (step >> 1) ^ ((near + y) & 1)
            for xl in range(2):
                block = blocks[core * 32 + ((step & 1) * 2 + near) * 8 + y * 2 + xl]
                at = ((near * 4 + y) * 2 + xl) * rows
                rows_in[at : at + 16, :] = block[:, 0:rows]
                rows_in[at + 16 : at + 32, :] = block[:, rows : 2 * rows]
                rows_in[at + 32 : at + 40, :] = block[0:8, 2 * rows : 3 * rows]
    high, low = split_pair(rows_in[...])
    value = contract(high, right[...]) + contract(low, right[...])
    pl.when(step == 0)(lambda: out.__setitem__(..., value))
    pl.when(step > 0)(lambda: out.__setitem__(..., out[...] + value))


def right_product(place, blocks, right, late):
    width, half = right.shape
    rows = width // 64
    return pl.pallas_call(
        right_kernel,
        out_shape=jax.ShapeDtypeStruct((rows, half), F32),
        grid_spec=pltpu.PrefetchScalarGridSpec(
            num_scalar_prefetch=1,
            grid=(4,),
            in_specs=[
                pl.BlockSpec((64, 16, 128), lambda k, p: (p[2] >> 1, 0, 0)),
                pl.BlockSpec((TILE, half), lambda k, p: (k, 0)),
                pl.BlockSpec(memory_space=pl.ANY),
            ],
            out_specs=pl.BlockSpec((rows, half), lambda k, p: (0, 0)),
            scratch_shapes=[pltpu.VMEM((TILE, rows), F32)],
        ),
        compiler_params=pltpu.CompilerParams(vmem_limit_bytes=16 * 2**20),
        cost_estimate=pl.CostEstimate(
            flops=8 * rows * half * half, bytes_accessed=4 * half * half, transcendentals=0
        ),
        name="right_product",
    )(place, blocks, right, late)


def per_device(hidden, out_grad, left_inverse, right_inverse):
    z, y, xl, c, o = (lax.axis_index(n) for n in ("z", "y", "xl", "c", "o"))
    tokens, width = hidden.shape
    half = width // 2
    token_total = tokens * 64
    first = o == 0
    h = c ^ ((z + y) & 1)
    place = jnp.stack([o, h, z, y]).astype(jnp.int32)
    second_me = jnp.where(h == 0, y, z).astype(jnp.int32)[None]

    grads_next = shift(cut(place, out_grad, out_grad, lambda p: 1 - p[1]), "c", 1)
    acts_next = shift(cut(place, hidden, hidden, lambda p: (1 - p[1]) ^ p[0]), "c", 1)
    rest_next = shift(cut(place, hidden, out_grad, lambda p: p[1]), "c", 1)

    own, m1, m2, m3 = cross_term(place, out_grad, grads_next, hidden, acts_next)
    m_parts = [own, turn(m1, 1, 0), turn(m2, 2, 0), turn(m3, 3, 0)]

    f_own, right, far_a, far_b, left = factor_term(
        place, hidden, out_grad, acts_next, grads_next, rest_next, m1
    )

    def second_round(parts):
        total, *pieces = fold(second_me, parts)
        return pieces[0], add(total, *[turn(piece, s, 1) for s, piece in enumerate(pieces, 1)])

    m_parts[0] = gate(m_parts[0], f_own)
    from_left, from_right = turn(far_a, 1, 0), turn(far_b, -1, 0)
    right, left = grow(right, from_left, 0), grow(left, from_right, 1)
    f_parts = [f_own, turn(right, 1, 0), turn(left, -1, 0)]

    _, m = second_round(m_parts)
    m = gate(m, right, left).reshape(2, half // 32, half)
    mine, theirs = pick(m, 0, xl), pick(m, 0, 1 - xl)
    across = lax.ppermute(theirs, ("xl", "o"), [(i, 3 - i) for i in range(4)])
    blocks = left_product(
        place, mine, shift(theirs, "xl", 1), shift(mine, "o", 1), across, left_inverse
    )
    blocks = lax.all_to_all(blocks, ("o", "c", "z", "y", "xl"), 0, 0, tiled=True)
    late, f = second_round(f_parts)
    update = right_product(place, blocks, right_inverse, late)

    f = f.reshape(2, width // 32, half)
    f = pick(f, 0, xl) + shift(pick(f, 0, 1 - xl).astype(BF), "xl", 1).astype(F32)
    f = f * jnp.where(first, 1.0 / token_total, 1.0).astype(F32)
    f = f.reshape(2, width // 64, half)
    mine = pick(f, 0, c)
    theirs = shift(pick(f, 0, 1 - c), "c", 1)
    factors = jnp.concatenate(
        [jnp.where(h == 0, mine, theirs), jnp.where(h == 0, theirs, mine)], axis=1
    )[None]
    return factors, update


def solution(mesh):
    fine = Mesh(mesh.devices.reshape(4, 4, 2, 2, 2), ("z", "y", "xl", "c", "o"))
    dp = ("z", "y", "xl", "c")
    in_specs = (P(dp, None), P(dp, None), P(None, "o"), P(None, "o"))
    out_specs = (P("o", dp, None), P(dp, "o"))
    return jax.shard_map(
        per_device, mesh=fine, in_specs=in_specs, out_specs=out_specs, check_vma=False
    )
```

```python
import functools

import jax
import jax.numpy as jnp
from jax import lax
from jax.experimental import pallas as pl
from jax.experimental.pallas import tpu as pltpu
from jax.sharding import Mesh, PartitionSpec as P

BF = jnp.bfloat16
F32 = jnp.float32
TILE = 640


def contract(first_rows, second_rows):
    return lax.dot_general(
        first_rows, second_rows, (((0,), (0,)), ((), ())), preferred_element_type=F32
    )


def shift(x, axis, step):
    size = lax.axis_size(axis)
    return lax.ppermute(x, axis, [(i, (i + step) % size) for i in range(size)])


def turn(x, step, stage):
    pairs = []
    for z in range(4):
        for y in range(4):
            for h in range(2):
                along_z = (h == 0) == (stage == 0)
                z2, y2 = ((z + step) % 4, y) if along_z else (z, (y + step) % 4)
                core, core2 = h ^ ((z + y) & 1), h ^ ((z2 + y2) & 1)
                pairs.append(((z * 4 + y) * 2 + core, (z2 * 4 + y2) * 2 + core2))
    return lax.ppermute(x, ("z", "y", "c"), pairs)


def pick(x, dim, index):
    return lax.dynamic_index_in_dim(x, index, dim, keepdims=False)


def split_pair(x):
    high = x.astype(BF)
    return high, (x - high.astype(F32)).astype(BF)


def place_tile(place, buffer, sem, outs, m, zs):
    rows = TILE // (zs * 4)

    def start(at, out, slot):
        block = buffer.at[m, pl.ds(at, rows)]
        pltpu.make_async_copy(block, out.at[slot], sem).start()

    for a in range(zs):
        z = m * zs + a

        @pl.when(place[1] == 0)
        def _():
            for r, out in enumerate(outs):

                @pl.when(((z - place[2] + 4) & 3) == r)
                def _():
                    for k in range(4):
                        if isinstance(out, tuple):
                            start((a * 4 + k) * rows, out[k // 2], k % 2)
                        else:
                            start((a * 4 + k) * rows, out, k)

        @pl.when(place[1] == 1)
        def _():
            for r, out in enumerate(outs):
                at = pl.multiple_of((a * 4 + ((place[3] + r) & 3)) * rows, 16)
                if isinstance(out, tuple):
                    pl.when(z < 2)(functools.partial(start, at, out[0], z & 1))
                    pl.when(z >= 2)(functools.partial(start, at, out[1], z & 1))
                else:
                    start(at, out, z)


def wait_all(buffer, sem):
    pltpu.make_async_copy(buffer, buffer, sem).wait()


def own_kernel(place, a, b, out):
    out[...] = contract(a[...], b[...])


def cross_kernel(place, a, b, partial, own, ahead1, ahead2, ahead3, held, buffer, held_sems, sem):
    m = pl.program_id(0)

    @pl.when(m == 0)
    def _():
        for k in range(2):
            rows = partial.at[pl.ds(k * TILE, TILE)]
            pltpu.make_async_copy(rows, held.at[k], held_sems.at[k]).start()

    tile = contract(a[...], b[...])
    wait_all(held.at[m], held_sems.at[m])
    buffer[m] = (held[m] + tile).astype(BF)
    place_tile(place, buffer, sem, [own, ahead1, ahead2, ahead3], m, 2)
    pl.when(m == 1)(lambda: wait_all(buffer, sem))


def cross_term(place, grads, grads_next, acts, acts_next):
    tokens, half = grads_next.shape
    anywhere = pl.BlockSpec(memory_space=pltpu.HBM)
    cost = pl.CostEstimate(
        flops=2 * tokens * half * half, bytes_accessed=10 * tokens * half, transcendentals=0
    )
    partial = pl.pallas_call(
        own_kernel,
        out_shape=jax.ShapeDtypeStruct((half, half), F32),
        grid_spec=pltpu.PrefetchScalarGridSpec(
            num_scalar_prefetch=1,
            grid=(2,),
            in_specs=[
                pl.BlockSpec((tokens, TILE), lambda m, p: (0, p[1] * 2 + m)),
                pl.BlockSpec((tokens, half), lambda m, p: (0, p[1] ^ p[0])),
            ],
            out_specs=pl.BlockSpec((TILE, half), lambda m, p: (m, 0)),
        ),
        compiler_params=pltpu.CompilerParams(vmem_limit_bytes=28 * 2**20),
        cost_estimate=cost,
        name="cross_own",
    )(place, grads, acts)
    out = jax.ShapeDtypeStruct((4, half // 16, half), BF)
    return pl.pallas_call(
        cross_kernel,
        out_shape=[out] * 4,
        grid_spec=pltpu.PrefetchScalarGridSpec(
            num_scalar_prefetch=1,
            grid=(2,),
            in_specs=[
                pl.BlockSpec((tokens, TILE), lambda m, p: (0, m)),
                pl.BlockSpec((tokens, half), lambda m, p: (0, 0)),
                anywhere,
            ],
            out_specs=[anywhere] * 4,
            scratch_shapes=[
                pltpu.VMEM((2, TILE, half), F32),
                pltpu.VMEM((2, TILE, half), BF),
                pltpu.SemaphoreType.DMA((2,)),
                pltpu.SemaphoreType.DMA,
            ],
        ),
        compiler_params=pltpu.CompilerParams(vmem_limit_bytes=28 * 2**20),
        cost_estimate=cost,
        name="cross_term",
    )(place, grads_next, acts_next, partial)


def factor_kernel(place, h_own, g_own, h_next, g_next, x_next, after, *rest):
    del after
    own, right, far_a, far_b, left, lhs, rhs, buffer, lhs_sems, rhs_sem, sem = rest
    m = pl.program_id(0)
    half = rhs.shape[2]

    def lanes(step, wide):
        return pl.ds(pl.multiple_of(step * wide, wide), wide)

    def fetch(step, with_rhs):
        slot = step & 1

        def left_block(ref, k, at):
            pltpu.make_async_copy(ref.at[:, lanes(at, TILE)], lhs.at[slot, k], lhs_sems.at[slot]).start()

        for owner, (mine, theirs) in enumerate(((h_own, h_next), (g_own, g_next))):

            @pl.when(place[0] == owner)
            def _():
                left_block(mine, 0, step)
                pl.when((step >> 1) == place[1])(lambda: left_block(theirs, 1, step & 1))
                if with_rhs:
                    at = lanes(place[1], half)
                    pltpu.make_async_copy(mine.at[:, at], rhs.at[0], rhs_sem).start()
                    pltpu.make_async_copy(theirs, rhs.at[1], rhs_sem).start()

        pl.when((step >> 1) != place[1])(lambda: left_block(x_next, 1, step & 1))

    pl.when(m == 0)(lambda: fetch(0, True))
    pl.when(m < 3)(lambda: fetch(m + 1, False))
    slot = m & 1
    wait_all(lhs.at[slot], lhs_sems.at[slot])
    pl.when(m == 0)(lambda: wait_all(rhs, rhs_sem))

    buffer[m] = (contract(lhs[slot, 0], rhs[0]) + contract(lhs[slot, 1], rhs[1])).astype(BF)
    place_tile(place, buffer, sem, [own, right, (far_a, far_b), left], m, 1)
    pl.when(m == 3)(lambda: wait_all(buffer, sem))


def factor_term(place, acts, grads, acts_next, grads_next, rest_next, after):
    tokens, width = acts.shape
    half = width // 2
    anywhere = pl.BlockSpec(memory_space=pltpu.HBM)
    out = jax.ShapeDtypeStruct((4, width // 16, half), BF)
    side = jax.ShapeDtypeStruct((2, width // 16, half), BF)
    return pl.pallas_call(
        factor_kernel,
        out_shape=[out, out, side, side, out],
        grid_spec=pltpu.PrefetchScalarGridSpec(
            num_scalar_prefetch=1,
            grid=(4,),
            in_specs=[anywhere] * 6,
            out_specs=[anywhere] * 5,
            scratch_shapes=[
                pltpu.VMEM((2, 2, tokens, TILE), BF),
                pltpu.VMEM((2, tokens, half), BF),
                pltpu.VMEM((4, TILE, half), BF),
                pltpu.SemaphoreType.DMA((2,)),
                pltpu.SemaphoreType.DMA,
                pltpu.SemaphoreType.DMA,
            ],
        ),
        compiler_params=pltpu.CompilerParams(vmem_limit_bytes=30 * 2**20),
        cost_estimate=pl.CostEstimate(
            flops=4 * tokens * width * half, bytes_accessed=16 * tokens * half, transcendentals=0
        ),
        name="factor_term",
    )(place, acts, grads, acts_next, grads_next, rest_next, after)


def add(first, *rest):
    total = first.astype(F32)
    for x in rest:
        total = total + x.astype(F32)
    return total


def fold_kernel(count, me, *refs):
    step = pl.program_id(0)
    own, *others = refs[-4:]
    total = add(*[part[0] for part in refs[:count]])

    @pl.when(step == 0)
    def _():
        own[...] = total

    for r, out in enumerate(others):

        @pl.when(step == r + 1)
        def _():
            out[...] = total.astype(BF)


def fold(me, parts, *after):
    _, rows, width = parts[0].shape
    block = pl.BlockSpec((1, rows, width), lambda s, m: ((m[0] + s) & 3, 0, 0))
    whole = pl.BlockSpec((rows, width), lambda s, m: (0, 0))
    return pl.pallas_call(
        functools.partial(fold_kernel, len(parts)),
        out_shape=[jax.ShapeDtypeStruct((rows, width), t) for t in (F32, BF, BF, BF)],
        grid_spec=pltpu.PrefetchScalarGridSpec(
            num_scalar_prefetch=1,
            grid=(4,),
            in_specs=[block] * len(parts) + [pl.BlockSpec(memory_space=pltpu.HBM)] * len(after),
            out_specs=[whole] * 4,
        ),
        compiler_params=pltpu.CompilerParams(vmem_limit_bytes=14 * 2**20),
        cost_estimate=pl.CostEstimate(
            flops=16 * rows * width, bytes_accessed=42 * rows * width, transcendentals=0
        ),
        name="fold",
    )(me, *parts, *after)


def settle_kernel(xl, total, r1, r2, r3, *refs):
    mine, theirs = refs[-2:]
    rows = mine.shape[0]
    for out, index in ((mine, xl[0]), (theirs, 1 - xl[0])):
        at = pl.ds(pl.multiple_of(index * rows, 8), rows)
        value = add(total[at], r1[at], r2[at], r3[at])
        out[...] = value.astype(out.dtype)


def settle(xl, total, received, dtype, *after):
    rows, width = total.shape
    whole = pl.BlockSpec((rows, width), lambda s, x: (0, 0))
    part = pl.BlockSpec((rows // 2, width), lambda s, x: (0, 0))
    return pl.pallas_call(
        settle_kernel,
        out_shape=[jax.ShapeDtypeStruct((rows // 2, width), t) for t in (F32, dtype)],
        grid_spec=pltpu.PrefetchScalarGridSpec(
            num_scalar_prefetch=1,
            grid=(1,),
            in_specs=[whole] * 4 + [pl.BlockSpec(memory_space=pltpu.HBM)] * len(after),
            out_specs=[part] * 2,
        ),
        compiler_params=pltpu.CompilerParams(vmem_limit_bytes=10 * 2**20),
        cost_estimate=pl.CostEstimate(
            flops=4 * rows * width, bytes_accessed=14 * rows * width, transcendentals=0
        ),
        name="settle",
    )(xl, total, *received, *after)


def cut_kernel(index, place, a, b, out, held, sems, out_sem):
    rows = held.shape[1]
    width = held.shape[2]
    at = pl.ds(pl.multiple_of(index(place) * width, width), width)
    for owner, ref in enumerate((a, b)):

        @pl.when(place[0] == owner)
        def _():
            for k in range(4):
                part = ref.at[pl.ds(k * rows, rows), at]
                pltpu.make_async_copy(part, held.at[k], sems.at[k]).start()

    for k in range(4):
        wait_all(held.at[k], sems.at[k])
        pltpu.make_async_copy(held.at[k], out.at[pl.ds(k * rows, rows)], out_sem).start()
    wait_all(held, out_sem)


def cut(place, a, b, index):
    tokens, width = a.shape
    hbm = pl.BlockSpec(memory_space=pltpu.HBM)
    return pl.pallas_call(
        functools.partial(cut_kernel, index),
        out_shape=jax.ShapeDtypeStruct((tokens, width // 2), a.dtype),
        grid_spec=pltpu.PrefetchScalarGridSpec(
            num_scalar_prefetch=1,
            grid=(1,),
            in_specs=[hbm, hbm],
            out_specs=hbm,
            scratch_shapes=[
                pltpu.VMEM((4, tokens // 4, width // 2), a.dtype),
                pltpu.SemaphoreType.DMA((4,)),
                pltpu.SemaphoreType.DMA,
            ],
        ),
        compiler_params=pltpu.CompilerParams(vmem_limit_bytes=4 * 2**20),
        cost_estimate=pl.CostEstimate(flops=0, bytes_accessed=2 * tokens * width, transcendentals=0),
        name="cut",
    )(place, a, b)


def grow_kernel(x, received, after, out):
    del after
    out[...] = add(x[...], received[...]).astype(BF)


def grow(x, received, side, after):
    block = pl.BlockSpec((1,) + x.shape[1:], lambda s: (side * 2 + s, 0, 0))
    return pl.pallas_call(
        grow_kernel,
        out_shape=jax.ShapeDtypeStruct(x.shape, x.dtype),
        grid=(2,),
        in_specs=[
            block,
            pl.BlockSpec((1,) + x.shape[1:], lambda s: (s, 0, 0)),
            pl.BlockSpec(memory_space=pltpu.HBM),
        ],
        out_specs=block,
        input_output_aliases={0: 0},
        compiler_params=pltpu.CompilerParams(vmem_limit_bytes=8 * 2**20),
        cost_estimate=pl.CostEstimate(flops=x.size // 2, bytes_accessed=3 * x.size, transcendentals=0),
        name="grow",
    )(x, received, after)


def left_kernel(place, mine, other, partner, partner_other, left, out, total):
    step = pl.program_id(0)
    at = pl.ds(pl.multiple_of((step & 1) * TILE, TILE), TILE)
    rows = mine.shape[0]

    def term(a, b):
        stacked = jnp.concatenate(split_pair(a[:, at] + b[:, at]), axis=0)
        value = jnp.dot(stacked, left[...], preferred_element_type=F32)
        total[...] = jnp.where(step == 0, value, total[...] + value)

    own = (step >> 1) == (place[1] ^ place[0])
    pl.when(own)(lambda: term(mine, other))
    pl.when(jnp.logical_not(own))(lambda: term(partner, partner_other))

    @pl.when(step == 3)
    def _():
        value = total[:rows] + total[rows:]
        for z in range(2):
            for y in range(4):
                for xl in range(2):
                    for c in range(2):
                        at = (((z * 4 + y) * 2 + xl) * 2 + c) * rows
                        block = value[:, at : at + rows]
                        for there in (0, 2):
                            d = c * 32 + (there + z) * 8 + y * 2 + xl
                            for owner in (0, 64):
                                out[owner + d, 0:16, 0:rows] = block[0:16]
                                out[owner + d, 0:16, rows : 2 * rows] = block[16:32]
                                out[owner + d, 0:8, 2 * rows : 3 * rows] = block[32:40]


def left_product(place, mine, other, partner, partner_other, left):
    rows, half = mine.shape
    whole = pl.BlockSpec((rows, half), lambda k, p: (0, 0))
    return pl.pallas_call(
        left_kernel,
        out_shape=jax.ShapeDtypeStruct((128, 16, 128), F32),
        grid_spec=pltpu.PrefetchScalarGridSpec(
            num_scalar_prefetch=1,
            grid=(4,),
            in_specs=[whole] * 4 + [pl.BlockSpec((TILE, half), lambda k, p: (k, 0))],
            out_specs=pl.BlockSpec((128, 16, 128), lambda k, p: (0, 0, 0)),
            scratch_shapes=[pltpu.VMEM((2 * rows, half), F32)],
        ),
        compiler_params=pltpu.CompilerParams(vmem_limit_bytes=16 * 2**20),
        cost_estimate=pl.CostEstimate(
            flops=256 * rows * half * half, bytes_accessed=4 * half * half, transcendentals=0
        ),
        name="left_product",
    )(place, mine, other, partner, partner_other, left)


def right_kernel(place, blocks, right, late, out, rows_in):
    del late
    step = pl.program_id(0)
    rows = out.shape[0]
    for near in range(2):
        for y in range(4):
            core = (step >> 1) ^ ((near + y) & 1)
            for xl in range(2):
                block = blocks[core * 32 + ((step & 1) * 2 + near) * 8 + y * 2 + xl]
                at = ((near * 4 + y) * 2 + xl) * rows
                rows_in[at : at + 16, :] = block[:, 0:rows]
                rows_in[at + 16 : at + 32, :] = block[:, rows : 2 * rows]
                rows_in[at + 32 : at + 40, :] = block[0:8, 2 * rows : 3 * rows]
    high, low = split_pair(rows_in[...])
    value = contract(high, right[...]) + contract(low, right[...])
    pl.when(step == 0)(lambda: out.__setitem__(..., value))
    pl.when(step > 0)(lambda: out.__setitem__(..., out[...] + value))


def right_product(place, blocks, right, late):
    width, half = right.shape
    rows = width // 64
    return pl.pallas_call(
        right_kernel,
        out_shape=jax.ShapeDtypeStruct((rows, half), F32),
        grid_spec=pltpu.PrefetchScalarGridSpec(
            num_scalar_prefetch=1,
            grid=(4,),
            in_specs=[
                pl.BlockSpec((64, 16, 128), lambda k, p: (p[2] >> 1, 0, 0)),
                pl.BlockSpec((TILE, half), lambda k, p: (k, 0)),
                pl.BlockSpec(memory_space=pltpu.HBM),
            ],
            out_specs=pl.BlockSpec((rows, half), lambda k, p: (0, 0)),
            scratch_shapes=[pltpu.VMEM((TILE, rows), F32)],
        ),
        compiler_params=pltpu.CompilerParams(vmem_limit_bytes=16 * 2**20),
        cost_estimate=pl.CostEstimate(
            flops=640 * rows * half * half, bytes_accessed=4 * half * half, transcendentals=0
        ),
        name="right_product",
    )(place, blocks, right, late)


def per_device(hidden, out_grad, left_inverse, right_inverse):
    z, y, xl, c, o = (lax.axis_index(n) for n in ("z", "y", "xl", "c", "o"))
    tokens, width = hidden.shape
    half = width // 2
    token_total = tokens * 64
    first = o == 0
    h = c ^ ((z + y) & 1)
    place = jnp.stack([o, h, z, y]).astype(jnp.int32)
    second_me = jnp.where(h == 0, y, z).astype(jnp.int32)[None]

    grads_next = shift(cut(place, out_grad, out_grad, lambda p: 1 - p[1]), "c", 1)
    acts_next = shift(cut(place, hidden, hidden, lambda p: (1 - p[1]) ^ p[0]), "c", 1)
    rest_next = shift(cut(place, hidden, out_grad, lambda p: p[1]), "c", 1)

    own, m1, m2, m3 = cross_term(place, out_grad, grads_next, hidden, acts_next)
    m_parts = [own, turn(m1, 1, 0), turn(m2, 2, 0), turn(m3, 3, 0)]

    f_own, right, far_a, far_b, left = factor_term(
        place, hidden, out_grad, acts_next, grads_next, rest_next, m1
    )

    my_xl = xl.astype(jnp.int32)[None]

    def second_sends(pieces):
        return [turn(piece, s, 1) for s, piece in enumerate(pieces, 1)]

    from_left, from_right = turn(far_a, 1, 0), turn(far_b, -1, 0)
    m, *m_pieces = fold(second_me, m_parts, f_own)
    m_received = second_sends(m_pieces)
    right = grow(right, from_left, 0, m_received[1])
    left = grow(left, from_right, 1, m_received[1])
    f_parts = [f_own, turn(right, 1, 0), turn(left, -1, 0)]

    mine, theirs = settle(my_xl, m, m_received, F32)
    across = lax.ppermute(theirs, ("xl", "o"), [(i, 3 - i) for i in range(4)])
    blocks = left_product(
        place, mine, shift(theirs, "xl", 1), shift(mine, "o", 1), across, left_inverse
    )
    blocks = lax.all_to_all(blocks, ("o", "c", "z", "y", "xl"), 0, 0, tiled=True)
    f, *f_pieces = fold(second_me, f_parts)
    f_mine, f_theirs = settle(my_xl, f, second_sends(f_pieces), BF)
    update = right_product(place, blocks, right_inverse, f_pieces[0])

    f = add(f_mine, shift(f_theirs, "xl", 1))
    f = f * jnp.where(first, 1.0 / token_total, 1.0).astype(F32)
    f = f.reshape(2, width // 64, half)
    mine = pick(f, 0, c)
    theirs = shift(pick(f, 0, 1 - c), "c", 1)
    factors = jnp.concatenate(
        [jnp.where(h == 0, mine, theirs), jnp.where(h == 0, theirs, mine)], axis=1
    )[None]
    return factors, update


def solution(mesh):
    fine = Mesh(mesh.devices.reshape(4, 4, 2, 2, 2), ("z", "y", "xl", "c", "o"))
    dp = ("z", "y", "xl", "c")
    in_specs = (P(dp, None), P(dp, None), P(None, "o"), P(None, "o"))
    out_specs = (P("o", dp, None), P(dp, "o"))
    return jax.shard_map(
        per_device, mesh=fine, in_specs=in_specs, out_specs=out_specs, check_vma=False
    )
```

```python
import functools

import jax
import jax.numpy as jnp
from jax import lax
from jax.experimental import pallas as pl
from jax.experimental.pallas import tpu as pltpu
from jax.sharding import Mesh, PartitionSpec as P

BF = jnp.bfloat16
F32 = jnp.float32
TILE = 640
ANY = pl.BlockSpec(memory_space=pl.ANY)


def contract(first_rows, second_rows):
    return lax.dot_general(
        first_rows, second_rows, (((0,), (0,)), ((), ())), preferred_element_type=F32
    )


def shift(x, axis, step):
    size = lax.axis_size(axis)
    return lax.ppermute(x, axis, [(i, (i + step) % size) for i in range(size)])


def turn(x, step, stage):
    pairs = []
    for z in range(4):
        for y in range(4):
            for h in range(2):
                along_z = (h == 0) == (stage == 0)
                z2, y2 = ((z + step) % 4, y) if along_z else (z, (y + step) % 4)
                core, core2 = h ^ ((z + y) & 1), h ^ ((z2 + y2) & 1)
                pairs.append(((z * 4 + y) * 2 + core, (z2 * 4 + y2) * 2 + core2))
    return lax.ppermute(x, ("z", "y", "c"), pairs)


def pick(x, dim, index):
    return lax.dynamic_index_in_dim(x, index, dim, keepdims=False)


def split_pair(x):
    high = x.astype(BF)
    return high, (x - high.astype(F32)).astype(BF)


def place_tile(place, buffer, sem, outs, m, zs):
    rows = TILE // (zs * 4)

    def start(at, out, slot):
        block = buffer.at[m, pl.ds(at, rows)]
        pltpu.make_async_copy(block, out.at[slot], sem).start()

    for a in range(zs):
        z = m * zs + a

        @pl.when(place[1] == 0)
        def _():
            for r, out in enumerate(outs):

                @pl.when(((z - place[2] + 4) & 3) == r)
                def _():
                    for k in range(4):
                        if isinstance(out, tuple):
                            start((a * 4 + k) * rows, out[k // 2], k % 2)
                        else:
                            start((a * 4 + k) * rows, out, k)

        @pl.when(place[1] == 1)
        def _():
            for r, out in enumerate(outs):
                at = pl.multiple_of((a * 4 + ((place[3] + r) & 3)) * rows, 16)
                if isinstance(out, tuple):
                    pl.when(z < 2)(functools.partial(start, at, out[0], z & 1))
                    pl.when(z >= 2)(functools.partial(start, at, out[1], z & 1))
                else:
                    start(at, out, z)


def wait_all(buffer, sem):
    pltpu.make_async_copy(buffer, buffer, sem).wait()


def own_kernel(place, a, b, out, lhs, rhs, lhs_sems, rhs_sem):
    m = pl.program_id(0)
    half = rhs.shape[1]

    @pl.when(m == 0)
    def _():
        at = pl.ds(pl.multiple_of((place[1] ^ place[0]) * half, half), half)
        pltpu.make_async_copy(b.at[:, at], rhs, rhs_sem).start()
        for k in range(2):
            at = pl.ds(pl.multiple_of(place[1] * half + k * TILE, TILE), TILE)
            pltpu.make_async_copy(a.at[:, at], lhs.at[k], lhs_sems.at[k]).start()
        wait_all(rhs, rhs_sem)

    wait_all(lhs.at[m], lhs_sems.at[m])
    out[...] = contract(lhs[m], rhs[...])


def cross_kernel(place, a, b, partial, own, ahead1, ahead2, ahead3, held, buffer, held_sems, sem):
    m = pl.program_id(0)

    @pl.when(m == 0)
    def _():
        for k in range(2):
            rows = partial.at[pl.ds(k * TILE, TILE)]
            pltpu.make_async_copy(rows, held.at[k], held_sems.at[k]).start()

    tile = contract(a[...], b[...])
    wait_all(held.at[m], held_sems.at[m])
    buffer[m] = (held[m] + tile).astype(BF)
    place_tile(place, buffer, sem, [own, ahead1, ahead2, ahead3], m, 2)
    pl.when(m == 1)(lambda: wait_all(buffer, sem))


def cross_own(place, grads, acts):
    tokens, half = grads.shape[0], grads.shape[1] // 2
    return pl.pallas_call(
        own_kernel,
        out_shape=jax.ShapeDtypeStruct((half, half), F32),
        grid_spec=pltpu.PrefetchScalarGridSpec(
            num_scalar_prefetch=1,
            grid=(2,),
            in_specs=[pl.BlockSpec(memory_space=pltpu.HBM)] * 2,
            out_specs=pl.BlockSpec((TILE, half), lambda m, p: (m, 0)),
            scratch_shapes=[
                pltpu.VMEM((2, tokens, TILE), BF),
                pltpu.VMEM((tokens, half), BF),
                pltpu.SemaphoreType.DMA((2,)),
                pltpu.SemaphoreType.DMA,
            ],
        ),
        compiler_params=pltpu.CompilerParams(vmem_limit_bytes=28 * 2**20),
        cost_estimate=pl.CostEstimate(
            flops=2 * tokens * half * half, bytes_accessed=8 * tokens * half, transcendentals=0
        ),
        name="cross_own",
    )(place, grads, acts)


def cross_term(place, grads_next, acts_next, partial):
    tokens, half = grads_next.shape
    out = jax.ShapeDtypeStruct((4, half // 16, half), BF)
    return pl.pallas_call(
        cross_kernel,
        out_shape=[out] * 4,
        grid_spec=pltpu.PrefetchScalarGridSpec(
            num_scalar_prefetch=1,
            grid=(2,),
            in_specs=[
                pl.BlockSpec((tokens, TILE), lambda m, p: (0, m)),
                pl.BlockSpec((tokens, half), lambda m, p: (0, 0)),
                ANY,
            ],
            out_specs=[pl.BlockSpec(memory_space=pltpu.HBM)] * 4,
            scratch_shapes=[
                pltpu.VMEM((2, TILE, half), F32),
                pltpu.VMEM((2, TILE, half), BF),
                pltpu.SemaphoreType.DMA((2,)),
                pltpu.SemaphoreType.DMA,
            ],
        ),
        compiler_params=pltpu.CompilerParams(vmem_limit_bytes=28 * 2**20),
        cost_estimate=pl.CostEstimate(
            flops=2 * tokens * half * half, bytes_accessed=10 * tokens * half, transcendentals=0
        ),
        name="cross_term",
    )(place, grads_next, acts_next, partial)


def factor_kernel(place, h_own, g_own, h_next, g_next, x_next, after, *rest):
    del after
    own, right, far_a, far_b, left, lhs, rhs, buffer, lhs_sems, rhs_sem, sem = rest
    m = pl.program_id(0)
    half = rhs.shape[2]

    def lanes(step, wide):
        return pl.ds(pl.multiple_of(step * wide, wide), wide)

    def fetch(step, with_rhs):
        slot = step & 1

        def left_block(ref, k, at):
            pltpu.make_async_copy(ref.at[:, lanes(at, TILE)], lhs.at[slot, k], lhs_sems.at[slot]).start()

        for owner, (mine, theirs) in enumerate(((h_own, h_next), (g_own, g_next))):

            @pl.when(place[0] == owner)
            def _():
                left_block(mine, 0, step)
                pl.when((step >> 1) == place[1])(lambda: left_block(theirs, 1, step & 1))
                if with_rhs:
                    at = lanes(place[1], half)
                    pltpu.make_async_copy(mine.at[:, at], rhs.at[0], rhs_sem).start()
                    pltpu.make_async_copy(theirs, rhs.at[1], rhs_sem).start()

        pl.when((step >> 1) != place[1])(lambda: left_block(x_next, 1, step & 1))

    pl.when(m == 0)(lambda: fetch(0, True))
    pl.when(m < 3)(lambda: fetch(m + 1, False))
    slot = m & 1
    wait_all(lhs.at[slot], lhs_sems.at[slot])
    pl.when(m == 0)(lambda: wait_all(rhs, rhs_sem))

    buffer[m] = (contract(lhs[slot, 0], rhs[0]) + contract(lhs[slot, 1], rhs[1])).astype(BF)
    place_tile(place, buffer, sem, [own, right, (far_a, far_b), left], m, 1)
    pl.when(m == 3)(lambda: wait_all(buffer, sem))


def factor_term(place, acts, grads, acts_next, grads_next, rest_next, after):
    tokens, width = acts.shape
    half = width // 2
    hbm = pl.BlockSpec(memory_space=pltpu.HBM)
    out = jax.ShapeDtypeStruct((4, width // 16, half), BF)
    side = jax.ShapeDtypeStruct((2, width // 16, half), BF)
    return pl.pallas_call(
        factor_kernel,
        out_shape=[out, out, side, side, out],
        grid_spec=pltpu.PrefetchScalarGridSpec(
            num_scalar_prefetch=1,
            grid=(4,),
            in_specs=[hbm] * 2 + [ANY] * 4,
            out_specs=[hbm] * 5,
            scratch_shapes=[
                pltpu.VMEM((2, 2, tokens, TILE), BF),
                pltpu.VMEM((2, tokens, half), BF),
                pltpu.VMEM((4, TILE, half), BF),
                pltpu.SemaphoreType.DMA((2,)),
                pltpu.SemaphoreType.DMA,
                pltpu.SemaphoreType.DMA,
            ],
        ),
        compiler_params=pltpu.CompilerParams(vmem_limit_bytes=30 * 2**20),
        cost_estimate=pl.CostEstimate(
            flops=4 * tokens * width * half, bytes_accessed=16 * tokens * half, transcendentals=0
        ),
        name="factor_term",
    )(place, acts, grads, acts_next, grads_next, rest_next, after)


def add(first, *rest):
    total = first.astype(F32)
    for x in rest:
        total = total + x.astype(F32)
    return total


def fold_kernel(count, me, *refs):
    step = pl.program_id(0)
    own, *others = refs[-6:-2]
    held, sems = refs[-2:]

    @pl.when(step == 0)
    def _():
        for k in range(4):
            pltpu.make_async_copy(refs[0].at[(me[0] + k) & 3], held.at[k], sems.at[k]).start()

    wait_all(held.at[step], sems.at[step])
    total = add(held[step], *[part[0] for part in refs[1:count]])

    @pl.when(step == 0)
    def _():
        own[...] = total

    for r, out in enumerate(others):

        @pl.when(step == r + 1)
        def _():
            out[...] = total.astype(BF)


def fold(me, parts, *after):
    _, rows, width = parts[0].shape
    block = pl.BlockSpec((1, rows, width), lambda s, m: ((m[0] + s) & 3, 0, 0))
    whole = pl.BlockSpec((rows, width), lambda s, m: (0, 0))
    return pl.pallas_call(
        functools.partial(fold_kernel, len(parts)),
        out_shape=[jax.ShapeDtypeStruct((rows, width), t) for t in (F32, BF, BF, BF)],
        grid_spec=pltpu.PrefetchScalarGridSpec(
            num_scalar_prefetch=1,
            grid=(4,),
            in_specs=[pl.BlockSpec(memory_space=pltpu.HBM)]
            + [block] * (len(parts) - 1)
            + [ANY] * len(after),
            out_specs=[whole] * 4,
            scratch_shapes=[pltpu.VMEM((4, rows, width), BF), pltpu.SemaphoreType.DMA((4,))],
        ),
        compiler_params=pltpu.CompilerParams(vmem_limit_bytes=16 * 2**20),
        cost_estimate=pl.CostEstimate(
            flops=16 * rows * width, bytes_accessed=42 * rows * width, transcendentals=0
        ),
        name="fold",
    )(me, *parts, *after)


def settle_kernel(xl, total, r1, r2, r3, mine, theirs):
    rows = mine.shape[0]
    for out, index in ((mine, xl[0]), (theirs, 1 - xl[0])):
        at = pl.ds(pl.multiple_of(index * rows, 8), rows)
        value = add(total[at], r1[at], r2[at], r3[at])
        out[...] = value.astype(out.dtype)


def settle(xl, total, received, dtype):
    rows, width = total.shape
    whole = pl.BlockSpec((rows, width), lambda s, x: (0, 0))
    part = pl.BlockSpec((rows // 2, width), lambda s, x: (0, 0))
    return pl.pallas_call(
        settle_kernel,
        out_shape=[jax.ShapeDtypeStruct((rows // 2, width), t) for t in (F32, dtype)],
        grid_spec=pltpu.PrefetchScalarGridSpec(
            num_scalar_prefetch=1,
            grid=(1,),
            in_specs=[whole] * 4,
            out_specs=[part] * 2,
        ),
        compiler_params=pltpu.CompilerParams(vmem_limit_bytes=10 * 2**20),
        cost_estimate=pl.CostEstimate(
            flops=4 * rows * width, bytes_accessed=14 * rows * width, transcendentals=0
        ),
        name="settle",
    )(xl, total, *received)


def cut_kernel(pairs, indices, place, *refs):
    sources, outs = refs[: 2 * pairs], refs[-3 - pairs : -3]
    held, sems, out_sem = refs[-3:]
    rows, width = held.shape[2:]

    for i in range(pairs):
        at = pl.ds(pl.multiple_of(indices[i](place) * width, width), width)
        for owner in range(2):

            @pl.when(place[0] == owner)
            def _():
                for k in range(4):
                    part = sources[2 * i + owner].at[pl.ds(k * rows, rows), at]
                    pltpu.make_async_copy(part, held.at[i, k], sems.at[i, k]).start()

    for i in range(pairs):
        for k in range(4):
            wait_all(held.at[i, k], sems.at[i, k])
            target = outs[i].at[pl.ds(k * rows, rows)]
            pltpu.make_async_copy(held.at[i, k], target, out_sem).start()
    wait_all(held, out_sem)


def cut(place, sources, indices, *after):
    tokens, width = sources[0][0].shape
    pairs = len(sources)
    hbm = pl.BlockSpec(memory_space=pltpu.HBM)
    dtype = sources[0][0].dtype
    return pl.pallas_call(
        functools.partial(cut_kernel, pairs, indices),
        out_shape=[jax.ShapeDtypeStruct((tokens, width // 2), dtype)] * pairs,
        grid_spec=pltpu.PrefetchScalarGridSpec(
            num_scalar_prefetch=1,
            grid=(1,),
            in_specs=[hbm] * (2 * pairs) + [ANY] * len(after),
            out_specs=[hbm] * pairs,
            scratch_shapes=[
                pltpu.VMEM((pairs, 4, tokens // 4, width // 2), dtype),
                pltpu.SemaphoreType.DMA((pairs, 4)),
                pltpu.SemaphoreType.DMA,
            ],
        ),
        compiler_params=pltpu.CompilerParams(vmem_limit_bytes=8 * 2**20),
        cost_estimate=pl.CostEstimate(
            flops=0, bytes_accessed=2 * pairs * tokens * width, transcendentals=0
        ),
        name="cut",
    )(place, *[x for pair in sources for x in pair], *after)


def grow_kernel(side, x, received, *refs):
    out, held, sems, out_sem = refs[-4:]
    for k in range(2):
        pltpu.make_async_copy(x.at[side * 2 + k], held.at[k], sems.at[k]).start()
    for k in range(2):
        wait_all(held.at[k], sems.at[k])
        held[k] = add(held[k], received[k]).astype(BF)
        pltpu.make_async_copy(held.at[k], out.at[side * 2 + k], out_sem).start()
    wait_all(held, out_sem)


def grow(x, received, side, *after):
    hbm = pl.BlockSpec(memory_space=pltpu.HBM)
    return pl.pallas_call(
        functools.partial(grow_kernel, side),
        out_shape=jax.ShapeDtypeStruct(x.shape, x.dtype),
        grid=(1,),
        in_specs=[hbm, pl.BlockSpec(received.shape, lambda s: (0, 0, 0))] + [ANY] * len(after),
        out_specs=hbm,
        scratch_shapes=[
            pltpu.VMEM(received.shape, x.dtype),
            pltpu.SemaphoreType.DMA((2,)),
            pltpu.SemaphoreType.DMA,
        ],
        input_output_aliases={0: 0},
        compiler_params=pltpu.CompilerParams(vmem_limit_bytes=8 * 2**20),
        cost_estimate=pl.CostEstimate(flops=x.size // 2, bytes_accessed=3 * x.size, transcendentals=0),
        name="grow",
    )(x, received, *after)


def fetch_tiles(step, source, held, sems):
    @pl.when(step == 0)
    def _():
        for k in range(4):
            rows = source.at[pl.ds(k * TILE, TILE)]
            pltpu.make_async_copy(rows, held.at[k], sems.at[k]).start()

    wait_all(held.at[step], sems.at[step])


def left_kernel(place, mine, other, partner, partner_other, left, out, total, held, sems):
    step = pl.program_id(0)
    fetch_tiles(step, left, held, sems)
    at = pl.ds(pl.multiple_of((step & 1) * TILE, TILE), TILE)
    rows = mine.shape[0]

    def term(a, b):
        stacked = jnp.concatenate(split_pair(a[:, at] + b[:, at]), axis=0)
        value = jnp.dot(stacked, held[step], preferred_element_type=F32)
        total[...] = jnp.where(step == 0, value, total[...] + value)

    own = (step >> 1) == (place[1] ^ place[0])
    pl.when(own)(lambda: term(mine, other))
    pl.when(jnp.logical_not(own))(lambda: term(partner, partner_other))

    @pl.when(step == 3)
    def _():
        value = total[:rows] + total[rows:]
        for z in range(2):
            for y in range(4):
                for xl in range(2):
                    for c in range(2):
                        at = (((z * 4 + y) * 2 + xl) * 2 + c) * rows
                        block = value[:, at : at + rows]
                        for there in (0, 2):
                            d = c * 32 + (there + z) * 8 + y * 2 + xl
                            for owner in (0, 64):
                                out[owner + d, 0:16, 0:rows] = block[0:16]
                                out[owner + d, 0:16, rows : 2 * rows] = block[16:32]
                                out[owner + d, 0:8, 2 * rows : 3 * rows] = block[32:40]


def left_product(place, mine, other, partner, partner_other, left):
    rows, half = mine.shape
    whole = pl.BlockSpec((rows, half), lambda k, p: (0, 0))
    return pl.pallas_call(
        left_kernel,
        out_shape=jax.ShapeDtypeStruct((128, 16, 128), F32),
        grid_spec=pltpu.PrefetchScalarGridSpec(
            num_scalar_prefetch=1,
            grid=(4,),
            in_specs=[whole] * 4 + [pl.BlockSpec(memory_space=pltpu.HBM)],
            out_specs=pl.BlockSpec((128, 16, 128), lambda k, p: (0, 0, 0)),
            scratch_shapes=[
                pltpu.VMEM((2 * rows, half), F32),
                pltpu.VMEM((4, TILE, half), BF),
                pltpu.SemaphoreType.DMA((4,)),
            ],
        ),
        compiler_params=pltpu.CompilerParams(vmem_limit_bytes=20 * 2**20),
        cost_estimate=pl.CostEstimate(
            flops=256 * rows * half * half, bytes_accessed=4 * half * half, transcendentals=0
        ),
        name="left_product",
    )(place, mine, other, partner, partner_other, left)


def right_kernel(place, blocks, right, late, out, rows_in, held, sems):
    del late
    step = pl.program_id(0)
    fetch_tiles(step, right, held, sems)
    rows = out.shape[0]
    for near in range(2):
        for y in range(4):
            core = (step >> 1) ^ ((near + y) & 1)
            for xl in range(2):
                block = blocks[core * 32 + ((step & 1) * 2 + near) * 8 + y * 2 + xl]
                at = ((near * 4 + y) * 2 + xl) * rows
                rows_in[at : at + 16, :] = block[:, 0:rows]
                rows_in[at + 16 : at + 32, :] = block[:, rows : 2 * rows]
                rows_in[at + 32 : at + 40, :] = block[0:8, 2 * rows : 3 * rows]
    high, low = split_pair(rows_in[...])
    value = contract(high, held[step]) + contract(low, held[step])
    pl.when(step == 0)(lambda: out.__setitem__(..., value))
    pl.when(step > 0)(lambda: out.__setitem__(..., out[...] + value))


def right_product(place, blocks, right, late):
    width, half = right.shape
    rows = width // 64
    return pl.pallas_call(
        right_kernel,
        out_shape=jax.ShapeDtypeStruct((rows, half), F32),
        grid_spec=pltpu.PrefetchScalarGridSpec(
            num_scalar_prefetch=1,
            grid=(4,),
            in_specs=[
                pl.BlockSpec((64, 16, 128), lambda k, p: (p[2] >> 1, 0, 0)),
                pl.BlockSpec(memory_space=pltpu.HBM),
                ANY,
            ],
            out_specs=pl.BlockSpec((rows, half), lambda k, p: (0, 0)),
            scratch_shapes=[
                pltpu.VMEM((TILE, rows), F32),
                pltpu.VMEM((4, TILE, half), BF),
                pltpu.SemaphoreType.DMA((4,)),
            ],
        ),
        compiler_params=pltpu.CompilerParams(vmem_limit_bytes=20 * 2**20),
        cost_estimate=pl.CostEstimate(
            flops=640 * rows * half * half, bytes_accessed=4 * half * half, transcendentals=0
        ),
        name="right_product",
    )(place, blocks, right, late)


def per_device(hidden, out_grad, left_inverse, right_inverse):
    z, y, xl, c, o = (lax.axis_index(n) for n in ("z", "y", "xl", "c", "o"))
    tokens, width = hidden.shape
    half = width // 2
    token_total = tokens * 64
    first = o == 0
    h = c ^ ((z + y) & 1)
    hidden, out_grad, left_inverse, right_inverse = (
        pltpu.with_memory_space_constraint(x, pltpu.HBM)
        for x in (hidden, out_grad, left_inverse, right_inverse)
    )
    place = jnp.stack([o, h, z, y]).astype(jnp.int32)
    second_me = jnp.where(h == 0, y, z).astype(jnp.int32)[None]

    grads_cut, acts_cut = cut(
        place,
        [(out_grad, out_grad), (hidden, hidden)],
        [lambda p: 1 - p[1], lambda p: (1 - p[1]) ^ p[0]],
    )
    grads_next, acts_next = shift(grads_cut, "c", 1), shift(acts_cut, "c", 1)
    partial = cross_own(place, out_grad, hidden)
    (rest_cut,) = cut(place, [(hidden, out_grad)], [lambda p: p[1]], partial)
    rest_next = shift(rest_cut, "c", 1)

    own, m1, m2, m3 = cross_term(place, grads_next, acts_next, partial)
    m_parts = [own, turn(m1, 1, 0), turn(m2, 2, 0), turn(m3, 3, 0)]

    f_own, right, far_a, far_b, left = factor_term(
        place, hidden, out_grad, acts_next, grads_next, rest_next, m1
    )

    my_xl = xl.astype(jnp.int32)[None]

    def second_sends(pieces):
        return [turn(piece, s, 1) for s, piece in enumerate(pieces, 1)]

    from_left, from_right = turn(far_a, 1, 0), turn(far_b, -1, 0)
    m, *m_pieces = fold(second_me, m_parts, f_own)
    m_received = second_sends(m_pieces)
    right = grow(right, from_left, 0, *m_received)
    left = grow(left, from_right, 1, *m_received)
    f_parts = [f_own, turn(right, 1, 0), turn(left, -1, 0)]

    mine, theirs = settle(my_xl, m, m_received, F32)
    across = lax.ppermute(theirs, ("xl", "o"), [(i, 3 - i) for i in range(4)])
    products = left_product(
        place, mine, shift(theirs, "xl", 1), shift(mine, "o", 1), across, left_inverse
    )
    blocks = lax.all_to_all(products, ("o", "c", "z", "y", "xl"), 0, 0, tiled=True)
    f, *f_pieces = fold(second_me, f_parts, products)
    f_mine, f_theirs = settle(my_xl, f, second_sends(f_pieces), BF)
    update = right_product(place, blocks, right_inverse, f_pieces[0])

    f = add(f_mine, shift(f_theirs, "xl", 1))
    f = f * jnp.where(first, 1.0 / token_total, 1.0).astype(F32)
    f = f.reshape(2, width // 64, half)
    mine = pick(f, 0, c)
    theirs = shift(pick(f, 0, 1 - c), "c", 1)
    factors = jnp.concatenate(
        [jnp.where(h == 0, mine, theirs), jnp.where(h == 0, theirs, mine)], axis=1
    )[None]
    return factors, update


def solution(mesh):
    fine = Mesh(mesh.devices.reshape(4, 4, 2, 2, 2), ("z", "y", "xl", "c", "o"))
    dp = ("z", "y", "xl", "c")
    in_specs = (P(dp, None), P(dp, None), P(None, "o"), P(None, "o"))
    out_specs = (P("o", dp, None), P(dp, "o"))
    return jax.shard_map(
        per_device, mesh=fine, in_specs=in_specs, out_specs=out_specs, check_vma=False
    )
```

```python
import functools

import jax
import jax.numpy as jnp
from jax import lax
from jax.experimental import pallas as pl
from jax.experimental.pallas import tpu as pltpu
from jax.sharding import Mesh, PartitionSpec as P

BF = jnp.bfloat16
F32 = jnp.float32
TILE = 640
ANY = pl.BlockSpec(memory_space=pl.ANY)


def contract(first_rows, second_rows):
    return lax.dot_general(
        first_rows, second_rows, (((0,), (0,)), ((), ())), preferred_element_type=F32
    )


def shift(x, axis, step):
    size = lax.axis_size(axis)
    return lax.ppermute(x, axis, [(i, (i + step) % size) for i in range(size)])


def turn(x, step, stage):
    pairs = []
    for z in range(4):
        for y in range(4):
            for h in range(2):
                along_z = (h == 0) == (stage == 0)
                z2, y2 = ((z + step) % 4, y) if along_z else (z, (y + step) % 4)
                core, core2 = h ^ ((z + y) & 1), h ^ ((z2 + y2) & 1)
                pairs.append(((z * 4 + y) * 2 + core, (z2 * 4 + y2) * 2 + core2))
    return lax.ppermute(x, ("z", "y", "c"), pairs)


def in_hbm(x):
    return pltpu.with_memory_space_constraint(x, pltpu.HBM)


def pick(x, dim, index):
    return lax.dynamic_index_in_dim(x, index, dim, keepdims=False)


def split_pair(x):
    high = x.astype(BF)
    return high, (x - high.astype(F32)).astype(BF)


def place_tile(place, buffer, sem, outs, m, zs):
    rows = TILE // (zs * 4)

    def start(at, out, slot):
        block = buffer.at[m, pl.ds(at, rows)]
        pltpu.make_async_copy(block, out.at[slot], sem).start()

    for a in range(zs):
        z = m * zs + a

        @pl.when(place[1] == 0)
        def _():
            for r, out in enumerate(outs):

                @pl.when(((z - place[2] + 4) & 3) == r)
                def _():
                    for k in range(4):
                        if isinstance(out, tuple):
                            start((a * 4 + k) * rows, out[k // 2], k % 2)
                        else:
                            start((a * 4 + k) * rows, out, k)

        @pl.when(place[1] == 1)
        def _():
            for r, out in enumerate(outs):
                at = pl.multiple_of((a * 4 + ((place[3] + r) & 3)) * rows, 16)
                if isinstance(out, tuple):
                    pl.when(z < 2)(functools.partial(start, at, out[0], z & 1))
                    pl.when(z >= 2)(functools.partial(start, at, out[1], z & 1))
                else:
                    start(at, out, z)


def wait_all(buffer, sem):
    pltpu.make_async_copy(buffer, buffer, sem).wait()


def own_kernel(place, a, b, out, lhs, rhs, lhs_sems, rhs_sem):
    m = pl.program_id(0)
    half = rhs.shape[1]

    @pl.when(m == 0)
    def _():
        at = pl.ds(pl.multiple_of((place[1] ^ place[0]) * half, half), half)
        pltpu.make_async_copy(b.at[:, at], rhs, rhs_sem).start()
        for k in range(2):
            at = pl.ds(pl.multiple_of(place[1] * half + k * TILE, TILE), TILE)
            pltpu.make_async_copy(a.at[:, at], lhs.at[k], lhs_sems.at[k]).start()
        wait_all(rhs, rhs_sem)

    wait_all(lhs.at[m], lhs_sems.at[m])
    out[...] = contract(lhs[m], rhs[...])


def cross_kernel(place, a, b, partial, own, ahead1, ahead2, ahead3, held, buffer, held_sems, sem):
    m = pl.program_id(0)

    @pl.when(m == 0)
    def _():
        for k in range(2):
            rows = partial.at[pl.ds(k * TILE, TILE)]
            pltpu.make_async_copy(rows, held.at[k], held_sems.at[k]).start()

    tile = contract(a[...], b[...])
    wait_all(held.at[m], held_sems.at[m])
    buffer[m] = (held[m] + tile).astype(BF)
    place_tile(place, buffer, sem, [own, ahead1, ahead2, ahead3], m, 2)
    pl.when(m == 1)(lambda: wait_all(buffer, sem))


def cross_own(place, grads, acts):
    tokens, half = grads.shape[0], grads.shape[1] // 2
    return pl.pallas_call(
        own_kernel,
        out_shape=jax.ShapeDtypeStruct((half, half), F32),
        grid_spec=pltpu.PrefetchScalarGridSpec(
            num_scalar_prefetch=1,
            grid=(2,),
            in_specs=[pl.BlockSpec(memory_space=pltpu.HBM)] * 2,
            out_specs=pl.BlockSpec((TILE, half), lambda m, p: (m, 0)),
            scratch_shapes=[
                pltpu.VMEM((2, tokens, TILE), BF),
                pltpu.VMEM((tokens, half), BF),
                pltpu.SemaphoreType.DMA((2,)),
                pltpu.SemaphoreType.DMA,
            ],
        ),
        compiler_params=pltpu.CompilerParams(vmem_limit_bytes=28 * 2**20),
        cost_estimate=pl.CostEstimate(
            flops=2 * tokens * half * half, bytes_accessed=8 * tokens * half, transcendentals=0
        ),
        name="cross_own",
    )(place, grads, acts)


def cross_term(place, grads_next, acts_next, partial):
    tokens, half = grads_next.shape
    out = pltpu.HBM((4, half // 16, half), BF)
    return pl.pallas_call(
        cross_kernel,
        out_shape=[out] * 4,
        grid_spec=pltpu.PrefetchScalarGridSpec(
            num_scalar_prefetch=1,
            grid=(2,),
            in_specs=[
                pl.BlockSpec((tokens, TILE), lambda m, p: (0, m)),
                pl.BlockSpec((tokens, half), lambda m, p: (0, 0)),
                ANY,
            ],
            out_specs=[pl.BlockSpec(memory_space=pltpu.HBM)] * 4,
            scratch_shapes=[
                pltpu.VMEM((2, TILE, half), F32),
                pltpu.VMEM((2, TILE, half), BF),
                pltpu.SemaphoreType.DMA((2,)),
                pltpu.SemaphoreType.DMA,
            ],
        ),
        compiler_params=pltpu.CompilerParams(vmem_limit_bytes=28 * 2**20),
        cost_estimate=pl.CostEstimate(
            flops=2 * tokens * half * half, bytes_accessed=10 * tokens * half, transcendentals=0
        ),
        name="cross_term",
    )(place, grads_next, acts_next, partial)


def factor_kernel(place, h_own, g_own, h_next, g_next, x_next, after, *rest):
    del after
    own, right, far_a, far_b, left, lhs, rhs, buffer, lhs_sems, rhs_sem, sem = rest
    m = pl.program_id(0)
    half = rhs.shape[2]

    def lanes(step, wide):
        return pl.ds(pl.multiple_of(step * wide, wide), wide)

    def fetch(step, with_rhs):
        slot = step & 1

        def left_block(ref, k, at):
            pltpu.make_async_copy(ref.at[:, lanes(at, TILE)], lhs.at[slot, k], lhs_sems.at[slot]).start()

        for owner, (mine, theirs) in enumerate(((h_own, h_next), (g_own, g_next))):

            @pl.when(place[0] == owner)
            def _():
                left_block(mine, 0, step)
                pl.when((step >> 1) == place[1])(lambda: left_block(theirs, 1, step & 1))
                if with_rhs:
                    at = lanes(place[1], half)
                    pltpu.make_async_copy(mine.at[:, at], rhs.at[0], rhs_sem).start()
                    pltpu.make_async_copy(theirs, rhs.at[1], rhs_sem).start()

        pl.when((step >> 1) != place[1])(lambda: left_block(x_next, 1, step & 1))

    pl.when(m == 0)(lambda: fetch(0, True))
    pl.when(m < 3)(lambda: fetch(m + 1, False))
    slot = m & 1
    wait_all(lhs.at[slot], lhs_sems.at[slot])
    pl.when(m == 0)(lambda: wait_all(rhs, rhs_sem))

    buffer[m] = (contract(lhs[slot, 0], rhs[0]) + contract(lhs[slot, 1], rhs[1])).astype(BF)
    place_tile(place, buffer, sem, [own, right, (far_a, far_b), left], m, 1)
    pl.when(m == 3)(lambda: wait_all(buffer, sem))


def factor_term(place, acts, grads, acts_next, grads_next, rest_next, after):
    tokens, width = acts.shape
    half = width // 2
    hbm = pl.BlockSpec(memory_space=pltpu.HBM)
    out = pltpu.HBM((4, width // 16, half), BF)
    side = pltpu.HBM((2, width // 16, half), BF)
    return pl.pallas_call(
        factor_kernel,
        out_shape=[out, out, side, side, out],
        grid_spec=pltpu.PrefetchScalarGridSpec(
            num_scalar_prefetch=1,
            grid=(4,),
            in_specs=[hbm] * 2 + [ANY] * 4,
            out_specs=[hbm] * 5,
            scratch_shapes=[
                pltpu.VMEM((2, 2, tokens, TILE), BF),
                pltpu.VMEM((2, tokens, half), BF),
                pltpu.VMEM((4, TILE, half), BF),
                pltpu.SemaphoreType.DMA((2,)),
                pltpu.SemaphoreType.DMA,
                pltpu.SemaphoreType.DMA,
            ],
        ),
        compiler_params=pltpu.CompilerParams(vmem_limit_bytes=30 * 2**20),
        cost_estimate=pl.CostEstimate(
            flops=4 * tokens * width * half, bytes_accessed=16 * tokens * half, transcendentals=0
        ),
        name="factor_term",
    )(place, acts, grads, acts_next, grads_next, rest_next, after)


def add(first, *rest):
    total = first.astype(F32)
    for x in rest:
        total = total + x.astype(F32)
    return total


def fold_kernel(count, me, *refs):
    own, *others = refs[-6:-2]
    held, sem = refs[-2:]
    copy = pltpu.make_async_copy(refs[0], held, sem)
    copy.start()
    copy.wait()
    for r, out in enumerate([own, *others]):
        at = (me[0] + r) & 3
        out[...] = add(held[at], *[part[at] for part in refs[1:count]]).astype(out.dtype)


def fold(me, parts, *after):
    _, rows, width = parts[0].shape
    block = pl.BlockSpec((4, rows, width), lambda s, m: (0, 0, 0))
    whole = pl.BlockSpec((rows, width), lambda s, m: (0, 0))
    return pl.pallas_call(
        functools.partial(fold_kernel, len(parts)),
        out_shape=[jax.ShapeDtypeStruct((rows, width), t) for t in (F32, BF, BF, BF)],
        grid_spec=pltpu.PrefetchScalarGridSpec(
            num_scalar_prefetch=1,
            grid=(1,),
            in_specs=[pl.BlockSpec(memory_space=pltpu.HBM)]
            + [block] * (len(parts) - 1)
            + [ANY] * len(after),
            out_specs=[whole] * 4,
            scratch_shapes=[pltpu.VMEM((4, rows, width), BF), pltpu.SemaphoreType.DMA],
        ),
        compiler_params=pltpu.CompilerParams(vmem_limit_bytes=20 * 2**20),
        cost_estimate=pl.CostEstimate(flops=0, bytes_accessed=0, transcendentals=0),
        name="fold",
    )(me, in_hbm(parts[0]), *parts[1:], *after)


def settle_kernel(xl, total, r1, r2, r3, *refs):
    mine, theirs = refs[-2:]
    rows = mine.shape[0]
    for out, index in ((mine, xl[0]), (theirs, 1 - xl[0])):
        at = pl.ds(pl.multiple_of(index * rows, 8), rows)
        value = add(total[at], r1[at], r2[at], r3[at])
        out[...] = value.astype(out.dtype)


def settle(xl, total, received, dtype, *after):
    rows, width = total.shape
    whole = pl.BlockSpec((rows, width), lambda s, x: (0, 0))
    part = pl.BlockSpec((rows // 2, width), lambda s, x: (0, 0))
    return pl.pallas_call(
        settle_kernel,
        out_shape=[jax.ShapeDtypeStruct((rows // 2, width), t) for t in (F32, dtype)],
        grid_spec=pltpu.PrefetchScalarGridSpec(
            num_scalar_prefetch=1,
            grid=(1,),
            in_specs=[whole] * 4 + [ANY] * len(after),
            out_specs=[part] * 2,
        ),
        compiler_params=pltpu.CompilerParams(vmem_limit_bytes=10 * 2**20),
        cost_estimate=pl.CostEstimate(flops=0, bytes_accessed=0, transcendentals=0),
        name="settle",
    )(xl, total, *received, *after)


def cut_kernel(pairs, indices, place, *refs):
    sources, outs, sem = refs[: 2 * pairs], refs[-1 - pairs : -1], refs[-1]
    tokens, width = outs[0].shape
    rows = tokens // 4
    for i in range(pairs):
        at = pl.ds(pl.multiple_of(indices[i](place) * width, width), width)
        for owner in range(2):

            @pl.when(place[0] == owner)
            def _():
                for k in range(4):
                    part = pl.ds(k * rows, rows)
                    source = sources[2 * i + owner].at[part, at]
                    pltpu.make_async_copy(source, outs[i].at[part], sem).start()

    for out in outs:
        wait_all(out, sem)


def cut(place, sources, indices, *after):
    tokens, width = sources[0][0].shape
    pairs = len(sources)
    hbm = pl.BlockSpec(memory_space=pltpu.HBM)
    dtype = sources[0][0].dtype
    return pl.pallas_call(
        functools.partial(cut_kernel, pairs, indices),
        out_shape=[pltpu.HBM((tokens, width // 2), dtype)] * pairs,
        grid_spec=pltpu.PrefetchScalarGridSpec(
            num_scalar_prefetch=1,
            grid=(1,),
            in_specs=[hbm] * (2 * pairs) + [ANY] * len(after),
            out_specs=[hbm] * pairs,
            scratch_shapes=[pltpu.SemaphoreType.DMA],
        ),
        compiler_params=pltpu.CompilerParams(vmem_limit_bytes=8 * 2**20),
        cost_estimate=pl.CostEstimate(
            flops=0, bytes_accessed=2 * pairs * tokens * width, transcendentals=0
        ),
        name="cut",
    )(place, *[x for pair in sources for x in pair], *after)


def grow_kernel(side, x, received, *refs):
    out, held, sems, out_sem = refs[-4:]
    for k in range(2):
        pltpu.make_async_copy(x.at[side * 2 + k], held.at[k], sems.at[k]).start()
    for k in range(2):
        wait_all(held.at[k], sems.at[k])
        held[k] = add(held[k], received[k]).astype(BF)
        pltpu.make_async_copy(held.at[k], out.at[side * 2 + k], out_sem).start()
    wait_all(held, out_sem)


def grow(x, received, side, *after):
    hbm = pl.BlockSpec(memory_space=pltpu.HBM)
    return pl.pallas_call(
        functools.partial(grow_kernel, side),
        out_shape=pltpu.HBM(x.shape, x.dtype),
        grid=(1,),
        in_specs=[hbm, pl.BlockSpec(received.shape, lambda s: (0, 0, 0))] + [ANY] * len(after),
        out_specs=hbm,
        scratch_shapes=[
            pltpu.VMEM(received.shape, x.dtype),
            pltpu.SemaphoreType.DMA((2,)),
            pltpu.SemaphoreType.DMA,
        ],
        input_output_aliases={0: 0},
        compiler_params=pltpu.CompilerParams(vmem_limit_bytes=8 * 2**20),
        cost_estimate=pl.CostEstimate(flops=0, bytes_accessed=0, transcendentals=0),
        name="grow",
    )(in_hbm(x), received, *after)


def fetch_tiles(step, source, held, sems):
    @pl.when(step == 0)
    def _():
        for k in range(4):
            rows = source.at[pl.ds(k * TILE, TILE)]
            pltpu.make_async_copy(rows, held.at[k], sems.at[k]).start()

    wait_all(held.at[step], sems.at[step])


def left_kernel(place, mine, other, partner, partner_other, left, out, total, held, sems):
    step = pl.program_id(0)
    fetch_tiles(step, left, held, sems)
    at = pl.ds(pl.multiple_of((step & 1) * TILE, TILE), TILE)
    rows = mine.shape[0]

    def term(a, b):
        stacked = jnp.concatenate(split_pair(a[:, at] + b[:, at]), axis=0)
        value = jnp.dot(stacked, held[step], preferred_element_type=F32)
        total[...] = jnp.where(step == 0, value, total[...] + value)

    own = (step >> 1) == (place[1] ^ place[0])
    pl.when(own)(lambda: term(mine, other))
    pl.when(jnp.logical_not(own))(lambda: term(partner, partner_other))

    @pl.when(step == 3)
    def _():
        value = total[:rows] + total[rows:]
        for z in range(2):
            for y in range(4):
                for xl in range(2):
                    for c in range(2):
                        at = (((z * 4 + y) * 2 + xl) * 2 + c) * rows
                        block = value[:, at : at + rows]
                        for there in (0, 2):
                            d = c * 32 + (there + z) * 8 + y * 2 + xl
                            for owner in (0, 64):
                                out[owner + d, 0:16, 0:rows] = block[0:16]
                                out[owner + d, 0:16, rows : 2 * rows] = block[16:32]
                                out[owner + d, 0:8, 2 * rows : 3 * rows] = block[32:40]


def left_product(place, mine, other, partner, partner_other, left):
    rows, half = mine.shape
    whole = pl.BlockSpec((rows, half), lambda k, p: (0, 0))
    return pl.pallas_call(
        left_kernel,
        out_shape=jax.ShapeDtypeStruct((128, 16, 128), F32),
        grid_spec=pltpu.PrefetchScalarGridSpec(
            num_scalar_prefetch=1,
            grid=(4,),
            in_specs=[whole] * 4 + [pl.BlockSpec(memory_space=pltpu.HBM)],
            out_specs=pl.BlockSpec((128, 16, 128), lambda k, p: (0, 0, 0)),
            scratch_shapes=[
                pltpu.VMEM((2 * rows, half), F32),
                pltpu.VMEM((4, TILE, half), BF),
                pltpu.SemaphoreType.DMA((4,)),
            ],
        ),
        compiler_params=pltpu.CompilerParams(vmem_limit_bytes=20 * 2**20),
        cost_estimate=pl.CostEstimate(
            flops=256 * rows * half * half, bytes_accessed=4 * half * half, transcendentals=0
        ),
        name="left_product",
    )(place, mine, other, partner, partner_other, left)


def right_kernel(place, blocks, right, late, out, rows_in, held, sems):
    del late
    step = pl.program_id(0)
    fetch_tiles(step, right, held, sems)
    rows = out.shape[0]
    for near in range(2):
        for y in range(4):
            core = (step >> 1) ^ ((near + y) & 1)
            for xl in range(2):
                block = blocks[core * 32 + ((step & 1) * 2 + near) * 8 + y * 2 + xl]
                at = ((near * 4 + y) * 2 + xl) * rows
                rows_in[at : at + 16, :] = block[:, 0:rows]
                rows_in[at + 16 : at + 32, :] = block[:, rows : 2 * rows]
                rows_in[at + 32 : at + 40, :] = block[0:8, 2 * rows : 3 * rows]
    high, low = split_pair(rows_in[...])
    value = contract(high, held[step]) + contract(low, held[step])
    pl.when(step == 0)(lambda: out.__setitem__(..., value))
    pl.when(step > 0)(lambda: out.__setitem__(..., out[...] + value))


def right_product(place, blocks, right, late):
    width, half = right.shape
    rows = width // 64
    return pl.pallas_call(
        right_kernel,
        out_shape=jax.ShapeDtypeStruct((rows, half), F32),
        grid_spec=pltpu.PrefetchScalarGridSpec(
            num_scalar_prefetch=1,
            grid=(4,),
            in_specs=[
                pl.BlockSpec((64, 16, 128), lambda k, p: (p[2] >> 1, 0, 0)),
                pl.BlockSpec(memory_space=pltpu.HBM),
                ANY,
            ],
            out_specs=pl.BlockSpec((rows, half), lambda k, p: (0, 0)),
            scratch_shapes=[
                pltpu.VMEM((TILE, rows), F32),
                pltpu.VMEM((4, TILE, half), BF),
                pltpu.SemaphoreType.DMA((4,)),
            ],
        ),
        compiler_params=pltpu.CompilerParams(vmem_limit_bytes=20 * 2**20),
        cost_estimate=pl.CostEstimate(
            flops=640 * rows * half * half, bytes_accessed=4 * half * half, transcendentals=0
        ),
        name="right_product",
    )(place, blocks, right, late)


def per_device(hidden, out_grad, left_inverse, right_inverse):
    z, y, xl, c, o = (lax.axis_index(n) for n in ("z", "y", "xl", "c", "o"))
    tokens, width = hidden.shape
    half = width // 2
    token_total = tokens * 64
    first = o == 0
    h = c ^ ((z + y) & 1)
    hidden, out_grad = in_hbm(hidden), in_hbm(out_grad)
    left_inverse, right_inverse = in_hbm(left_inverse), in_hbm(right_inverse)
    place = jnp.stack([o, h, z, y]).astype(jnp.int32)
    second_me = jnp.where(h == 0, y, z).astype(jnp.int32)[None]

    grads_cut, acts_cut = cut(
        place,
        [(out_grad, out_grad), (hidden, hidden)],
        [lambda p: 1 - p[1], lambda p: (1 - p[1]) ^ p[0]],
    )
    grads_next, acts_next = shift(grads_cut, "c", 1), shift(acts_cut, "c", 1)
    partial = cross_own(place, out_grad, hidden)
    (rest_cut,) = cut(place, [(hidden, out_grad)], [lambda p: p[1]], partial)
    rest_next = shift(rest_cut, "c", 1)

    own, m1, m2, m3 = cross_term(place, grads_next, acts_next, partial)
    m_parts = [own, turn(m1, 1, 0), turn(m2, 2, 0), turn(m3, 3, 0)]

    f_own, right, far_a, far_b, left = factor_term(
        place, hidden, out_grad, acts_next, grads_next, rest_next, in_hbm(m1)
    )

    my_xl = xl.astype(jnp.int32)[None]

    def second_sends(pieces):
        return [turn(piece, s, 1) for s, piece in enumerate(pieces, 1)]

    from_left, from_right = turn(far_a, 1, 0), turn(far_b, -1, 0)
    m, *m_pieces = fold(second_me, m_parts, in_hbm(f_own))
    m_received = second_sends(m_pieces)
    right = grow(right, from_left, 0, *m_received)
    left = grow(left, from_right, 1, *m_received)
    f_parts = [f_own, turn(right, 1, 0), turn(left, -1, 0)]

    mine, theirs = settle(my_xl, m, m_received, F32)
    across = lax.ppermute(theirs, ("xl", "o"), [(i, 3 - i) for i in range(4)])
    products = left_product(
        place, mine, shift(theirs, "xl", 1), shift(mine, "o", 1), across, left_inverse
    )
    blocks = lax.all_to_all(products, ("o", "c", "z", "y", "xl"), 0, 0, tiled=True)
    f, *f_pieces = fold(second_me, f_parts, products)
    f_mine, f_theirs = settle(my_xl, f, second_sends(f_pieces), BF, blocks)
    update = right_product(place, blocks, right_inverse, f_pieces[0])

    f = add(f_mine, shift(f_theirs, "xl", 1))
    f = f * jnp.where(first, 1.0 / token_total, 1.0).astype(F32)
    f = f.reshape(2, width // 64, half)
    mine = pick(f, 0, c)
    theirs = shift(pick(f, 0, 1 - c), "c", 1)
    factors = jnp.concatenate(
        [jnp.where(h == 0, mine, theirs), jnp.where(h == 0, theirs, mine)], axis=1
    )[None]
    return factors, update


def solution(mesh):
    fine = Mesh(mesh.devices.reshape(4, 4, 2, 2, 2), ("z", "y", "xl", "c", "o"))
    dp = ("z", "y", "xl", "c")
    in_specs = (P(dp, None), P(dp, None), P(None, "o"), P(None, "o"))
    out_specs = (P("o", dp, None), P(dp, "o"))
    return jax.shard_map(
        per_device, mesh=fine, in_specs=in_specs, out_specs=out_specs, check_vma=False
    )
```

```python
import functools

import jax
import jax.numpy as jnp
from jax import lax
from jax.experimental import pallas as pl
from jax.experimental.pallas import tpu as pltpu
from jax.sharding import Mesh, PartitionSpec as P

BF = jnp.bfloat16
F32 = jnp.float32
TILE = 640
NO_COST = pl.CostEstimate(flops=0, bytes_accessed=0, transcendentals=0)
ANY = pl.BlockSpec(memory_space=pl.ANY)


def contract(first_rows, second_rows):
    return lax.dot_general(
        first_rows, second_rows, (((0,), (0,)), ((), ())), preferred_element_type=F32
    )


def shift(x, axis, step):
    size = lax.axis_size(axis)
    return lax.ppermute(x, axis, [(i, (i + step) % size) for i in range(size)])


def turn(x, step, stage):
    pairs = []
    for z in range(4):
        for y in range(4):
            for h in range(2):
                along_z = (h == 0) == (stage == 0)
                z2, y2 = ((z + step) % 4, y) if along_z else (z, (y + step) % 4)
                core, core2 = h ^ ((z + y) & 1), h ^ ((z2 + y2) & 1)
                pairs.append(((z * 4 + y) * 2 + core, (z2 * 4 + y2) * 2 + core2))
    return lax.ppermute(x, ("z", "y", "c"), pairs)


def in_hbm(x):
    return pltpu.with_memory_space_constraint(x, pltpu.HBM)


def pick(x, dim, index):
    return lax.dynamic_index_in_dim(x, index, dim, keepdims=False)


def split_pair(x):
    high = x.astype(BF)
    return high, (x - high.astype(F32)).astype(BF)


def place_tile(place, buffer, sem, outs, m, zs):
    rows = TILE // (zs * 4)

    def start(at, out, slot):
        block = buffer.at[m, pl.ds(at, rows)]
        pltpu.make_async_copy(block, out.at[slot], sem).start()

    for a in range(zs):
        z = m * zs + a

        @pl.when(place[1] == 0)
        def _():
            for r, out in enumerate(outs):

                @pl.when(((z - place[2] + 4) & 3) == r)
                def _():
                    for k in range(4):
                        start((a * 4 + k) * rows, out, k)

        @pl.when(place[1] == 1)
        def _():
            for r, out in enumerate(outs):
                at = pl.multiple_of((a * 4 + ((place[3] + r) & 3)) * rows, 16)
                start(at, out, z)


def wait_all(buffer, sem):
    pltpu.make_async_copy(buffer, buffer, sem).wait()


def own_kernel(place, a, b, out, lhs, rhs, lhs_sems, rhs_sem):
    m = pl.program_id(0)
    half = rhs.shape[1]

    @pl.when(m == 0)
    def _():
        at = pl.ds(pl.multiple_of((place[1] ^ place[0]) * half, half), half)
        pltpu.make_async_copy(b.at[:, at], rhs, rhs_sem).start()
        for k in range(2):
            at = pl.ds(pl.multiple_of(place[1] * half + k * TILE, TILE), TILE)
            pltpu.make_async_copy(a.at[:, at], lhs.at[k], lhs_sems.at[k]).start()
        wait_all(rhs, rhs_sem)

    wait_all(lhs.at[m], lhs_sems.at[m])
    out[...] = contract(lhs[m], rhs[...])


def cross_kernel(place, a, b, partial, own, ahead1, ahead2, ahead3, held, buffer, held_sems, sem):
    m = pl.program_id(0)

    @pl.when(m == 0)
    def _():
        for k in range(2):
            rows = partial.at[pl.ds(k * TILE, TILE)]
            pltpu.make_async_copy(rows, held.at[k], held_sems.at[k]).start()

    tile = contract(a[...], b[...])
    wait_all(held.at[m], held_sems.at[m])
    buffer[m] = (held[m] + tile).astype(BF)
    place_tile(place, buffer, sem, [own, ahead1, ahead2, ahead3], m, 2)
    pl.when(m == 1)(lambda: wait_all(buffer, sem))


def cross_own(place, grads, acts):
    tokens, half = grads.shape[0], grads.shape[1] // 2
    return pl.pallas_call(
        own_kernel,
        out_shape=jax.ShapeDtypeStruct((half, half), F32),
        grid_spec=pltpu.PrefetchScalarGridSpec(
            num_scalar_prefetch=1,
            grid=(2,),
            in_specs=[pl.BlockSpec(memory_space=pltpu.HBM)] * 2,
            out_specs=pl.BlockSpec((TILE, half), lambda m, p: (m, 0)),
            scratch_shapes=[
                pltpu.VMEM((2, tokens, TILE), BF),
                pltpu.VMEM((tokens, half), BF),
                pltpu.SemaphoreType.DMA((2,)),
                pltpu.SemaphoreType.DMA,
            ],
        ),
        compiler_params=pltpu.CompilerParams(vmem_limit_bytes=28 * 2**20),
        cost_estimate=NO_COST,
        name="cross_own",
    )(place, grads, acts)


def cross_term(place, grads_next, acts_next, partial):
    tokens, half = grads_next.shape[0], grads_next.shape[1] // 2
    out = pltpu.HBM((4, half // 16, half), BF)
    return pl.pallas_call(
        cross_kernel,
        out_shape=[out] * 4,
        grid_spec=pltpu.PrefetchScalarGridSpec(
            num_scalar_prefetch=1,
            grid=(2,),
            in_specs=[
                pl.BlockSpec((tokens, TILE), lambda m, p: (0, p[1] * 2 + m)),
                pl.BlockSpec((tokens, half), lambda m, p: (0, p[1] ^ p[0])),
                ANY,
            ],
            out_specs=[pl.BlockSpec(memory_space=pltpu.HBM)] * 4,
            scratch_shapes=[
                pltpu.VMEM((2, TILE, half), F32),
                pltpu.VMEM((2, TILE, half), BF),
                pltpu.SemaphoreType.DMA((2,)),
                pltpu.SemaphoreType.DMA,
            ],
        ),
        compiler_params=pltpu.CompilerParams(vmem_limit_bytes=28 * 2**20),
        cost_estimate=NO_COST,
        name="cross_term",
    )(place, grads_next, acts_next, partial)


def factor_kernel(place, h_own, g_own, h_next, g_next, after, *rest):
    del after
    outs, (lhs, rhs, buffer, lhs_sems, rhs_sem, sem) = rest[:4], rest[4:]
    m = pl.program_id(0)
    half = rhs.shape[2]

    def fetch(step, with_rhs):
        slot = step & 1
        at = pl.ds(pl.multiple_of(step * TILE, TILE), TILE)
        right = pl.ds(pl.multiple_of(place[1] * half, half), half)
        for owner, refs in enumerate(((h_own, h_next), (g_own, g_next))):

            @pl.when(place[0] == owner)
            def _():
                for k, ref in enumerate(refs):
                    pltpu.make_async_copy(ref.at[:, at], lhs.at[slot, k], lhs_sems.at[slot]).start()
                    if with_rhs:
                        pltpu.make_async_copy(ref.at[:, right], rhs.at[k], rhs_sem).start()

    pl.when(m == 0)(lambda: fetch(0, True))
    pl.when(m < 3)(lambda: fetch(m + 1, False))
    slot = m & 1
    wait_all(lhs.at[slot], lhs_sems.at[slot])
    pl.when(m == 0)(lambda: wait_all(rhs, rhs_sem))

    buffer[m] = (contract(lhs[slot, 0], rhs[0]) + contract(lhs[slot, 1], rhs[1])).astype(BF)
    place_tile(place, buffer, sem, outs, m, 1)
    pl.when(m == 3)(lambda: wait_all(buffer, sem))


def factor_term(place, acts, grads, acts_next, grads_next, after):
    tokens, width = acts.shape
    half = width // 2
    hbm = pl.BlockSpec(memory_space=pltpu.HBM)
    out = pltpu.HBM((4, width // 16, half), BF)
    return pl.pallas_call(
        factor_kernel,
        out_shape=[out] * 4,
        grid_spec=pltpu.PrefetchScalarGridSpec(
            num_scalar_prefetch=1,
            grid=(4,),
            in_specs=[hbm] * 2 + [ANY] * 3,
            out_specs=[hbm] * 4,
            scratch_shapes=[
                pltpu.VMEM((2, 2, tokens, TILE), BF),
                pltpu.VMEM((2, tokens, half), BF),
                pltpu.VMEM((4, TILE, half), BF),
                pltpu.SemaphoreType.DMA((2,)),
                pltpu.SemaphoreType.DMA,
                pltpu.SemaphoreType.DMA,
            ],
        ),
        compiler_params=pltpu.CompilerParams(vmem_limit_bytes=30 * 2**20),
        cost_estimate=NO_COST,
        name="factor_term",
    )(place, acts, grads, acts_next, grads_next, after)


def add(first, *rest):
    total = first.astype(F32)
    for x in rest:
        total = total + x.astype(F32)
    return total


def fold_kernel(count, me, *refs):
    own, *others = refs[-6:-2]
    held, sem = refs[-2:]
    copy = pltpu.make_async_copy(refs[0], held, sem)
    copy.start()
    copy.wait()
    for r, out in enumerate([own, *others]):
        at = (me[0] + r) & 3
        out[...] = add(held[at], *[part[at] for part in refs[1:count]]).astype(out.dtype)


def fold(me, parts, *after):
    _, rows, width = parts[0].shape
    block = pl.BlockSpec((4, rows, width), lambda s, m: (0, 0, 0))
    whole = pl.BlockSpec((rows, width), lambda s, m: (0, 0))
    return pl.pallas_call(
        functools.partial(fold_kernel, len(parts)),
        out_shape=[jax.ShapeDtypeStruct((rows, width), t) for t in (F32, BF, BF, BF)],
        grid_spec=pltpu.PrefetchScalarGridSpec(
            num_scalar_prefetch=1,
            grid=(1,),
            in_specs=[pl.BlockSpec(memory_space=pltpu.HBM)]
            + [block] * (len(parts) - 1)
            + [ANY] * len(after),
            out_specs=[whole] * 4,
            scratch_shapes=[pltpu.VMEM((4, rows, width), BF), pltpu.SemaphoreType.DMA],
        ),
        compiler_params=pltpu.CompilerParams(vmem_limit_bytes=26 * 2**20),
        cost_estimate=NO_COST,
        name="fold",
    )(me, in_hbm(parts[0]), *parts[1:], *after)


def settle_kernel(xl, total, r1, r2, r3, *refs):
    mine, theirs = refs[-2:]
    rows = mine.shape[0]
    for out, index in ((mine, xl[0]), (theirs, 1 - xl[0])):
        at = pl.ds(pl.multiple_of(index * rows, 8), rows)
        value = add(total[at], r1[at], r2[at], r3[at])
        out[...] = value.astype(out.dtype)


def settle(xl, total, received, dtype, *after):
    rows, width = total.shape
    whole = pl.BlockSpec((rows, width), lambda s, x: (0, 0))
    part = pl.BlockSpec((rows // 2, width), lambda s, x: (0, 0))
    return pl.pallas_call(
        settle_kernel,
        out_shape=[jax.ShapeDtypeStruct((rows // 2, width), t) for t in (F32, dtype)],
        grid_spec=pltpu.PrefetchScalarGridSpec(
            num_scalar_prefetch=1,
            grid=(1,),
            in_specs=[whole] * 4 + [ANY] * len(after),
            out_specs=[part] * 2,
        ),
        compiler_params=pltpu.CompilerParams(vmem_limit_bytes=10 * 2**20),
        cost_estimate=NO_COST,
        name="settle",
    )(xl, total, *received, *after)


def fetch_tiles(step, source, held, sems):
    @pl.when(step == 0)
    def _():
        for k in range(4):
            rows = source.at[pl.ds(k * TILE, TILE)]
            pltpu.make_async_copy(rows, held.at[k], sems.at[k]).start()

    wait_all(held.at[step], sems.at[step])


def left_kernel(place, mine, other, partner, partner_other, left, out, total, held, sems):
    step = pl.program_id(0)
    fetch_tiles(step, left, held, sems)
    at = pl.ds(pl.multiple_of((step & 1) * TILE, TILE), TILE)
    rows = mine.shape[0]

    def term(a, b):
        stacked = jnp.concatenate(split_pair(a[:, at] + b[:, at]), axis=0)
        value = jnp.dot(stacked, held[step], preferred_element_type=F32)
        total[...] = jnp.where(step == 0, value, total[...] + value)

    own = (step >> 1) == (place[1] ^ place[0])
    pl.when(own)(lambda: term(mine, other))
    pl.when(jnp.logical_not(own))(lambda: term(partner, partner_other))

    @pl.when(step == 3)
    def _():
        value = total[:rows] + total[rows:]
        for z in range(2):
            for y in range(4):
                for xl in range(2):
                    for c in range(2):
                        at = (((z * 4 + y) * 2 + xl) * 2 + c) * rows
                        block = value[:, at : at + rows]
                        for there in (0, 2):
                            d = c * 32 + (there + z) * 8 + y * 2 + xl
                            for owner in (0, 64):
                                out[owner + d, 0:16, 0:rows] = block[0:16]
                                out[owner + d, 0:16, rows : 2 * rows] = block[16:32]
                                out[owner + d, 0:8, 2 * rows : 3 * rows] = block[32:40]


def left_product(place, mine, other, partner, partner_other, left):
    rows, half = mine.shape
    whole = pl.BlockSpec((rows, half), lambda k, p: (0, 0))
    return pl.pallas_call(
        left_kernel,
        out_shape=jax.ShapeDtypeStruct((128, 16, 128), F32),
        grid_spec=pltpu.PrefetchScalarGridSpec(
            num_scalar_prefetch=1,
            grid=(4,),
            in_specs=[whole] * 4 + [pl.BlockSpec(memory_space=pltpu.HBM)],
            out_specs=pl.BlockSpec((128, 16, 128), lambda k, p: (0, 0, 0)),
            scratch_shapes=[
                pltpu.VMEM((2 * rows, half), F32),
                pltpu.VMEM((4, TILE, half), BF),
                pltpu.SemaphoreType.DMA((4,)),
            ],
        ),
        compiler_params=pltpu.CompilerParams(vmem_limit_bytes=20 * 2**20),
        cost_estimate=NO_COST,
        name="left_product",
    )(place, mine, other, partner, partner_other, left)


def right_kernel(place, blocks, right, late, out, rows_in, held, sems):
    del late
    step = pl.program_id(0)
    fetch_tiles(step, right, held, sems)
    rows = out.shape[0]
    for near in range(2):
        for y in range(4):
            core = (step >> 1) ^ ((near + y) & 1)
            for xl in range(2):
                block = blocks[core * 32 + ((step & 1) * 2 + near) * 8 + y * 2 + xl]
                at = ((near * 4 + y) * 2 + xl) * rows
                rows_in[at : at + 16, :] = block[:, 0:rows]
                rows_in[at + 16 : at + 32, :] = block[:, rows : 2 * rows]
                rows_in[at + 32 : at + 40, :] = block[0:8, 2 * rows : 3 * rows]
    high, low = split_pair(rows_in[...])
    value = contract(high, held[step]) + contract(low, held[step])
    pl.when(step == 0)(lambda: out.__setitem__(..., value))
    pl.when(step > 0)(lambda: out.__setitem__(..., out[...] + value))


def right_product(place, blocks, right, late):
    width, half = right.shape
    rows = width // 64
    return pl.pallas_call(
        right_kernel,
        out_shape=jax.ShapeDtypeStruct((rows, half), F32),
        grid_spec=pltpu.PrefetchScalarGridSpec(
            num_scalar_prefetch=1,
            grid=(4,),
            in_specs=[
                pl.BlockSpec((64, 16, 128), lambda k, p: (p[2] >> 1, 0, 0)),
                pl.BlockSpec(memory_space=pltpu.HBM),
                ANY,
            ],
            out_specs=pl.BlockSpec((rows, half), lambda k, p: (0, 0)),
            scratch_shapes=[
                pltpu.VMEM((TILE, rows), F32),
                pltpu.VMEM((4, TILE, half), BF),
                pltpu.SemaphoreType.DMA((4,)),
            ],
        ),
        compiler_params=pltpu.CompilerParams(vmem_limit_bytes=20 * 2**20),
        cost_estimate=NO_COST,
        name="right_product",
    )(place, blocks, right, late)


def per_device(hidden, out_grad, left_inverse, right_inverse):
    z, y, xl, c, o = (lax.axis_index(n) for n in ("z", "y", "xl", "c", "o"))
    tokens, width = hidden.shape
    half = width // 2
    token_total = tokens * 64
    first = o == 0
    h = c ^ ((z + y) & 1)
    hidden, out_grad = in_hbm(hidden), in_hbm(out_grad)
    left_inverse, right_inverse = in_hbm(left_inverse), in_hbm(right_inverse)
    place = jnp.stack([o, h, z, y]).astype(jnp.int32)
    second_me = jnp.where(h == 0, y, z).astype(jnp.int32)[None]

    grads_next, acts_next = in_hbm(shift(out_grad, "c", 1)), in_hbm(shift(hidden, "c", 1))
    partial = cross_own(place, out_grad, hidden)

    own, m1, m2, m3 = cross_term(place, grads_next, acts_next, partial)
    m_parts = [own, turn(m1, 1, 0), turn(m2, 2, 0), turn(m3, 3, 0)]

    f_own, f1, f2, f3 = factor_term(place, hidden, out_grad, acts_next, grads_next, in_hbm(m1))
    f_parts = [f_own, turn(f1, 1, 0), turn(f2, 2, 0), turn(f3, 3, 0)]

    my_xl = xl.astype(jnp.int32)[None]

    def second_sends(pieces):
        return [turn(piece, s, 1) for s, piece in enumerate(pieces, 1)]

    m, *m_pieces = fold(second_me, m_parts, in_hbm(f_own))
    m_received = second_sends(m_pieces)
    mine, theirs = settle(my_xl, m, m_received, F32)
    across = lax.ppermute(theirs, ("xl", "o"), [(i, 3 - i) for i in range(4)])
    products = left_product(
        place, mine, shift(theirs, "xl", 1), shift(mine, "o", 1), across, left_inverse
    )
    blocks = lax.all_to_all(products, ("o", "c", "z", "y", "xl"), 0, 0, tiled=True)
    f, *f_pieces = fold(second_me, f_parts, products)
    f_mine, f_theirs = settle(my_xl, f, second_sends(f_pieces), BF, blocks)
    update = right_product(place, blocks, right_inverse, f_pieces[0])

    f = add(f_mine, shift(f_theirs, "xl", 1))
    f = f * jnp.where(first, 1.0 / token_total, 1.0).astype(F32)
    f = f.reshape(2, width // 64, half)
    mine = pick(f, 0, c)
    theirs = shift(pick(f, 0, 1 - c), "c", 1)
    factors = jnp.concatenate(
        [jnp.where(h == 0, mine, theirs), jnp.where(h == 0, theirs, mine)], axis=1
    )[None]
    return factors, update


def solution(mesh):
    fine = Mesh(mesh.devices.reshape(4, 4, 2, 2, 2), ("z", "y", "xl", "c", "o"))
    dp = ("z", "y", "xl", "c")
    in_specs = (P(dp, None), P(dp, None), P(None, "o"), P(None, "o"))
    out_specs = (P("o", dp, None), P(dp, "o"))
    return jax.shard_map(
        per_device, mesh=fine, in_specs=in_specs, out_specs=out_specs, check_vma=False
    )
```

```python
import functools

import jax
import jax.numpy as jnp
from jax import lax
from jax.experimental import pallas as pl
from jax.experimental.pallas import tpu as pltpu
from jax.sharding import Mesh, PartitionSpec as P

BF = jnp.bfloat16
F32 = jnp.float32
TILE = 640
NO_COST = pl.CostEstimate(flops=0, bytes_accessed=0, transcendentals=0)
ANY = pl.BlockSpec(memory_space=pl.ANY)


def contract(first_rows, second_rows):
    return lax.dot_general(
        first_rows, second_rows, (((0,), (0,)), ((), ())), preferred_element_type=F32
    )


def shift(x, axis, step):
    size = lax.axis_size(axis)
    return lax.ppermute(x, axis, [(i, (i + step) % size) for i in range(size)])


def turn(x, step, stage):
    pairs = []
    for z in range(4):
        for y in range(4):
            for h in range(2):
                along_z = (h == 0) == (stage == 0)
                z2, y2 = ((z + step) % 4, y) if along_z else (z, (y + step) % 4)
                core, core2 = h ^ ((z + y) & 1), h ^ ((z2 + y2) & 1)
                pairs.append(((z * 4 + y) * 2 + core, (z2 * 4 + y2) * 2 + core2))
    return lax.ppermute(x, ("z", "y", "c"), pairs)


def in_hbm(x):
    return pltpu.with_memory_space_constraint(x, pltpu.HBM)


def pick(x, dim, index):
    return lax.dynamic_index_in_dim(x, index, dim, keepdims=False)


def split_pair(x):
    high = x.astype(BF)
    return high, (x - high.astype(F32)).astype(BF)


def place_tile(place, buffer, sem, outs, z):
    rows = TILE // 4

    def start(at, out, slot):
        block = buffer.at[z, pl.ds(at, rows)]
        pltpu.make_async_copy(block, out.at[slot], sem).start()

    @pl.when(place[1] == 0)
    def _():
        for r, out in enumerate(outs):

            @pl.when(((z - place[2] + 4) & 3) == r)
            def _():
                for k in range(4):
                    if isinstance(out, tuple):
                        start(k * rows, out[k // 2], k % 2)
                    else:
                        start(k * rows, out, k)

    @pl.when(place[1] == 1)
    def _():
        for r, out in enumerate(outs):
            at = pl.multiple_of(((place[3] + r) & 3) * rows, 16)
            if isinstance(out, tuple):
                pl.when(z < 2)(functools.partial(start, at, out[0], z & 1))
                pl.when(z >= 2)(functools.partial(start, at, out[1], z & 1))
            else:
                start(at, out, z)


def wait_all(buffer, sem):
    pltpu.make_async_copy(buffer, buffer, sem).wait()


def own_kernel(place, a, b, out, lhs, rhs, lhs_sems, rhs_sem):
    m = pl.program_id(0)
    half = rhs.shape[1]

    @pl.when(m == 0)
    def _():
        at = pl.ds(pl.multiple_of((place[1] ^ place[0]) * half, half), half)
        pltpu.make_async_copy(b.at[:, at], rhs, rhs_sem).start()
        for k in range(2):
            at = pl.ds(pl.multiple_of(place[1] * half + k * TILE, TILE), TILE)
            pltpu.make_async_copy(a.at[:, at], lhs.at[k], lhs_sems.at[k]).start()
        wait_all(rhs, rhs_sem)

    wait_all(lhs.at[m], lhs_sems.at[m])
    out[...] = contract(lhs[m], rhs[...])


def cross_kernel(place, a, b, partial, out, held, held_sems):
    m = pl.program_id(0)

    @pl.when(m == 0)
    def _():
        for k in range(2):
            rows = partial.at[pl.ds(k * TILE, TILE)]
            pltpu.make_async_copy(rows, held.at[k], held_sems.at[k]).start()

    tile = contract(a[...], b[...])
    wait_all(held.at[m], held_sems.at[m])
    out[...] = (held[m] + tile).astype(BF).reshape(out.shape)


def cross_own(place, grads, acts):
    tokens, half = grads.shape[0], grads.shape[1] // 2
    return pl.pallas_call(
        own_kernel,
        out_shape=jax.ShapeDtypeStruct((half, half), F32),
        grid_spec=pltpu.PrefetchScalarGridSpec(
            num_scalar_prefetch=1,
            grid=(2,),
            in_specs=[pl.BlockSpec(memory_space=pltpu.HBM)] * 2,
            out_specs=pl.BlockSpec((TILE, half), lambda m, p: (m, 0)),
            scratch_shapes=[
                pltpu.VMEM((2, tokens, TILE), BF),
                pltpu.VMEM((tokens, half), BF),
                pltpu.SemaphoreType.DMA((2,)),
                pltpu.SemaphoreType.DMA,
            ],
        ),
        compiler_params=pltpu.CompilerParams(vmem_limit_bytes=28 * 2**20),
        cost_estimate=NO_COST,
        name="cross_own",
    )(place, grads, acts)


def cross_term(place, grads_next, acts_next, partial):
    tokens, half = grads_next.shape[0], grads_next.shape[1] // 2
    return pl.pallas_call(
        cross_kernel,
        out_shape=pltpu.HBM((16, half // 16, half), BF),
        grid_spec=pltpu.PrefetchScalarGridSpec(
            num_scalar_prefetch=1,
            grid=(2,),
            in_specs=[
                pl.BlockSpec((tokens, TILE), lambda m, p: (0, p[1] * 2 + m)),
                pl.BlockSpec((tokens, half), lambda m, p: (0, p[1] ^ p[0])),
                ANY,
            ],
            out_specs=pl.BlockSpec((8, half // 16, half), lambda m, p: (m, 0, 0)),
            scratch_shapes=[pltpu.VMEM((2, TILE, half), F32), pltpu.SemaphoreType.DMA((2,))],
        ),
        compiler_params=pltpu.CompilerParams(vmem_limit_bytes=28 * 2**20),
        cost_estimate=NO_COST,
        name="cross_term",
    )(place, grads_next, acts_next, partial)


def factor_kernel(place, h_own, g_own, h_next, g_next, after, *rest):
    del after
    own, right, far_a, far_b, left, lhs, rhs, buffer, lhs_sems, rhs_sem, sem = rest
    m = pl.program_id(0)
    half = rhs.shape[2]

    def fetch(step, with_rhs):
        slot = step & 1
        at = pl.ds(pl.multiple_of(step * TILE, TILE), TILE)
        columns = pl.ds(pl.multiple_of(place[1] * half, half), half)
        for owner, refs in enumerate(((h_own, h_next), (g_own, g_next))):

            @pl.when(place[0] == owner)
            def _():
                for k, ref in enumerate(refs):
                    pltpu.make_async_copy(ref.at[:, at], lhs.at[slot, k], lhs_sems.at[slot]).start()
                    if with_rhs:
                        pltpu.make_async_copy(ref.at[:, columns], rhs.at[k], rhs_sem).start()

    pl.when(m == 0)(lambda: fetch(0, True))
    pl.when(m < 3)(lambda: fetch(m + 1, False))
    slot = m & 1
    wait_all(lhs.at[slot], lhs_sems.at[slot])
    pl.when(m == 0)(lambda: wait_all(rhs, rhs_sem))

    buffer[m] = (contract(lhs[slot, 0], rhs[0]) + contract(lhs[slot, 1], rhs[1])).astype(BF)
    place_tile(place, buffer, sem, [own, right, (far_a, far_b), left], m)
    pl.when(m == 3)(lambda: wait_all(buffer, sem))


def factor_term(place, acts, grads, acts_next, grads_next, after):
    tokens, width = acts.shape
    half = width // 2
    hbm = pl.BlockSpec(memory_space=pltpu.HBM)
    out = pltpu.HBM((4, width // 16, half), BF)
    side = pltpu.HBM((2, width // 16, half), BF)
    return pl.pallas_call(
        factor_kernel,
        out_shape=[out, out, side, side, out],
        grid_spec=pltpu.PrefetchScalarGridSpec(
            num_scalar_prefetch=1,
            grid=(4,),
            in_specs=[hbm] * 2 + [ANY] * 3,
            out_specs=[hbm] * 5,
            scratch_shapes=[
                pltpu.VMEM((2, 2, tokens, TILE), BF),
                pltpu.VMEM((2, tokens, half), BF),
                pltpu.VMEM((4, TILE, half), BF),
                pltpu.SemaphoreType.DMA((2,)),
                pltpu.SemaphoreType.DMA,
                pltpu.SemaphoreType.DMA,
            ],
        ),
        compiler_params=pltpu.CompilerParams(vmem_limit_bytes=30 * 2**20),
        cost_estimate=NO_COST,
        name="factor_term",
    )(place, acts, grads, acts_next, grads_next, after)


def add(first, *rest):
    total = first.astype(F32)
    for x in rest:
        total = total + x.astype(F32)
    return total


def fold_kernel(count, me, *refs):
    own, *others = refs[-6:-2]
    held, sem = refs[-2:]
    copy = pltpu.make_async_copy(refs[0], held, sem)
    copy.start()
    copy.wait()
    for r, out in enumerate([own, *others]):
        at = (me[0] + r) & 3
        out[...] = add(held[at], *[part[at] for part in refs[1:count]]).astype(out.dtype)


def fold(me, parts, *after):
    _, rows, width = parts[0].shape
    block = pl.BlockSpec((4, rows, width), lambda s, m: (0, 0, 0))
    whole = pl.BlockSpec((rows, width), lambda s, m: (0, 0))
    return pl.pallas_call(
        functools.partial(fold_kernel, len(parts)),
        out_shape=[jax.ShapeDtypeStruct((rows, width), t) for t in (F32, BF, BF, BF)],
        grid_spec=pltpu.PrefetchScalarGridSpec(
            num_scalar_prefetch=1,
            grid=(1,),
            in_specs=[pl.BlockSpec(memory_space=pltpu.HBM)]
            + [block] * (len(parts) - 1)
            + [ANY] * len(after),
            out_specs=[whole] * 4,
            scratch_shapes=[pltpu.VMEM((4, rows, width), BF), pltpu.SemaphoreType.DMA],
        ),
        compiler_params=pltpu.CompilerParams(vmem_limit_bytes=26 * 2**20),
        cost_estimate=NO_COST,
        name="fold",
    )(me, in_hbm(parts[0]), *parts[1:], *after)


def settle_kernel(count, xl, *refs):
    mine, theirs, total = refs[-3:]
    rows = mine.shape[0]
    value = None
    for ref in refs[:count]:
        for part in [ref[...]] if len(ref.shape) == 2 else [ref[k] for k in range(ref.shape[0])]:
            value = part.astype(F32) if value is None else value + part.astype(F32)
    total[...] = value
    for out, index in ((mine, xl[0]), (theirs, 1 - xl[0])):
        out[...] = total[pl.ds(pl.multiple_of(index * rows, 8), rows)].astype(out.dtype)


def settle(xl, parts, dtype, *after):
    rows, width = parts[0].shape[-2:]
    half = pl.BlockSpec((rows // 2, width), lambda s, x: (0, 0))
    return pl.pallas_call(
        functools.partial(settle_kernel, len(parts)),
        out_shape=[jax.ShapeDtypeStruct((rows // 2, width), t) for t in (F32, dtype)],
        grid_spec=pltpu.PrefetchScalarGridSpec(
            num_scalar_prefetch=1,
            grid=(1,),
            in_specs=[pl.BlockSpec(p.shape, lambda s, x, n=p.ndim: (0,) * n) for p in parts]
            + [ANY] * len(after),
            out_specs=[half] * 2,
            scratch_shapes=[pltpu.VMEM((rows, width), F32)],
        ),
        compiler_params=pltpu.CompilerParams(vmem_limit_bytes=16 * 2**20),
        cost_estimate=NO_COST,
        name="settle",
    )(xl, *parts, *after)


def grow_kernel(side, x, received, *refs):
    out, held, sems, out_sem = refs[-4:]
    for k in range(2):
        pltpu.make_async_copy(x.at[side * 2 + k], held.at[k], sems.at[k]).start()
    for k in range(2):
        wait_all(held.at[k], sems.at[k])
        held[k] = add(held[k], received[k]).astype(BF)
        pltpu.make_async_copy(held.at[k], out.at[side * 2 + k], out_sem).start()
    wait_all(held, out_sem)


def grow(x, received, side, *after):
    hbm = pl.BlockSpec(memory_space=pltpu.HBM)
    return pl.pallas_call(
        functools.partial(grow_kernel, side),
        out_shape=pltpu.HBM(x.shape, x.dtype),
        grid=(1,),
        in_specs=[hbm, pl.BlockSpec(received.shape, lambda s: (0, 0, 0))] + [ANY] * len(after),
        out_specs=hbm,
        scratch_shapes=[
            pltpu.VMEM(received.shape, x.dtype),
            pltpu.SemaphoreType.DMA((2,)),
            pltpu.SemaphoreType.DMA,
        ],
        input_output_aliases={0: 0},
        compiler_params=pltpu.CompilerParams(vmem_limit_bytes=8 * 2**20),
        cost_estimate=NO_COST,
        name="grow",
    )(in_hbm(x), received, *after)


def fetch_tiles(step, source, held, sems):
    @pl.when(step == 0)
    def _():
        for k in range(4):
            rows = source.at[pl.ds(k * TILE, TILE)]
            pltpu.make_async_copy(rows, held.at[k], sems.at[k]).start()

    wait_all(held.at[step], sems.at[step])


def left_kernel(place, mine, other, partner, partner_other, left, out, total, packed, held, sems):
    step = pl.program_id(0)
    fetch_tiles(step, left, held, sems)
    at = pl.ds(pl.multiple_of((step & 1) * TILE, TILE), TILE)
    rows = mine.shape[0]

    def term(a, b):
        stacked = jnp.concatenate(split_pair(a[:, at] + b[:, at]), axis=0)
        value = jnp.dot(stacked, held[step], preferred_element_type=F32)
        total[...] = jnp.where(step == 0, value, total[...] + value)

    own = (step >> 1) == (place[1] ^ place[0])
    pl.when(own)(lambda: term(mine, other))
    pl.when(jnp.logical_not(own))(lambda: term(partner, partner_other))

    @pl.when(step == 3)
    def _():
        value = total[:rows] + total[rows:]
        for z in range(2):
            for y in range(4):
                for xl in range(2):
                    for c in range(2):
                        n = ((z * 4 + y) * 2 + xl) * 2 + c
                        block = value[:, n * rows : (n + 1) * rows]
                        packed[n, 0:16, 0:rows] = block[0:16]
                        packed[n, 0:16, rows : 2 * rows] = block[16:32]
                        packed[n, 0:8, 2 * rows : 3 * rows] = block[32:40]
                        ready = packed[n].astype(BF)
                        for there in (0, 2):
                            d = c * 32 + (there + z) * 8 + y * 2 + xl
                            out[d] = ready
                            out[64 + d] = ready


def left_product(place, mine, other, partner, partner_other, left):
    rows, half = mine.shape
    whole = pl.BlockSpec((rows, half), lambda k, p: (0, 0))
    return pl.pallas_call(
        left_kernel,
        out_shape=jax.ShapeDtypeStruct((128, 16, 128), BF),
        grid_spec=pltpu.PrefetchScalarGridSpec(
            num_scalar_prefetch=1,
            grid=(4,),
            in_specs=[whole] * 4 + [pl.BlockSpec(memory_space=pltpu.HBM)],
            out_specs=pl.BlockSpec((128, 16, 128), lambda k, p: (0, 0, 0)),
            scratch_shapes=[
                pltpu.VMEM((2 * rows, half), F32),
                pltpu.VMEM((32, 16, 128), F32),
                pltpu.VMEM((4, TILE, half), BF),
                pltpu.SemaphoreType.DMA((4,)),
            ],
        ),
        compiler_params=pltpu.CompilerParams(vmem_limit_bytes=20 * 2**20),
        cost_estimate=NO_COST,
        name="left_product",
    )(place, mine, other, partner, partner_other, left)


def right_kernel(place, blocks, right, late, out, rows_in, held, sems):
    del late
    step = pl.program_id(0)
    fetch_tiles(step, right, held, sems)
    rows = out.shape[0]
    for near in range(2):
        for y in range(4):
            for xl in range(2):
                block = blocks[(step >> 1) * 32 + ((step & 1) * 2 + near) * 8 + y * 2 + xl].astype(F32)
                at = ((near * 4 + y) * 2 + xl) * rows
                rows_in[at : at + 16, :] = block[:, 0:rows]
                rows_in[at + 16 : at + 32, :] = block[:, rows : 2 * rows]
                rows_in[at + 32 : at + 40, :] = block[0:8, 2 * rows : 3 * rows]
    value = contract(rows_in[...].astype(BF), held[step])
    pl.when(step == 0)(lambda: out.__setitem__(..., value))
    pl.when(step > 0)(lambda: out.__setitem__(..., out[...] + value))


def right_product(place, blocks, right, late):
    width, half = right.shape
    rows = width // 64
    return pl.pallas_call(
        right_kernel,
        out_shape=jax.ShapeDtypeStruct((rows, half), F32),
        grid_spec=pltpu.PrefetchScalarGridSpec(
            num_scalar_prefetch=1,
            grid=(4,),
            in_specs=[
                pl.BlockSpec((64, 16, 128), lambda k, p: (p[2] >> 1, 0, 0)),
                pl.BlockSpec(memory_space=pltpu.HBM),
                ANY,
            ],
            out_specs=pl.BlockSpec((rows, half), lambda k, p: (0, 0)),
            scratch_shapes=[
                pltpu.VMEM((TILE, rows), F32),
                pltpu.VMEM((4, TILE, half), BF),
                pltpu.SemaphoreType.DMA((4,)),
            ],
        ),
        compiler_params=pltpu.CompilerParams(vmem_limit_bytes=20 * 2**20),
        cost_estimate=NO_COST,
        name="right_product",
    )(place, blocks, right, late)


def per_device(hidden, out_grad, left_inverse, right_inverse):
    z, y, xl, c, o = (lax.axis_index(n) for n in ("z", "y", "xl", "c", "o"))
    tokens, width = hidden.shape
    half = width // 2
    token_total = tokens * 64
    first = o == 0
    h = c ^ ((z + y) & 1)
    hidden, out_grad = in_hbm(hidden), in_hbm(out_grad)
    left_inverse, right_inverse = in_hbm(left_inverse), in_hbm(right_inverse)
    place = jnp.stack([o, c, z, y]).astype(jnp.int32)
    place_h = jnp.stack([o, h, z, y]).astype(jnp.int32)
    second_me = jnp.where(h == 0, y, z).astype(jnp.int32)[None]

    grads_next, acts_next = in_hbm(shift(out_grad, "c", 1)), in_hbm(shift(hidden, "c", 1))
    partial = cross_own(place, out_grad, hidden)

    m = cross_term(place, grads_next, acts_next, partial)
    m_blocks = lax.all_to_all(m, ("z", "y"), 0, 0, tiled=True)

    f_own, right, far_a, far_b, left = factor_term(
        place_h, hidden, out_grad, acts_next, grads_next, in_hbm(m)
    )
    from_left, from_right = turn(far_a, 1, 0), turn(far_b, -1, 0)

    my_xl = xl.astype(jnp.int32)[None]

    def second_sends(pieces):
        return [turn(piece, s, 1) for s, piece in enumerate(pieces, 1)]

    right, left = grow(right, from_left, 0), grow(left, from_right, 1)
    f_parts = [f_own, turn(right, 1, 0), turn(left, -1, 0)]

    mine, theirs = settle(my_xl, [m_blocks], F32, in_hbm(right), in_hbm(left))
    across = lax.ppermute(theirs, ("xl", "o"), [(i, 3 - i) for i in range(4)])
    products = left_product(
        place, mine, shift(theirs, "xl", 1), shift(mine, "o", 1), across, left_inverse
    )
    blocks = lax.all_to_all(products, ("o", "c", "z", "y", "xl"), 0, 0, tiled=True)
    f, *f_pieces = fold(second_me, f_parts, products)
    f_mine, f_theirs = settle(my_xl, [f, *second_sends(f_pieces)], BF)
    update = right_product(place, blocks, right_inverse, f_pieces[0])

    f = add(f_mine, shift(f_theirs, "xl", 1))
    f = f * jnp.where(first, 1.0 / token_total, 1.0).astype(F32)
    f = f.reshape(2, width // 64, half)
    mine = pick(f, 0, c)
    theirs = shift(pick(f, 0, 1 - c), "c", 1)
    factors = jnp.concatenate(
        [jnp.where(h == 0, mine, theirs), jnp.where(h == 0, theirs, mine)], axis=1
    )[None]
    return factors, update


def solution(mesh):
    fine = Mesh(mesh.devices.reshape(4, 4, 2, 2, 2), ("z", "y", "xl", "c", "o"))
    dp = ("z", "y", "xl", "c")
    in_specs = (P(dp, None), P(dp, None), P(None, "o"), P(None, "o"))
    out_specs = (P("o", dp, None), P(dp, "o"))
    return jax.shard_map(
        per_device, mesh=fine, in_specs=in_specs, out_specs=out_specs, check_vma=False
    )
```

```python
import functools

import jax
import jax.numpy as jnp
from jax import lax
from jax.experimental import pallas as pl
from jax.experimental.pallas import tpu as pltpu
from jax.sharding import Mesh, PartitionSpec as P

BF = jnp.bfloat16
F32 = jnp.float32
TILE = 640
NO_COST = pl.CostEstimate(flops=0, bytes_accessed=0, transcendentals=0)
ANY = pl.BlockSpec(memory_space=pl.ANY)


def contract(first_rows, second_rows):
    return lax.dot_general(
        first_rows, second_rows, (((0,), (0,)), ((), ())), preferred_element_type=F32
    )


def shift(x, axis, step):
    size = lax.axis_size(axis)
    return lax.ppermute(x, axis, [(i, (i + step) % size) for i in range(size)])


def turn(x, step, stage):
    pairs = []
    for z in range(4):
        for y in range(4):
            for h in range(2):
                along_z = (h == 0) == (stage == 0)
                z2, y2 = ((z + step) % 4, y) if along_z else (z, (y + step) % 4)
                core, core2 = h ^ ((z + y) & 1), h ^ ((z2 + y2) & 1)
                pairs.append(((z * 4 + y) * 2 + core, (z2 * 4 + y2) * 2 + core2))
    return lax.ppermute(x, ("z", "y", "c"), pairs)


def in_hbm(x):
    return pltpu.with_memory_space_constraint(x, pltpu.HBM)


def pick(x, dim, index):
    return lax.dynamic_index_in_dim(x, index, dim, keepdims=False)


def split_pair(x):
    high = x.astype(BF)
    return high, (x - high.astype(F32)).astype(BF)


def place_tile(place, buffer, sem, outs, m, zs):
    rows = TILE // (zs * 4)

    def start(at, out, slot):
        block = buffer.at[m, pl.ds(at, rows)]
        pltpu.make_async_copy(block, out.at[slot], sem).start()

    for a in range(zs):
        z = m * zs + a

        @pl.when(place[1] == 0)
        def _():
            for r, out in enumerate(outs):

                @pl.when(((z - place[2] + 4) & 3) == r)
                def _():
                    for k in range(4):
                        if isinstance(out, tuple):
                            start((a * 4 + k) * rows, out[k // 2], k % 2)
                        else:
                            start((a * 4 + k) * rows, out, k)

        @pl.when(place[1] == 1)
        def _():
            for r, out in enumerate(outs):
                at = pl.multiple_of((a * 4 + ((place[3] + r) & 3)) * rows, 16)
                if isinstance(out, tuple):
                    pl.when(z < 2)(functools.partial(start, at, out[0], z & 1))
                    pl.when(z >= 2)(functools.partial(start, at, out[1], z & 1))
                else:
                    start(at, out, z)


def wait_all(buffer, sem):
    pltpu.make_async_copy(buffer, buffer, sem).wait()


def own_kernel(place, a, b, out, lhs, rhs, lhs_sems, rhs_sem):
    m = pl.program_id(0)
    half = rhs.shape[1]

    @pl.when(m == 0)
    def _():
        at = pl.ds(pl.multiple_of((place[1] ^ place[0]) * half, half), half)
        pltpu.make_async_copy(b.at[:, at], rhs, rhs_sem).start()
        for k in range(2):
            at = pl.ds(pl.multiple_of(place[1] * half + k * TILE, TILE), TILE)
            pltpu.make_async_copy(a.at[:, at], lhs.at[k], lhs_sems.at[k]).start()
        wait_all(rhs, rhs_sem)

    wait_all(lhs.at[m], lhs_sems.at[m])
    out[...] = contract(lhs[m], rhs[...])


def cross_kernel(place, a, b, partial, own, ahead1, ahead2, ahead3, held, buffer, held_sems, sem):
    m = pl.program_id(0)

    @pl.when(m == 0)
    def _():
        for k in range(2):
            rows = partial.at[pl.ds(k * TILE, TILE)]
            pltpu.make_async_copy(rows, held.at[k], held_sems.at[k]).start()

    tile = contract(a[...], b[...])
    wait_all(held.at[m], held_sems.at[m])
    buffer[m] = (held[m] + tile).astype(BF)
    place_tile(place, buffer, sem, [own, ahead1, ahead2, ahead3], m, 2)
    pl.when(m == 1)(lambda: wait_all(buffer, sem))


def cross_own(place, grads, acts):
    tokens, half = grads.shape[0], grads.shape[1] // 2
    return pl.pallas_call(
        own_kernel,
        out_shape=jax.ShapeDtypeStruct((half, half), F32),
        grid_spec=pltpu.PrefetchScalarGridSpec(
            num_scalar_prefetch=1,
            grid=(2,),
            in_specs=[pl.BlockSpec(memory_space=pltpu.HBM)] * 2,
            out_specs=pl.BlockSpec((TILE, half), lambda m, p: (m, 0)),
            scratch_shapes=[
                pltpu.VMEM((2, tokens, TILE), BF),
                pltpu.VMEM((tokens, half), BF),
                pltpu.SemaphoreType.DMA((2,)),
                pltpu.SemaphoreType.DMA,
            ],
        ),
        compiler_params=pltpu.CompilerParams(vmem_limit_bytes=28 * 2**20),
        cost_estimate=NO_COST,
        name="cross_own",
    )(place, grads, acts)


def cross_term(place, grads_next, acts_next, partial):
    tokens, half = grads_next.shape[0], grads_next.shape[1] // 2
    out = pltpu.HBM((4, half // 16, half), BF)
    return pl.pallas_call(
        cross_kernel,
        out_shape=[out] * 4,
        grid_spec=pltpu.PrefetchScalarGridSpec(
            num_scalar_prefetch=1,
            grid=(2,),
            in_specs=[
                pl.BlockSpec((tokens, TILE), lambda m, p: (0, p[1] * 2 + m)),
                pl.BlockSpec((tokens, half), lambda m, p: (0, p[1] ^ p[0])),
                ANY,
            ],
            out_specs=[pl.BlockSpec(memory_space=pltpu.HBM)] * 4,
            scratch_shapes=[
                pltpu.VMEM((2, TILE, half), F32),
                pltpu.VMEM((2, TILE, half), BF),
                pltpu.SemaphoreType.DMA((2,)),
                pltpu.SemaphoreType.DMA,
            ],
        ),
        compiler_params=pltpu.CompilerParams(vmem_limit_bytes=28 * 2**20),
        cost_estimate=NO_COST,
        name="cross_term",
    )(place, grads_next, acts_next, partial)


def factor_kernel(place, h_own, g_own, h_next, g_next, after, *rest):
    del after
    own, right, far_a, far_b, left, lhs, rhs, buffer, lhs_sems, rhs_sem, sem = rest
    m = pl.program_id(0)
    half = rhs.shape[2]

    def fetch(step, with_rhs):
        slot = step & 1
        at = pl.ds(pl.multiple_of(step * TILE, TILE), TILE)
        columns = pl.ds(pl.multiple_of(place[1] * half, half), half)
        for owner, refs in enumerate(((h_own, h_next), (g_own, g_next))):

            @pl.when(place[0] == owner)
            def _():
                for k, ref in enumerate(refs):
                    pltpu.make_async_copy(ref.at[:, at], lhs.at[slot, k], lhs_sems.at[slot]).start()
                    if with_rhs:
                        pltpu.make_async_copy(ref.at[:, columns], rhs.at[k], rhs_sem).start()

    pl.when(m == 0)(lambda: fetch(0, True))
    pl.when(m < 3)(lambda: fetch(m + 1, False))
    slot = m & 1
    wait_all(lhs.at[slot], lhs_sems.at[slot])
    pl.when(m == 0)(lambda: wait_all(rhs, rhs_sem))

    buffer[m] = (contract(lhs[slot, 0], rhs[0]) + contract(lhs[slot, 1], rhs[1])).astype(BF)
    place_tile(place, buffer, sem, [own, right, (far_a, far_b), left], m, 1)
    pl.when(m == 3)(lambda: wait_all(buffer, sem))


def factor_term(place, acts, grads, acts_next, grads_next, after):
    tokens, width = acts.shape
    half = width // 2
    hbm = pl.BlockSpec(memory_space=pltpu.HBM)
    out = pltpu.HBM((4, width // 16, half), BF)
    side = pltpu.HBM((2, width // 16, half), BF)
    return pl.pallas_call(
        factor_kernel,
        out_shape=[out, out, side, side, out],
        grid_spec=pltpu.PrefetchScalarGridSpec(
            num_scalar_prefetch=1,
            grid=(4,),
            in_specs=[hbm] * 2 + [ANY] * 3,
            out_specs=[hbm] * 5,
            scratch_shapes=[
                pltpu.VMEM((2, 2, tokens, TILE), BF),
                pltpu.VMEM((2, tokens, half), BF),
                pltpu.VMEM((4, TILE, half), BF),
                pltpu.SemaphoreType.DMA((2,)),
                pltpu.SemaphoreType.DMA,
                pltpu.SemaphoreType.DMA,
            ],
        ),
        compiler_params=pltpu.CompilerParams(vmem_limit_bytes=30 * 2**20),
        cost_estimate=NO_COST,
        name="factor_term",
    )(place, acts, grads, acts_next, grads_next, after)


def add(first, *rest):
    total = first.astype(F32)
    for x in rest:
        total = total + x.astype(F32)
    return total


def fold_kernel(count, me, *refs):
    own, *others = refs[-6:-2]
    held, sem = refs[-2:]
    copy = pltpu.make_async_copy(refs[0], held, sem)
    copy.start()
    copy.wait()
    for r, out in enumerate([own, *others]):
        at = (me[0] + r) & 3
        out[...] = add(held[at], *[part[at] for part in refs[1:count]]).astype(out.dtype)


def fold(me, parts, *after):
    _, rows, width = parts[0].shape
    block = pl.BlockSpec((4, rows, width), lambda s, m: (0, 0, 0))
    whole = pl.BlockSpec((rows, width), lambda s, m: (0, 0))
    return pl.pallas_call(
        functools.partial(fold_kernel, len(parts)),
        out_shape=[jax.ShapeDtypeStruct((rows, width), t) for t in (F32, BF, BF, BF)],
        grid_spec=pltpu.PrefetchScalarGridSpec(
            num_scalar_prefetch=1,
            grid=(1,),
            in_specs=[pl.BlockSpec(memory_space=pltpu.HBM)]
            + [block] * (len(parts) - 1)
            + [ANY] * len(after),
            out_specs=[whole] * 4,
            scratch_shapes=[pltpu.VMEM((4, rows, width), BF), pltpu.SemaphoreType.DMA],
        ),
        compiler_params=pltpu.CompilerParams(vmem_limit_bytes=26 * 2**20),
        cost_estimate=NO_COST,
        name="fold",
    )(me, in_hbm(parts[0]), *parts[1:], *after)


def settle_kernel(count, xl, *refs):
    mine, theirs, total = refs[-3:]
    rows = mine.shape[0]
    value = None
    for ref in refs[:count]:
        for part in [ref[...]] if len(ref.shape) == 2 else [ref[k] for k in range(ref.shape[0])]:
            value = part.astype(F32) if value is None else value + part.astype(F32)
    total[...] = value
    for out, index in ((mine, xl[0]), (theirs, 1 - xl[0])):
        out[...] = total[pl.ds(pl.multiple_of(index * rows, 8), rows)].astype(out.dtype)


def settle(xl, parts, dtype, *after):
    rows, width = parts[0].shape[-2:]
    half = pl.BlockSpec((rows // 2, width), lambda s, x: (0, 0))
    return pl.pallas_call(
        functools.partial(settle_kernel, len(parts)),
        out_shape=[jax.ShapeDtypeStruct((rows // 2, width), t) for t in (F32, dtype)],
        grid_spec=pltpu.PrefetchScalarGridSpec(
            num_scalar_prefetch=1,
            grid=(1,),
            in_specs=[pl.BlockSpec(p.shape, lambda s, x, n=p.ndim: (0,) * n) for p in parts]
            + [ANY] * len(after),
            out_specs=[half] * 2,
            scratch_shapes=[pltpu.VMEM((rows, width), F32)],
        ),
        compiler_params=pltpu.CompilerParams(vmem_limit_bytes=16 * 2**20),
        cost_estimate=pl.CostEstimate(flops=0, bytes_accessed=0, transcendentals=0),
        name="settle",
    )(xl, *parts, *after)


def grow_kernel(side, x, received, *refs):
    out, held, sems, out_sem = refs[-4:]
    for k in range(2):
        pltpu.make_async_copy(x.at[side * 2 + k], held.at[k], sems.at[k]).start()
    for k in range(2):
        wait_all(held.at[k], sems.at[k])
        held[k] = add(held[k], received[k]).astype(BF)
        pltpu.make_async_copy(held.at[k], out.at[side * 2 + k], out_sem).start()
    wait_all(held, out_sem)


def grow(x, received, side, *after):
    hbm = pl.BlockSpec(memory_space=pltpu.HBM)
    return pl.pallas_call(
        functools.partial(grow_kernel, side),
        out_shape=pltpu.HBM(x.shape, x.dtype),
        grid=(1,),
        in_specs=[hbm, pl.BlockSpec(received.shape, lambda s: (0, 0, 0))] + [ANY] * len(after),
        out_specs=hbm,
        scratch_shapes=[
            pltpu.VMEM(received.shape, x.dtype),
            pltpu.SemaphoreType.DMA((2,)),
            pltpu.SemaphoreType.DMA,
        ],
        input_output_aliases={0: 0},
        compiler_params=pltpu.CompilerParams(vmem_limit_bytes=8 * 2**20),
        cost_estimate=NO_COST,
        name="grow",
    )(in_hbm(x), received, *after)


def fetch_tiles(step, source, held, sems):
    @pl.when(step == 0)
    def _():
        for k in range(4):
            rows = source.at[pl.ds(k * TILE, TILE)]
            pltpu.make_async_copy(rows, held.at[k], sems.at[k]).start()

    wait_all(held.at[step], sems.at[step])


def left_kernel(place, mine, other, partner, partner_other, left, out, total, packed, held, sems):
    step = pl.program_id(0)
    fetch_tiles(step, left, held, sems)
    at = pl.ds(pl.multiple_of((step & 1) * TILE, TILE), TILE)
    rows = mine.shape[0]

    def term(a, b):
        stacked = jnp.concatenate(split_pair(a[:, at] + b[:, at]), axis=0)
        value = jnp.dot(stacked, held[step], preferred_element_type=F32)
        total[...] = jnp.where(step == 0, value, total[...] + value)

    own = (step >> 1) == (place[1] ^ place[0])
    pl.when(own)(lambda: term(mine, other))
    pl.when(jnp.logical_not(own))(lambda: term(partner, partner_other))

    @pl.when(step == 3)
    def _():
        value = total[:rows] + total[rows:]
        for z in range(2):
            for y in range(4):
                for xl in range(2):
                    for c in range(2):
                        n = ((z * 4 + y) * 2 + xl) * 2 + c
                        block = value[:, n * rows : (n + 1) * rows]
                        packed[n, 0:16, 0:rows] = block[0:16]
                        packed[n, 0:16, rows : 2 * rows] = block[16:32]
                        packed[n, 0:8, 2 * rows : 3 * rows] = block[32:40]
                        ready = packed[n].astype(BF)
                        for there in (0, 2):
                            d = c * 32 + (there + z) * 8 + y * 2 + xl
                            out[d] = ready
                            out[64 + d] = ready


def left_product(place, mine, other, partner, partner_other, left):
    rows, half = mine.shape
    whole = pl.BlockSpec((rows, half), lambda k, p: (0, 0))
    return pl.pallas_call(
        left_kernel,
        out_shape=jax.ShapeDtypeStruct((128, 16, 128), BF),
        grid_spec=pltpu.PrefetchScalarGridSpec(
            num_scalar_prefetch=1,
            grid=(4,),
            in_specs=[whole] * 4 + [pl.BlockSpec(memory_space=pltpu.HBM)],
            out_specs=pl.BlockSpec((128, 16, 128), lambda k, p: (0, 0, 0)),
            scratch_shapes=[
                pltpu.VMEM((2 * rows, half), F32),
                pltpu.VMEM((32, 16, 128), F32),
                pltpu.VMEM((4, TILE, half), BF),
                pltpu.SemaphoreType.DMA((4,)),
            ],
        ),
        compiler_params=pltpu.CompilerParams(vmem_limit_bytes=20 * 2**20),
        cost_estimate=NO_COST,
        name="left_product",
    )(place, mine, other, partner, partner_other, left)


def right_kernel(place, blocks, right, late, out, rows_in, held, sems):
    del late
    step = pl.program_id(0)
    fetch_tiles(step, right, held, sems)
    rows = out.shape[0]
    for near in range(2):
        for y in range(4):
            for xl in range(2):
                core = (step >> 1) ^ ((near + y) & 1)
                block = blocks[core * 32 + ((step & 1) * 2 + near) * 8 + y * 2 + xl].astype(F32)
                at = ((near * 4 + y) * 2 + xl) * rows
                rows_in[at : at + 16, :] = block[:, 0:rows]
                rows_in[at + 16 : at + 32, :] = block[:, rows : 2 * rows]
                rows_in[at + 32 : at + 40, :] = block[0:8, 2 * rows : 3 * rows]
    value = contract(rows_in[...].astype(BF), held[step])
    pl.when(step == 0)(lambda: out.__setitem__(..., value))
    pl.when(step > 0)(lambda: out.__setitem__(..., out[...] + value))


def right_product(place, blocks, right, late):
    width, half = right.shape
    rows = width // 64
    return pl.pallas_call(
        right_kernel,
        out_shape=jax.ShapeDtypeStruct((rows, half), F32),
        grid_spec=pltpu.PrefetchScalarGridSpec(
            num_scalar_prefetch=1,
            grid=(4,),
            in_specs=[
                pl.BlockSpec((64, 16, 128), lambda k, p: (p[2] >> 1, 0, 0)),
                pl.BlockSpec(memory_space=pltpu.HBM),
                ANY,
            ],
            out_specs=pl.BlockSpec((rows, half), lambda k, p: (0, 0)),
            scratch_shapes=[
                pltpu.VMEM((TILE, rows), F32),
                pltpu.VMEM((4, TILE, half), BF),
                pltpu.SemaphoreType.DMA((4,)),
            ],
        ),
        compiler_params=pltpu.CompilerParams(vmem_limit_bytes=20 * 2**20),
        cost_estimate=NO_COST,
        name="right_product",
    )(place, blocks, right, late)


def per_device(hidden, out_grad, left_inverse, right_inverse):
    z, y, xl, c, o = (lax.axis_index(n) for n in ("z", "y", "xl", "c", "o"))
    tokens, width = hidden.shape
    half = width // 2
    token_total = tokens * 64
    first = o == 0
    h = c ^ ((z + y) & 1)
    hidden, out_grad = in_hbm(hidden), in_hbm(out_grad)
    left_inverse, right_inverse = in_hbm(left_inverse), in_hbm(right_inverse)
    place = jnp.stack([o, h, z, y]).astype(jnp.int32)
    second_me = jnp.where(h == 0, y, z).astype(jnp.int32)[None]

    grads_next, acts_next = in_hbm(shift(out_grad, "c", 1)), in_hbm(shift(hidden, "c", 1))
    partial = cross_own(place, out_grad, hidden)

    own, m1, m2, m3 = cross_term(place, grads_next, acts_next, partial)
    m_parts = [own, turn(m1, 1, 0), turn(m2, 2, 0), turn(m3, 3, 0)]

    f_own, right, far_a, far_b, left = factor_term(
        place, hidden, out_grad, acts_next, grads_next, in_hbm(m1)
    )
    from_left, from_right = turn(far_a, 1, 0), turn(far_b, -1, 0)

    my_xl = xl.astype(jnp.int32)[None]

    def second_sends(pieces):
        return [turn(piece, s, 1) for s, piece in enumerate(pieces, 1)]

    m, *m_pieces = fold(second_me, m_parts, in_hbm(f_own))
    m_received = second_sends(m_pieces)
    right = grow(right, from_left, 0, m_received[0])
    left = grow(left, from_right, 1, m_received[1], m_received[2])
    f_parts = [f_own, turn(right, 1, 0), turn(left, -1, 0)]

    mine, theirs = settle(my_xl, [m, *m_received], F32)
    across = lax.ppermute(theirs, ("xl", "o"), [(i, 3 - i) for i in range(4)])
    products = left_product(
        place, mine, shift(theirs, "xl", 1), shift(mine, "o", 1), across, left_inverse
    )
    blocks = lax.all_to_all(products, ("o", "c", "z", "y", "xl"), 0, 0, tiled=True)
    f, *f_pieces = fold(second_me, f_parts, products)
    f_mine, f_theirs = settle(my_xl, [f, *second_sends(f_pieces)], BF, blocks)
    update = right_product(place, blocks, right_inverse, f_pieces[0])

    f = add(f_mine, shift(f_theirs, "xl", 1))
    f = f * jnp.where(first, 1.0 / token_total, 1.0).astype(F32)
    f = f.reshape(2, width // 64, half)
    mine = pick(f, 0, c)
    theirs = shift(pick(f, 0, 1 - c), "c", 1)
    factors = jnp.concatenate(
        [jnp.where(h == 0, mine, theirs), jnp.where(h == 0, theirs, mine)], axis=1
    )[None]
    return factors, update


def solution(mesh):
    fine = Mesh(mesh.devices.reshape(4, 4, 2, 2, 2), ("z", "y", "xl", "c", "o"))
    dp = ("z", "y", "xl", "c")
    in_specs = (P(dp, None), P(dp, None), P(None, "o"), P(None, "o"))
    out_specs = (P("o", dp, None), P(dp, "o"))
    return jax.shard_map(
        per_device, mesh=fine, in_specs=in_specs, out_specs=out_specs, check_vma=False
    )
```

```python
import functools

import jax
import jax.numpy as jnp
from jax import lax
from jax.experimental import pallas as pl
from jax.experimental.pallas import tpu as pltpu
from jax.sharding import Mesh, PartitionSpec as P

BF = jnp.bfloat16
F32 = jnp.float32
TILE = 640
ANY = pl.BlockSpec(memory_space=pl.ANY)


def contract(first_rows, second_rows):
    return lax.dot_general(
        first_rows, second_rows, (((0,), (0,)), ((), ())), preferred_element_type=F32
    )


def shift(x, axis, step):
    size = lax.axis_size(axis)
    return lax.ppermute(x, axis, [(i, (i + step) % size) for i in range(size)])


def turn(x, step, stage):
    pairs = []
    for z in range(4):
        for y in range(4):
            for h in range(2):
                along_z = (h == 0) == (stage == 0)
                z2, y2 = ((z + step) % 4, y) if along_z else (z, (y + step) % 4)
                core, core2 = h ^ ((z + y) & 1), h ^ ((z2 + y2) & 1)
                pairs.append(((z * 4 + y) * 2 + core, (z2 * 4 + y2) * 2 + core2))
    return lax.ppermute(x, ("z", "y", "c"), pairs)


def in_hbm(x):
    return pltpu.with_memory_space_constraint(x, pltpu.HBM)


def pick(x, dim, index):
    return lax.dynamic_index_in_dim(x, index, dim, keepdims=False)


def split_pair(x):
    high = x.astype(BF)
    return high, (x - high.astype(F32)).astype(BF)


def place_tile(place, buffer, sem, outs, m, zs):
    rows = TILE // (zs * 4)

    def start(at, out, slot):
        block = buffer.at[m, pl.ds(at, rows)]
        pltpu.make_async_copy(block, out.at[slot], sem).start()

    for a in range(zs):
        z = m * zs + a

        @pl.when(place[1] == 0)
        def _():
            for r, out in enumerate(outs):

                @pl.when(((z - place[2] + 4) & 3) == r)
                def _():
                    for k in range(4):
                        if isinstance(out, tuple):
                            start((a * 4 + k) * rows, out[k // 2], k % 2)
                        else:
                            start((a * 4 + k) * rows, out, k)

        @pl.when(place[1] == 1)
        def _():
            for r, out in enumerate(outs):
                at = pl.multiple_of((a * 4 + ((place[3] + r) & 3)) * rows, 16)
                if isinstance(out, tuple):
                    pl.when(z < 2)(functools.partial(start, at, out[0], z & 1))
                    pl.when(z >= 2)(functools.partial(start, at, out[1], z & 1))
                else:
                    start(at, out, z)


def wait_all(buffer, sem):
    pltpu.make_async_copy(buffer, buffer, sem).wait()


def own_kernel(place, a, b, out, lhs, rhs, lhs_sems, rhs_sem):
    m = pl.program_id(0)
    half = rhs.shape[1]

    @pl.when(m == 0)
    def _():
        at = pl.ds(pl.multiple_of((place[1] ^ place[0]) * half, half), half)
        pltpu.make_async_copy(b.at[:, at], rhs, rhs_sem).start()
        for k in range(2):
            at = pl.ds(pl.multiple_of(place[1] * half + k * TILE, TILE), TILE)
            pltpu.make_async_copy(a.at[:, at], lhs.at[k], lhs_sems.at[k]).start()
        wait_all(rhs, rhs_sem)

    wait_all(lhs.at[m], lhs_sems.at[m])
    out[...] = contract(lhs[m], rhs[...])


def cross_kernel(place, a, b, partial, own, ahead1, ahead2, ahead3, held, buffer, held_sems, sem):
    m = pl.program_id(0)

    @pl.when(m == 0)
    def _():
        for k in range(2):
            rows = partial.at[pl.ds(k * TILE, TILE)]
            pltpu.make_async_copy(rows, held.at[k], held_sems.at[k]).start()

    tile = contract(a[...], b[...])
    wait_all(held.at[m], held_sems.at[m])
    buffer[m] = (held[m] + tile).astype(BF)
    place_tile(place, buffer, sem, [own, ahead1, ahead2, ahead3], m, 2)
    pl.when(m == 1)(lambda: wait_all(buffer, sem))


def cross_own(place, grads, acts):
    tokens, half = grads.shape[0], grads.shape[1] // 2
    return pl.pallas_call(
        own_kernel,
        out_shape=jax.ShapeDtypeStruct((half, half), F32),
        grid_spec=pltpu.PrefetchScalarGridSpec(
            num_scalar_prefetch=1,
            grid=(2,),
            in_specs=[pl.BlockSpec(memory_space=pltpu.HBM)] * 2,
            out_specs=pl.BlockSpec((TILE, half), lambda m, p: (m, 0)),
            scratch_shapes=[
                pltpu.VMEM((2, tokens, TILE), BF),
                pltpu.VMEM((tokens, half), BF),
                pltpu.SemaphoreType.DMA((2,)),
                pltpu.SemaphoreType.DMA,
            ],
        ),
        compiler_params=pltpu.CompilerParams(vmem_limit_bytes=28 * 2**20),
        cost_estimate=pl.CostEstimate(
            flops=2 * tokens * half * half, bytes_accessed=8 * tokens * half, transcendentals=0
        ),
        name="cross_own",
    )(place, grads, acts)


def cross_term(place, grads_next, acts_next, partial):
    tokens, half = grads_next.shape[0], grads_next.shape[1] // 2
    out = pltpu.HBM((4, half // 16, half), BF)
    return pl.pallas_call(
        cross_kernel,
        out_shape=[out] * 4,
        grid_spec=pltpu.PrefetchScalarGridSpec(
            num_scalar_prefetch=1,
            grid=(2,),
            in_specs=[
                pl.BlockSpec((tokens, TILE), lambda m, p: (0, p[1] * 2 + m)),
                pl.BlockSpec((tokens, half), lambda m, p: (0, p[1] ^ p[0])),
                ANY,
            ],
            out_specs=[pl.BlockSpec(memory_space=pltpu.HBM)] * 4,
            scratch_shapes=[
                pltpu.VMEM((2, TILE, half), F32),
                pltpu.VMEM((2, TILE, half), BF),
                pltpu.SemaphoreType.DMA((2,)),
                pltpu.SemaphoreType.DMA,
            ],
        ),
        compiler_params=pltpu.CompilerParams(vmem_limit_bytes=28 * 2**20),
        cost_estimate=pl.CostEstimate(
            flops=2 * tokens * half * half, bytes_accessed=10 * tokens * half, transcendentals=0
        ),
        name="cross_term",
    )(place, grads_next, acts_next, partial)


def factor_kernel(place, h_own, g_own, h_next, g_next, after, *rest):
    del after
    own, right, far_a, far_b, left, lhs, rhs, buffer, lhs_sems, rhs_sem, sem = rest
    m = pl.program_id(0)
    half = rhs.shape[2]

    def fetch(step, with_rhs):
        slot = step & 1
        at = pl.ds(pl.multiple_of(step * TILE, TILE), TILE)
        columns = pl.ds(pl.multiple_of(place[1] * half, half), half)
        for owner, refs in enumerate(((h_own, h_next), (g_own, g_next))):

            @pl.when(place[0] == owner)
            def _():
                for k, ref in enumerate(refs):
                    pltpu.make_async_copy(ref.at[:, at], lhs.at[slot, k], lhs_sems.at[slot]).start()
                    if with_rhs:
                        pltpu.make_async_copy(ref.at[:, columns], rhs.at[k], rhs_sem).start()

    pl.when(m == 0)(lambda: fetch(0, True))
    pl.when(m < 3)(lambda: fetch(m + 1, False))
    slot = m & 1
    wait_all(lhs.at[slot], lhs_sems.at[slot])
    pl.when(m == 0)(lambda: wait_all(rhs, rhs_sem))

    buffer[m] = (contract(lhs[slot, 0], rhs[0]) + contract(lhs[slot, 1], rhs[1])).astype(BF)
    place_tile(place, buffer, sem, [own, right, (far_a, far_b), left], m, 1)
    pl.when(m == 3)(lambda: wait_all(buffer, sem))


def factor_term(place, acts, grads, acts_next, grads_next, after):
    tokens, width = acts.shape
    half = width // 2
    hbm = pl.BlockSpec(memory_space=pltpu.HBM)
    out = pltpu.HBM((4, width // 16, half), BF)
    side = pltpu.HBM((2, width // 16, half), BF)
    return pl.pallas_call(
        factor_kernel,
        out_shape=[out, out, side, side, out],
        grid_spec=pltpu.PrefetchScalarGridSpec(
            num_scalar_prefetch=1,
            grid=(4,),
            in_specs=[hbm] * 2 + [ANY] * 3,
            out_specs=[hbm] * 5,
            scratch_shapes=[
                pltpu.VMEM((2, 2, tokens, TILE), BF),
                pltpu.VMEM((2, tokens, half), BF),
                pltpu.VMEM((4, TILE, half), BF),
                pltpu.SemaphoreType.DMA((2,)),
                pltpu.SemaphoreType.DMA,
                pltpu.SemaphoreType.DMA,
            ],
        ),
        compiler_params=pltpu.CompilerParams(vmem_limit_bytes=30 * 2**20),
        cost_estimate=pl.CostEstimate(
            flops=4 * tokens * width * half, bytes_accessed=16 * tokens * half, transcendentals=0
        ),
        name="factor_term",
    )(place, acts, grads, acts_next, grads_next, after)


def add(first, *rest):
    total = first.astype(F32)
    for x in rest:
        total = total + x.astype(F32)
    return total


def fold_kernel(count, me, *refs):
    own, *others = refs[-6:-2]
    held, sem = refs[-2:]
    copy = pltpu.make_async_copy(refs[0], held, sem)
    copy.start()
    copy.wait()
    for r, out in enumerate([own, *others]):
        at = (me[0] + r) & 3
        out[...] = add(held[at], *[part[at] for part in refs[1:count]]).astype(out.dtype)


def fold(me, parts, *after):
    _, rows, width = parts[0].shape
    block = pl.BlockSpec((4, rows, width), lambda s, m: (0, 0, 0))
    whole = pl.BlockSpec((rows, width), lambda s, m: (0, 0))
    return pl.pallas_call(
        functools.partial(fold_kernel, len(parts)),
        out_shape=[pltpu.HBM((rows, width), F32)]
        + [jax.ShapeDtypeStruct((rows, width), BF)] * 3,
        grid_spec=pltpu.PrefetchScalarGridSpec(
            num_scalar_prefetch=1,
            grid=(1,),
            in_specs=[pl.BlockSpec(memory_space=pltpu.HBM)]
            + [block] * (len(parts) - 1)
            + [ANY] * len(after),
            out_specs=[whole] * 4,
            scratch_shapes=[pltpu.VMEM((4, rows, width), BF), pltpu.SemaphoreType.DMA],
        ),
        compiler_params=pltpu.CompilerParams(vmem_limit_bytes=26 * 2**20),
        cost_estimate=pl.CostEstimate(flops=0, bytes_accessed=0, transcendentals=0),
        name="fold",
    )(me, in_hbm(parts[0]), *parts[1:], *after)


def settle_kernel(count, xl, *refs):
    mine, theirs, total = refs[-3:]
    rows = mine.shape[0]
    value = None
    for ref in refs[:count]:
        for part in [ref[...]] if len(ref.shape) == 2 else [ref[k] for k in range(ref.shape[0])]:
            value = part.astype(F32) if value is None else value + part.astype(F32)
    total[...] = value
    for out, index in ((mine, xl[0]), (theirs, 1 - xl[0])):
        out[...] = total[pl.ds(pl.multiple_of(index * rows, 8), rows)].astype(out.dtype)


def settle(xl, parts, dtype, *after):
    rows, width = parts[0].shape[-2:]
    half = pl.BlockSpec((rows // 2, width), lambda s, x: (0, 0))
    return pl.pallas_call(
        functools.partial(settle_kernel, len(parts)),
        out_shape=[jax.ShapeDtypeStruct((rows // 2, width), t) for t in (F32, dtype)],
        grid_spec=pltpu.PrefetchScalarGridSpec(
            num_scalar_prefetch=1,
            grid=(1,),
            in_specs=[pl.BlockSpec(p.shape, lambda s, x, n=p.ndim: (0,) * n) for p in parts]
            + [ANY] * len(after),
            out_specs=[half] * 2,
            scratch_shapes=[pltpu.VMEM((rows, width), F32)],
        ),
        compiler_params=pltpu.CompilerParams(vmem_limit_bytes=16 * 2**20),
        cost_estimate=pl.CostEstimate(flops=0, bytes_accessed=0, transcendentals=0),
        name="settle",
    )(xl, *parts, *after)


def grow_kernel(side, x, received, *refs):
    out, held, sems, out_sem = refs[-4:]
    for k in range(2):
        pltpu.make_async_copy(x.at[side * 2 + k], held.at[k], sems.at[k]).start()
    for k in range(2):
        wait_all(held.at[k], sems.at[k])
        held[k] = add(held[k], received[k]).astype(BF)
        pltpu.make_async_copy(held.at[k], out.at[side * 2 + k], out_sem).start()
    wait_all(held, out_sem)


def grow(x, received, side, *after):
    hbm = pl.BlockSpec(memory_space=pltpu.HBM)
    return pl.pallas_call(
        functools.partial(grow_kernel, side),
        out_shape=pltpu.HBM(x.shape, x.dtype),
        grid=(1,),
        in_specs=[hbm, pl.BlockSpec(received.shape, lambda s: (0, 0, 0))] + [ANY] * len(after),
        out_specs=hbm,
        scratch_shapes=[
            pltpu.VMEM(received.shape, x.dtype),
            pltpu.SemaphoreType.DMA((2,)),
            pltpu.SemaphoreType.DMA,
        ],
        input_output_aliases={0: 0},
        compiler_params=pltpu.CompilerParams(vmem_limit_bytes=8 * 2**20),
        cost_estimate=pl.CostEstimate(flops=0, bytes_accessed=0, transcendentals=0),
        name="grow",
    )(in_hbm(x), received, *after)


def fetch_tiles(step, source, held, sems):
    @pl.when(step == 0)
    def _():
        for k in range(4):
            rows = source.at[pl.ds(k * TILE, TILE)]
            pltpu.make_async_copy(rows, held.at[k], sems.at[k]).start()

    wait_all(held.at[step], sems.at[step])


def left_kernel(place, mine, other, partner, partner_other, left, out, total, packed, held, sems):
    step = pl.program_id(0)
    fetch_tiles(step, left, held, sems)
    at = pl.ds(pl.multiple_of((step & 1) * TILE, TILE), TILE)
    rows = mine.shape[0]

    def term(a, b):
        stacked = jnp.concatenate(split_pair(a[:, at] + b[:, at]), axis=0)
        value = jnp.dot(stacked, held[step], preferred_element_type=F32)
        total[...] = jnp.where(step == 0, value, total[...] + value)

    own = (step >> 1) == (place[1] ^ place[0])
    pl.when(own)(lambda: term(mine, other))
    pl.when(jnp.logical_not(own))(lambda: term(partner, partner_other))

    @pl.when(step == 3)
    def _():
        value = total[:rows] + total[rows:]
        for z in range(2):
            for y in range(4):
                for xl in range(2):
                    for c in range(2):
                        n = ((z * 4 + y) * 2 + xl) * 2 + c
                        block = value[:, n * rows : (n + 1) * rows]
                        packed[n, 0:16, 0:rows] = block[0:16]
                        packed[n, 0:16, rows : 2 * rows] = block[16:32]
                        packed[n, 0:8, 2 * rows : 3 * rows] = block[32:40]
                        ready = packed[n].astype(BF)
                        for there in (0, 2):
                            d = c * 32 + (there + z) * 8 + y * 2 + xl
                            out[d] = ready
                            out[64 + d] = ready


def left_product(place, mine, other, partner, partner_other, left):
    rows, half = mine.shape
    whole = pl.BlockSpec((rows, half), lambda k, p: (0, 0))
    return pl.pallas_call(
        left_kernel,
        out_shape=jax.ShapeDtypeStruct((128, 16, 128), BF),
        grid_spec=pltpu.PrefetchScalarGridSpec(
            num_scalar_prefetch=1,
            grid=(4,),
            in_specs=[whole] * 4 + [pl.BlockSpec(memory_space=pltpu.HBM)],
            out_specs=pl.BlockSpec((128, 16, 128), lambda k, p: (0, 0, 0)),
            scratch_shapes=[
                pltpu.VMEM((2 * rows, half), F32),
                pltpu.VMEM((32, 16, 128), F32),
                pltpu.VMEM((4, TILE, half), BF),
                pltpu.SemaphoreType.DMA((4,)),
            ],
        ),
        compiler_params=pltpu.CompilerParams(vmem_limit_bytes=20 * 2**20),
        cost_estimate=pl.CostEstimate(
            flops=256 * rows * half * half, bytes_accessed=4 * half * half, transcendentals=0
        ),
        name="left_product",
    )(place, mine, other, partner, partner_other, left)


def right_kernel(place, blocks, right, late, out, rows_in, held, sems):
    del late
    step = pl.program_id(0)
    fetch_tiles(step, right, held, sems)
    rows = out.shape[0]
    for near in range(2):
        for y in range(4):
            for xl in range(2):
                core = (step >> 1) ^ ((near + y) & 1)
                block = blocks[core * 32 + ((step & 1) * 2 + near) * 8 + y * 2 + xl].astype(F32)
                at = ((near * 4 + y) * 2 + xl) * rows
                rows_in[at : at + 16, :] = block[:, 0:rows]
                rows_in[at + 16 : at + 32, :] = block[:, rows : 2 * rows]
                rows_in[at + 32 : at + 40, :] = block[0:8, 2 * rows : 3 * rows]
    value = contract(rows_in[...].astype(BF), held[step])
    pl.when(step == 0)(lambda: out.__setitem__(..., value))
    pl.when(step > 0)(lambda: out.__setitem__(..., out[...] + value))


def right_product(place, blocks, right, late):
    width, half = right.shape
    rows = width // 64
    return pl.pallas_call(
        right_kernel,
        out_shape=jax.ShapeDtypeStruct((rows, half), F32),
        grid_spec=pltpu.PrefetchScalarGridSpec(
            num_scalar_prefetch=1,
            grid=(4,),
            in_specs=[
                pl.BlockSpec((64, 16, 128), lambda k, p: (p[2] >> 1, 0, 0)),
                pl.BlockSpec(memory_space=pltpu.HBM),
                ANY,
            ],
            out_specs=pl.BlockSpec((rows, half), lambda k, p: (0, 0)),
            scratch_shapes=[
                pltpu.VMEM((TILE, rows), F32),
                pltpu.VMEM((4, TILE, half), BF),
                pltpu.SemaphoreType.DMA((4,)),
            ],
        ),
        compiler_params=pltpu.CompilerParams(vmem_limit_bytes=20 * 2**20),
        cost_estimate=pl.CostEstimate(
            flops=640 * rows * half * half, bytes_accessed=4 * half * half, transcendentals=0
        ),
        name="right_product",
    )(place, blocks, right, late)


def per_device(hidden, out_grad, left_inverse, right_inverse):
    z, y, xl, c, o = (lax.axis_index(n) for n in ("z", "y", "xl", "c", "o"))
    tokens, width = hidden.shape
    half = width // 2
    token_total = tokens * 64
    first = o == 0
    h = c ^ ((z + y) & 1)
    hidden, out_grad = in_hbm(hidden), in_hbm(out_grad)
    left_inverse, right_inverse = in_hbm(left_inverse), in_hbm(right_inverse)
    place = jnp.stack([o, h, z, y]).astype(jnp.int32)
    second_me = jnp.where(h == 0, y, z).astype(jnp.int32)[None]

    grads_next, acts_next = in_hbm(shift(out_grad, "c", 1)), in_hbm(shift(hidden, "c", 1))
    partial = cross_own(place, out_grad, hidden)

    own, m1, m2, m3 = cross_term(place, grads_next, acts_next, partial)
    m_parts = [own, turn(m1, 1, 0), turn(m2, 2, 0), turn(m3, 3, 0)]

    f_own, right, far_a, far_b, left = factor_term(
        place, hidden, out_grad, acts_next, grads_next, in_hbm(m1)
    )
    from_left, from_right = turn(far_a, 1, 0), turn(far_b, -1, 0)

    my_xl = xl.astype(jnp.int32)[None]

    def second_sends(pieces):
        return [turn(piece, s, 1) for s, piece in enumerate(pieces, 1)]

    m, *m_pieces = fold(second_me, m_parts, in_hbm(f_own))
    m_received = second_sends(m_pieces)
    right = grow(right, from_left, 0, *m_received)
    left = grow(left, from_right, 1, *m_received)
    f_parts = [f_own, turn(right, 1, 0), turn(left, -1, 0)]

    mine, theirs = settle(my_xl, [in_hbm(m), *m_received], F32)
    across = lax.ppermute(theirs, ("xl", "o"), [(i, 3 - i) for i in range(4)])
    products = left_product(
        place, mine, shift(theirs, "xl", 1), shift(mine, "o", 1), across, left_inverse
    )
    blocks = lax.all_to_all(products, ("o", "c", "z", "y", "xl"), 0, 0, tiled=True)
    f, *f_pieces = fold(second_me, f_parts, products)
    update = right_product(place, blocks, right_inverse, f_pieces[0])
    f_mine, f_theirs = settle(my_xl, [in_hbm(f), *second_sends(f_pieces)], BF, in_hbm(update))

    f = add(f_mine, shift(f_theirs, "xl", 1))
    f = f * jnp.where(first, 1.0 / token_total, 1.0).astype(F32)
    f = f.reshape(2, width // 64, half)
    mine = pick(f, 0, c)
    theirs = shift(pick(f, 0, 1 - c), "c", 1)
    factors = jnp.concatenate(
        [jnp.where(h == 0, mine, theirs), jnp.where(h == 0, theirs, mine)], axis=1
    )[None]
    return factors, update


def solution(mesh):
    fine = Mesh(mesh.devices.reshape(4, 4, 2, 2, 2), ("z", "y", "xl", "c", "o"))
    dp = ("z", "y", "xl", "c")
    in_specs = (P(dp, None), P(dp, None), P(None, "o"), P(None, "o"))
    out_specs = (P("o", dp, None), P(dp, "o"))
    return jax.shard_map(
        per_device, mesh=fine, in_specs=in_specs, out_specs=out_specs, check_vma=False
    )
```

```python
import functools

import jax
import jax.numpy as jnp
from jax import lax
from jax.experimental import pallas as pl
from jax.experimental.pallas import tpu as pltpu
from jax.sharding import Mesh, PartitionSpec as P

BF = jnp.bfloat16
F32 = jnp.float32
TILE = 640
NO_COST = pl.CostEstimate(flops=0, bytes_accessed=0, transcendentals=0)
ANY = pl.BlockSpec(memory_space=pl.ANY)


def contract(first_rows, second_rows):
    return lax.dot_general(
        first_rows, second_rows, (((0,), (0,)), ((), ())), preferred_element_type=F32
    )


def shift(x, axis, step):
    size = lax.axis_size(axis)
    return lax.ppermute(x, axis, [(i, (i + step) % size) for i in range(size)])


def turn(x, step, stage):
    pairs = []
    for z in range(4):
        for y in range(4):
            for h in range(2):
                along_z = (h == 0) == (stage == 0)
                z2, y2 = ((z + step) % 4, y) if along_z else (z, (y + step) % 4)
                core, core2 = h ^ ((z + y) & 1), h ^ ((z2 + y2) & 1)
                pairs.append(((z * 4 + y) * 2 + core, (z2 * 4 + y2) * 2 + core2))
    return lax.ppermute(x, ("z", "y", "c"), pairs)


def in_hbm(x):
    return pltpu.with_memory_space_constraint(x, pltpu.HBM)


def pick(x, dim, index):
    return lax.dynamic_index_in_dim(x, index, dim, keepdims=False)


def split_pair(x):
    high = x.astype(BF)
    return high, (x - high.astype(F32)).astype(BF)


def place_tile(place, buffer, sem, outs, m, zs):
    rows = TILE // (zs * 4)

    def start(at, out, slot):
        block = buffer.at[m, pl.ds(at, rows)]
        pltpu.make_async_copy(block, out.at[slot], sem).start()

    for a in range(zs):
        z = m * zs + a

        @pl.when(place[1] == 0)
        def _():
            for r, out in enumerate(outs):

                @pl.when(((z - place[2] + 4) & 3) == r)
                def _():
                    for k in range(4):
                        if isinstance(out, tuple):
                            start((a * 4 + k) * rows, out[k // 2], k % 2)
                        else:
                            start((a * 4 + k) * rows, out, k)

        @pl.when(place[1] == 1)
        def _():
            for r, out in enumerate(outs):
                at = pl.multiple_of((a * 4 + ((place[3] + r) & 3)) * rows, 16)
                if isinstance(out, tuple):
                    pl.when(z < 2)(functools.partial(start, at, out[0], z & 1))
                    pl.when(z >= 2)(functools.partial(start, at, out[1], z & 1))
                else:
                    start(at, out, z)


def wait_all(buffer, sem):
    pltpu.make_async_copy(buffer, buffer, sem).wait()


def own_kernel(place, a, b, out, lhs, rhs, lhs_sems, rhs_sem):
    m = pl.program_id(0)
    half = rhs.shape[1]

    @pl.when(m == 0)
    def _():
        at = pl.ds(pl.multiple_of((place[1] ^ place[0]) * half, half), half)
        pltpu.make_async_copy(b.at[:, at], rhs, rhs_sem).start()
        for k in range(2):
            at = pl.ds(pl.multiple_of(place[1] * half + k * TILE, TILE), TILE)
            pltpu.make_async_copy(a.at[:, at], lhs.at[k], lhs_sems.at[k]).start()
        wait_all(rhs, rhs_sem)

    wait_all(lhs.at[m], lhs_sems.at[m])
    out[...] = contract(lhs[m], rhs[...])


def cross_kernel(place, a, b, partial, after, *rest):
    del after
    own, ahead1, ahead2, ahead3, held, buffer, held_sems, sem = rest
    m = pl.program_id(0)

    @pl.when(m == 0)
    def _():
        for k in range(2):
            rows = partial.at[pl.ds(k * TILE, TILE)]
            pltpu.make_async_copy(rows, held.at[k], held_sems.at[k]).start()

    tile = contract(a[...], b[...])
    wait_all(held.at[m], held_sems.at[m])
    buffer[m] = (held[m] + tile).astype(BF)
    place_tile(place, buffer, sem, [own, ahead1, ahead2, ahead3], m, 2)
    pl.when(m == 1)(lambda: wait_all(buffer, sem))


def cross_own(place, grads, acts):
    tokens, half = grads.shape[0], grads.shape[1] // 2
    return pl.pallas_call(
        own_kernel,
        out_shape=jax.ShapeDtypeStruct((half, half), F32),
        grid_spec=pltpu.PrefetchScalarGridSpec(
            num_scalar_prefetch=1,
            grid=(2,),
            in_specs=[pl.BlockSpec(memory_space=pltpu.HBM)] * 2,
            out_specs=pl.BlockSpec((TILE, half), lambda m, p: (m, 0)),
            scratch_shapes=[
                pltpu.VMEM((2, tokens, TILE), BF),
                pltpu.VMEM((tokens, half), BF),
                pltpu.SemaphoreType.DMA((2,)),
                pltpu.SemaphoreType.DMA,
            ],
        ),
        compiler_params=pltpu.CompilerParams(vmem_limit_bytes=28 * 2**20),
        cost_estimate=NO_COST,
        name="cross_own",
    )(place, grads, acts)


def cross_term(place, grads_next, acts_next, partial, after):
    tokens, half = grads_next.shape[0], grads_next.shape[1] // 2
    out = pltpu.HBM((4, half // 16, half), BF)
    return pl.pallas_call(
        cross_kernel,
        out_shape=[out] * 4,
        grid_spec=pltpu.PrefetchScalarGridSpec(
            num_scalar_prefetch=1,
            grid=(2,),
            in_specs=[
                pl.BlockSpec((tokens, TILE), lambda m, p: (0, p[1] * 2 + m)),
                pl.BlockSpec((tokens, half), lambda m, p: (0, p[1] ^ p[0])),
                ANY,
                ANY,
            ],
            out_specs=[pl.BlockSpec(memory_space=pltpu.HBM)] * 4,
            scratch_shapes=[
                pltpu.VMEM((2, TILE, half), F32),
                pltpu.VMEM((2, TILE, half), BF),
                pltpu.SemaphoreType.DMA((2,)),
                pltpu.SemaphoreType.DMA,
            ],
        ),
        compiler_params=pltpu.CompilerParams(vmem_limit_bytes=28 * 2**20),
        cost_estimate=NO_COST,
        name="cross_term",
    )(place, grads_next, acts_next, partial, after)


def factor_fetch(place, refs, step, lhs, rhs, lhs_sems, rhs_sem):
    half = rhs.shape[1]
    at = pl.ds(pl.multiple_of(step * TILE, TILE), TILE)
    columns = pl.ds(pl.multiple_of(place[1] * half, half), half)
    for owner, ref in enumerate(refs):

        @pl.when(place[0] == owner)
        def _():
            slot = step & 1
            pltpu.make_async_copy(ref.at[:, at], lhs.at[slot], lhs_sems.at[slot]).start()
            if isinstance(step, int):
                pltpu.make_async_copy(ref.at[:, columns], rhs, rhs_sem).start()


def factor_tile(place, refs, lhs, rhs, lhs_sems, rhs_sem):
    m = pl.program_id(0)
    pl.when(m == 0)(lambda: factor_fetch(place, refs, 0, lhs, rhs, lhs_sems, rhs_sem))
    pl.when(m < 3)(lambda: factor_fetch(place, refs, m + 1, lhs, rhs, lhs_sems, rhs_sem))
    wait_all(lhs.at[m & 1], lhs_sems.at[m & 1])
    pl.when(m == 0)(lambda: wait_all(rhs, rhs_sem))
    return contract(lhs[m & 1], rhs[...])


def factor_own_kernel(place, acts, grads, after, out, *scratch):
    del after
    out[...] = factor_tile(place, (acts, grads), *scratch)


def factor_scratch(tokens, half):
    return [
        pltpu.VMEM((2, tokens, TILE), BF),
        pltpu.VMEM((tokens, half), BF),
        pltpu.SemaphoreType.DMA((2,)),
        pltpu.SemaphoreType.DMA,
    ]


def factor_own(place, acts, grads, after):
    tokens, width = acts.shape
    half = width // 2
    return pl.pallas_call(
        factor_own_kernel,
        out_shape=pltpu.HBM((width, half), F32),
        grid_spec=pltpu.PrefetchScalarGridSpec(
            num_scalar_prefetch=1,
            grid=(4,),
            in_specs=[pl.BlockSpec(memory_space=pltpu.HBM)] * 2 + [ANY],
            out_specs=pl.BlockSpec((TILE, half), lambda m, p: (m, 0)),
            scratch_shapes=factor_scratch(tokens, half),
        ),
        compiler_params=pltpu.CompilerParams(vmem_limit_bytes=24 * 2**20),
        cost_estimate=NO_COST,
        name="factor_own",
    )(place, acts, grads, after)


def factor_kernel(place, acts, grads, partial, after, *rest):
    del after
    own, right, far_a, far_b, left, held, buffer, held_sems, sem = rest[:9]
    m = pl.program_id(0)

    def fetch_partial(step):
        rows = partial.at[pl.ds(pl.multiple_of(step * TILE, TILE), TILE)]
        pltpu.make_async_copy(rows, held.at[step & 1], held_sems.at[step & 1]).start()

    pl.when(m == 0)(lambda: fetch_partial(0))
    pl.when(m < 3)(lambda: fetch_partial(m + 1))
    tile = factor_tile(place, (acts, grads), *rest[9:])
    wait_all(held.at[m & 1], held_sems.at[m & 1])
    buffer[m] = (held[m & 1] + tile).astype(BF)
    place_tile(place, buffer, sem, [own, right, (far_a, far_b), left], m, 1)
    pl.when(m == 3)(lambda: wait_all(buffer, sem))


def factor_term(place, acts_next, grads_next, partial, after):
    tokens, width = acts_next.shape
    half = width // 2
    hbm = pl.BlockSpec(memory_space=pltpu.HBM)
    out = pltpu.HBM((4, width // 16, half), BF)
    side = pltpu.HBM((2, width // 16, half), BF)
    return pl.pallas_call(
        factor_kernel,
        out_shape=[out, out, side, side, out],
        grid_spec=pltpu.PrefetchScalarGridSpec(
            num_scalar_prefetch=1,
            grid=(4,),
            in_specs=[hbm] * 4,
            out_specs=[hbm] * 5,
            scratch_shapes=[
                pltpu.VMEM((2, TILE, half), F32),
                pltpu.VMEM((4, TILE, half), BF),
                pltpu.SemaphoreType.DMA((2,)),
                pltpu.SemaphoreType.DMA,
            ]
            + factor_scratch(tokens, half),
        ),
        compiler_params=pltpu.CompilerParams(vmem_limit_bytes=30 * 2**20),
        cost_estimate=NO_COST,
        name="factor_term",
    )(place, acts_next, grads_next, partial, after)


def add(first, *rest):
    total = first.astype(F32)
    for x in rest:
        total = total + x.astype(F32)
    return total


def fold_kernel(count, me, *refs):
    own, *others = refs[-6:-2]
    held, sem = refs[-2:]
    copy = pltpu.make_async_copy(refs[0], held, sem)
    copy.start()
    copy.wait()
    for r, out in enumerate([own, *others]):
        at = (me[0] + r) & 3
        out[...] = add(held[at], *[part[at] for part in refs[1:count]]).astype(out.dtype)


def fold(me, parts, *after):
    _, rows, width = parts[0].shape
    block = pl.BlockSpec((4, rows, width), lambda s, m: (0, 0, 0))
    whole = pl.BlockSpec((rows, width), lambda s, m: (0, 0))
    return pl.pallas_call(
        functools.partial(fold_kernel, len(parts)),
        out_shape=[pltpu.HBM((rows, width), F32)]
        + [jax.ShapeDtypeStruct((rows, width), BF)] * 3,
        grid_spec=pltpu.PrefetchScalarGridSpec(
            num_scalar_prefetch=1,
            grid=(1,),
            in_specs=[pl.BlockSpec(memory_space=pltpu.HBM)]
            + [block] * (len(parts) - 1)
            + [ANY] * len(after),
            out_specs=[whole] * 4,
            scratch_shapes=[pltpu.VMEM((4, rows, width), BF), pltpu.SemaphoreType.DMA],
        ),
        compiler_params=pltpu.CompilerParams(vmem_limit_bytes=26 * 2**20),
        cost_estimate=NO_COST,
        name="fold",
    )(me, in_hbm(parts[0]), *parts[1:], *after)


def settle_kernel(count, xl, *refs):
    mine, theirs, total = refs[-3:]
    rows = mine.shape[0]
    value = None
    for ref in refs[:count]:
        for part in [ref[...]] if len(ref.shape) == 2 else [ref[k] for k in range(ref.shape[0])]:
            value = part.astype(F32) if value is None else value + part.astype(F32)
    total[...] = value
    for out, index in ((mine, xl[0]), (theirs, 1 - xl[0])):
        out[...] = total[pl.ds(pl.multiple_of(index * rows, 8), rows)].astype(out.dtype)


def settle(xl, parts, dtype, *after):
    rows, width = parts[0].shape[-2:]
    half = pl.BlockSpec((rows // 2, width), lambda s, x: (0, 0))
    return pl.pallas_call(
        functools.partial(settle_kernel, len(parts)),
        out_shape=[jax.ShapeDtypeStruct((rows // 2, width), t) for t in (F32, dtype)],
        grid_spec=pltpu.PrefetchScalarGridSpec(
            num_scalar_prefetch=1,
            grid=(1,),
            in_specs=[pl.BlockSpec(p.shape, lambda s, x, n=p.ndim: (0,) * n) for p in parts]
            + [ANY] * len(after),
            out_specs=[half] * 2,
            scratch_shapes=[pltpu.VMEM((rows, width), F32)],
        ),
        compiler_params=pltpu.CompilerParams(vmem_limit_bytes=16 * 2**20),
        cost_estimate=pl.CostEstimate(flops=0, bytes_accessed=0, transcendentals=0),
        name="settle",
    )(xl, *parts, *after)


def grow_kernel(side, x, received, *refs):
    out, held, sems, out_sem = refs[-4:]
    for k in range(2):
        pltpu.make_async_copy(x.at[side * 2 + k], held.at[k], sems.at[k]).start()
    for k in range(2):
        wait_all(held.at[k], sems.at[k])
        held[k] = add(held[k], received[k]).astype(BF)
        pltpu.make_async_copy(held.at[k], out.at[side * 2 + k], out_sem).start()
    wait_all(held, out_sem)


def grow(x, received, side, *after):
    hbm = pl.BlockSpec(memory_space=pltpu.HBM)
    return pl.pallas_call(
        functools.partial(grow_kernel, side),
        out_shape=pltpu.HBM(x.shape, x.dtype),
        grid=(1,),
        in_specs=[hbm, pl.BlockSpec(received.shape, lambda s: (0, 0, 0))] + [ANY] * len(after),
        out_specs=hbm,
        scratch_shapes=[
            pltpu.VMEM(received.shape, x.dtype),
            pltpu.SemaphoreType.DMA((2,)),
            pltpu.SemaphoreType.DMA,
        ],
        input_output_aliases={0: 0},
        compiler_params=pltpu.CompilerParams(vmem_limit_bytes=8 * 2**20),
        cost_estimate=NO_COST,
        name="grow",
    )(in_hbm(x), received, *after)


def fetch_tiles(step, source, held, sems):
    @pl.when(step == 0)
    def _():
        for k in range(4):
            rows = source.at[pl.ds(k * TILE, TILE)]
            pltpu.make_async_copy(rows, held.at[k], sems.at[k]).start()

    wait_all(held.at[step], sems.at[step])


def left_kernel(place, mine, other, partner, partner_other, left, out, total, packed, held, sems):
    step = pl.program_id(0)
    fetch_tiles(step, left, held, sems)
    at = pl.ds(pl.multiple_of((step & 1) * TILE, TILE), TILE)
    rows = mine.shape[0]

    def term(a, b):
        stacked = jnp.concatenate(split_pair(a[:, at] + b[:, at]), axis=0)
        value = jnp.dot(stacked, held[step], preferred_element_type=F32)
        total[...] = jnp.where(step == 0, value, total[...] + value)

    own = (step >> 1) == (place[1] ^ place[0])
    pl.when(own)(lambda: term(mine, other))
    pl.when(jnp.logical_not(own))(lambda: term(partner, partner_other))

    @pl.when(step == 3)
    def _():
        value = total[:rows] + total[rows:]
        for z in range(2):
            for y in range(4):
                for xl in range(2):
                    for c in range(2):
                        n = ((z * 4 + y) * 2 + xl) * 2 + c
                        block = value[:, n * rows : (n + 1) * rows]
                        packed[n, 0:16, 0:rows] = block[0:16]
                        packed[n, 0:16, rows : 2 * rows] = block[16:32]
                        packed[n, 0:8, 2 * rows : 3 * rows] = block[32:40]
                        ready = packed[n].astype(BF)
                        for there in (0, 2):
                            d = c * 32 + (there + z) * 8 + y * 2 + xl
                            out[d] = ready
                            out[64 + d] = ready


def left_product(place, mine, other, partner, partner_other, left):
    rows, half = mine.shape
    whole = pl.BlockSpec((rows, half), lambda k, p: (0, 0))
    return pl.pallas_call(
        left_kernel,
        out_shape=jax.ShapeDtypeStruct((128, 16, 128), BF),
        grid_spec=pltpu.PrefetchScalarGridSpec(
            num_scalar_prefetch=1,
            grid=(4,),
            in_specs=[whole] * 4 + [pl.BlockSpec(memory_space=pltpu.HBM)],
            out_specs=pl.BlockSpec((128, 16, 128), lambda k, p: (0, 0, 0)),
            scratch_shapes=[
                pltpu.VMEM((2 * rows, half), F32),
                pltpu.VMEM((32, 16, 128), F32),
                pltpu.VMEM((4, TILE, half), BF),
                pltpu.SemaphoreType.DMA((4,)),
            ],
        ),
        compiler_params=pltpu.CompilerParams(vmem_limit_bytes=20 * 2**20),
        cost_estimate=NO_COST,
        name="left_product",
    )(place, mine, other, partner, partner_other, left)


def right_kernel(place, blocks, right, late, out, rows_in, held, sems):
    del late
    step = pl.program_id(0)
    fetch_tiles(step, right, held, sems)
    rows = out.shape[0]
    for near in range(2):
        for y in range(4):
            for xl in range(2):
                core = (step >> 1) ^ ((near + y) & 1)
                block = blocks[core * 32 + ((step & 1) * 2 + near) * 8 + y * 2 + xl].astype(F32)
                at = ((near * 4 + y) * 2 + xl) * rows
                rows_in[at : at + 16, :] = block[:, 0:rows]
                rows_in[at + 16 : at + 32, :] = block[:, rows : 2 * rows]
                rows_in[at + 32 : at + 40, :] = block[0:8, 2 * rows : 3 * rows]
    value = contract(rows_in[...].astype(BF), held[step])
    pl.when(step == 0)(lambda: out.__setitem__(..., value))
    pl.when(step > 0)(lambda: out.__setitem__(..., out[...] + value))


def right_product(place, blocks, right, late):
    width, half = right.shape
    rows = width // 64
    return pl.pallas_call(
        right_kernel,
        out_shape=jax.ShapeDtypeStruct((rows, half), F32),
        grid_spec=pltpu.PrefetchScalarGridSpec(
            num_scalar_prefetch=1,
            grid=(4,),
            in_specs=[
                pl.BlockSpec((64, 16, 128), lambda k, p: (p[2] >> 1, 0, 0)),
                pl.BlockSpec(memory_space=pltpu.HBM),
                ANY,
            ],
            out_specs=pl.BlockSpec((rows, half), lambda k, p: (0, 0)),
            scratch_shapes=[
                pltpu.VMEM((TILE, rows), F32),
                pltpu.VMEM((4, TILE, half), BF),
                pltpu.SemaphoreType.DMA((4,)),
            ],
        ),
        compiler_params=pltpu.CompilerParams(vmem_limit_bytes=20 * 2**20),
        cost_estimate=NO_COST,
        name="right_product",
    )(place, blocks, right, late)


def per_device(hidden, out_grad, left_inverse, right_inverse):
    z, y, xl, c, o = (lax.axis_index(n) for n in ("z", "y", "xl", "c", "o"))
    tokens, width = hidden.shape
    half = width // 2
    token_total = tokens * 64
    first = o == 0
    h = c ^ ((z + y) & 1)
    hidden, out_grad = in_hbm(hidden), in_hbm(out_grad)
    left_inverse, right_inverse = in_hbm(left_inverse), in_hbm(right_inverse)
    place = jnp.stack([o, h, z, y]).astype(jnp.int32)
    second_me = jnp.where(h == 0, y, z).astype(jnp.int32)[None]

    grads_next, acts_next = in_hbm(shift(out_grad, "c", 1)), in_hbm(shift(hidden, "c", 1))
    partial = cross_own(place, out_grad, hidden)
    factor_partial = factor_own(place, hidden, out_grad, partial)

    own, m1, m2, m3 = cross_term(
        place, grads_next, acts_next, partial, in_hbm(factor_partial)
    )
    m_parts = [own, turn(m1, 1, 0), turn(m2, 2, 0), turn(m3, 3, 0)]

    f_own, right, far_a, far_b, left = factor_term(
        place, acts_next, grads_next, in_hbm(factor_partial), in_hbm(m1)
    )
    from_left, from_right = turn(far_a, 1, 0), turn(far_b, -1, 0)

    my_xl = xl.astype(jnp.int32)[None]

    def second_sends(pieces):
        return [turn(piece, s, 1) for s, piece in enumerate(pieces, 1)]

    m, *m_pieces = fold(second_me, m_parts, in_hbm(f_own))
    m_received = second_sends(m_pieces)
    right = grow(right, from_left, 0, m_received[0])
    left = grow(left, from_right, 1, m_received[1], m_received[2])
    f_parts = [f_own, turn(right, 1, 0), turn(left, -1, 0)]

    mine, theirs = settle(my_xl, [in_hbm(m), *m_received], F32)
    across = lax.ppermute(theirs, ("xl", "o"), [(i, 3 - i) for i in range(4)])
    products = left_product(
        place, mine, shift(theirs, "xl", 1), shift(mine, "o", 1), across, left_inverse
    )
    blocks = lax.all_to_all(products, ("o", "c", "z", "y", "xl"), 0, 0, tiled=True)
    f, *f_pieces = fold(second_me, f_parts, products)
    update = right_product(place, blocks, right_inverse, f_pieces[0])
    f_mine, f_theirs = settle(my_xl, [in_hbm(f), *second_sends(f_pieces)], BF, in_hbm(update))

    f = add(f_mine, shift(f_theirs, "xl", 1))
    f = f * jnp.where(first, 1.0 / token_total, 1.0).astype(F32)
    f = f.reshape(2, width // 64, half)
    mine = pick(f, 0, c)
    theirs = shift(pick(f, 0, 1 - c), "c", 1)
    factors = jnp.concatenate(
        [jnp.where(h == 0, mine, theirs), jnp.where(h == 0, theirs, mine)], axis=1
    )[None]
    return factors, update


def solution(mesh):
    fine = Mesh(mesh.devices.reshape(4, 4, 2, 2, 2), ("z", "y", "xl", "c", "o"))
    dp = ("z", "y", "xl", "c")
    in_specs = (P(dp, None), P(dp, None), P(None, "o"), P(None, "o"))
    out_specs = (P("o", dp, None), P(dp, "o"))
    return jax.shard_map(
        per_device, mesh=fine, in_specs=in_specs, out_specs=out_specs, check_vma=False
    )
```

```python
import functools

import jax
import jax.numpy as jnp
from jax import lax
from jax.experimental import pallas as pl
from jax.experimental.pallas import tpu as pltpu
from jax.sharding import Mesh, PartitionSpec as P

BF = jnp.bfloat16
F32 = jnp.float32
TILE = 640
ANY = pl.BlockSpec(memory_space=pl.ANY)
VMEM = pl.BlockSpec(memory_space=pltpu.VMEM)


def contract(first_rows, second_rows):
    return lax.dot_general(
        first_rows, second_rows, (((0,), (0,)), ((), ())), preferred_element_type=F32
    )


def shift(x, axis, step):
    size = lax.axis_size(axis)
    return lax.ppermute(x, axis, [(i, (i + step) % size) for i in range(size)])


def turn(x, step, stage):
    pairs = []
    for z in range(4):
        for y in range(4):
            for h in range(2):
                along_z = (h == 0) == (stage == 0)
                z2, y2 = ((z + step) % 4, y) if along_z else (z, (y + step) % 4)
                core, core2 = h ^ ((z + y) & 1), h ^ ((z2 + y2) & 1)
                pairs.append(((z * 4 + y) * 2 + core, (z2 * 4 + y2) * 2 + core2))
    return lax.ppermute(x, ("z", "y", "c"), pairs)


def in_hbm(x):
    return pltpu.with_memory_space_constraint(x, pltpu.HBM)


def pick(x, dim, index):
    return lax.dynamic_index_in_dim(x, index, dim, keepdims=False)


def split_pair(x):
    high = x.astype(BF)
    return high, (x - high.astype(F32)).astype(BF)


def place_tile(place, buffer, sem, outs, m, zs):
    rows = TILE // (zs * 4)

    def start(at, out, slot):
        block = buffer.at[m, pl.ds(at, rows)]
        pltpu.make_async_copy(block, out.at[slot], sem).start()

    for a in range(zs):
        z = m * zs + a

        @pl.when(place[1] == 0)
        def _():
            for r, out in enumerate(outs):

                @pl.when(((z - place[2] + 4) & 3) == r)
                def _():
                    for k in range(4):
                        if isinstance(out, tuple):
                            start((a * 4 + k) * rows, out[k // 2], k % 2)
                        else:
                            start((a * 4 + k) * rows, out, k)

        @pl.when(place[1] == 1)
        def _():
            for r, out in enumerate(outs):
                at = pl.multiple_of((a * 4 + ((place[3] + r) & 3)) * rows, 16)
                if isinstance(out, tuple):
                    pl.when(z < 2)(functools.partial(start, at, out[0], z & 1))
                    pl.when(z >= 2)(functools.partial(start, at, out[1], z & 1))
                else:
                    start(at, out, z)


def wait_all(buffer, sem):
    pltpu.make_async_copy(buffer, buffer, sem).wait()


def own_kernel(place, a, b, out, lhs, rhs, lhs_sems, rhs_sem):
    m = pl.program_id(0)
    half = rhs.shape[1]

    @pl.when(m == 0)
    def _():
        at = pl.ds(pl.multiple_of((place[1] ^ place[0]) * half, half), half)
        pltpu.make_async_copy(b.at[:, at], rhs, rhs_sem).start()
        for k in range(2):
            at = pl.ds(pl.multiple_of(place[1] * half + k * TILE, TILE), TILE)
            pltpu.make_async_copy(a.at[:, at], lhs.at[k], lhs_sems.at[k]).start()
        wait_all(rhs, rhs_sem)

    wait_all(lhs.at[m], lhs_sems.at[m])
    out[...] = contract(lhs[m], rhs[...])


def cross_kernel(place, a, b, partial, own, ahead1, ahead2, ahead3, held, buffer, held_sems, sem):
    m = pl.program_id(0)

    @pl.when(m == 0)
    def _():
        for k in range(2):
            rows = partial.at[pl.ds(k * TILE, TILE)]
            pltpu.make_async_copy(rows, held.at[k], held_sems.at[k]).start()

    tile = contract(a[...], b[...])
    wait_all(held.at[m], held_sems.at[m])
    buffer[m] = (held[m] + tile).astype(BF)
    place_tile(place, buffer, sem, [own, ahead1, ahead2, ahead3], m, 2)
    pl.when(m == 1)(lambda: wait_all(buffer, sem))


def cross_own(place, grads, acts):
    tokens, half = grads.shape[0], grads.shape[1] // 2
    return pl.pallas_call(
        own_kernel,
        out_shape=jax.ShapeDtypeStruct((half, half), F32),
        grid_spec=pltpu.PrefetchScalarGridSpec(
            num_scalar_prefetch=1,
            grid=(2,),
            in_specs=[pl.BlockSpec(memory_space=pltpu.HBM)] * 2,
            out_specs=pl.BlockSpec((TILE, half), lambda m, p: (m, 0)),
            scratch_shapes=[
                pltpu.VMEM((2, tokens, TILE), BF),
                pltpu.VMEM((tokens, half), BF),
                pltpu.SemaphoreType.DMA((2,)),
                pltpu.SemaphoreType.DMA,
            ],
        ),
        compiler_params=pltpu.CompilerParams(vmem_limit_bytes=28 * 2**20),
        cost_estimate=pl.CostEstimate(
            flops=2 * tokens * half * half, bytes_accessed=8 * tokens * half, transcendentals=0
        ),
        name="cross_own",
    )(place, grads, acts)


def cross_term(place, grads_next, acts_next, partial):
    tokens, half = grads_next.shape[0], grads_next.shape[1] // 2
    out = pltpu.HBM((4, half // 16, half), BF)
    return pl.pallas_call(
        cross_kernel,
        out_shape=[out] * 4,
        grid_spec=pltpu.PrefetchScalarGridSpec(
            num_scalar_prefetch=1,
            grid=(2,),
            in_specs=[
                pl.BlockSpec((tokens, TILE), lambda m, p: (0, p[1] * 2 + m)),
                pl.BlockSpec((tokens, half), lambda m, p: (0, p[1] ^ p[0])),
                ANY,
            ],
            out_specs=[pl.BlockSpec(memory_space=pltpu.HBM)] * 4,
            scratch_shapes=[
                pltpu.VMEM((2, TILE, half), F32),
                pltpu.VMEM((2, TILE, half), BF),
                pltpu.SemaphoreType.DMA((2,)),
                pltpu.SemaphoreType.DMA,
            ],
        ),
        compiler_params=pltpu.CompilerParams(vmem_limit_bytes=28 * 2**20),
        cost_estimate=pl.CostEstimate(
            flops=2 * tokens * half * half, bytes_accessed=10 * tokens * half, transcendentals=0
        ),
        name="cross_term",
    )(place, grads_next, acts_next, partial)


def factor_kernel(place, h_own, g_own, h_next, g_next, after, *rest):
    del after
    own, right, far_a, far_b, left, lhs, rhs, buffer, lhs_sems, rhs_sem, sem = rest
    m = pl.program_id(0)
    half = rhs.shape[2]

    def fetch(step, with_rhs):
        slot = step & 1
        at = pl.ds(pl.multiple_of(step * TILE, TILE), TILE)
        columns = pl.ds(pl.multiple_of(place[1] * half, half), half)
        for owner, refs in enumerate(((h_own, h_next), (g_own, g_next))):

            @pl.when(place[0] == owner)
            def _():
                for k, ref in enumerate(refs):
                    pltpu.make_async_copy(ref.at[:, at], lhs.at[slot, k], lhs_sems.at[slot]).start()
                    if with_rhs:
                        pltpu.make_async_copy(ref.at[:, columns], rhs.at[k], rhs_sem).start()

    pl.when(m == 0)(lambda: fetch(0, True))
    pl.when(m < 3)(lambda: fetch(m + 1, False))
    slot = m & 1
    wait_all(lhs.at[slot], lhs_sems.at[slot])
    pl.when(m == 0)(lambda: wait_all(rhs, rhs_sem))

    buffer[m] = (contract(lhs[slot, 0], rhs[0]) + contract(lhs[slot, 1], rhs[1])).astype(BF)
    place_tile(place, buffer, sem, [own, right, (far_a, far_b), left], m, 1)
    pl.when(m == 3)(lambda: wait_all(buffer, sem))


def factor_term(place, acts, grads, acts_next, grads_next, after):
    tokens, width = acts.shape
    half = width // 2
    hbm = pl.BlockSpec(memory_space=pltpu.HBM)
    out = pltpu.HBM((4, width // 16, half), BF)
    side = pltpu.HBM((2, width // 16, half), BF)
    return pl.pallas_call(
        factor_kernel,
        out_shape=[out, out, side, side, out],
        grid_spec=pltpu.PrefetchScalarGridSpec(
            num_scalar_prefetch=1,
            grid=(4,),
            in_specs=[hbm] * 2 + [ANY] * 3,
            out_specs=[hbm] * 5,
            scratch_shapes=[
                pltpu.VMEM((2, 2, tokens, TILE), BF),
                pltpu.VMEM((2, tokens, half), BF),
                pltpu.VMEM((4, TILE, half), BF),
                pltpu.SemaphoreType.DMA((2,)),
                pltpu.SemaphoreType.DMA,
                pltpu.SemaphoreType.DMA,
            ],
        ),
        compiler_params=pltpu.CompilerParams(vmem_limit_bytes=30 * 2**20),
        cost_estimate=pl.CostEstimate(
            flops=4 * tokens * width * half, bytes_accessed=16 * tokens * half, transcendentals=0
        ),
        name="factor_term",
    )(place, acts, grads, acts_next, grads_next, after)


def add(first, *rest):
    total = first.astype(F32)
    for x in rest:
        total = total + x.astype(F32)
    return total


def fold_kernel(count, me, *refs):
    own, *others = refs[-6:-2]
    held, sem = refs[-2:]
    copy = pltpu.make_async_copy(refs[0], held, sem)
    copy.start()
    copy.wait()
    for r, out in enumerate([own, *others]):
        at = (me[0] + r) & 3
        out[...] = add(held[at], *[part[at] for part in refs[1:count]]).astype(out.dtype)


def fold(me, parts, *after):
    _, rows, width = parts[0].shape
    whole = pl.BlockSpec((rows, width), lambda s, m: (0, 0))
    return pl.pallas_call(
        functools.partial(fold_kernel, len(parts)),
        out_shape=[pltpu.HBM((rows, width), F32)]
        + [pltpu.VMEM((rows, width), BF)] * 3,
        grid_spec=pltpu.PrefetchScalarGridSpec(
            num_scalar_prefetch=1,
            grid=(1,),
            in_specs=[pl.BlockSpec(memory_space=pltpu.HBM)]
            + [VMEM] * (len(parts) - 1)
            + [ANY] * len(after),
            out_specs=[whole] + [VMEM] * 3,
            scratch_shapes=[pltpu.VMEM((4, rows, width), BF), pltpu.SemaphoreType.DMA],
        ),
        compiler_params=pltpu.CompilerParams(vmem_limit_bytes=12 * 2**20),
        cost_estimate=pl.CostEstimate(flops=0, bytes_accessed=0, transcendentals=0),
        name="fold",
    )(me, in_hbm(parts[0]), *parts[1:], *after)


def settle_kernel(count, xl, *refs):
    mine, theirs, total = refs[-3:]
    rows = mine.shape[0]
    value = None
    for ref in refs[:count]:
        for part in [ref[...]] if len(ref.shape) == 2 else [ref[k] for k in range(ref.shape[0])]:
            value = part.astype(F32) if value is None else value + part.astype(F32)
    total[...] = value
    for out, index in ((mine, xl[0]), (theirs, 1 - xl[0])):
        out[...] = total[pl.ds(pl.multiple_of(index * rows, 8), rows)].astype(out.dtype)


def settle(xl, parts, dtype, *after):
    rows, width = parts[0].shape[-2:]
    half = pl.BlockSpec((rows // 2, width), lambda s, x: (0, 0))
    return pl.pallas_call(
        functools.partial(settle_kernel, len(parts)),
        out_shape=[jax.ShapeDtypeStruct((rows // 2, width), t) for t in (F32, dtype)],
        grid_spec=pltpu.PrefetchScalarGridSpec(
            num_scalar_prefetch=1,
            grid=(1,),
            in_specs=[pl.BlockSpec((rows, width), lambda s, x: (0, 0))]
            + [VMEM] * (len(parts) - 1)
            + [ANY] * len(after),
            out_specs=[half] * 2,
            scratch_shapes=[pltpu.VMEM((rows, width), F32)],
        ),
        compiler_params=pltpu.CompilerParams(vmem_limit_bytes=8 * 2**20),
        cost_estimate=pl.CostEstimate(flops=0, bytes_accessed=0, transcendentals=0),
        name="settle",
    )(xl, *parts, *after)


def grow_kernel(side, x, received, *refs):
    out, held, sems, out_sem = refs[-4:]
    for k in range(2):
        pltpu.make_async_copy(x.at[side * 2 + k], held.at[k], sems.at[k]).start()
    for k in range(2):
        wait_all(held.at[k], sems.at[k])
        held[k] = add(held[k], received[k]).astype(BF)
        pltpu.make_async_copy(held.at[k], out.at[side * 2 + k], out_sem).start()
    wait_all(held, out_sem)


def grow(x, received, side, *after):
    hbm = pl.BlockSpec(memory_space=pltpu.HBM)
    return pl.pallas_call(
        functools.partial(grow_kernel, side),
        out_shape=pltpu.HBM(x.shape, x.dtype),
        grid=(1,),
        in_specs=[hbm, VMEM] + [ANY] * len(after),
        out_specs=hbm,
        scratch_shapes=[
            pltpu.VMEM(received.shape, x.dtype),
            pltpu.SemaphoreType.DMA((2,)),
            pltpu.SemaphoreType.DMA,
        ],
        input_output_aliases={0: 0},
        compiler_params=pltpu.CompilerParams(vmem_limit_bytes=8 * 2**20),
        cost_estimate=pl.CostEstimate(flops=0, bytes_accessed=0, transcendentals=0),
        name="grow",
    )(in_hbm(x), received, *after)


def fetch_tiles(step, source, held, sems):
    @pl.when(step == 0)
    def _():
        for k in range(4):
            rows = source.at[pl.ds(k * TILE, TILE)]
            pltpu.make_async_copy(rows, held.at[k], sems.at[k]).start()

    wait_all(held.at[step], sems.at[step])


def left_kernel(own, place, a, b, left, *rest):
    before = None if own else rest[0]
    out, total, held, sems = rest[-4:] if own else (rest[1], rest[2], *rest[4:])
    step = pl.program_id(0)
    rows = a.shape[0]
    at = pl.ds(pl.multiple_of(step * TILE, TILE), TILE)
    part = place[1] ^ place[0] if own else 1 - (place[1] ^ place[0])

    @pl.when(step == 0)
    def _():
        for k in range(2):
            tile = left.at[pl.ds(pl.multiple_of((part * 2 + k) * TILE, TILE), TILE)]
            pltpu.make_async_copy(tile, held.at[k], sems.at[k]).start()

    stacked = jnp.concatenate(split_pair(a[:, at] + b[:, at]), axis=0)
    wait_all(held.at[step], sems.at[step])
    value = jnp.dot(stacked, held[step], preferred_element_type=F32)
    pl.when(step == 0)(lambda: total.__setitem__(..., value if own else before[...] + value))
    pl.when(step == 1)(lambda: total.__setitem__(..., total[...] + value))
    if own:
        pl.when(step == 1)(lambda: out.__setitem__(..., total[...]))
        return
    packed = rest[3]

    @pl.when(step == 1)
    def _():
        result = total[:rows] + total[rows:]
        for z in range(2):
            for y in range(4):
                for xl in range(2):
                    for c in range(2):
                        n = ((z * 4 + y) * 2 + xl) * 2 + c
                        block = result[:, n * rows : (n + 1) * rows]
                        packed[n, 0:16, 0:rows] = block[0:16]
                        packed[n, 0:16, rows : 2 * rows] = block[16:32]
                        packed[n, 0:8, 2 * rows : 3 * rows] = block[32:40]
                        ready = packed[n].astype(BF)
                        for there in (0, 2):
                            d = c * 32 + (there + z) * 8 + y * 2 + xl
                            out[d] = ready
                            out[64 + d] = ready


def left_product(place, a, b, left, before=None):
    rows, half = a.shape
    own = before is None
    total = pltpu.VMEM((2 * rows, half), F32)
    return pl.pallas_call(
        functools.partial(left_kernel, own),
        out_shape=total if own else pltpu.VMEM((128, 16, 128), BF),
        grid_spec=pltpu.PrefetchScalarGridSpec(
            num_scalar_prefetch=1,
            grid=(2,),
            in_specs=[VMEM, VMEM, pl.BlockSpec(memory_space=pltpu.HBM)] + [VMEM] * (not own),
            out_specs=VMEM,
            scratch_shapes=[total]
            + [pltpu.VMEM((32, 16, 128), F32)] * (not own)
            + [pltpu.VMEM((2, TILE, half), BF), pltpu.SemaphoreType.DMA((2,))],
        ),
        compiler_params=pltpu.CompilerParams(vmem_limit_bytes=16 * 2**20),
        cost_estimate=pl.CostEstimate(
            flops=0 if own else 256 * rows * half * half, bytes_accessed=0, transcendentals=0
        ),
        name="left_own" if own else "left_product",
    )(place, a, b, left, *([] if own else [before]))


def right_kernel(place, blocks, right, late, out, rows_in, held, sems):
    del late
    step = pl.program_id(0)
    fetch_tiles(step, right, held, sems)
    rows = out.shape[0]
    for near in range(2):
        for y in range(4):
            for xl in range(2):
                core = (step >> 1) ^ ((near + y) & 1)
                block = blocks[core * 32 + ((step & 1) * 2 + near) * 8 + y * 2 + xl].astype(F32)
                at = ((near * 4 + y) * 2 + xl) * rows
                rows_in[at : at + 16, :] = block[:, 0:rows]
                rows_in[at + 16 : at + 32, :] = block[:, rows : 2 * rows]
                rows_in[at + 32 : at + 40, :] = block[0:8, 2 * rows : 3 * rows]
    value = contract(rows_in[...].astype(BF), held[step])
    pl.when(step == 0)(lambda: out.__setitem__(..., value))
    pl.when(step > 0)(lambda: out.__setitem__(..., out[...] + value))


def right_product(place, blocks, right, late):
    width, half = right.shape
    rows = width // 64
    return pl.pallas_call(
        right_kernel,
        out_shape=jax.ShapeDtypeStruct((rows, half), F32),
        grid_spec=pltpu.PrefetchScalarGridSpec(
            num_scalar_prefetch=1,
            grid=(4,),
            in_specs=[
                pl.BlockSpec((64, 16, 128), lambda k, p: (p[2] >> 1, 0, 0)),
                pl.BlockSpec(memory_space=pltpu.HBM),
                ANY,
            ],
            out_specs=pl.BlockSpec((rows, half), lambda k, p: (0, 0)),
            scratch_shapes=[
                pltpu.VMEM((TILE, rows), F32),
                pltpu.VMEM((4, TILE, half), BF),
                pltpu.SemaphoreType.DMA((4,)),
            ],
        ),
        compiler_params=pltpu.CompilerParams(vmem_limit_bytes=20 * 2**20),
        cost_estimate=pl.CostEstimate(
            flops=640 * rows * half * half, bytes_accessed=4 * half * half, transcendentals=0
        ),
        name="right_product",
    )(place, blocks, right, late)


def per_device(hidden, out_grad, left_inverse, right_inverse):
    z, y, xl, c, o = (lax.axis_index(n) for n in ("z", "y", "xl", "c", "o"))
    tokens, width = hidden.shape
    half = width // 2
    token_total = tokens * 64
    first = o == 0
    h = c ^ ((z + y) & 1)
    hidden, out_grad = in_hbm(hidden), in_hbm(out_grad)
    left_inverse, right_inverse = in_hbm(left_inverse), in_hbm(right_inverse)
    place = jnp.stack([o, h, z, y]).astype(jnp.int32)
    second_me = jnp.where(h == 0, y, z).astype(jnp.int32)[None]

    grads_next, acts_next = in_hbm(shift(out_grad, "c", 1)), in_hbm(shift(hidden, "c", 1))
    partial = cross_own(place, out_grad, hidden)

    own, m1, m2, m3 = cross_term(place, grads_next, acts_next, partial)
    m_parts = [own, turn(m1, 1, 0), turn(m2, 2, 0), turn(m3, 3, 0)]

    f_own, right, far_a, far_b, left = factor_term(
        place, hidden, out_grad, acts_next, grads_next, in_hbm(m1)
    )
    from_left, from_right = turn(far_a, 1, 0), turn(far_b, -1, 0)

    my_xl = xl.astype(jnp.int32)[None]

    def second_sends(pieces):
        return [turn(piece, s, 1) for s, piece in enumerate(pieces, 1)]

    m, *m_pieces = fold(second_me, m_parts, in_hbm(f_own))
    m_received = second_sends(m_pieces)
    right = grow(right, from_left, 0, *m_received)
    left = grow(left, from_right, 1, *m_received)
    f_parts = [f_own, turn(right, 1, 0), turn(left, -1, 0)]

    mine, theirs = settle(my_xl, [in_hbm(m), *m_received], F32)
    across = lax.ppermute(theirs, ("xl", "o"), [(i, 3 - i) for i in range(4)])
    products = left_product(place, mine, shift(theirs, "xl", 1), left_inverse)
    products = left_product(place, shift(mine, "o", 1), across, left_inverse, products)
    blocks = lax.all_to_all(products, ("o", "c", "z", "y", "xl"), 0, 0, tiled=True)
    f, *f_pieces = fold(second_me, f_parts, products)
    update = right_product(place, blocks, right_inverse, f_pieces[0])
    f_mine, f_theirs = settle(my_xl, [in_hbm(f), *second_sends(f_pieces)], BF, in_hbm(update))

    f = add(f_mine, shift(f_theirs, "xl", 1))
    f = f * jnp.where(first, 1.0 / token_total, 1.0).astype(F32)
    f = f.reshape(2, width // 64, half)
    mine = pick(f, 0, c)
    theirs = shift(pick(f, 0, 1 - c), "c", 1)
    factors = jnp.concatenate(
        [jnp.where(h == 0, mine, theirs), jnp.where(h == 0, theirs, mine)], axis=1
    )[None]
    return factors, update


def solution(mesh):
    fine = Mesh(mesh.devices.reshape(4, 4, 2, 2, 2), ("z", "y", "xl", "c", "o"))
    dp = ("z", "y", "xl", "c")
    in_specs = (P(dp, None), P(dp, None), P(None, "o"), P(None, "o"))
    out_specs = (P("o", dp, None), P(dp, "o"))
    return jax.shard_map(
        per_device, mesh=fine, in_specs=in_specs, out_specs=out_specs, check_vma=False
    )
```

```python
import functools

import jax
import jax.numpy as jnp
from jax import lax
from jax.experimental import pallas as pl
from jax.experimental.pallas import tpu as pltpu
from jax.sharding import Mesh, PartitionSpec as P

BF = jnp.bfloat16
F32 = jnp.float32
TILE = 640
ANY = pl.BlockSpec(memory_space=pl.ANY)
VMEM = pl.BlockSpec(memory_space=pltpu.VMEM)


def contract(first_rows, second_rows):
    return lax.dot_general(
        first_rows, second_rows, (((0,), (0,)), ((), ())), preferred_element_type=F32
    )


def shift(x, axis, step):
    size = lax.axis_size(axis)
    return lax.ppermute(x, axis, [(i, (i + step) % size) for i in range(size)])


def turn(x, step, stage):
    pairs = []
    for z in range(4):
        for y in range(4):
            for h in range(2):
                along_z = (h == 0) == (stage == 0)
                z2, y2 = ((z + step) % 4, y) if along_z else (z, (y + step) % 4)
                core, core2 = h ^ ((z + y) & 1), h ^ ((z2 + y2) & 1)
                pairs.append(((z * 4 + y) * 2 + core, (z2 * 4 + y2) * 2 + core2))
    return lax.ppermute(x, ("z", "y", "c"), pairs)


def in_hbm(x):
    return pltpu.with_memory_space_constraint(x, pltpu.HBM)


def pick(x, dim, index):
    return lax.dynamic_index_in_dim(x, index, dim, keepdims=False)


def split_pair(x):
    high = x.astype(BF)
    return high, (x - high.astype(F32)).astype(BF)


def place_tile(place, buffer, sem, outs, m, zs):
    rows = TILE // (zs * 4)

    def start(at, out, slot):
        block = buffer.at[m, pl.ds(at, rows)]
        pltpu.make_async_copy(block, out.at[slot], sem).start()

    for a in range(zs):
        z = m * zs + a

        @pl.when(place[1] == 0)
        def _():
            for r, out in enumerate(outs):

                @pl.when(((z - place[2] + 4) & 3) == r)
                def _():
                    for k in range(4):
                        if isinstance(out, tuple):
                            start((a * 4 + k) * rows, out[k // 2], k % 2)
                        else:
                            start((a * 4 + k) * rows, out, k)

        @pl.when(place[1] == 1)
        def _():
            for r, out in enumerate(outs):
                at = pl.multiple_of((a * 4 + ((place[3] + r) & 3)) * rows, 16)
                if isinstance(out, tuple):
                    pl.when(z < 2)(functools.partial(start, at, out[0], z & 1))
                    pl.when(z >= 2)(functools.partial(start, at, out[1], z & 1))
                else:
                    start(at, out, z)


def wait_all(buffer, sem):
    pltpu.make_async_copy(buffer, buffer, sem).wait()


def own_kernel(place, a, b, out, lhs, rhs, lhs_sems, rhs_sem):
    m = pl.program_id(0)
    half = rhs.shape[1]

    @pl.when(m == 0)
    def _():
        at = pl.ds(pl.multiple_of((place[1] ^ place[0]) * half, half), half)
        pltpu.make_async_copy(b.at[:, at], rhs, rhs_sem).start()
        for k in range(2):
            at = pl.ds(pl.multiple_of(place[1] * half + k * TILE, TILE), TILE)
            pltpu.make_async_copy(a.at[:, at], lhs.at[k], lhs_sems.at[k]).start()
        wait_all(rhs, rhs_sem)

    wait_all(lhs.at[m], lhs_sems.at[m])
    out[...] = contract(lhs[m], rhs[...])


def cross_kernel(place, a, b, partial, own, ahead1, ahead2, ahead3, held, buffer, held_sems, sem):
    m = pl.program_id(0)

    @pl.when(m == 0)
    def _():
        for k in range(2):
            rows = partial.at[pl.ds(k * TILE, TILE)]
            pltpu.make_async_copy(rows, held.at[k], held_sems.at[k]).start()

    tile = contract(a[...], b[...])
    wait_all(held.at[m], held_sems.at[m])
    buffer[m] = (held[m] + tile).astype(BF)
    place_tile(place, buffer, sem, [own, ahead1, ahead2, ahead3], m, 2)
    pl.when(m == 1)(lambda: wait_all(buffer, sem))


def cross_own(place, grads, acts):
    tokens, half = grads.shape[0], grads.shape[1] // 2
    return pl.pallas_call(
        own_kernel,
        out_shape=jax.ShapeDtypeStruct((half, half), F32),
        grid_spec=pltpu.PrefetchScalarGridSpec(
            num_scalar_prefetch=1,
            grid=(2,),
            in_specs=[pl.BlockSpec(memory_space=pltpu.HBM)] * 2,
            out_specs=pl.BlockSpec((TILE, half), lambda m, p: (m, 0)),
            scratch_shapes=[
                pltpu.VMEM((2, tokens, TILE), BF),
                pltpu.VMEM((tokens, half), BF),
                pltpu.SemaphoreType.DMA((2,)),
                pltpu.SemaphoreType.DMA,
            ],
        ),
        compiler_params=pltpu.CompilerParams(vmem_limit_bytes=28 * 2**20),
        cost_estimate=pl.CostEstimate(
            flops=2 * tokens * half * half, bytes_accessed=8 * tokens * half, transcendentals=0
        ),
        name="cross_own",
    )(place, grads, acts)


def cross_term(place, grads_next, acts_next, partial):
    tokens, half = grads_next.shape[0], grads_next.shape[1] // 2
    out = pltpu.HBM((4, half // 16, half), BF)
    return pl.pallas_call(
        cross_kernel,
        out_shape=[out] * 4,
        grid_spec=pltpu.PrefetchScalarGridSpec(
            num_scalar_prefetch=1,
            grid=(2,),
            in_specs=[
                pl.BlockSpec((tokens, TILE), lambda m, p: (0, p[1] * 2 + m)),
                pl.BlockSpec((tokens, half), lambda m, p: (0, p[1] ^ p[0])),
                ANY,
            ],
            out_specs=[pl.BlockSpec(memory_space=pltpu.HBM)] * 4,
            scratch_shapes=[
                pltpu.VMEM((2, TILE, half), F32),
                pltpu.VMEM((2, TILE, half), BF),
                pltpu.SemaphoreType.DMA((2,)),
                pltpu.SemaphoreType.DMA,
            ],
        ),
        compiler_params=pltpu.CompilerParams(vmem_limit_bytes=28 * 2**20),
        cost_estimate=pl.CostEstimate(
            flops=2 * tokens * half * half, bytes_accessed=10 * tokens * half, transcendentals=0
        ),
        name="cross_term",
    )(place, grads_next, acts_next, partial)


def factor_kernel(place, h_own, g_own, h_next, g_next, after, *rest):
    del after
    own, right, far_a, far_b, left, lhs, rhs, buffer, lhs_sems, rhs_sem, sem = rest
    m = pl.program_id(0)
    half = rhs.shape[2]

    def fetch(step, with_rhs):
        slot = step & 1
        at = pl.ds(pl.multiple_of(step * TILE, TILE), TILE)
        columns = pl.ds(pl.multiple_of(place[1] * half, half), half)
        for owner, refs in enumerate(((h_own, h_next), (g_own, g_next))):

            @pl.when(place[0] == owner)
            def _():
                for k, ref in enumerate(refs):
                    pltpu.make_async_copy(ref.at[:, at], lhs.at[slot, k], lhs_sems.at[slot]).start()
                    if with_rhs:
                        pltpu.make_async_copy(ref.at[:, columns], rhs.at[k], rhs_sem).start()

    pl.when(m == 0)(lambda: fetch(0, True))
    pl.when(m < 3)(lambda: fetch(m + 1, False))
    slot = m & 1
    wait_all(lhs.at[slot], lhs_sems.at[slot])
    pl.when(m == 0)(lambda: wait_all(rhs, rhs_sem))

    buffer[m] = (contract(lhs[slot, 0], rhs[0]) + contract(lhs[slot, 1], rhs[1])).astype(BF)
    place_tile(place, buffer, sem, [own, right, (far_a, far_b), left], m, 1)
    pl.when(m == 3)(lambda: wait_all(buffer, sem))


def factor_term(place, acts, grads, acts_next, grads_next, after):
    tokens, width = acts.shape
    half = width // 2
    hbm = pl.BlockSpec(memory_space=pltpu.HBM)
    out = pltpu.HBM((4, width // 16, half), BF)
    side = pltpu.HBM((2, width // 16, half), BF)
    return pl.pallas_call(
        factor_kernel,
        out_shape=[out, out, side, side, out],
        grid_spec=pltpu.PrefetchScalarGridSpec(
            num_scalar_prefetch=1,
            grid=(4,),
            in_specs=[hbm] * 2 + [ANY] * 3,
            out_specs=[hbm] * 5,
            scratch_shapes=[
                pltpu.VMEM((2, 2, tokens, TILE), BF),
                pltpu.VMEM((2, tokens, half), BF),
                pltpu.VMEM((4, TILE, half), BF),
                pltpu.SemaphoreType.DMA((2,)),
                pltpu.SemaphoreType.DMA,
                pltpu.SemaphoreType.DMA,
            ],
        ),
        compiler_params=pltpu.CompilerParams(vmem_limit_bytes=30 * 2**20),
        cost_estimate=pl.CostEstimate(
            flops=4 * tokens * width * half, bytes_accessed=16 * tokens * half, transcendentals=0
        ),
        name="factor_term",
    )(place, acts, grads, acts_next, grads_next, after)


def add(first, *rest):
    total = first.astype(F32)
    for x in rest:
        total = total + x.astype(F32)
    return total


def fold_kernel(count, me, *refs):
    own, *others = refs[-6:-2]
    held, sems = refs[-2:]
    steps = [(1, others[0]), (2, others[1]), (3, others[2]), (0, own)]
    for r, _ in steps:
        pltpu.make_async_copy(refs[0].at[(me[0] + r) & 3], held.at[r], sems.at[r]).start()
    for r, out in steps:
        wait_all(held.at[r], sems.at[r])
        at = (me[0] + r) & 3
        out[...] = add(held[r], *[part[at] for part in refs[1:count]]).astype(out.dtype)


def fold(me, parts, *after):
    _, rows, width = parts[0].shape
    whole = pl.BlockSpec((rows, width), lambda s, m: (0, 0))
    return pl.pallas_call(
        functools.partial(fold_kernel, len(parts)),
        out_shape=[pltpu.HBM((rows, width), F32)]
        + [pltpu.VMEM((rows, width), BF)] * 3,
        grid_spec=pltpu.PrefetchScalarGridSpec(
            num_scalar_prefetch=1,
            grid=(1,),
            in_specs=[pl.BlockSpec(memory_space=pltpu.HBM)]
            + [VMEM] * (len(parts) - 1)
            + [ANY] * len(after),
            out_specs=[whole] + [VMEM] * 3,
            scratch_shapes=[pltpu.VMEM((4, rows, width), BF), pltpu.SemaphoreType.DMA((4,))],
        ),
        compiler_params=pltpu.CompilerParams(vmem_limit_bytes=12 * 2**20),
        cost_estimate=pl.CostEstimate(flops=0, bytes_accessed=0, transcendentals=0),
        name="fold",
    )(me, in_hbm(parts[0]), *parts[1:], *after)


def settle_kernel(count, xl, *refs):
    mine, theirs, total = refs[-3:]
    rows = mine.shape[0]
    value = None
    for ref in refs[:count]:
        for part in [ref[...]] if len(ref.shape) == 2 else [ref[k] for k in range(ref.shape[0])]:
            value = part.astype(F32) if value is None else value + part.astype(F32)
    total[...] = value
    for out, index in ((mine, xl[0]), (theirs, 1 - xl[0])):
        out[...] = total[pl.ds(pl.multiple_of(index * rows, 8), rows)].astype(out.dtype)


def settle(xl, parts, dtype, *after):
    rows, width = parts[0].shape[-2:]
    half = pl.BlockSpec((rows // 2, width), lambda s, x: (0, 0))
    return pl.pallas_call(
        functools.partial(settle_kernel, len(parts)),
        out_shape=[jax.ShapeDtypeStruct((rows // 2, width), t) for t in (F32, dtype)],
        grid_spec=pltpu.PrefetchScalarGridSpec(
            num_scalar_prefetch=1,
            grid=(1,),
            in_specs=[pl.BlockSpec((rows, width), lambda s, x: (0, 0))]
            + [VMEM] * (len(parts) - 1)
            + [ANY] * len(after),
            out_specs=[half] * 2,
            scratch_shapes=[pltpu.VMEM((rows, width), F32)],
        ),
        compiler_params=pltpu.CompilerParams(vmem_limit_bytes=8 * 2**20),
        cost_estimate=pl.CostEstimate(flops=0, bytes_accessed=0, transcendentals=0),
        name="settle",
    )(xl, *parts, *after)


def grow_kernel(right, left, from_left, from_right, *refs):
    out_right, out_left, held, sems, out_sem = refs[-5:]
    jobs = [(right, 0, from_left, 0, out_right), (left, 2, from_right, 0, out_left)]
    jobs += [(right, 1, from_left, 1, out_right), (left, 3, from_right, 1, out_left)]
    for n, (x, at, _, _, _) in enumerate(jobs):
        pltpu.make_async_copy(x.at[at], held.at[n], sems.at[n]).start()
    for n, (_, at, received, k, out) in enumerate(jobs):
        wait_all(held.at[n], sems.at[n])
        held[n] = add(held[n], received[k]).astype(BF)
        pltpu.make_async_copy(held.at[n], out.at[at], out_sem).start()
    wait_all(held, out_sem)


def grow(right, left, from_left, from_right, *after):
    hbm = pl.BlockSpec(memory_space=pltpu.HBM)
    return pl.pallas_call(
        grow_kernel,
        out_shape=[pltpu.HBM(x.shape, x.dtype) for x in (right, left)],
        grid=(1,),
        in_specs=[hbm, hbm, VMEM, VMEM] + [ANY] * len(after),
        out_specs=[hbm, hbm],
        scratch_shapes=[
            pltpu.VMEM(right.shape, right.dtype),
            pltpu.SemaphoreType.DMA((4,)),
            pltpu.SemaphoreType.DMA,
        ],
        input_output_aliases={0: 0, 1: 1},
        compiler_params=pltpu.CompilerParams(vmem_limit_bytes=8 * 2**20),
        cost_estimate=pl.CostEstimate(flops=0, bytes_accessed=0, transcendentals=0),
        name="grow",
    )(in_hbm(right), in_hbm(left), from_left, from_right, *after)


def gate_kernel(x, after, out):
    del x, after, out


def gate(x, after):
    return pl.pallas_call(
        gate_kernel,
        out_shape=pltpu.HBM(x.shape, x.dtype),
        in_specs=[pl.BlockSpec(memory_space=pltpu.HBM), ANY],
        out_specs=pl.BlockSpec(memory_space=pltpu.HBM),
        input_output_aliases={0: 0},
        compiler_params=pltpu.CompilerParams(vmem_limit_bytes=2**20),
        cost_estimate=pl.CostEstimate(flops=0, bytes_accessed=0, transcendentals=0),
        name="gate",
    )(in_hbm(x), after)


def fetch_tiles(step, source, held, sems):
    @pl.when(step == 0)
    def _():
        for k in range(4):
            rows = source.at[pl.ds(k * TILE, TILE)]
            pltpu.make_async_copy(rows, held.at[k], sems.at[k]).start()

    wait_all(held.at[step], sems.at[step])


def left_kernel(own, place, a, b, left, *rest):
    before = None if own else rest[0]
    out, total, held, sems = rest[-4:] if own else (rest[1], rest[2], *rest[4:])
    step = pl.program_id(0)
    rows = a.shape[0]
    at = pl.ds(pl.multiple_of(step * TILE, TILE), TILE)
    part = place[1] ^ place[0] if own else 1 - (place[1] ^ place[0])

    @pl.when(step == 0)
    def _():
        for k in range(2):
            tile = left.at[pl.ds(pl.multiple_of((part * 2 + k) * TILE, TILE), TILE)]
            pltpu.make_async_copy(tile, held.at[k], sems.at[k]).start()

    stacked = jnp.concatenate(split_pair(a[:, at] + b[:, at]), axis=0)
    wait_all(held.at[step], sems.at[step])
    value = jnp.dot(stacked, held[step], preferred_element_type=F32)
    pl.when(step == 0)(lambda: total.__setitem__(..., value if own else before[...] + value))
    pl.when(step == 1)(lambda: total.__setitem__(..., total[...] + value))
    if own:
        pl.when(step == 1)(lambda: out.__setitem__(..., total[...]))
        return
    packed = rest[3]

    @pl.when(step == 1)
    def _():
        result = total[:rows] + total[rows:]
        for z in range(2):
            for y in range(4):
                for xl in range(2):
                    for c in range(2):
                        n = ((z * 4 + y) * 2 + xl) * 2 + c
                        block = result[:, n * rows : (n + 1) * rows]
                        packed[n, 0:16, 0:rows] = block[0:16]
                        packed[n, 0:16, rows : 2 * rows] = block[16:32]
                        packed[n, 0:8, 2 * rows : 3 * rows] = block[32:40]
                        ready = packed[n].astype(BF)
                        for there in (0, 2):
                            d = c * 32 + (there + z) * 8 + y * 2 + xl
                            out[d] = ready
                            out[64 + d] = ready


def left_product(place, a, b, left, before=None):
    rows, half = a.shape
    own = before is None
    total = pltpu.VMEM((2 * rows, half), F32)
    return pl.pallas_call(
        functools.partial(left_kernel, own),
        out_shape=total if own else pltpu.HBM((128, 16, 128), BF),
        grid_spec=pltpu.PrefetchScalarGridSpec(
            num_scalar_prefetch=1,
            grid=(2,),
            in_specs=[VMEM, VMEM, pl.BlockSpec(memory_space=pltpu.HBM)] + [VMEM] * (not own),
            out_specs=VMEM if own else pl.BlockSpec((128, 16, 128), lambda k, p: (0, 0, 0)),
            scratch_shapes=[total]
            + [pltpu.VMEM((32, 16, 128), F32)] * (not own)
            + [pltpu.VMEM((2, TILE, half), BF), pltpu.SemaphoreType.DMA((2,))],
        ),
        compiler_params=pltpu.CompilerParams(vmem_limit_bytes=16 * 2**20),
        cost_estimate=pl.CostEstimate(
            flops=0 if own else 256 * rows * half * half, bytes_accessed=0, transcendentals=0
        ),
        name="left_own" if own else "left_product",
    )(place, a, b, left, *([] if own else [before]))


def right_kernel(place, blocks, right, late, out, rows_in, held, sems):
    del late
    step = pl.program_id(0)
    fetch_tiles(step, right, held, sems)
    rows = out.shape[0]
    for near in range(2):
        for y in range(4):
            for xl in range(2):
                core = (step >> 1) ^ ((near + y) & 1)
                block = blocks[core * 32 + ((step & 1) * 2 + near) * 8 + y * 2 + xl].astype(F32)
                at = ((near * 4 + y) * 2 + xl) * rows
                rows_in[at : at + 16, :] = block[:, 0:rows]
                rows_in[at + 16 : at + 32, :] = block[:, rows : 2 * rows]
                rows_in[at + 32 : at + 40, :] = block[0:8, 2 * rows : 3 * rows]
    value = contract(rows_in[...].astype(BF), held[step])
    pl.when(step == 0)(lambda: out.__setitem__(..., value))
    pl.when(step > 0)(lambda: out.__setitem__(..., out[...] + value))


def right_product(place, blocks, right, late):
    width, half = right.shape
    rows = width // 64
    return pl.pallas_call(
        right_kernel,
        out_shape=jax.ShapeDtypeStruct((rows, half), F32),
        grid_spec=pltpu.PrefetchScalarGridSpec(
            num_scalar_prefetch=1,
            grid=(4,),
            in_specs=[
                pl.BlockSpec((64, 16, 128), lambda k, p: (p[2] >> 1, 0, 0)),
                pl.BlockSpec(memory_space=pltpu.HBM),
                ANY,
            ],
            out_specs=pl.BlockSpec((rows, half), lambda k, p: (0, 0)),
            scratch_shapes=[
                pltpu.VMEM((TILE, rows), F32),
                pltpu.VMEM((4, TILE, half), BF),
                pltpu.SemaphoreType.DMA((4,)),
            ],
        ),
        compiler_params=pltpu.CompilerParams(vmem_limit_bytes=20 * 2**20),
        cost_estimate=pl.CostEstimate(
            flops=640 * rows * half * half, bytes_accessed=4 * half * half, transcendentals=0
        ),
        name="right_product",
    )(place, blocks, right, late)


def per_device(hidden, out_grad, left_inverse, right_inverse):
    z, y, xl, c, o = (lax.axis_index(n) for n in ("z", "y", "xl", "c", "o"))
    tokens, width = hidden.shape
    half = width // 2
    token_total = tokens * 64
    first = o == 0
    h = c ^ ((z + y) & 1)
    hidden, out_grad = in_hbm(hidden), in_hbm(out_grad)
    left_inverse, right_inverse = in_hbm(left_inverse), in_hbm(right_inverse)
    place = jnp.stack([o, h, z, y]).astype(jnp.int32)
    second_me = jnp.where(h == 0, y, z).astype(jnp.int32)[None]

    grads_next, acts_next = in_hbm(shift(out_grad, "c", 1)), in_hbm(shift(hidden, "c", 1))
    partial = cross_own(place, out_grad, hidden)

    own, m1, m2, m3 = cross_term(place, grads_next, acts_next, partial)
    m_parts = [own, turn(m1, 1, 0), turn(m2, 2, 0), turn(m3, 3, 0)]

    f_own, right, far_a, far_b, left = factor_term(
        place, hidden, out_grad, acts_next, grads_next, in_hbm(m1)
    )
    from_left, from_right = turn(far_a, 1, 0), turn(far_b, -1, 0)

    my_xl = xl.astype(jnp.int32)[None]

    def second_sends(pieces):
        return [turn(piece, s, 1) for s, piece in enumerate(pieces, 1)]

    m, *m_pieces = fold(second_me, m_parts, in_hbm(f_own))
    m_received = second_sends(m_pieces)
    right, left = grow(right, left, from_left, from_right, *m_received)
    f_parts = [f_own, turn(right, 1, 0), turn(left, -1, 0)]

    mine, theirs = settle(my_xl, [in_hbm(m), *m_received], F32)
    across = lax.ppermute(theirs, ("xl", "o"), [(i, 3 - i) for i in range(4)])
    products = left_product(place, mine, shift(theirs, "xl", 1), left_inverse)
    products = left_product(place, shift(mine, "o", 1), across, left_inverse, products)
    f, *f_pieces = fold(second_me, f_parts, in_hbm(products))
    products = gate(products, f_pieces[0])
    blocks = lax.all_to_all(products, ("o", "c", "z", "y", "xl"), 0, 0, tiled=True)
    f_mine, f_theirs = settle(my_xl, [in_hbm(f), *second_sends(f_pieces)], BF)
    update = right_product(place, blocks, right_inverse, f_theirs)

    f = add(f_mine, shift(f_theirs, "xl", 1))
    f = f * jnp.where(first, 1.0 / token_total, 1.0).astype(F32)
    f = f.reshape(2, width // 64, half)
    mine = pick(f, 0, c)
    theirs = shift(pick(f, 0, 1 - c), "c", 1)
    factors = jnp.concatenate(
        [jnp.where(h == 0, mine, theirs), jnp.where(h == 0, theirs, mine)], axis=1
    )[None]
    return factors, update


def solution(mesh):
    fine = Mesh(mesh.devices.reshape(4, 4, 2, 2, 2), ("z", "y", "xl", "c", "o"))
    dp = ("z", "y", "xl", "c")
    in_specs = (P(dp, None), P(dp, None), P(None, "o"), P(None, "o"))
    out_specs = (P("o", dp, None), P(dp, "o"))
    return jax.shard_map(
        per_device, mesh=fine, in_specs=in_specs, out_specs=out_specs, check_vma=False
    )
```

```python
import functools

import jax
import jax.numpy as jnp
from jax import lax
from jax.experimental import pallas as pl
from jax.experimental.pallas import tpu as pltpu
from jax.sharding import Mesh, PartitionSpec as P

BF = jnp.bfloat16
F32 = jnp.float32
TILE = 640
ANY = pl.BlockSpec(memory_space=pl.ANY)
VMEM = pl.BlockSpec(memory_space=pltpu.VMEM)


def contract(first_rows, second_rows):
    return lax.dot_general(
        first_rows, second_rows, (((0,), (0,)), ((), ())), preferred_element_type=F32
    )


def shift(x, axis, step):
    size = lax.axis_size(axis)
    return lax.ppermute(x, axis, [(i, (i + step) % size) for i in range(size)])


def turn(x, step, stage):
    pairs = []
    for z in range(4):
        for y in range(4):
            for h in range(2):
                along_z = (h == 0) == (stage == 0)
                z2, y2 = ((z + step) % 4, y) if along_z else (z, (y + step) % 4)
                core, core2 = h ^ ((z + y) & 1), h ^ ((z2 + y2) & 1)
                pairs.append(((z * 4 + y) * 2 + core, (z2 * 4 + y2) * 2 + core2))
    return lax.ppermute(x, ("z", "y", "c"), pairs)


def in_hbm(x):
    return pltpu.with_memory_space_constraint(x, pltpu.HBM)


def pick(x, dim, index):
    return lax.dynamic_index_in_dim(x, index, dim, keepdims=False)


def split_pair(x):
    high = x.astype(BF)
    return high, (x - high.astype(F32)).astype(BF)


def place_tile(place, buffer, sem, outs, m, zs):
    rows = TILE // (zs * 4)

    def start(at, out, slot):
        block = buffer.at[m, pl.ds(at, rows)]
        pltpu.make_async_copy(block, out.at[slot], sem).start()

    for a in range(zs):
        z = m * zs + a

        @pl.when(place[1] == 0)
        def _():
            for r, out in enumerate(outs):

                @pl.when(((z - place[2] + 4) & 3) == r)
                def _():
                    for k in range(4):
                        if isinstance(out, tuple):
                            start((a * 4 + k) * rows, out[k // 2], k % 2)
                        else:
                            start((a * 4 + k) * rows, out, k)

        @pl.when(place[1] == 1)
        def _():
            for r, out in enumerate(outs):
                at = pl.multiple_of((a * 4 + ((place[3] + r) & 3)) * rows, 16)
                if isinstance(out, tuple):
                    pl.when(z < 2)(functools.partial(start, at, out[0], z & 1))
                    pl.when(z >= 2)(functools.partial(start, at, out[1], z & 1))
                else:
                    start(at, out, z)


def wait_all(buffer, sem):
    pltpu.make_async_copy(buffer, buffer, sem).wait()


def own_kernel(place, a, b, out, lhs, rhs, lhs_sems, rhs_sem):
    m = pl.program_id(0)
    half = rhs.shape[1]

    @pl.when(m == 0)
    def _():
        at = pl.ds(pl.multiple_of((place[1] ^ place[0]) * half, half), half)
        pltpu.make_async_copy(b.at[:, at], rhs, rhs_sem).start()
        for k in range(2):
            at = pl.ds(pl.multiple_of(place[1] * half + k * TILE, TILE), TILE)
            pltpu.make_async_copy(a.at[:, at], lhs.at[k], lhs_sems.at[k]).start()
        wait_all(rhs, rhs_sem)

    wait_all(lhs.at[m], lhs_sems.at[m])
    out[...] = contract(lhs[m], rhs[...])


def cross_kernel(place, a, b, partial, own, ahead1, ahead2, ahead3, held, buffer, held_sems, sem):
    m = pl.program_id(0)

    @pl.when(m == 0)
    def _():
        for k in range(2):
            rows = partial.at[pl.ds(k * TILE, TILE)]
            pltpu.make_async_copy(rows, held.at[k], held_sems.at[k]).start()

    tile = contract(a[...], b[...])
    wait_all(held.at[m], held_sems.at[m])
    buffer[m] = (held[m] + tile).astype(BF)
    place_tile(place, buffer, sem, [own, ahead1, ahead2, ahead3], m, 2)
    pl.when(m == 1)(lambda: wait_all(buffer, sem))


def cross_own(place, grads, acts):
    tokens, half = grads.shape[0], grads.shape[1] // 2
    return pl.pallas_call(
        own_kernel,
        out_shape=jax.ShapeDtypeStruct((half, half), F32),
        grid_spec=pltpu.PrefetchScalarGridSpec(
            num_scalar_prefetch=1,
            grid=(2,),
            in_specs=[pl.BlockSpec(memory_space=pltpu.HBM)] * 2,
            out_specs=pl.BlockSpec((TILE, half), lambda m, p: (m, 0)),
            scratch_shapes=[
                pltpu.VMEM((2, tokens, TILE), BF),
                pltpu.VMEM((tokens, half), BF),
                pltpu.SemaphoreType.DMA((2,)),
                pltpu.SemaphoreType.DMA,
            ],
        ),
        compiler_params=pltpu.CompilerParams(vmem_limit_bytes=28 * 2**20),
        cost_estimate=pl.CostEstimate(
            flops=2 * tokens * half * half, bytes_accessed=8 * tokens * half, transcendentals=0
        ),
        name="cross_own",
    )(place, grads, acts)


def cross_term(place, grads_next, acts_next, partial):
    tokens, half = grads_next.shape[0], grads_next.shape[1] // 2
    out = pltpu.HBM((4, half // 16, half), BF)
    return pl.pallas_call(
        cross_kernel,
        out_shape=[out] * 4,
        grid_spec=pltpu.PrefetchScalarGridSpec(
            num_scalar_prefetch=1,
            grid=(2,),
            in_specs=[
                pl.BlockSpec((tokens, TILE), lambda m, p: (0, p[1] * 2 + m)),
                pl.BlockSpec((tokens, half), lambda m, p: (0, p[1] ^ p[0])),
                ANY,
            ],
            out_specs=[pl.BlockSpec(memory_space=pltpu.HBM)] * 4,
            scratch_shapes=[
                pltpu.VMEM((2, TILE, half), F32),
                pltpu.VMEM((2, TILE, half), BF),
                pltpu.SemaphoreType.DMA((2,)),
                pltpu.SemaphoreType.DMA,
            ],
        ),
        compiler_params=pltpu.CompilerParams(vmem_limit_bytes=28 * 2**20),
        cost_estimate=pl.CostEstimate(
            flops=2 * tokens * half * half, bytes_accessed=10 * tokens * half, transcendentals=0
        ),
        name="cross_term",
    )(place, grads_next, acts_next, partial)


def factor_kernel(place, h_own, g_own, h_next, g_next, after, *rest):
    del after
    own, right, far_a, far_b, left, lhs, rhs, buffer, lhs_sems, rhs_sem, sem = rest
    m = pl.program_id(0)
    half = rhs.shape[2]

    def fetch(step, with_rhs):
        slot = step & 1
        at = pl.ds(pl.multiple_of(step * TILE, TILE), TILE)
        columns = pl.ds(pl.multiple_of(place[1] * half, half), half)
        for owner, refs in enumerate(((h_own, h_next), (g_own, g_next))):

            @pl.when(place[0] == owner)
            def _():
                for k, ref in enumerate(refs):
                    pltpu.make_async_copy(ref.at[:, at], lhs.at[slot, k], lhs_sems.at[slot]).start()
                    if with_rhs:
                        pltpu.make_async_copy(ref.at[:, columns], rhs.at[k], rhs_sem).start()

    pl.when(m == 0)(lambda: fetch(0, True))
    pl.when(m < 3)(lambda: fetch(m + 1, False))
    slot = m & 1
    wait_all(lhs.at[slot], lhs_sems.at[slot])
    pl.when(m == 0)(lambda: wait_all(rhs, rhs_sem))

    buffer[m] = (contract(lhs[slot, 0], rhs[0]) + contract(lhs[slot, 1], rhs[1])).astype(BF)
    place_tile(place, buffer, sem, [own, right, (far_a, far_b), left], m, 1)
    pl.when(m == 3)(lambda: wait_all(buffer, sem))


def factor_term(place, acts, grads, acts_next, grads_next, after):
    tokens, width = acts.shape
    half = width // 2
    hbm = pl.BlockSpec(memory_space=pltpu.HBM)
    out = pltpu.HBM((4, width // 16, half), BF)
    side = pltpu.HBM((2, width // 16, half), BF)
    return pl.pallas_call(
        factor_kernel,
        out_shape=[out, out, side, side, out],
        grid_spec=pltpu.PrefetchScalarGridSpec(
            num_scalar_prefetch=1,
            grid=(4,),
            in_specs=[hbm] * 2 + [ANY] * 3,
            out_specs=[hbm] * 5,
            scratch_shapes=[
                pltpu.VMEM((2, 2, tokens, TILE), BF),
                pltpu.VMEM((2, tokens, half), BF),
                pltpu.VMEM((4, TILE, half), BF),
                pltpu.SemaphoreType.DMA((2,)),
                pltpu.SemaphoreType.DMA,
                pltpu.SemaphoreType.DMA,
            ],
        ),
        compiler_params=pltpu.CompilerParams(vmem_limit_bytes=30 * 2**20),
        cost_estimate=pl.CostEstimate(
            flops=4 * tokens * width * half, bytes_accessed=16 * tokens * half, transcendentals=0
        ),
        name="factor_term",
    )(place, acts, grads, acts_next, grads_next, after)


def add(first, *rest):
    total = first.astype(F32)
    for x in rest:
        total = total + x.astype(F32)
    return total


def fold_kernel(count, me, *refs):
    own, *others = refs[-6:-2]
    held, sems = refs[-2:]
    steps = [(1, others[0]), (2, others[1]), (3, others[2]), (0, own)]
    for r, _ in steps:
        pltpu.make_async_copy(refs[0].at[(me[0] + r) & 3], held.at[r], sems.at[r]).start()
    for r, out in steps:
        wait_all(held.at[r], sems.at[r])
        at = (me[0] + r) & 3
        out[...] = add(held[r], *[part[at] for part in refs[1:count]]).astype(out.dtype)


def fold(me, parts, *after):
    _, rows, width = parts[0].shape
    whole = pl.BlockSpec((rows, width), lambda s, m: (0, 0))
    return pl.pallas_call(
        functools.partial(fold_kernel, len(parts)),
        out_shape=[pltpu.HBM((rows, width), F32)]
        + [pltpu.VMEM((rows, width), BF)] * 3,
        grid_spec=pltpu.PrefetchScalarGridSpec(
            num_scalar_prefetch=1,
            grid=(1,),
            in_specs=[pl.BlockSpec(memory_space=pltpu.HBM)]
            + [VMEM] * (len(parts) - 1)
            + [ANY] * len(after),
            out_specs=[whole] + [VMEM] * 3,
            scratch_shapes=[pltpu.VMEM((4, rows, width), BF), pltpu.SemaphoreType.DMA((4,))],
        ),
        compiler_params=pltpu.CompilerParams(vmem_limit_bytes=12 * 2**20),
        cost_estimate=pl.CostEstimate(flops=0, bytes_accessed=0, transcendentals=0),
        name="fold",
    )(me, in_hbm(parts[0]), *parts[1:], *after)


def settle_kernel(count, xl, *refs):
    mine, theirs, total = refs[-3:]
    rows = mine.shape[0]
    value = None
    for ref in refs[:count]:
        for part in [ref[...]] if len(ref.shape) == 2 else [ref[k] for k in range(ref.shape[0])]:
            value = part.astype(F32) if value is None else value + part.astype(F32)
    total[...] = value
    for out, index in ((mine, xl[0]), (theirs, 1 - xl[0])):
        out[...] = total[pl.ds(pl.multiple_of(index * rows, 8), rows)].astype(out.dtype)


def settle(xl, parts, dtype, *after):
    rows, width = parts[0].shape[-2:]
    half = pl.BlockSpec((rows // 2, width), lambda s, x: (0, 0))
    return pl.pallas_call(
        functools.partial(settle_kernel, len(parts)),
        out_shape=[jax.ShapeDtypeStruct((rows // 2, width), t) for t in (F32, dtype)],
        grid_spec=pltpu.PrefetchScalarGridSpec(
            num_scalar_prefetch=1,
            grid=(1,),
            in_specs=[pl.BlockSpec((rows, width), lambda s, x: (0, 0))]
            + [VMEM] * (len(parts) - 1)
            + [ANY] * len(after),
            out_specs=[half] * 2,
            scratch_shapes=[pltpu.VMEM((rows, width), F32)],
        ),
        compiler_params=pltpu.CompilerParams(vmem_limit_bytes=8 * 2**20),
        cost_estimate=pl.CostEstimate(flops=0, bytes_accessed=0, transcendentals=0),
        name="settle",
    )(xl, *parts, *after)


def grow_kernel(right, left, from_left, from_right, *refs):
    out_right, out_left, held, sems, out_sem = refs[-5:]
    jobs = [(right, 0, from_left, 0, out_right), (left, 2, from_right, 0, out_left)]
    jobs += [(right, 1, from_left, 1, out_right), (left, 3, from_right, 1, out_left)]
    for n, (x, at, _, _, _) in enumerate(jobs):
        pltpu.make_async_copy(x.at[at], held.at[n], sems.at[n]).start()
    for n, (_, at, received, k, out) in enumerate(jobs):
        wait_all(held.at[n], sems.at[n])
        held[n] = add(held[n], received[k]).astype(BF)
        pltpu.make_async_copy(held.at[n], out.at[at], out_sem).start()
    wait_all(held, out_sem)


def grow(right, left, from_left, from_right, *after):
    hbm = pl.BlockSpec(memory_space=pltpu.HBM)
    return pl.pallas_call(
        grow_kernel,
        out_shape=[pltpu.HBM(x.shape, x.dtype) for x in (right, left)],
        grid=(1,),
        in_specs=[hbm, hbm, VMEM, VMEM] + [ANY] * len(after),
        out_specs=[hbm, hbm],
        scratch_shapes=[
            pltpu.VMEM(right.shape, right.dtype),
            pltpu.SemaphoreType.DMA((4,)),
            pltpu.SemaphoreType.DMA,
        ],
        input_output_aliases={0: 0, 1: 1},
        compiler_params=pltpu.CompilerParams(vmem_limit_bytes=8 * 2**20),
        cost_estimate=pl.CostEstimate(flops=0, bytes_accessed=0, transcendentals=0),
        name="grow",
    )(in_hbm(right), in_hbm(left), from_left, from_right, *after)


def fetch_tiles(step, source, held, sems):
    @pl.when(step == 0)
    def _():
        for k in range(4):
            rows = source.at[pl.ds(k * TILE, TILE)]
            pltpu.make_async_copy(rows, held.at[k], sems.at[k]).start()

    wait_all(held.at[step], sems.at[step])


def left_kernel(own, place, a, b, left, *rest):
    before = None if own else rest[0]
    out, total, held, sems = rest[-4:] if own else (rest[1], rest[2], *rest[4:])
    step = pl.program_id(0)
    rows = a.shape[0]
    at = pl.ds(pl.multiple_of(step * TILE, TILE), TILE)
    part = place[1] ^ place[0] if own else 1 - (place[1] ^ place[0])

    @pl.when(step == 0)
    def _():
        for k in range(2):
            tile = left.at[pl.ds(pl.multiple_of((part * 2 + k) * TILE, TILE), TILE)]
            pltpu.make_async_copy(tile, held.at[k], sems.at[k]).start()

    stacked = jnp.concatenate(split_pair(a[:, at] + b[:, at]), axis=0)
    wait_all(held.at[step], sems.at[step])
    value = jnp.dot(stacked, held[step], preferred_element_type=F32)
    pl.when(step == 0)(lambda: total.__setitem__(..., value if own else before[...] + value))
    pl.when(step == 1)(lambda: total.__setitem__(..., total[...] + value))
    if own:
        pl.when(step == 1)(lambda: out.__setitem__(..., total[...]))
        return
    packed = rest[3]

    @pl.when(step == 1)
    def _():
        result = total[:rows] + total[rows:]
        for z in range(2):
            for y in range(4):
                for xl in range(2):
                    for c in range(2):
                        n = ((z * 4 + y) * 2 + xl) * 2 + c
                        block = result[:, n * rows : (n + 1) * rows]
                        packed[n, 0:16, 0:rows] = block[0:16]
                        packed[n, 0:16, rows : 2 * rows] = block[16:32]
                        packed[n, 0:8, 2 * rows : 3 * rows] = block[32:40]
                        ready = packed[n].astype(BF)
                        for there in (0, 2):
                            d = c * 32 + (there + z) * 8 + y * 2 + xl
                            out[d] = ready
                            out[64 + d] = ready


def left_product(place, a, b, left, before=None):
    rows, half = a.shape
    own = before is None
    total = pltpu.VMEM((2 * rows, half), F32)
    return pl.pallas_call(
        functools.partial(left_kernel, own),
        out_shape=total if own else pltpu.HBM((128, 16, 128), BF),
        grid_spec=pltpu.PrefetchScalarGridSpec(
            num_scalar_prefetch=1,
            grid=(2,),
            in_specs=[VMEM, VMEM, pl.BlockSpec(memory_space=pltpu.HBM)] + [VMEM] * (not own),
            out_specs=VMEM if own else pl.BlockSpec((128, 16, 128), lambda k, p: (0, 0, 0)),
            scratch_shapes=[total]
            + [pltpu.VMEM((32, 16, 128), F32)] * (not own)
            + [pltpu.VMEM((2, TILE, half), BF), pltpu.SemaphoreType.DMA((2,))],
        ),
        compiler_params=pltpu.CompilerParams(vmem_limit_bytes=16 * 2**20),
        cost_estimate=pl.CostEstimate(
            flops=0 if own else 256 * rows * half * half, bytes_accessed=0, transcendentals=0
        ),
        name="left_own" if own else "left_product",
    )(place, a, b, left, *([] if own else [before]))


def right_kernel(place, blocks, right, late, out, rows_in, held, sems):
    del late
    step = pl.program_id(0)
    fetch_tiles(step, right, held, sems)
    rows = out.shape[0]
    for near in range(2):
        for y in range(4):
            for xl in range(2):
                core = (step >> 1) ^ ((near + y) & 1)
                block = blocks[core * 32 + ((step & 1) * 2 + near) * 8 + y * 2 + xl].astype(F32)
                at = ((near * 4 + y) * 2 + xl) * rows
                rows_in[at : at + 16, :] = block[:, 0:rows]
                rows_in[at + 16 : at + 32, :] = block[:, rows : 2 * rows]
                rows_in[at + 32 : at + 40, :] = block[0:8, 2 * rows : 3 * rows]
    value = contract(rows_in[...].astype(BF), held[step])
    pl.when(step == 0)(lambda: out.__setitem__(..., value))
    pl.when(step > 0)(lambda: out.__setitem__(..., out[...] + value))


def right_product(place, blocks, right, late):
    width, half = right.shape
    rows = width // 64
    return pl.pallas_call(
        right_kernel,
        out_shape=jax.ShapeDtypeStruct((rows, half), F32),
        grid_spec=pltpu.PrefetchScalarGridSpec(
            num_scalar_prefetch=1,
            grid=(4,),
            in_specs=[
                pl.BlockSpec((64, 16, 128), lambda k, p: (p[2] >> 1, 0, 0)),
                pl.BlockSpec(memory_space=pltpu.HBM),
                ANY,
            ],
            out_specs=pl.BlockSpec((rows, half), lambda k, p: (0, 0)),
            scratch_shapes=[
                pltpu.VMEM((TILE, rows), F32),
                pltpu.VMEM((4, TILE, half), BF),
                pltpu.SemaphoreType.DMA((4,)),
            ],
        ),
        compiler_params=pltpu.CompilerParams(vmem_limit_bytes=20 * 2**20),
        cost_estimate=pl.CostEstimate(
            flops=640 * rows * half * half, bytes_accessed=4 * half * half, transcendentals=0
        ),
        name="right_product",
    )(place, blocks, right, late)


def per_device(hidden, out_grad, left_inverse, right_inverse):
    z, y, xl, c, o = (lax.axis_index(n) for n in ("z", "y", "xl", "c", "o"))
    tokens, width = hidden.shape
    half = width // 2
    token_total = tokens * 64
    first = o == 0
    h = c ^ ((z + y) & 1)
    hidden, out_grad = in_hbm(hidden), in_hbm(out_grad)
    left_inverse, right_inverse = in_hbm(left_inverse), in_hbm(right_inverse)
    place = jnp.stack([o, h, z, y]).astype(jnp.int32)
    second_me = jnp.where(h == 0, y, z).astype(jnp.int32)[None]

    grads_next, acts_next = in_hbm(shift(out_grad, "c", 1)), in_hbm(shift(hidden, "c", 1))
    partial = cross_own(place, out_grad, hidden)

    own, m1, m2, m3 = cross_term(place, grads_next, acts_next, partial)
    m_parts = [own, turn(m1, 1, 0), turn(m2, 2, 0), turn(m3, 3, 0)]

    f_own, right, far_a, far_b, left = factor_term(
        place, hidden, out_grad, acts_next, grads_next, in_hbm(m1)
    )
    from_left, from_right = turn(far_a, 1, 0), turn(far_b, -1, 0)

    my_xl = xl.astype(jnp.int32)[None]

    def second_sends(pieces):
        return [turn(piece, s, 1) for s, piece in enumerate(pieces, 1)]

    m, *m_pieces = fold(second_me, m_parts, in_hbm(f_own))
    m_received = second_sends(m_pieces)
    right, left = grow(right, left, from_left, from_right, *m_received)
    f_parts = [f_own, turn(right, 1, 0), turn(left, -1, 0)]

    mine, theirs = settle(my_xl, [in_hbm(m), *m_received], F32)
    across = lax.ppermute(theirs, ("xl", "o"), [(i, 3 - i) for i in range(4)])
    products = left_product(place, mine, shift(theirs, "xl", 1), left_inverse)
    products = left_product(place, shift(mine, "o", 1), across, left_inverse, products)
    blocks = lax.all_to_all(products, ("o", "c", "z", "y", "xl"), 0, 0, tiled=True)
    f, *f_pieces = fold(second_me, f_parts, in_hbm(products))
    update = right_product(place, blocks, right_inverse, f_pieces[0])
    f_mine, f_theirs = settle(my_xl, [in_hbm(f), *second_sends(f_pieces)], BF, in_hbm(update))

    f = add(f_mine, shift(f_theirs, "xl", 1))
    f = f * jnp.where(first, 1.0 / token_total, 1.0).astype(F32)
    f = f.reshape(2, width // 64, half)
    mine = pick(f, 0, c)
    theirs = shift(pick(f, 0, 1 - c), "c", 1)
    factors = jnp.concatenate(
        [jnp.where(h == 0, mine, theirs), jnp.where(h == 0, theirs, mine)], axis=1
    )[None]
    return factors, update


def solution(mesh):
    fine = Mesh(mesh.devices.reshape(4, 4, 2, 2, 2), ("z", "y", "xl", "c", "o"))
    dp = ("z", "y", "xl", "c")
    in_specs = (P(dp, None), P(dp, None), P(None, "o"), P(None, "o"))
    out_specs = (P("o", dp, None), P(dp, "o"))
    return jax.shard_map(
        per_device, mesh=fine, in_specs=in_specs, out_specs=out_specs, check_vma=False
    )
```

```python
import functools

import jax
import jax.numpy as jnp
from jax import lax
from jax.experimental import pallas as pl
from jax.experimental.pallas import tpu as pltpu
from jax.sharding import Mesh, PartitionSpec as P

BF = jnp.bfloat16
F32 = jnp.float32
TILE = 640
ANY = pl.BlockSpec(memory_space=pl.ANY)
VMEM = pl.BlockSpec(memory_space=pltpu.VMEM)


def contract(first_rows, second_rows):
    return lax.dot_general(
        first_rows, second_rows, (((0,), (0,)), ((), ())), preferred_element_type=F32
    )


def shift(x, axis, step):
    size = lax.axis_size(axis)
    return lax.ppermute(x, axis, [(i, (i + step) % size) for i in range(size)])


def turn(x, step, stage):
    pairs = []
    for z in range(4):
        for y in range(4):
            for h in range(2):
                along_z = (h == 0) == (stage == 0)
                z2, y2 = ((z + step) % 4, y) if along_z else (z, (y + step) % 4)
                core, core2 = h ^ ((z + y) & 1), h ^ ((z2 + y2) & 1)
                pairs.append(((z * 4 + y) * 2 + core, (z2 * 4 + y2) * 2 + core2))
    return lax.ppermute(x, ("z", "y", "c"), pairs)


def in_hbm(x):
    return pltpu.with_memory_space_constraint(x, pltpu.HBM)


def pick(x, dim, index):
    return lax.dynamic_index_in_dim(x, index, dim, keepdims=False)


def split_pair(x):
    high = x.astype(BF)
    return high, (x - high.astype(F32)).astype(BF)


def place_tile(place, buffer, sem, outs, m, zs):
    rows = TILE // (zs * 4)

    def start(at, out, slot):
        block = buffer.at[m, pl.ds(at, rows)]
        pltpu.make_async_copy(block, out.at[slot], sem).start()

    for a in range(zs):
        z = m * zs + a

        @pl.when(place[1] == 0)
        def _():
            for r, out in enumerate(outs):

                @pl.when(((z - place[2] + 4) & 3) == r)
                def _():
                    for k in range(4):
                        if isinstance(out, tuple):
                            start((a * 4 + k) * rows, out[k // 2], k % 2)
                        else:
                            start((a * 4 + k) * rows, out, k)

        @pl.when(place[1] == 1)
        def _():
            for r, out in enumerate(outs):
                at = pl.multiple_of((a * 4 + ((place[3] + r) & 3)) * rows, 16)
                if isinstance(out, tuple):
                    pl.when(z < 2)(functools.partial(start, at, out[0], z & 1))
                    pl.when(z >= 2)(functools.partial(start, at, out[1], z & 1))
                else:
                    start(at, out, z)


def wait_all(buffer, sem):
    pltpu.make_async_copy(buffer, buffer, sem).wait()


def own_kernel(place, a, b, out, lhs, rhs, lhs_sems, rhs_sem):
    m = pl.program_id(0)
    half = rhs.shape[1]

    @pl.when(m == 0)
    def _():
        at = pl.ds(pl.multiple_of((place[1] ^ place[0]) * half, half), half)
        pltpu.make_async_copy(b.at[:, at], rhs, rhs_sem).start()
        for k in range(2):
            at = pl.ds(pl.multiple_of(place[1] * half + k * TILE, TILE), TILE)
            pltpu.make_async_copy(a.at[:, at], lhs.at[k], lhs_sems.at[k]).start()
        wait_all(rhs, rhs_sem)

    wait_all(lhs.at[m], lhs_sems.at[m])
    out[...] = contract(lhs[m], rhs[...])


def cross_kernel(place, a, b, partial, after, *rest):
    del after
    own, ahead1, ahead2, ahead3, held, buffer, held_sems, sem = rest
    m = pl.program_id(0)

    @pl.when(m == 0)
    def _():
        for k in range(2):
            rows = partial.at[pl.ds(k * TILE, TILE)]
            pltpu.make_async_copy(rows, held.at[k], held_sems.at[k]).start()

    tile = contract(a[...], b[...])
    wait_all(held.at[m], held_sems.at[m])
    buffer[m] = (held[m] + tile).astype(BF)
    place_tile(place, buffer, sem, [own, ahead1, ahead2, ahead3], m, 2)
    pl.when(m == 1)(lambda: wait_all(buffer, sem))


def cross_own(place, grads, acts):
    tokens, half = grads.shape[0], grads.shape[1] // 2
    return pl.pallas_call(
        own_kernel,
        out_shape=jax.ShapeDtypeStruct((half, half), F32),
        grid_spec=pltpu.PrefetchScalarGridSpec(
            num_scalar_prefetch=1,
            grid=(2,),
            in_specs=[pl.BlockSpec(memory_space=pltpu.HBM)] * 2,
            out_specs=pl.BlockSpec((TILE, half), lambda m, p: (m, 0)),
            scratch_shapes=[
                pltpu.VMEM((2, tokens, TILE), BF),
                pltpu.VMEM((tokens, half), BF),
                pltpu.SemaphoreType.DMA((2,)),
                pltpu.SemaphoreType.DMA,
            ],
        ),
        compiler_params=pltpu.CompilerParams(vmem_limit_bytes=28 * 2**20),
        cost_estimate=pl.CostEstimate(
            flops=2 * tokens * half * half, bytes_accessed=8 * tokens * half, transcendentals=0
        ),
        name="cross_own",
    )(place, grads, acts)


def cross_term(place, grads_next, acts_next, partial, after):
    tokens, half = grads_next.shape[0], grads_next.shape[1] // 2
    out = pltpu.HBM((4, half // 16, half), BF)
    return pl.pallas_call(
        cross_kernel,
        out_shape=[out] * 4,
        grid_spec=pltpu.PrefetchScalarGridSpec(
            num_scalar_prefetch=1,
            grid=(2,),
            in_specs=[
                pl.BlockSpec((tokens, TILE), lambda m, p: (0, p[1] * 2 + m)),
                pl.BlockSpec((tokens, half), lambda m, p: (0, p[1] ^ p[0])),
                ANY,
                pl.BlockSpec(memory_space=pltpu.HBM),
            ],
            out_specs=[pl.BlockSpec(memory_space=pltpu.HBM)] * 4,
            scratch_shapes=[
                pltpu.VMEM((2, TILE, half), F32),
                pltpu.VMEM((2, TILE, half), BF),
                pltpu.SemaphoreType.DMA((2,)),
                pltpu.SemaphoreType.DMA,
            ],
        ),
        compiler_params=pltpu.CompilerParams(vmem_limit_bytes=28 * 2**20),
        cost_estimate=pl.CostEstimate(
            flops=2 * tokens * half * half, bytes_accessed=10 * tokens * half, transcendentals=0
        ),
        name="cross_term",
    )(place, grads_next, acts_next, partial, after)


def factor_fetch(place, pairs, step, lhs, lhs_sems, rhs=None, rhs_sem=None):
    at = pl.ds(pl.multiple_of(step * TILE, TILE), TILE)
    for owner in range(2):

        @pl.when(place[0] == owner)
        def _():
            for k, pair in pairs:
                slot = step & 1
                target = lhs.at[slot, k]
                pltpu.make_async_copy(pair[owner].at[:, at], target, lhs_sems.at[slot, k]).start()
                if rhs is not None:
                    half = rhs.shape[2]
                    columns = pl.ds(pl.multiple_of(place[1] * half, half), half)
                    pltpu.make_async_copy(pair[owner].at[:, columns], rhs.at[k], rhs_sem).start()


def factor_own_kernel(place, h_own, g_own, after, out, lhs, rhs, lhs_sems, rhs_sem):
    del after
    m = pl.program_id(0)
    pairs = [(0, (h_own, g_own))]
    pl.when(m == 0)(lambda: factor_fetch(place, pairs, 0, lhs, lhs_sems, rhs, rhs_sem))
    pl.when(m == 0)(lambda: factor_fetch(place, pairs, 1, lhs, lhs_sems))
    wait_all(lhs.at[m, 0], lhs_sems.at[m, 0])
    pl.when(m == 0)(lambda: wait_all(rhs, rhs_sem))
    out[...] = contract(lhs[m, 0], rhs[0])


def factor_own(place, acts, grads, after):
    tokens, width = acts.shape
    half = width // 2
    hbm = pl.BlockSpec(memory_space=pltpu.HBM)
    return pl.pallas_call(
        factor_own_kernel,
        out_shape=pltpu.HBM((half, half), F32),
        grid_spec=pltpu.PrefetchScalarGridSpec(
            num_scalar_prefetch=1,
            grid=(2,),
            in_specs=[hbm, hbm, ANY],
            out_specs=pl.BlockSpec((TILE, half), lambda m, p: (m, 0)),
            scratch_shapes=[
                pltpu.VMEM((2, 1, tokens, TILE), BF),
                pltpu.VMEM((1, tokens, half), BF),
                pltpu.SemaphoreType.DMA((2, 1)),
                pltpu.SemaphoreType.DMA,
            ],
        ),
        compiler_params=pltpu.CompilerParams(vmem_limit_bytes=20 * 2**20),
        cost_estimate=pl.CostEstimate(flops=0, bytes_accessed=0, transcendentals=0),
        name="factor_own",
    )(place, acts, grads, after)


def factor_kernel(place, h_own, g_own, h_next, g_next, partial, after, *rest):
    del after
    own, right, far_a, far_b, left, lhs, rhs, held, buffer = rest[:9]
    lhs_sems, rhs_sem, held_sems, sem = rest[9:]
    m = pl.program_id(0)
    both = [(0, (h_own, g_own)), (1, (h_next, g_next))]

    @pl.when(m == 0)
    def _():
        for k in range(2):
            rows = partial.at[pl.ds(k * TILE, TILE)]
            pltpu.make_async_copy(rows, held.at[k], held_sems.at[k]).start()
        factor_fetch(place, both[1:], 0, lhs, lhs_sems)
        factor_fetch(place, both, 1, lhs, lhs_sems, rhs, rhs_sem)

    pl.when((m == 1) | (m == 2))(lambda: factor_fetch(place, both, m + 1, lhs, lhs_sems))
    slot = m & 1
    wait_all(lhs.at[slot, 1], lhs_sems.at[slot, 1])
    pl.when(m > 0)(lambda: wait_all(lhs.at[slot, 0], lhs_sems.at[slot, 0]))
    pl.when(m == 0)(lambda: wait_all(rhs, rhs_sem))
    tile = contract(lhs[slot, 1], rhs[1])

    @pl.when(m < 2)
    def _():
        wait_all(held.at[m], held_sems.at[m])
        buffer[m] = (held[m] + tile).astype(BF)

    @pl.when(m >= 2)
    def _():
        buffer[m] = (contract(lhs[slot, 0], rhs[0]) + tile).astype(BF)

    place_tile(place, buffer, sem, [own, right, (far_a, far_b), left], m, 1)
    pl.when(m == 3)(lambda: wait_all(buffer, sem))


def factor_term(place, acts, grads, acts_next, grads_next, partial, after):
    tokens, width = acts.shape
    half = width // 2
    hbm = pl.BlockSpec(memory_space=pltpu.HBM)
    out = pltpu.HBM((4, width // 16, half), BF)
    side = pltpu.HBM((2, width // 16, half), BF)
    return pl.pallas_call(
        factor_kernel,
        out_shape=[out, out, side, side, out],
        grid_spec=pltpu.PrefetchScalarGridSpec(
            num_scalar_prefetch=1,
            grid=(4,),
            in_specs=[hbm] * 6,
            out_specs=[hbm] * 5,
            scratch_shapes=[
                pltpu.VMEM((2, 2, tokens, TILE), BF),
                pltpu.VMEM((2, tokens, half), BF),
                pltpu.VMEM((2, TILE, half), F32),
                pltpu.VMEM((4, TILE, half), BF),
                pltpu.SemaphoreType.DMA((2, 2)),
                pltpu.SemaphoreType.DMA,
                pltpu.SemaphoreType.DMA((2,)),
                pltpu.SemaphoreType.DMA,
            ],
        ),
        compiler_params=pltpu.CompilerParams(vmem_limit_bytes=36 * 2**20),
        cost_estimate=pl.CostEstimate(
            flops=4 * tokens * width * half, bytes_accessed=16 * tokens * half, transcendentals=0
        ),
        name="factor_term",
    )(place, acts, grads, acts_next, grads_next, partial, after)


def add(first, *rest):
    total = first.astype(F32)
    for x in rest:
        total = total + x.astype(F32)
    return total


def fold_kernel(count, me, *refs):
    own, *others = refs[-6:-2]
    held, sems = refs[-2:]
    steps = [(1, others[0]), (2, others[1]), (3, others[2]), (0, own)]
    for r, _ in steps:
        pltpu.make_async_copy(refs[0].at[(me[0] + r) & 3], held.at[r], sems.at[r]).start()
    for r, out in steps:
        wait_all(held.at[r], sems.at[r])
        at = (me[0] + r) & 3
        out[...] = add(held[r], *[part[at] for part in refs[1:count]]).astype(out.dtype)


def fold(me, parts, *after):
    _, rows, width = parts[0].shape
    whole = pl.BlockSpec((rows, width), lambda s, m: (0, 0))
    return pl.pallas_call(
        functools.partial(fold_kernel, len(parts)),
        out_shape=[pltpu.HBM((rows, width), F32)]
        + [pltpu.VMEM((rows, width), BF)] * 3,
        grid_spec=pltpu.PrefetchScalarGridSpec(
            num_scalar_prefetch=1,
            grid=(1,),
            in_specs=[pl.BlockSpec(memory_space=pltpu.HBM)]
            + [VMEM] * (len(parts) - 1)
            + [ANY] * len(after),
            out_specs=[whole] + [VMEM] * 3,
            scratch_shapes=[pltpu.VMEM((4, rows, width), BF), pltpu.SemaphoreType.DMA((4,))],
        ),
        compiler_params=pltpu.CompilerParams(vmem_limit_bytes=12 * 2**20),
        cost_estimate=pl.CostEstimate(flops=0, bytes_accessed=0, transcendentals=0),
        name="fold",
    )(me, in_hbm(parts[0]), *parts[1:], *after)


def settle_kernel(count, xl, *refs):
    mine, theirs, total = refs[-3:]
    rows = mine.shape[0]
    value = None
    for ref in refs[:count]:
        for part in [ref[...]] if len(ref.shape) == 2 else [ref[k] for k in range(ref.shape[0])]:
            value = part.astype(F32) if value is None else value + part.astype(F32)
    total[...] = value
    for out, index in ((mine, xl[0]), (theirs, 1 - xl[0])):
        out[...] = total[pl.ds(pl.multiple_of(index * rows, 8), rows)].astype(out.dtype)


def settle(xl, parts, dtype, *after):
    rows, width = parts[0].shape[-2:]
    half = pl.BlockSpec((rows // 2, width), lambda s, x: (0, 0))
    return pl.pallas_call(
        functools.partial(settle_kernel, len(parts)),
        out_shape=[jax.ShapeDtypeStruct((rows // 2, width), t) for t in (F32, dtype)],
        grid_spec=pltpu.PrefetchScalarGridSpec(
            num_scalar_prefetch=1,
            grid=(1,),
            in_specs=[pl.BlockSpec((rows, width), lambda s, x: (0, 0))]
            + [VMEM] * (len(parts) - 1)
            + [ANY] * len(after),
            out_specs=[half] * 2,
            scratch_shapes=[pltpu.VMEM((rows, width), F32)],
        ),
        compiler_params=pltpu.CompilerParams(vmem_limit_bytes=8 * 2**20),
        cost_estimate=pl.CostEstimate(flops=0, bytes_accessed=0, transcendentals=0),
        name="settle",
    )(xl, *parts, *after)


def grow_kernel(right, left, from_left, from_right, *refs):
    out_right, out_left, held, sems, out_sem = refs[-5:]
    jobs = [(right, 0, from_left, 0, out_right), (left, 2, from_right, 0, out_left)]
    jobs += [(right, 1, from_left, 1, out_right), (left, 3, from_right, 1, out_left)]
    for n, (x, at, _, _, _) in enumerate(jobs):
        pltpu.make_async_copy(x.at[at], held.at[n], sems.at[n]).start()
    for n, (_, at, received, k, out) in enumerate(jobs):
        wait_all(held.at[n], sems.at[n])
        held[n] = add(held[n], received[k]).astype(BF)
        pltpu.make_async_copy(held.at[n], out.at[at], out_sem).start()
    wait_all(held, out_sem)


def grow(right, left, from_left, from_right, *after):
    hbm = pl.BlockSpec(memory_space=pltpu.HBM)
    return pl.pallas_call(
        grow_kernel,
        out_shape=[pltpu.HBM(x.shape, x.dtype) for x in (right, left)],
        grid=(1,),
        in_specs=[hbm, hbm, VMEM, VMEM] + [ANY] * len(after),
        out_specs=[hbm, hbm],
        scratch_shapes=[
            pltpu.VMEM(right.shape, right.dtype),
            pltpu.SemaphoreType.DMA((4,)),
            pltpu.SemaphoreType.DMA,
        ],
        input_output_aliases={0: 0, 1: 1},
        compiler_params=pltpu.CompilerParams(vmem_limit_bytes=8 * 2**20),
        cost_estimate=pl.CostEstimate(flops=0, bytes_accessed=0, transcendentals=0),
        name="grow",
    )(in_hbm(right), in_hbm(left), from_left, from_right, *after)


def fetch_tiles(step, source, held, sems):
    @pl.when(step == 0)
    def _():
        for k in range(4):
            rows = source.at[pl.ds(k * TILE, TILE)]
            pltpu.make_async_copy(rows, held.at[k], sems.at[k]).start()

    wait_all(held.at[step], sems.at[step])


def left_kernel(own, place, a, b, left, *rest):
    before = None if own else rest[0]
    out, total, held, sems = rest[-4:] if own else (rest[1], rest[2], *rest[4:])
    step = pl.program_id(0)
    rows = a.shape[0]
    at = pl.ds(pl.multiple_of(step * TILE, TILE), TILE)
    part = place[1] ^ place[0] if own else 1 - (place[1] ^ place[0])

    @pl.when(step == 0)
    def _():
        for k in range(2):
            tile = left.at[pl.ds(pl.multiple_of((part * 2 + k) * TILE, TILE), TILE)]
            pltpu.make_async_copy(tile, held.at[k], sems.at[k]).start()

    stacked = jnp.concatenate(split_pair(a[:, at] + b[:, at]), axis=0)
    wait_all(held.at[step], sems.at[step])
    value = jnp.dot(stacked, held[step], preferred_element_type=F32)
    pl.when(step == 0)(lambda: total.__setitem__(..., value if own else before[...] + value))
    pl.when(step == 1)(lambda: total.__setitem__(..., total[...] + value))
    if own:
        pl.when(step == 1)(lambda: out.__setitem__(..., total[...]))
        return
    packed = rest[3]

    @pl.when(step == 1)
    def _():
        result = total[:rows] + total[rows:]
        for z in range(2):
            for y in range(4):
                for xl in range(2):
                    for c in range(2):
                        n = ((z * 4 + y) * 2 + xl) * 2 + c
                        block = result[:, n * rows : (n + 1) * rows]
                        packed[n, 0:16, 0:rows] = block[0:16]
                        packed[n, 0:16, rows : 2 * rows] = block[16:32]
                        packed[n, 0:8, 2 * rows : 3 * rows] = block[32:40]
                        ready = packed[n].astype(BF)
                        for there in (0, 2):
                            d = c * 32 + (there + z) * 8 + y * 2 + xl
                            out[d] = ready
                            out[64 + d] = ready


def left_product(place, a, b, left, before=None):
    rows, half = a.shape
    own = before is None
    total = pltpu.VMEM((2 * rows, half), F32)
    return pl.pallas_call(
        functools.partial(left_kernel, own),
        out_shape=total if own else pltpu.HBM((128, 16, 128), BF),
        grid_spec=pltpu.PrefetchScalarGridSpec(
            num_scalar_prefetch=1,
            grid=(2,),
            in_specs=[VMEM, VMEM, pl.BlockSpec(memory_space=pltpu.HBM)] + [VMEM] * (not own),
            out_specs=VMEM if own else pl.BlockSpec((128, 16, 128), lambda k, p: (0, 0, 0)),
            scratch_shapes=[total]
            + [pltpu.VMEM((32, 16, 128), F32)] * (not own)
            + [pltpu.VMEM((2, TILE, half), BF), pltpu.SemaphoreType.DMA((2,))],
        ),
        compiler_params=pltpu.CompilerParams(vmem_limit_bytes=16 * 2**20),
        cost_estimate=pl.CostEstimate(
            flops=0 if own else 256 * rows * half * half, bytes_accessed=0, transcendentals=0
        ),
        name="left_own" if own else "left_product",
    )(place, a, b, left, *([] if own else [before]))


def right_kernel(place, blocks, right, late, out, rows_in, held, sems):
    del late
    step = pl.program_id(0)
    fetch_tiles(step, right, held, sems)
    rows = out.shape[0]
    for near in range(2):
        for y in range(4):
            for xl in range(2):
                core = (step >> 1) ^ ((near + y) & 1)
                block = blocks[core * 32 + ((step & 1) * 2 + near) * 8 + y * 2 + xl].astype(F32)
                at = ((near * 4 + y) * 2 + xl) * rows
                rows_in[at : at + 16, :] = block[:, 0:rows]
                rows_in[at + 16 : at + 32, :] = block[:, rows : 2 * rows]
                rows_in[at + 32 : at + 40, :] = block[0:8, 2 * rows : 3 * rows]
    value = contract(rows_in[...].astype(BF), held[step])
    pl.when(step == 0)(lambda: out.__setitem__(..., value))
    pl.when(step > 0)(lambda: out.__setitem__(..., out[...] + value))


def right_product(place, blocks, right, late):
    width, half = right.shape
    rows = width // 64
    return pl.pallas_call(
        right_kernel,
        out_shape=jax.ShapeDtypeStruct((rows, half), F32),
        grid_spec=pltpu.PrefetchScalarGridSpec(
            num_scalar_prefetch=1,
            grid=(4,),
            in_specs=[
                pl.BlockSpec((64, 16, 128), lambda k, p: (p[2] >> 1, 0, 0)),
                pl.BlockSpec(memory_space=pltpu.HBM),
                ANY,
            ],
            out_specs=pl.BlockSpec((rows, half), lambda k, p: (0, 0)),
            scratch_shapes=[
                pltpu.VMEM((TILE, rows), F32),
                pltpu.VMEM((4, TILE, half), BF),
                pltpu.SemaphoreType.DMA((4,)),
            ],
        ),
        compiler_params=pltpu.CompilerParams(vmem_limit_bytes=20 * 2**20),
        cost_estimate=pl.CostEstimate(
            flops=640 * rows * half * half, bytes_accessed=4 * half * half, transcendentals=0
        ),
        name="right_product",
    )(place, blocks, right, late)


def per_device(hidden, out_grad, left_inverse, right_inverse):
    z, y, xl, c, o = (lax.axis_index(n) for n in ("z", "y", "xl", "c", "o"))
    tokens, width = hidden.shape
    half = width // 2
    token_total = tokens * 64
    first = o == 0
    h = c ^ ((z + y) & 1)
    hidden, out_grad = in_hbm(hidden), in_hbm(out_grad)
    left_inverse, right_inverse = in_hbm(left_inverse), in_hbm(right_inverse)
    place = jnp.stack([o, h, z, y]).astype(jnp.int32)
    second_me = jnp.where(h == 0, y, z).astype(jnp.int32)[None]

    grads_next, acts_next = in_hbm(shift(out_grad, "c", 1)), in_hbm(shift(hidden, "c", 1))
    partial = cross_own(place, out_grad, hidden)
    factor_partial = in_hbm(factor_own(place, hidden, out_grad, partial))

    own, m1, m2, m3 = cross_term(place, grads_next, acts_next, partial, factor_partial)
    m_parts = [own, turn(m1, 1, 0), turn(m2, 2, 0), turn(m3, 3, 0)]

    f_own, right, far_a, far_b, left = factor_term(
        place, hidden, out_grad, acts_next, grads_next, factor_partial, in_hbm(m1)
    )
    from_left, from_right = turn(far_a, 1, 0), turn(far_b, -1, 0)

    my_xl = xl.astype(jnp.int32)[None]

    def second_sends(pieces):
        return [turn(piece, s, 1) for s, piece in enumerate(pieces, 1)]

    m, *m_pieces = fold(second_me, m_parts, in_hbm(f_own))
    m_received = second_sends(m_pieces)
    right, left = grow(right, left, from_left, from_right, *m_received)
    f_parts = [f_own, turn(right, 1, 0), turn(left, -1, 0)]

    mine, theirs = settle(my_xl, [in_hbm(m), *m_received], F32)
    across = lax.ppermute(theirs, ("xl", "o"), [(i, 3 - i) for i in range(4)])
    products = left_product(place, mine, shift(theirs, "xl", 1), left_inverse)
    products = left_product(place, shift(mine, "o", 1), across, left_inverse, products)
    blocks = lax.all_to_all(products, ("o", "c", "z", "y", "xl"), 0, 0, tiled=True)
    f, *f_pieces = fold(second_me, f_parts, in_hbm(products))
    update = right_product(place, blocks, right_inverse, f_pieces[0])
    f_mine, f_theirs = settle(my_xl, [in_hbm(f), *second_sends(f_pieces)], BF, in_hbm(update))

    f = add(f_mine, shift(f_theirs, "xl", 1))
    f = f * jnp.where(first, 1.0 / token_total, 1.0).astype(F32)
    f = f.reshape(2, width // 64, half)
    mine = pick(f, 0, c)
    theirs = shift(pick(f, 0, 1 - c), "c", 1)
    factors = jnp.concatenate(
        [jnp.where(h == 0, mine, theirs), jnp.where(h == 0, theirs, mine)], axis=1
    )[None]
    return factors, update


def solution(mesh):
    fine = Mesh(mesh.devices.reshape(4, 4, 2, 2, 2), ("z", "y", "xl", "c", "o"))
    dp = ("z", "y", "xl", "c")
    in_specs = (P(dp, None), P(dp, None), P(None, "o"), P(None, "o"))
    out_specs = (P("o", dp, None), P(dp, "o"))
    return jax.shard_map(
        per_device, mesh=fine, in_specs=in_specs, out_specs=out_specs, check_vma=False
    )
```

```python
import functools

import jax
import jax.numpy as jnp
from jax import lax
from jax.experimental import pallas as pl
from jax.experimental.pallas import tpu as pltpu
from jax.sharding import Mesh, PartitionSpec as P

BF = jnp.bfloat16
F32 = jnp.float32
TILE = 640
ANY = pl.BlockSpec(memory_space=pl.ANY)
VMEM = pl.BlockSpec(memory_space=pltpu.VMEM)


def contract(first_rows, second_rows):
    return lax.dot_general(
        first_rows, second_rows, (((0,), (0,)), ((), ())), preferred_element_type=F32
    )


def shift(x, axis, step):
    size = lax.axis_size(axis)
    return lax.ppermute(x, axis, [(i, (i + step) % size) for i in range(size)])


def turn(x, step, stage):
    pairs = []
    for z in range(4):
        for y in range(4):
            for h in range(2):
                along_z = (h == 0) == (stage == 0)
                z2, y2 = ((z + step) % 4, y) if along_z else (z, (y + step) % 4)
                core, core2 = h ^ ((z + y) & 1), h ^ ((z2 + y2) & 1)
                pairs.append(((z * 4 + y) * 2 + core, (z2 * 4 + y2) * 2 + core2))
    return lax.ppermute(x, ("z", "y", "c"), pairs)


def in_hbm(x):
    return pltpu.with_memory_space_constraint(x, pltpu.HBM)


def pick(x, dim, index):
    return lax.dynamic_index_in_dim(x, index, dim, keepdims=False)


def split_pair(x):
    high = x.astype(BF)
    return high, (x - high.astype(F32)).astype(BF)


def place_tile(place, buffer, sem, outs, m, zs):
    rows = TILE // (zs * 4)

    def start(at, out, slot):
        block = buffer.at[m, pl.ds(at, rows)]
        pltpu.make_async_copy(block, out.at[slot], sem).start()

    for a in range(zs):
        z = m * zs + a

        @pl.when(place[1] == 0)
        def _():
            for r, out in enumerate(outs):

                @pl.when(((z - place[2] + 4) & 3) == r)
                def _():
                    for k in range(4):
                        if isinstance(out, tuple):
                            start((a * 4 + k) * rows, out[k // 2], k % 2)
                        else:
                            start((a * 4 + k) * rows, out, k)

        @pl.when(place[1] == 1)
        def _():
            for r, out in enumerate(outs):
                at = pl.multiple_of((a * 4 + ((place[3] + r) & 3)) * rows, 16)
                if isinstance(out, tuple):
                    pl.when(z < 2)(functools.partial(start, at, out[0], z & 1))
                    pl.when(z >= 2)(functools.partial(start, at, out[1], z & 1))
                else:
                    start(at, out, z)


def wait_all(buffer, sem):
    pltpu.make_async_copy(buffer, buffer, sem).wait()


def cut_kernel(place, x, out):
    del place
    out[...] = x[...]


def cut(place, x, index):
    tokens, width = x.shape
    block = (tokens // 4, width // 2)
    return pl.pallas_call(
        cut_kernel,
        out_shape=pltpu.HBM((tokens, width // 2), x.dtype),
        grid_spec=pltpu.PrefetchScalarGridSpec(
            num_scalar_prefetch=1,
            grid=(4,),
            in_specs=[pl.BlockSpec(block, lambda m, p: (m, index(p)))],
            out_specs=pl.BlockSpec(block, lambda m, p: (m, 0)),
        ),
        compiler_params=pltpu.CompilerParams(vmem_limit_bytes=4 * 2**20),
        cost_estimate=pl.CostEstimate(flops=0, bytes_accessed=0, transcendentals=0),
        name="cut",
    )(place, x)


def own_kernel(place, a, b, out, rest, lhs, rhs, part, lhs_sems, rhs_sem, part_sems):
    m = pl.program_id(0)
    half = rhs.shape[1]

    @pl.when(m == 0)
    def _():
        at = pl.ds(pl.multiple_of((place[1] ^ place[0]) * half, half), half)
        pltpu.make_async_copy(b.at[:, at], rhs, rhs_sem).start()
        for k in range(2):
            at = pl.ds(pl.multiple_of(place[1] * half + k * TILE, TILE), TILE)
            pltpu.make_async_copy(a.at[:, at], lhs.at[k], lhs_sems.at[k]).start()
        wait_all(rhs, rhs_sem)
        at = pl.ds(pl.multiple_of(place[1] * half, half), half)
        for owner, ref in enumerate((b, a)):

            @pl.when(place[0] == owner)
            def _():
                pltpu.make_async_copy(ref.at[:, at], part, part_sems.at[0]).start()

    @pl.when(m == 1)
    def _():
        wait_all(part, part_sems.at[0])
        pltpu.make_async_copy(part, rest, part_sems.at[1]).start()

    wait_all(lhs.at[m], lhs_sems.at[m])
    out[...] = contract(lhs[m], rhs[...])
    pl.when(m == 1)(lambda: wait_all(part, part_sems.at[1]))


def cross_kernel(place, a, b, partial, own, ahead1, ahead2, ahead3, held, buffer, held_sems, sem):
    m = pl.program_id(0)

    @pl.when(m == 0)
    def _():
        for k in range(2):
            rows = partial.at[pl.ds(k * TILE, TILE)]
            pltpu.make_async_copy(rows, held.at[k], held_sems.at[k]).start()

    tile = contract(a[...], b[...])
    wait_all(held.at[m], held_sems.at[m])
    buffer[m] = (held[m] + tile).astype(BF)
    place_tile(place, buffer, sem, [own, ahead1, ahead2, ahead3], m, 2)
    pl.when(m == 1)(lambda: wait_all(buffer, sem))


def cross_own(place, grads, acts):
    tokens, half = grads.shape[0], grads.shape[1] // 2
    return pl.pallas_call(
        own_kernel,
        out_shape=[jax.ShapeDtypeStruct((half, half), F32), pltpu.HBM((tokens, half), BF)],
        grid_spec=pltpu.PrefetchScalarGridSpec(
            num_scalar_prefetch=1,
            grid=(2,),
            in_specs=[pl.BlockSpec(memory_space=pltpu.HBM)] * 2,
            out_specs=[
                pl.BlockSpec((TILE, half), lambda m, p: (m, 0)),
                pl.BlockSpec(memory_space=pltpu.HBM),
            ],
            scratch_shapes=[
                pltpu.VMEM((2, tokens, TILE), BF),
                pltpu.VMEM((tokens, half), BF),
                pltpu.VMEM((tokens, half), BF),
                pltpu.SemaphoreType.DMA((2,)),
                pltpu.SemaphoreType.DMA,
                pltpu.SemaphoreType.DMA((2,)),
            ],
        ),
        compiler_params=pltpu.CompilerParams(vmem_limit_bytes=28 * 2**20),
        cost_estimate=pl.CostEstimate(
            flops=2 * tokens * half * half, bytes_accessed=8 * tokens * half, transcendentals=0
        ),
        name="cross_own",
    )(place, grads, acts)


def cross_term(place, grads_next, acts_next, partial):
    tokens, half = grads_next.shape
    out = pltpu.HBM((4, half // 16, half), BF)
    return pl.pallas_call(
        cross_kernel,
        out_shape=[out] * 4,
        grid_spec=pltpu.PrefetchScalarGridSpec(
            num_scalar_prefetch=1,
            grid=(2,),
            in_specs=[
                pl.BlockSpec((tokens, TILE), lambda m, p: (0, m)),
                pl.BlockSpec((tokens, half), lambda m, p: (0, 0)),
                ANY,
            ],
            out_specs=[pl.BlockSpec(memory_space=pltpu.HBM)] * 4,
            scratch_shapes=[
                pltpu.VMEM((2, TILE, half), F32),
                pltpu.VMEM((2, TILE, half), BF),
                pltpu.SemaphoreType.DMA((2,)),
                pltpu.SemaphoreType.DMA,
            ],
        ),
        compiler_params=pltpu.CompilerParams(vmem_limit_bytes=28 * 2**20),
        cost_estimate=pl.CostEstimate(
            flops=2 * tokens * half * half, bytes_accessed=10 * tokens * half, transcendentals=0
        ),
        name="cross_term",
    )(place, grads_next, acts_next, partial)


def factor_kernel(place, h_own, g_own, h_next, g_next, x_next, after, *rest):
    del after
    own, right, far_a, far_b, left, lhs, rhs, buffer, lhs_sems, rhs_sem, sem = rest
    m = pl.program_id(0)
    half = rhs.shape[2]

    def lanes(step, wide):
        return pl.ds(pl.multiple_of(step * wide, wide), wide)

    def fetch(step, with_rhs):
        slot = step & 1

        def left_block(ref, k, at):
            pltpu.make_async_copy(ref.at[:, lanes(at, TILE)], lhs.at[slot, k], lhs_sems.at[slot]).start()

        for owner, (mine, theirs) in enumerate(((h_own, h_next), (g_own, g_next))):

            @pl.when(place[0] == owner)
            def _():
                left_block(mine, 0, step)
                pl.when((step >> 1) == place[1])(lambda: left_block(theirs, 1, step & 1))
                if with_rhs:
                    at = lanes(place[1], half)
                    pltpu.make_async_copy(mine.at[:, at], rhs.at[0], rhs_sem).start()
                    pltpu.make_async_copy(theirs, rhs.at[1], rhs_sem).start()

        pl.when((step >> 1) != place[1])(lambda: left_block(x_next, 1, step & 1))

    pl.when(m == 0)(lambda: fetch(0, True))
    pl.when(m < 3)(lambda: fetch(m + 1, False))
    slot = m & 1
    wait_all(lhs.at[slot], lhs_sems.at[slot])
    pl.when(m == 0)(lambda: wait_all(rhs, rhs_sem))

    buffer[m] = (contract(lhs[slot, 0], rhs[0]) + contract(lhs[slot, 1], rhs[1])).astype(BF)
    place_tile(place, buffer, sem, [own, right, (far_a, far_b), left], m, 1)
    pl.when(m == 3)(lambda: wait_all(buffer, sem))


def factor_term(place, acts, grads, acts_next, grads_next, rest_next, after):
    tokens, width = acts.shape
    half = width // 2
    hbm = pl.BlockSpec(memory_space=pltpu.HBM)
    out = pltpu.HBM((4, width // 16, half), BF)
    side = pltpu.HBM((2, width // 16, half), BF)
    return pl.pallas_call(
        factor_kernel,
        out_shape=[out, out, side, side, out],
        grid_spec=pltpu.PrefetchScalarGridSpec(
            num_scalar_prefetch=1,
            grid=(4,),
            in_specs=[hbm] * 2 + [ANY] * 4,
            out_specs=[hbm] * 5,
            scratch_shapes=[
                pltpu.VMEM((2, 2, tokens, TILE), BF),
                pltpu.VMEM((2, tokens, half), BF),
                pltpu.VMEM((4, TILE, half), BF),
                pltpu.SemaphoreType.DMA((2,)),
                pltpu.SemaphoreType.DMA,
                pltpu.SemaphoreType.DMA,
            ],
        ),
        compiler_params=pltpu.CompilerParams(vmem_limit_bytes=30 * 2**20),
        cost_estimate=pl.CostEstimate(
            flops=4 * tokens * width * half, bytes_accessed=16 * tokens * half, transcendentals=0
        ),
        name="factor_term",
    )(place, acts, grads, acts_next, grads_next, rest_next, after)


def add(first, *rest):
    total = first.astype(F32)
    for x in rest:
        total = total + x.astype(F32)
    return total


def fold_kernel(count, me, *refs):
    own, *others = refs[-6:-2]
    held, sems = refs[-2:]
    steps = [(1, others[0]), (2, others[1]), (3, others[2]), (0, own)]
    for r, _ in steps:
        pltpu.make_async_copy(refs[0].at[(me[0] + r) & 3], held.at[r], sems.at[r]).start()
    for r, out in steps:
        wait_all(held.at[r], sems.at[r])
        at = (me[0] + r) & 3
        out[...] = add(held[r], *[part[at] for part in refs[1:count]]).astype(out.dtype)


def fold(me, parts, *after):
    _, rows, width = parts[0].shape
    whole = pl.BlockSpec((rows, width), lambda s, m: (0, 0))
    return pl.pallas_call(
        functools.partial(fold_kernel, len(parts)),
        out_shape=[pltpu.HBM((rows, width), F32)]
        + [pltpu.VMEM((rows, width), BF)] * 3,
        grid_spec=pltpu.PrefetchScalarGridSpec(
            num_scalar_prefetch=1,
            grid=(1,),
            in_specs=[pl.BlockSpec(memory_space=pltpu.HBM)]
            + [VMEM] * (len(parts) - 1)
            + [ANY] * len(after),
            out_specs=[whole] + [VMEM] * 3,
            scratch_shapes=[pltpu.VMEM((4, rows, width), BF), pltpu.SemaphoreType.DMA((4,))],
        ),
        compiler_params=pltpu.CompilerParams(vmem_limit_bytes=12 * 2**20),
        cost_estimate=pl.CostEstimate(flops=0, bytes_accessed=0, transcendentals=0),
        name="fold",
    )(me, in_hbm(parts[0]), *parts[1:], *after)


def settle_kernel(count, xl, *refs):
    mine, theirs, total = refs[-3:]
    rows = mine.shape[0]
    value = None
    for ref in refs[:count]:
        for part in [ref[...]] if len(ref.shape) == 2 else [ref[k] for k in range(ref.shape[0])]:
            value = part.astype(F32) if value is None else value + part.astype(F32)
    total[...] = value
    for out, index in ((mine, xl[0]), (theirs, 1 - xl[0])):
        out[...] = total[pl.ds(pl.multiple_of(index * rows, 8), rows)].astype(out.dtype)


def settle(xl, parts, dtype, *after):
    rows, width = parts[0].shape[-2:]
    half = pl.BlockSpec((rows // 2, width), lambda s, x: (0, 0))
    return pl.pallas_call(
        functools.partial(settle_kernel, len(parts)),
        out_shape=[jax.ShapeDtypeStruct((rows // 2, width), t) for t in (F32, dtype)],
        grid_spec=pltpu.PrefetchScalarGridSpec(
            num_scalar_prefetch=1,
            grid=(1,),
            in_specs=[pl.BlockSpec((rows, width), lambda s, x: (0, 0))]
            + [VMEM] * (len(parts) - 1)
            + [ANY] * len(after),
            out_specs=[half] * 2,
            scratch_shapes=[pltpu.VMEM((rows, width), F32)],
        ),
        compiler_params=pltpu.CompilerParams(vmem_limit_bytes=8 * 2**20),
        cost_estimate=pl.CostEstimate(flops=0, bytes_accessed=0, transcendentals=0),
        name="settle",
    )(xl, *parts, *after)


def grow_kernel(right, left, from_left, from_right, *refs):
    out_right, out_left, held, sems, out_sem = refs[-5:]
    jobs = [(right, 0, from_left, 0, out_right), (left, 2, from_right, 0, out_left)]
    jobs += [(right, 1, from_left, 1, out_right), (left, 3, from_right, 1, out_left)]
    for n, (x, at, _, _, _) in enumerate(jobs):
        pltpu.make_async_copy(x.at[at], held.at[n], sems.at[n]).start()
    for n, (_, at, received, k, out) in enumerate(jobs):
        wait_all(held.at[n], sems.at[n])
        held[n] = add(held[n], received[k]).astype(BF)
        pltpu.make_async_copy(held.at[n], out.at[at], out_sem).start()
    wait_all(held, out_sem)


def grow(right, left, from_left, from_right, *after):
    hbm = pl.BlockSpec(memory_space=pltpu.HBM)
    return pl.pallas_call(
        grow_kernel,
        out_shape=[pltpu.HBM(x.shape, x.dtype) for x in (right, left)],
        grid=(1,),
        in_specs=[hbm, hbm, VMEM, VMEM] + [ANY] * len(after),
        out_specs=[hbm, hbm],
        scratch_shapes=[
            pltpu.VMEM(right.shape, right.dtype),
            pltpu.SemaphoreType.DMA((4,)),
            pltpu.SemaphoreType.DMA,
        ],
        input_output_aliases={0: 0, 1: 1},
        compiler_params=pltpu.CompilerParams(vmem_limit_bytes=8 * 2**20),
        cost_estimate=pl.CostEstimate(flops=0, bytes_accessed=0, transcendentals=0),
        name="grow",
    )(in_hbm(right), in_hbm(left), from_left, from_right, *after)


def fetch_tiles(step, source, held, sems):
    @pl.when(step == 0)
    def _():
        for k in range(4):
            rows = source.at[pl.ds(k * TILE, TILE)]
            pltpu.make_async_copy(rows, held.at[k], sems.at[k]).start()

    wait_all(held.at[step], sems.at[step])


def left_kernel(own, place, a, b, left, *rest):
    before = None if own else rest[0]
    out, total, held, sems = rest[-4:] if own else (rest[1], rest[2], *rest[4:])
    step = pl.program_id(0)
    rows = a.shape[0]
    at = pl.ds(pl.multiple_of(step * TILE, TILE), TILE)
    part = place[1] ^ place[0] if own else 1 - (place[1] ^ place[0])

    @pl.when(step == 0)
    def _():
        for k in range(2):
            tile = left.at[pl.ds(pl.multiple_of((part * 2 + k) * TILE, TILE), TILE)]
            pltpu.make_async_copy(tile, held.at[k], sems.at[k]).start()

    stacked = jnp.concatenate(split_pair(a[:, at] + b[:, at]), axis=0)
    wait_all(held.at[step], sems.at[step])
    value = jnp.dot(stacked, held[step], preferred_element_type=F32)
    pl.when(step == 0)(lambda: total.__setitem__(..., value if own else before[...] + value))
    pl.when(step == 1)(lambda: total.__setitem__(..., total[...] + value))
    if own:
        pl.when(step == 1)(lambda: out.__setitem__(..., total[...]))
        return
    packed = rest[3]

    @pl.when(step == 1)
    def _():
        result = total[:rows] + total[rows:]
        for z in range(2):
            for y in range(4):
                for xl in range(2):
                    for c in range(2):
                        n = ((z * 4 + y) * 2 + xl) * 2 + c
                        block = result[:, n * rows : (n + 1) * rows]
                        packed[n, 0:16, 0:rows] = block[0:16]
                        packed[n, 0:16, rows : 2 * rows] = block[16:32]
                        packed[n, 0:8, 2 * rows : 3 * rows] = block[32:40]
                        ready = packed[n].astype(BF)
                        for there in (0, 2):
                            d = c * 32 + (there + z) * 8 + y * 2 + xl
                            out[d] = ready
                            out[64 + d] = ready


def left_product(place, a, b, left, before=None):
    rows, half = a.shape
    own = before is None
    total = pltpu.VMEM((2 * rows, half), F32)
    return pl.pallas_call(
        functools.partial(left_kernel, own),
        out_shape=total if own else pltpu.HBM((128, 16, 128), BF),
        grid_spec=pltpu.PrefetchScalarGridSpec(
            num_scalar_prefetch=1,
            grid=(2,),
            in_specs=[VMEM, VMEM, pl.BlockSpec(memory_space=pltpu.HBM)] + [VMEM] * (not own),
            out_specs=VMEM if own else pl.BlockSpec((128, 16, 128), lambda k, p: (0, 0, 0)),
            scratch_shapes=[total]
            + [pltpu.VMEM((32, 16, 128), F32)] * (not own)
            + [pltpu.VMEM((2, TILE, half), BF), pltpu.SemaphoreType.DMA((2,))],
        ),
        compiler_params=pltpu.CompilerParams(vmem_limit_bytes=16 * 2**20),
        cost_estimate=pl.CostEstimate(
            flops=0 if own else 256 * rows * half * half, bytes_accessed=0, transcendentals=0
        ),
        name="left_own" if own else "left_product",
    )(place, a, b, left, *([] if own else [before]))


def right_kernel(place, blocks, right, late, out, rows_in, held, sems):
    del late
    step = pl.program_id(0)
    fetch_tiles(step, right, held, sems)
    rows = out.shape[0]
    for near in range(2):
        for y in range(4):
            for xl in range(2):
                core = (step >> 1) ^ ((near + y) & 1)
                block = blocks[core * 32 + ((step & 1) * 2 + near) * 8 + y * 2 + xl].astype(F32)
                at = ((near * 4 + y) * 2 + xl) * rows
                rows_in[at : at + 16, :] = block[:, 0:rows]
                rows_in[at + 16 : at + 32, :] = block[:, rows : 2 * rows]
                rows_in[at + 32 : at + 40, :] = block[0:8, 2 * rows : 3 * rows]
    value = contract(rows_in[...].astype(BF), held[step])
    pl.when(step == 0)(lambda: out.__setitem__(..., value))
    pl.when(step > 0)(lambda: out.__setitem__(..., out[...] + value))


def right_product(place, blocks, right, late):
    width, half = right.shape
    rows = width // 64
    return pl.pallas_call(
        right_kernel,
        out_shape=jax.ShapeDtypeStruct((rows, half), F32),
        grid_spec=pltpu.PrefetchScalarGridSpec(
            num_scalar_prefetch=1,
            grid=(4,),
            in_specs=[
                pl.BlockSpec((64, 16, 128), lambda k, p: (p[2] >> 1, 0, 0)),
                pl.BlockSpec(memory_space=pltpu.HBM),
                ANY,
            ],
            out_specs=pl.BlockSpec((rows, half), lambda k, p: (0, 0)),
            scratch_shapes=[
                pltpu.VMEM((TILE, rows), F32),
                pltpu.VMEM((4, TILE, half), BF),
                pltpu.SemaphoreType.DMA((4,)),
            ],
        ),
        compiler_params=pltpu.CompilerParams(vmem_limit_bytes=20 * 2**20),
        cost_estimate=pl.CostEstimate(
            flops=640 * rows * half * half, bytes_accessed=4 * half * half, transcendentals=0
        ),
        name="right_product",
    )(place, blocks, right, late)


def per_device(hidden, out_grad, left_inverse, right_inverse):
    z, y, xl, c, o = (lax.axis_index(n) for n in ("z", "y", "xl", "c", "o"))
    tokens, width = hidden.shape
    half = width // 2
    token_total = tokens * 64
    first = o == 0
    h = c ^ ((z + y) & 1)
    hidden, out_grad = in_hbm(hidden), in_hbm(out_grad)
    left_inverse, right_inverse = in_hbm(left_inverse), in_hbm(right_inverse)
    place = jnp.stack([o, h, z, y]).astype(jnp.int32)
    second_me = jnp.where(h == 0, y, z).astype(jnp.int32)[None]

    grads_next = in_hbm(shift(cut(place, out_grad, lambda p: 1 - p[1]), "c", 1))
    acts_next = in_hbm(shift(cut(place, hidden, lambda p: (1 - p[1]) ^ p[0]), "c", 1))
    partial, rest = cross_own(place, out_grad, hidden)
    rest_next = in_hbm(shift(rest, "c", 1))

    own, m1, m2, m3 = cross_term(place, grads_next, acts_next, partial)
    m_parts = [own, turn(m1, 1, 0), turn(m2, 2, 0), turn(m3, 3, 0)]

    f_own, right, far_a, far_b, left = factor_term(
        place, hidden, out_grad, acts_next, grads_next, rest_next, in_hbm(m1)
    )
    from_left, from_right = turn(far_a, 1, 0), turn(far_b, -1, 0)

    my_xl = xl.astype(jnp.int32)[None]

    def second_sends(pieces):
        return [turn(piece, s, 1) for s, piece in enumerate(pieces, 1)]

    m, *m_pieces = fold(second_me, m_parts, in_hbm(f_own))
    m_received = second_sends(m_pieces)
    right, left = grow(right, left, from_left, from_right, *m_received)
    f_parts = [f_own, turn(right, 1, 0), turn(left, -1, 0)]

    mine, theirs = settle(my_xl, [in_hbm(m), *m_received], F32)
    across = lax.ppermute(theirs, ("xl", "o"), [(i, 3 - i) for i in range(4)])
    products = left_product(place, mine, shift(theirs, "xl", 1), left_inverse)
    products = left_product(place, shift(mine, "o", 1), across, left_inverse, products)
    blocks = lax.all_to_all(products, ("o", "c", "z", "y", "xl"), 0, 0, tiled=True)
    f, *f_pieces = fold(second_me, f_parts, in_hbm(products))
    update = right_product(place, blocks, right_inverse, f_pieces[0])
    f_mine, f_theirs = settle(my_xl, [in_hbm(f), *second_sends(f_pieces)], BF, in_hbm(update))

    f = add(f_mine, shift(f_theirs, "xl", 1))
    f = f * jnp.where(first, 1.0 / token_total, 1.0).astype(F32)
    f = f.reshape(2, width // 64, half)
    mine = pick(f, 0, c)
    theirs = shift(pick(f, 0, 1 - c), "c", 1)
    factors = jnp.concatenate(
        [jnp.where(h == 0, mine, theirs), jnp.where(h == 0, theirs, mine)], axis=1
    )[None]
    return factors, update


def solution(mesh):
    fine = Mesh(mesh.devices.reshape(4, 4, 2, 2, 2), ("z", "y", "xl", "c", "o"))
    dp = ("z", "y", "xl", "c")
    in_specs = (P(dp, None), P(dp, None), P(None, "o"), P(None, "o"))
    out_specs = (P("o", dp, None), P(dp, "o"))
    return jax.shard_map(
        per_device, mesh=fine, in_specs=in_specs, out_specs=out_specs, check_vma=False
    )
```

```python
import functools

import jax
import jax.numpy as jnp
from jax import lax
from jax.experimental import pallas as pl
from jax.experimental.pallas import tpu as pltpu
from jax.sharding import Mesh, PartitionSpec as P

BF = jnp.bfloat16
F32 = jnp.float32
TILE = 640
ANY = pl.BlockSpec(memory_space=pl.ANY)
VMEM = pl.BlockSpec(memory_space=pltpu.VMEM)


def contract(first_rows, second_rows):
    return lax.dot_general(
        first_rows, second_rows, (((0,), (0,)), ((), ())), preferred_element_type=F32
    )


def shift(x, axis, step):
    size = lax.axis_size(axis)
    return lax.ppermute(x, axis, [(i, (i + step) % size) for i in range(size)])


def turn(x, step, stage):
    pairs = []
    for z in range(4):
        for y in range(4):
            for h in range(2):
                along_z = (h == 0) == (stage == 0)
                z2, y2 = ((z + step) % 4, y) if along_z else (z, (y + step) % 4)
                core, core2 = h ^ ((z + y) & 1), h ^ ((z2 + y2) & 1)
                pairs.append(((z * 4 + y) * 2 + core, (z2 * 4 + y2) * 2 + core2))
    return lax.ppermute(x, ("z", "y", "c"), pairs)


def in_hbm(x):
    return pltpu.with_memory_space_constraint(x, pltpu.HBM)


def pick(x, dim, index):
    return lax.dynamic_index_in_dim(x, index, dim, keepdims=False)


def split_pair(x):
    high = x.astype(BF)
    return high, (x - high.astype(F32)).astype(BF)


def place_tile(place, buffer, sem, outs, m, zs):
    rows = TILE // (zs * 4)

    def start(at, out, slot):
        block = buffer.at[m, pl.ds(at, rows)]
        pltpu.make_async_copy(block, out.at[slot], sem).start()

    for a in range(zs):
        z = m * zs + a

        @pl.when(place[1] == 0)
        def _():
            for r, out in enumerate(outs):

                @pl.when(((z - place[2] + 4) & 3) == r)
                def _():
                    for k in range(4):
                        if isinstance(out, tuple):
                            start((a * 4 + k) * rows, out[k // 2], k % 2)
                        else:
                            start((a * 4 + k) * rows, out, k)

        @pl.when(place[1] == 1)
        def _():
            for r, out in enumerate(outs):
                at = pl.multiple_of((a * 4 + ((place[3] + r) & 3)) * rows, 16)
                if isinstance(out, tuple):
                    pl.when(z < 2)(functools.partial(start, at, out[0], z & 1))
                    pl.when(z >= 2)(functools.partial(start, at, out[1], z & 1))
                else:
                    start(at, out, z)


def wait_all(buffer, sem):
    pltpu.make_async_copy(buffer, buffer, sem).wait()


def own_kernel(place, a, b, out, lhs, rhs, lhs_sems, rhs_sem):
    m = pl.program_id(0)
    half = rhs.shape[1]

    @pl.when(m == 0)
    def _():
        at = pl.ds(pl.multiple_of((place[1] ^ place[0]) * half, half), half)
        pltpu.make_async_copy(b.at[:, at], rhs, rhs_sem).start()
        for k in range(2):
            at = pl.ds(pl.multiple_of(place[1] * half + k * TILE, TILE), TILE)
            pltpu.make_async_copy(a.at[:, at], lhs.at[k], lhs_sems.at[k]).start()
        wait_all(rhs, rhs_sem)

    wait_all(lhs.at[m], lhs_sems.at[m])
    out[...] = contract(lhs[m], rhs[...])


def cross_kernel(place, a, b, partial, own, ahead1, ahead2, ahead3, held, buffer, held_sems, sem):
    m = pl.program_id(0)

    @pl.when(m == 0)
    def _():
        for k in range(2):
            rows = partial.at[pl.ds(k * TILE, TILE)]
            pltpu.make_async_copy(rows, held.at[k], held_sems.at[k]).start()

    tile = contract(a[...], b[...])
    wait_all(held.at[m], held_sems.at[m])
    buffer[m] = (held[m] + tile).astype(BF)
    place_tile(place, buffer, sem, [own, ahead1, ahead2, ahead3], m, 2)
    pl.when(m == 1)(lambda: wait_all(buffer, sem))


def cross_own(place, grads, acts):
    tokens, half = grads.shape[0], grads.shape[1] // 2
    return pl.pallas_call(
        own_kernel,
        out_shape=jax.ShapeDtypeStruct((half, half), F32),
        grid_spec=pltpu.PrefetchScalarGridSpec(
            num_scalar_prefetch=1,
            grid=(2,),
            in_specs=[pl.BlockSpec(memory_space=pltpu.HBM)] * 2,
            out_specs=pl.BlockSpec((TILE, half), lambda m, p: (m, 0)),
            scratch_shapes=[
                pltpu.VMEM((2, tokens, TILE), BF),
                pltpu.VMEM((tokens, half), BF),
                pltpu.SemaphoreType.DMA((2,)),
                pltpu.SemaphoreType.DMA,
            ],
        ),
        compiler_params=pltpu.CompilerParams(vmem_limit_bytes=28 * 2**20),
        cost_estimate=pl.CostEstimate(
            flops=2 * tokens * half * half, bytes_accessed=8 * tokens * half, transcendentals=0
        ),
        name="cross_own",
    )(place, grads, acts)


def cross_term(place, grads_next, acts_next, partial):
    tokens, half = grads_next.shape[0], grads_next.shape[1] // 2
    out = pltpu.HBM((4, half // 16, half), BF)
    return pl.pallas_call(
        cross_kernel,
        out_shape=[out] * 4,
        grid_spec=pltpu.PrefetchScalarGridSpec(
            num_scalar_prefetch=1,
            grid=(2,),
            in_specs=[
                pl.BlockSpec((tokens, TILE), lambda m, p: (0, p[1] * 2 + m)),
                pl.BlockSpec((tokens, half), lambda m, p: (0, p[1] ^ p[0])),
                ANY,
            ],
            out_specs=[pl.BlockSpec(memory_space=pltpu.HBM)] * 4,
            scratch_shapes=[
                pltpu.VMEM((2, TILE, half), F32),
                pltpu.VMEM((2, TILE, half), BF),
                pltpu.SemaphoreType.DMA((2,)),
                pltpu.SemaphoreType.DMA,
            ],
        ),
        compiler_params=pltpu.CompilerParams(vmem_limit_bytes=28 * 2**20),
        cost_estimate=pl.CostEstimate(
            flops=2 * tokens * half * half, bytes_accessed=10 * tokens * half, transcendentals=0
        ),
        name="cross_term",
    )(place, grads_next, acts_next, partial)


def factor_kernel(place, h_own, g_own, h_next, g_next, after, *rest):
    del after
    own, right, far_a, far_b, left, lhs, rhs, buffer, lhs_sems, rhs_sem, sem = rest
    m = pl.program_id(0)
    half = rhs.shape[2]

    def fetch(step, with_rhs):
        slot = step & 1
        at = pl.ds(pl.multiple_of(step * TILE, TILE), TILE)
        columns = pl.ds(pl.multiple_of(place[1] * half, half), half)
        for owner, refs in enumerate(((h_own, h_next), (g_own, g_next))):

            @pl.when(place[0] == owner)
            def _():
                for k, ref in enumerate(refs):
                    pltpu.make_async_copy(ref.at[:, at], lhs.at[slot, k], lhs_sems.at[slot]).start()
                    if with_rhs:
                        pltpu.make_async_copy(ref.at[:, columns], rhs.at[k], rhs_sem).start()

    pl.when(m == 0)(lambda: fetch(0, True))
    pl.when(m < 3)(lambda: fetch(m + 1, False))
    slot = m & 1
    wait_all(lhs.at[slot], lhs_sems.at[slot])
    pl.when(m == 0)(lambda: wait_all(rhs, rhs_sem))

    buffer[m] = (contract(lhs[slot, 0], rhs[0]) + contract(lhs[slot, 1], rhs[1])).astype(BF)
    place_tile(place, buffer, sem, [own, right, (far_a, far_b), left], m, 1)
    pl.when(m == 3)(lambda: wait_all(buffer, sem))


def factor_term(place, acts, grads, acts_next, grads_next, after):
    tokens, width = acts.shape
    half = width // 2
    hbm = pl.BlockSpec(memory_space=pltpu.HBM)
    out = pltpu.HBM((4, width // 16, half), BF)
    side = pltpu.HBM((2, width // 16, half), BF)
    return pl.pallas_call(
        factor_kernel,
        out_shape=[out, out, side, side, out],
        grid_spec=pltpu.PrefetchScalarGridSpec(
            num_scalar_prefetch=1,
            grid=(4,),
            in_specs=[hbm] * 2 + [ANY] * 3,
            out_specs=[hbm] * 5,
            scratch_shapes=[
                pltpu.VMEM((2, 2, tokens, TILE), BF),
                pltpu.VMEM((2, tokens, half), BF),
                pltpu.VMEM((4, TILE, half), BF),
                pltpu.SemaphoreType.DMA((2,)),
                pltpu.SemaphoreType.DMA,
                pltpu.SemaphoreType.DMA,
            ],
        ),
        compiler_params=pltpu.CompilerParams(vmem_limit_bytes=30 * 2**20),
        cost_estimate=pl.CostEstimate(
            flops=4 * tokens * width * half, bytes_accessed=16 * tokens * half, transcendentals=0
        ),
        name="factor_term",
    )(place, acts, grads, acts_next, grads_next, after)


def add(first, *rest):
    total = first.astype(F32)
    for x in rest:
        total = total + x.astype(F32)
    return total


def fold_kernel(count, me, *refs):
    own, *others = refs[-6:-2]
    held, sems = refs[-2:]
    steps = [(1, others[0]), (2, others[1]), (3, others[2]), (0, own)]
    for r, _ in steps:
        pltpu.make_async_copy(refs[0].at[(me[0] + r) & 3], held.at[r], sems.at[r]).start()
    for r, out in steps:
        wait_all(held.at[r], sems.at[r])
        at = (me[0] + r) & 3
        out[...] = add(held[r], *[part[at] for part in refs[1:count]]).astype(out.dtype)


def fold(me, parts, *after):
    _, rows, width = parts[0].shape
    whole = pl.BlockSpec((rows, width), lambda s, m: (0, 0))
    return pl.pallas_call(
        functools.partial(fold_kernel, len(parts)),
        out_shape=[pltpu.HBM((rows, width), F32)]
        + [pltpu.VMEM((rows, width), BF)] * 3,
        grid_spec=pltpu.PrefetchScalarGridSpec(
            num_scalar_prefetch=1,
            grid=(1,),
            in_specs=[pl.BlockSpec(memory_space=pltpu.HBM)]
            + [VMEM] * (len(parts) - 1)
            + [ANY] * len(after),
            out_specs=[whole] + [VMEM] * 3,
            scratch_shapes=[pltpu.VMEM((4, rows, width), BF), pltpu.SemaphoreType.DMA((4,))],
        ),
        compiler_params=pltpu.CompilerParams(vmem_limit_bytes=12 * 2**20),
        cost_estimate=pl.CostEstimate(flops=0, bytes_accessed=0, transcendentals=0),
        name="fold",
    )(me, in_hbm(parts[0]), *parts[1:], *after)


def settle_kernel(count, xl, *refs):
    mine, theirs, total = refs[-3:]
    rows = mine.shape[0]
    value = None
    for ref in refs[:count]:
        for part in [ref[...]] if len(ref.shape) == 2 else [ref[k] for k in range(ref.shape[0])]:
            value = part.astype(F32) if value is None else value + part.astype(F32)
    total[...] = value
    for out, index in ((mine, xl[0]), (theirs, 1 - xl[0])):
        out[...] = total[pl.ds(pl.multiple_of(index * rows, 8), rows)].astype(out.dtype)


def settle(xl, parts, dtype, *after):
    rows, width = parts[0].shape[-2:]
    half = pl.BlockSpec((rows // 2, width), lambda s, x: (0, 0))
    return pl.pallas_call(
        functools.partial(settle_kernel, len(parts)),
        out_shape=[jax.ShapeDtypeStruct((rows // 2, width), t) for t in (F32, dtype)],
        grid_spec=pltpu.PrefetchScalarGridSpec(
            num_scalar_prefetch=1,
            grid=(1,),
            in_specs=[pl.BlockSpec((rows, width), lambda s, x: (0, 0))]
            + [VMEM] * (len(parts) - 1)
            + [ANY] * len(after),
            out_specs=[half] * 2,
            scratch_shapes=[pltpu.VMEM((rows, width), F32)],
        ),
        compiler_params=pltpu.CompilerParams(vmem_limit_bytes=8 * 2**20),
        cost_estimate=pl.CostEstimate(flops=0, bytes_accessed=0, transcendentals=0),
        name="settle",
    )(xl, *parts, *after)


def grow_kernel(right, left, from_left, from_right, *refs):
    out_right, out_left, held, sems, out_sem = refs[-5:]
    jobs = [(right, 0, from_left, 0, out_right), (left, 2, from_right, 0, out_left)]
    jobs += [(right, 1, from_left, 1, out_right), (left, 3, from_right, 1, out_left)]
    for n, (x, at, _, _, _) in enumerate(jobs):
        pltpu.make_async_copy(x.at[at], held.at[n], sems.at[n]).start()
    for n, (_, at, received, k, out) in enumerate(jobs):
        wait_all(held.at[n], sems.at[n])
        held[n] = add(held[n], received[k]).astype(BF)
        pltpu.make_async_copy(held.at[n], out.at[at], out_sem).start()
    wait_all(held, out_sem)


def grow(right, left, from_left, from_right, *after):
    hbm = pl.BlockSpec(memory_space=pltpu.HBM)
    return pl.pallas_call(
        grow_kernel,
        out_shape=[pltpu.HBM(x.shape, x.dtype) for x in (right, left)],
        grid=(1,),
        in_specs=[hbm, hbm, VMEM, VMEM] + [ANY] * len(after),
        out_specs=[hbm, hbm],
        scratch_shapes=[
            pltpu.VMEM(right.shape, right.dtype),
            pltpu.SemaphoreType.DMA((4,)),
            pltpu.SemaphoreType.DMA,
        ],
        input_output_aliases={0: 0, 1: 1},
        compiler_params=pltpu.CompilerParams(vmem_limit_bytes=8 * 2**20),
        cost_estimate=pl.CostEstimate(flops=0, bytes_accessed=0, transcendentals=0),
        name="grow",
    )(in_hbm(right), in_hbm(left), from_left, from_right, *after)


def fetch_tiles(step, source, held, sems):
    @pl.when(step == 0)
    def _():
        for k in range(4):
            rows = source.at[pl.ds(k * TILE, TILE)]
            pltpu.make_async_copy(rows, held.at[k], sems.at[k]).start()

    wait_all(held.at[step], sems.at[step])


def left_kernel(own, place, a, b, left, *rest):
    before = None if own else rest[0]
    out, total, held, sems = rest[-4:] if own else (rest[1], rest[2], *rest[4:])
    step = pl.program_id(0)
    rows = a.shape[0]
    at = pl.ds(pl.multiple_of(step * TILE, TILE), TILE)
    part = place[1] ^ place[0] if own else 1 - (place[1] ^ place[0])

    @pl.when(step == 0)
    def _():
        for k in range(2):
            tile = left.at[pl.ds(pl.multiple_of((part * 2 + k) * TILE, TILE), TILE)]
            pltpu.make_async_copy(tile, held.at[k], sems.at[k]).start()

    stacked = jnp.concatenate(split_pair(a[:, at] + b[:, at]), axis=0)
    wait_all(held.at[step], sems.at[step])
    value = jnp.dot(stacked, held[step], preferred_element_type=F32)
    pl.when(step == 0)(lambda: total.__setitem__(..., value if own else before[...] + value))
    pl.when(step == 1)(lambda: total.__setitem__(..., total[...] + value))
    if own:
        pl.when(step == 1)(lambda: out.__setitem__(..., total[...]))
        return
    packed = rest[3]

    @pl.when(step == 1)
    def _():
        result = total[:rows] + total[rows:]
        for z in range(2):
            for y in range(4):
                for xl in range(2):
                    for c in range(2):
                        n = ((z * 4 + y) * 2 + xl) * 2 + c
                        block = result[:, n * rows : (n + 1) * rows]
                        packed[n, 0:16, 0:rows] = block[0:16]
                        packed[n, 0:16, rows : 2 * rows] = block[16:32]
                        packed[n, 0:8, 2 * rows : 3 * rows] = block[32:40]
                        ready = packed[n].astype(BF)
                        for there in (0, 2):
                            d = c * 32 + (there + z) * 8 + y * 2 + xl
                            out[d] = ready
                            out[64 + d] = ready


def left_product(place, a, b, left, before=None):
    rows, half = a.shape
    own = before is None
    total = pltpu.VMEM((2 * rows, half), F32)
    return pl.pallas_call(
        functools.partial(left_kernel, own),
        out_shape=total if own else pltpu.HBM((128, 16, 128), BF),
        grid_spec=pltpu.PrefetchScalarGridSpec(
            num_scalar_prefetch=1,
            grid=(2,),
            in_specs=[VMEM, VMEM, pl.BlockSpec(memory_space=pltpu.HBM)] + [VMEM] * (not own),
            out_specs=VMEM if own else pl.BlockSpec((128, 16, 128), lambda k, p: (0, 0, 0)),
            scratch_shapes=[total]
            + [pltpu.VMEM((32, 16, 128), F32)] * (not own)
            + [pltpu.VMEM((2, TILE, half), BF), pltpu.SemaphoreType.DMA((2,))],
        ),
        compiler_params=pltpu.CompilerParams(vmem_limit_bytes=16 * 2**20),
        cost_estimate=pl.CostEstimate(
            flops=0 if own else 256 * rows * half * half, bytes_accessed=0, transcendentals=0
        ),
        name="left_own" if own else "left_product",
    )(place, a, b, left, *([] if own else [before]))


def right_kernel(place, blocks, right, late, out, rows_in, held, sems):
    del late
    step = pl.program_id(0)
    fetch_tiles(step, right, held, sems)
    rows = out.shape[0]
    for near in range(2):
        for y in range(4):
            for xl in range(2):
                core = (step >> 1) ^ ((near + y) & 1)
                block = blocks[core * 32 + ((step & 1) * 2 + near) * 8 + y * 2 + xl].astype(F32)
                at = ((near * 4 + y) * 2 + xl) * rows
                rows_in[at : at + 16, :] = block[:, 0:rows]
                rows_in[at + 16 : at + 32, :] = block[:, rows : 2 * rows]
                rows_in[at + 32 : at + 40, :] = block[0:8, 2 * rows : 3 * rows]
    value = contract(rows_in[...].astype(BF), held[step])
    pl.when(step == 0)(lambda: out.__setitem__(..., value))
    pl.when(step > 0)(lambda: out.__setitem__(..., out[...] + value))


def right_product(place, blocks, right, late):
    width, half = right.shape
    rows = width // 64
    return pl.pallas_call(
        right_kernel,
        out_shape=jax.ShapeDtypeStruct((rows, half), F32),
        grid_spec=pltpu.PrefetchScalarGridSpec(
            num_scalar_prefetch=1,
            grid=(4,),
            in_specs=[
                pl.BlockSpec((64, 16, 128), lambda k, p: (p[2] >> 1, 0, 0)),
                pl.BlockSpec(memory_space=pltpu.HBM),
                ANY,
            ],
            out_specs=pl.BlockSpec((rows, half), lambda k, p: (0, 0)),
            scratch_shapes=[
                pltpu.VMEM((TILE, rows), F32),
                pltpu.VMEM((4, TILE, half), BF),
                pltpu.SemaphoreType.DMA((4,)),
            ],
        ),
        compiler_params=pltpu.CompilerParams(vmem_limit_bytes=20 * 2**20),
        cost_estimate=pl.CostEstimate(
            flops=640 * rows * half * half, bytes_accessed=4 * half * half, transcendentals=0
        ),
        name="right_product",
    )(place, blocks, right, late)


def per_device(hidden, out_grad, left_inverse, right_inverse):
    z, y, xl, c, o = (lax.axis_index(n) for n in ("z", "y", "xl", "c", "o"))
    tokens, width = hidden.shape
    half = width // 2
    token_total = tokens * 64
    first = o == 0
    h = c ^ ((z + y) & 1)
    hidden, out_grad = in_hbm(hidden), in_hbm(out_grad)
    left_inverse, right_inverse = in_hbm(left_inverse), in_hbm(right_inverse)
    place = jnp.stack([o, h, z, y]).astype(jnp.int32)
    second_me = jnp.where(h == 0, y, z).astype(jnp.int32)[None]

    grads_next, acts_next = in_hbm(shift(out_grad, "c", 1)), in_hbm(shift(hidden, "c", 1))
    partial = cross_own(place, out_grad, hidden)

    own, m1, m2, m3 = cross_term(place, grads_next, acts_next, partial)
    m_parts = [own, turn(m1, 1, 0), turn(m3, 3, 0), turn(m2, 2, 0)]

    f_own, right, far_a, far_b, left = factor_term(
        place, hidden, out_grad, acts_next, grads_next, in_hbm(m1)
    )
    from_left, from_right = turn(far_a, 1, 0), turn(far_b, -1, 0)

    my_xl = xl.astype(jnp.int32)[None]

    def second_sends(pieces):
        return [turn(pieces[s - 1], s, 1) for s in (1, 3, 2)]

    m, *m_pieces = fold(second_me, m_parts, in_hbm(f_own))
    m_received = second_sends(m_pieces)
    right, left = grow(right, left, from_left, from_right, *m_received)
    f_parts = [f_own, turn(right, 1, 0), turn(left, -1, 0)]

    mine, theirs = settle(my_xl, [in_hbm(m), *m_received], F32)
    across = lax.ppermute(theirs, ("xl", "o"), [(i, 3 - i) for i in range(4)])
    products = left_product(place, mine, shift(theirs, "xl", 1), left_inverse)
    products = left_product(place, shift(mine, "o", 1), across, left_inverse, products)
    blocks = lax.all_to_all(products, ("o", "c", "z", "y", "xl"), 0, 0, tiled=True)
    f, *f_pieces = fold(second_me, f_parts, in_hbm(products))
    update = right_product(place, blocks, right_inverse, f_pieces[0])
    f_mine, f_theirs = settle(my_xl, [in_hbm(f), *second_sends(f_pieces)], BF, in_hbm(update))

    f = add(f_mine, shift(f_theirs, "xl", 1))
    f = f * jnp.where(first, 1.0 / token_total, 1.0).astype(F32)
    f = f.reshape(2, width // 64, half)
    mine = pick(f, 0, c)
    theirs = shift(pick(f, 0, 1 - c), "c", 1)
    factors = jnp.concatenate(
        [jnp.where(h == 0, mine, theirs), jnp.where(h == 0, theirs, mine)], axis=1
    )[None]
    return factors, update


def solution(mesh):
    fine = Mesh(mesh.devices.reshape(4, 4, 2, 2, 2), ("z", "y", "xl", "c", "o"))
    dp = ("z", "y", "xl", "c")
    in_specs = (P(dp, None), P(dp, None), P(None, "o"), P(None, "o"))
    out_specs = (P("o", dp, None), P(dp, "o"))
    return jax.shard_map(
        per_device, mesh=fine, in_specs=in_specs, out_specs=out_specs, check_vma=False
    )
```

```python
import functools

import jax
import jax.numpy as jnp
from jax import lax
from jax.experimental import pallas as pl
from jax.experimental.pallas import tpu as pltpu
from jax.sharding import Mesh, PartitionSpec as P

BF = jnp.bfloat16
F32 = jnp.float32
TILE = 640
ANY = pl.BlockSpec(memory_space=pl.ANY)
VMEM = pl.BlockSpec(memory_space=pltpu.VMEM)


def contract(first_rows, second_rows):
    return lax.dot_general(
        first_rows, second_rows, (((0,), (0,)), ((), ())), preferred_element_type=F32
    )


def shift(x, axis, step):
    size = lax.axis_size(axis)
    return lax.ppermute(x, axis, [(i, (i + step) % size) for i in range(size)])


def turn(x, step, stage):
    pairs = []
    for z in range(4):
        for y in range(4):
            for h in range(2):
                along_z = (h == 0) == (stage == 0)
                z2, y2 = ((z + step) % 4, y) if along_z else (z, (y + step) % 4)
                core, core2 = h ^ ((z + y) & 1), h ^ ((z2 + y2) & 1)
                pairs.append(((z * 4 + y) * 2 + core, (z2 * 4 + y2) * 2 + core2))
    return lax.ppermute(x, ("z", "y", "c"), pairs)


def in_hbm(x):
    return pltpu.with_memory_space_constraint(x, pltpu.HBM)


def pick(x, dim, index):
    return lax.dynamic_index_in_dim(x, index, dim, keepdims=False)


def split_pair(x):
    high = x.astype(BF)
    return high, (x - high.astype(F32)).astype(BF)


def place_tile(place, buffer, sem, outs, m, zs):
    rows = TILE // (zs * 4)

    def start(at, out, slot):
        block = buffer.at[m, pl.ds(at, rows)]
        pltpu.make_async_copy(block, out.at[slot], sem).start()

    for a in range(zs):
        z = m * zs + a

        @pl.when(place[1] == 0)
        def _():
            for r, out in enumerate(outs):

                @pl.when(((z - place[2] + 4) & 3) == r)
                def _():
                    for k in range(4):
                        if isinstance(out, tuple):
                            start((a * 4 + k) * rows, out[k // 2], k % 2)
                        else:
                            start((a * 4 + k) * rows, out, k)

        @pl.when(place[1] == 1)
        def _():
            for r, out in enumerate(outs):
                at = pl.multiple_of((a * 4 + ((place[3] + r) & 3)) * rows, 16)
                if isinstance(out, tuple):
                    pl.when(z < 2)(functools.partial(start, at, out[0], z & 1))
                    pl.when(z >= 2)(functools.partial(start, at, out[1], z & 1))
                else:
                    start(at, out, z)


def wait_all(buffer, sem):
    pltpu.make_async_copy(buffer, buffer, sem).wait()


def own_kernel(place, a, b, out, lhs, rhs, lhs_sems, rhs_sem):
    m = pl.program_id(0)
    half = rhs.shape[1]

    @pl.when(m == 0)
    def _():
        at = pl.ds(pl.multiple_of((place[1] ^ place[0]) * half, half), half)
        pltpu.make_async_copy(b.at[:, at], rhs, rhs_sem).start()
        for k in range(2):
            at = pl.ds(pl.multiple_of(place[1] * half + k * TILE, TILE), TILE)
            pltpu.make_async_copy(a.at[:, at], lhs.at[k], lhs_sems.at[k]).start()
        wait_all(rhs, rhs_sem)

    wait_all(lhs.at[m], lhs_sems.at[m])
    out[...] = contract(lhs[m], rhs[...])


def cross_kernel(place, a, b, partial, own, ahead1, ahead2, ahead3, held, buffer, held_sems, sem):
    m = pl.program_id(0)

    @pl.when(m == 0)
    def _():
        for k in range(2):
            rows = partial.at[pl.ds(k * TILE, TILE)]
            pltpu.make_async_copy(rows, held.at[k], held_sems.at[k]).start()

    tile = contract(a[...], b[...])
    wait_all(held.at[m], held_sems.at[m])
    buffer[m] = (held[m] + tile).astype(BF)
    place_tile(place, buffer, sem, [own, ahead1, ahead2, ahead3], m, 2)
    pl.when(m == 1)(lambda: wait_all(buffer, sem))


def cross_own(place, grads, acts):
    tokens, half = grads.shape[0], grads.shape[1] // 2
    return pl.pallas_call(
        own_kernel,
        out_shape=jax.ShapeDtypeStruct((half, half), F32),
        grid_spec=pltpu.PrefetchScalarGridSpec(
            num_scalar_prefetch=1,
            grid=(2,),
            in_specs=[pl.BlockSpec(memory_space=pltpu.HBM)] * 2,
            out_specs=pl.BlockSpec((TILE, half), lambda m, p: (m, 0)),
            scratch_shapes=[
                pltpu.VMEM((2, tokens, TILE), BF),
                pltpu.VMEM((tokens, half), BF),
                pltpu.SemaphoreType.DMA((2,)),
                pltpu.SemaphoreType.DMA,
            ],
        ),
        compiler_params=pltpu.CompilerParams(vmem_limit_bytes=28 * 2**20),
        cost_estimate=pl.CostEstimate(
            flops=2 * tokens * half * half, bytes_accessed=8 * tokens * half, transcendentals=0
        ),
        name="cross_own",
    )(place, grads, acts)


def cross_term(place, grads_next, acts_next, partial):
    tokens, half = grads_next.shape[0], grads_next.shape[1] // 2
    out = pltpu.HBM((4, half // 16, half), BF)
    return pl.pallas_call(
        cross_kernel,
        out_shape=[out] * 4,
        grid_spec=pltpu.PrefetchScalarGridSpec(
            num_scalar_prefetch=1,
            grid=(2,),
            in_specs=[
                pl.BlockSpec((tokens, TILE), lambda m, p: (0, p[1] * 2 + m)),
                pl.BlockSpec((tokens, half), lambda m, p: (0, p[1] ^ p[0])),
                ANY,
            ],
            out_specs=[pl.BlockSpec(memory_space=pltpu.HBM)] * 4,
            scratch_shapes=[
                pltpu.VMEM((2, TILE, half), F32),
                pltpu.VMEM((2, TILE, half), BF),
                pltpu.SemaphoreType.DMA((2,)),
                pltpu.SemaphoreType.DMA,
            ],
        ),
        compiler_params=pltpu.CompilerParams(vmem_limit_bytes=28 * 2**20),
        cost_estimate=pl.CostEstimate(
            flops=2 * tokens * half * half, bytes_accessed=10 * tokens * half, transcendentals=0
        ),
        name="cross_term",
    )(place, grads_next, acts_next, partial)


def factor_kernel(place, h_own, g_own, h_next, g_next, after, *rest):
    del after
    own, right, far_a, far_b, left, lhs, rhs, buffer, lhs_sems, rhs_sem, sem = rest
    m = pl.program_id(0)
    half = rhs.shape[2]

    def fetch(step, with_rhs):
        slot = step & 1
        at = pl.ds(pl.multiple_of(step * TILE, TILE), TILE)
        columns = pl.ds(pl.multiple_of(place[1] * half, half), half)
        for owner, refs in enumerate(((h_own, h_next), (g_own, g_next))):

            @pl.when(place[0] == owner)
            def _():
                for k, ref in enumerate(refs):
                    pltpu.make_async_copy(ref.at[:, at], lhs.at[slot, k], lhs_sems.at[slot]).start()
                    if with_rhs:
                        pltpu.make_async_copy(ref.at[:, columns], rhs.at[k], rhs_sem).start()

    pl.when(m == 0)(lambda: fetch(0, True))
    pl.when(m < 3)(lambda: fetch(m + 1, False))
    slot = m & 1
    wait_all(lhs.at[slot], lhs_sems.at[slot])
    pl.when(m == 0)(lambda: wait_all(rhs, rhs_sem))

    buffer[m] = (contract(lhs[slot, 0], rhs[0]) + contract(lhs[slot, 1], rhs[1])).astype(BF)
    place_tile(place, buffer, sem, [own, right, (far_a, far_b), left], m, 1)
    pl.when(m == 3)(lambda: wait_all(buffer, sem))


def factor_term(place, acts, grads, acts_next, grads_next, after):
    tokens, width = acts.shape
    half = width // 2
    hbm = pl.BlockSpec(memory_space=pltpu.HBM)
    out = pltpu.HBM((4, width // 16, half), BF)
    held = pltpu.VMEM((4, width // 16, half), BF)
    side = pltpu.HBM((2, width // 16, half), BF)
    return pl.pallas_call(
        factor_kernel,
        out_shape=[out, held, side, side, held],
        grid_spec=pltpu.PrefetchScalarGridSpec(
            num_scalar_prefetch=1,
            grid=(4,),
            in_specs=[hbm] * 2 + [ANY] * 3,
            out_specs=[hbm, VMEM, hbm, hbm, VMEM],
            scratch_shapes=[
                pltpu.VMEM((2, 2, tokens, TILE), BF),
                pltpu.VMEM((2, tokens, half), BF),
                pltpu.VMEM((4, TILE, half), BF),
                pltpu.SemaphoreType.DMA((2,)),
                pltpu.SemaphoreType.DMA,
                pltpu.SemaphoreType.DMA,
            ],
        ),
        compiler_params=pltpu.CompilerParams(vmem_limit_bytes=30 * 2**20),
        cost_estimate=pl.CostEstimate(
            flops=4 * tokens * width * half, bytes_accessed=16 * tokens * half, transcendentals=0
        ),
        name="factor_term",
    )(place, acts, grads, acts_next, grads_next, after)


def add(first, *rest):
    total = first.astype(F32)
    for x in rest:
        total = total + x.astype(F32)
    return total


def fold_kernel(count, me, *refs):
    own, *others = refs[-6:-2]
    held, sems = refs[-2:]
    steps = [(1, others[0]), (2, others[1]), (3, others[2]), (0, own)]
    for r, _ in steps:
        pltpu.make_async_copy(refs[0].at[(me[0] + r) & 3], held.at[r], sems.at[r]).start()
    for r, out in steps:
        wait_all(held.at[r], sems.at[r])
        at = (me[0] + r) & 3
        out[...] = add(held[r], *[part[at] for part in refs[1:count]]).astype(out.dtype)


def fold(me, parts, *after):
    _, rows, width = parts[0].shape
    whole = pl.BlockSpec((rows, width), lambda s, m: (0, 0))
    return pl.pallas_call(
        functools.partial(fold_kernel, len(parts)),
        out_shape=[pltpu.HBM((rows, width), F32)]
        + [pltpu.VMEM((rows, width), BF)] * 3,
        grid_spec=pltpu.PrefetchScalarGridSpec(
            num_scalar_prefetch=1,
            grid=(1,),
            in_specs=[pl.BlockSpec(memory_space=pltpu.HBM)]
            + [VMEM] * (len(parts) - 1)
            + [ANY] * len(after),
            out_specs=[whole] + [VMEM] * 3,
            scratch_shapes=[pltpu.VMEM((4, rows, width), BF), pltpu.SemaphoreType.DMA((4,))],
        ),
        compiler_params=pltpu.CompilerParams(vmem_limit_bytes=12 * 2**20),
        cost_estimate=pl.CostEstimate(flops=0, bytes_accessed=0, transcendentals=0),
        name="fold",
    )(me, in_hbm(parts[0]), *parts[1:], *after)


def settle_kernel(count, xl, *refs):
    mine, theirs, total = refs[-3:]
    rows = mine.shape[0]
    value = None
    for ref in refs[:count]:
        for part in [ref[...]] if len(ref.shape) == 2 else [ref[k] for k in range(ref.shape[0])]:
            value = part.astype(F32) if value is None else value + part.astype(F32)
    total[...] = value
    for out, index in ((mine, xl[0]), (theirs, 1 - xl[0])):
        out[...] = total[pl.ds(pl.multiple_of(index * rows, 8), rows)].astype(out.dtype)


def settle(xl, parts, dtype, *after):
    rows, width = parts[0].shape[-2:]
    half = pl.BlockSpec((rows // 2, width), lambda s, x: (0, 0))
    return pl.pallas_call(
        functools.partial(settle_kernel, len(parts)),
        out_shape=[jax.ShapeDtypeStruct((rows // 2, width), t) for t in (F32, dtype)],
        grid_spec=pltpu.PrefetchScalarGridSpec(
            num_scalar_prefetch=1,
            grid=(1,),
            in_specs=[pl.BlockSpec((rows, width), lambda s, x: (0, 0))]
            + [VMEM] * (len(parts) - 1)
            + [ANY] * len(after),
            out_specs=[half] * 2,
            scratch_shapes=[pltpu.VMEM((rows, width), F32)],
        ),
        compiler_params=pltpu.CompilerParams(vmem_limit_bytes=8 * 2**20),
        cost_estimate=pl.CostEstimate(flops=0, bytes_accessed=0, transcendentals=0),
        name="settle",
    )(xl, *parts, *after)


def grow_kernel(right, left, from_left, from_right, *refs):
    out_right, out_left = refs[-2:]
    for k in range(2):
        out_right[k] = add(right[k], from_left[k]).astype(BF)
        out_left[2 + k] = add(left[2 + k], from_right[k]).astype(BF)


def grow(right, left, from_left, from_right, *after):
    return pl.pallas_call(
        grow_kernel,
        out_shape=[pltpu.VMEM(x.shape, x.dtype) for x in (right, left)],
        in_specs=[VMEM] * 4 + [ANY] * len(after),
        out_specs=[VMEM, VMEM],
        input_output_aliases={0: 0, 1: 1},
        compiler_params=pltpu.CompilerParams(vmem_limit_bytes=8 * 2**20),
        cost_estimate=pl.CostEstimate(flops=0, bytes_accessed=0, transcendentals=0),
        name="grow",
    )(right, left, from_left, from_right, *after)


def fetch_tiles(step, source, held, sems):
    @pl.when(step == 0)
    def _():
        for k in range(4):
            rows = source.at[pl.ds(k * TILE, TILE)]
            pltpu.make_async_copy(rows, held.at[k], sems.at[k]).start()

    wait_all(held.at[step], sems.at[step])


def left_kernel(own, place, a, b, left, *rest):
    before = None if own else rest[0]
    out, total, held, sems = rest[-4:] if own else (rest[1], rest[2], *rest[4:])
    step = pl.program_id(0)
    rows = a.shape[0]
    at = pl.ds(pl.multiple_of(step * TILE, TILE), TILE)
    part = place[1] ^ place[0] if own else 1 - (place[1] ^ place[0])

    @pl.when(step == 0)
    def _():
        for k in range(2):
            tile = left.at[pl.ds(pl.multiple_of((part * 2 + k) * TILE, TILE), TILE)]
            pltpu.make_async_copy(tile, held.at[k], sems.at[k]).start()

    stacked = jnp.concatenate(split_pair(a[:, at] + b[:, at]), axis=0)
    wait_all(held.at[step], sems.at[step])
    value = jnp.dot(stacked, held[step], preferred_element_type=F32)
    pl.when(step == 0)(lambda: total.__setitem__(..., value if own else before[...] + value))
    pl.when(step == 1)(lambda: total.__setitem__(..., total[...] + value))
    if own:
        pl.when(step == 1)(lambda: out.__setitem__(..., total[...]))
        return
    packed = rest[3]

    @pl.when(step == 1)
    def _():
        result = total[:rows] + total[rows:]
        for z in range(2):
            for y in range(4):
                for xl in range(2):
                    for c in range(2):
                        n = ((z * 4 + y) * 2 + xl) * 2 + c
                        block = result[:, n * rows : (n + 1) * rows]
                        packed[n, 0:16, 0:rows] = block[0:16]
                        packed[n, 0:16, rows : 2 * rows] = block[16:32]
                        packed[n, 0:8, 2 * rows : 3 * rows] = block[32:40]
                        ready = packed[n].astype(BF)
                        for there in (0, 2):
                            d = c * 32 + (there + z) * 8 + y * 2 + xl
                            out[d] = ready
                            out[64 + d] = ready


def left_product(place, a, b, left, before=None):
    rows, half = a.shape
    own = before is None
    total = pltpu.VMEM((2 * rows, half), F32)
    return pl.pallas_call(
        functools.partial(left_kernel, own),
        out_shape=total if own else pltpu.HBM((128, 16, 128), BF),
        grid_spec=pltpu.PrefetchScalarGridSpec(
            num_scalar_prefetch=1,
            grid=(2,),
            in_specs=[VMEM, VMEM, pl.BlockSpec(memory_space=pltpu.HBM)] + [VMEM] * (not own),
            out_specs=VMEM if own else pl.BlockSpec((128, 16, 128), lambda k, p: (0, 0, 0)),
            scratch_shapes=[total]
            + [pltpu.VMEM((32, 16, 128), F32)] * (not own)
            + [pltpu.VMEM((2, TILE, half), BF), pltpu.SemaphoreType.DMA((2,))],
        ),
        compiler_params=pltpu.CompilerParams(vmem_limit_bytes=16 * 2**20),
        cost_estimate=pl.CostEstimate(
            flops=0 if own else 256 * rows * half * half, bytes_accessed=0, transcendentals=0
        ),
        name="left_own" if own else "left_product",
    )(place, a, b, left, *([] if own else [before]))


def right_kernel(place, blocks, right, late, out, rows_in, held, sems):
    del late
    step = pl.program_id(0)
    fetch_tiles(step, right, held, sems)
    rows = out.shape[0]
    for near in range(2):
        for y in range(4):
            for xl in range(2):
                core = (step >> 1) ^ ((near + y) & 1)
                block = blocks[core * 32 + ((step & 1) * 2 + near) * 8 + y * 2 + xl].astype(F32)
                at = ((near * 4 + y) * 2 + xl) * rows
                rows_in[at : at + 16, :] = block[:, 0:rows]
                rows_in[at + 16 : at + 32, :] = block[:, rows : 2 * rows]
                rows_in[at + 32 : at + 40, :] = block[0:8, 2 * rows : 3 * rows]
    value = contract(rows_in[...].astype(BF), held[step])
    pl.when(step == 0)(lambda: out.__setitem__(..., value))
    pl.when(step > 0)(lambda: out.__setitem__(..., out[...] + value))


def right_product(place, blocks, right, late):
    width, half = right.shape
    rows = width // 64
    return pl.pallas_call(
        right_kernel,
        out_shape=jax.ShapeDtypeStruct((rows, half), F32),
        grid_spec=pltpu.PrefetchScalarGridSpec(
            num_scalar_prefetch=1,
            grid=(4,),
            in_specs=[
                pl.BlockSpec((64, 16, 128), lambda k, p: (p[2] >> 1, 0, 0)),
                pl.BlockSpec(memory_space=pltpu.HBM),
                ANY,
            ],
            out_specs=pl.BlockSpec((rows, half), lambda k, p: (0, 0)),
            scratch_shapes=[
                pltpu.VMEM((TILE, rows), F32),
                pltpu.VMEM((4, TILE, half), BF),
                pltpu.SemaphoreType.DMA((4,)),
            ],
        ),
        compiler_params=pltpu.CompilerParams(vmem_limit_bytes=20 * 2**20),
        cost_estimate=pl.CostEstimate(
            flops=640 * rows * half * half, bytes_accessed=4 * half * half, transcendentals=0
        ),
        name="right_product",
    )(place, blocks, right, late)


def per_device(hidden, out_grad, left_inverse, right_inverse):
    z, y, xl, c, o = (lax.axis_index(n) for n in ("z", "y", "xl", "c", "o"))
    tokens, width = hidden.shape
    half = width // 2
    token_total = tokens * 64
    first = o == 0
    h = c ^ ((z + y) & 1)
    hidden, out_grad = in_hbm(hidden), in_hbm(out_grad)
    left_inverse, right_inverse = in_hbm(left_inverse), in_hbm(right_inverse)
    place = jnp.stack([o, h, z, y]).astype(jnp.int32)
    second_me = jnp.where(h == 0, y, z).astype(jnp.int32)[None]

    grads_next, acts_next = in_hbm(shift(out_grad, "c", 1)), in_hbm(shift(hidden, "c", 1))
    partial = cross_own(place, out_grad, hidden)

    own, m1, m2, m3 = cross_term(place, grads_next, acts_next, partial)
    m_parts = [own, turn(m1, 1, 0), turn(m3, 3, 0), turn(m2, 2, 0)]

    f_own, right, far_a, far_b, left = factor_term(
        place, hidden, out_grad, acts_next, grads_next, in_hbm(m1)
    )
    from_left, from_right = turn(far_a, 1, 0), turn(far_b, -1, 0)

    my_xl = xl.astype(jnp.int32)[None]

    def second_sends(pieces):
        return [turn(pieces[s - 1], s, 1) for s in (1, 3, 2)]

    m, *m_pieces = fold(second_me, m_parts, in_hbm(f_own))
    m_received = second_sends(m_pieces)
    right, left = grow(right, left, from_left, from_right, *m_received)
    f_parts = [f_own, turn(right, 1, 0), turn(left, -1, 0)]

    mine, theirs = settle(my_xl, [in_hbm(m), *m_received], F32)
    across = lax.ppermute(theirs, ("xl", "o"), [(i, 3 - i) for i in range(4)])
    products = left_product(place, mine, shift(theirs, "xl", 1), left_inverse)
    products = left_product(place, shift(mine, "o", 1), across, left_inverse, products)
    blocks = lax.all_to_all(products, ("o", "c", "z", "y", "xl"), 0, 0, tiled=True)
    f, *f_pieces = fold(second_me, f_parts, in_hbm(products))
    update = right_product(place, blocks, right_inverse, f_pieces[0])
    f_mine, f_theirs = settle(my_xl, [in_hbm(f), *second_sends(f_pieces)], BF, in_hbm(update))

    f = add(f_mine, shift(f_theirs, "xl", 1))
    f = f * jnp.where(first, 1.0 / token_total, 1.0).astype(F32)
    f = f.reshape(2, width // 64, half)
    mine = pick(f, 0, c)
    theirs = shift(pick(f, 0, 1 - c), "c", 1)
    factors = jnp.concatenate(
        [jnp.where(h == 0, mine, theirs), jnp.where(h == 0, theirs, mine)], axis=1
    )[None]
    return factors, update


def solution(mesh):
    fine = Mesh(mesh.devices.reshape(4, 4, 2, 2, 2), ("z", "y", "xl", "c", "o"))
    dp = ("z", "y", "xl", "c")
    in_specs = (P(dp, None), P(dp, None), P(None, "o"), P(None, "o"))
    out_specs = (P("o", dp, None), P(dp, "o"))
    return jax.shard_map(
        per_device, mesh=fine, in_specs=in_specs, out_specs=out_specs, check_vma=False
    )
```

```python
import functools

import jax
import jax.numpy as jnp
from jax import lax
from jax.experimental import pallas as pl
from jax.experimental.pallas import tpu as pltpu
from jax.sharding import Mesh, PartitionSpec as P

BF = jnp.bfloat16
F32 = jnp.float32
TILE = 640
ANY = pl.BlockSpec(memory_space=pl.ANY)
VMEM = pl.BlockSpec(memory_space=pltpu.VMEM)


def contract(first_rows, second_rows):
    return lax.dot_general(
        first_rows, second_rows, (((0,), (0,)), ((), ())), preferred_element_type=F32
    )


def shift(x, axis, step):
    size = lax.axis_size(axis)
    return lax.ppermute(x, axis, [(i, (i + step) % size) for i in range(size)])


def turn(x, step, stage):
    pairs = []
    for z in range(4):
        for y in range(4):
            for h in range(2):
                along_z = (h == 0) == (stage == 0)
                z2, y2 = ((z + step) % 4, y) if along_z else (z, (y + step) % 4)
                core, core2 = h ^ ((z + y) & 1), h ^ ((z2 + y2) & 1)
                pairs.append(((z * 4 + y) * 2 + core, (z2 * 4 + y2) * 2 + core2))
    return lax.ppermute(x, ("z", "y", "c"), pairs)


def in_hbm(x):
    return pltpu.with_memory_space_constraint(x, pltpu.HBM)


def pick(x, dim, index):
    return lax.dynamic_index_in_dim(x, index, dim, keepdims=False)


def split_pair(x):
    high = x.astype(BF)
    return high, (x - high.astype(F32)).astype(BF)


def place_tile(place, buffer, sem, outs, m, zs):
    rows = TILE // (zs * 4)

    def start(at, out, slot):
        block = buffer.at[m, pl.ds(at, rows)]
        pltpu.make_async_copy(block, out.at[slot], sem).start()

    for a in range(zs):
        z = m * zs + a

        @pl.when(place[1] == 0)
        def _():
            for r, out in enumerate(outs):

                @pl.when(((z - place[2] + 4) & 3) == r)
                def _():
                    for k in range(4):
                        if isinstance(out, tuple):
                            start((a * 4 + k) * rows, out[k // 2], k % 2)
                        else:
                            start((a * 4 + k) * rows, out, k)

        @pl.when(place[1] == 1)
        def _():
            for r, out in enumerate(outs):
                at = pl.multiple_of((a * 4 + ((place[3] + r) & 3)) * rows, 16)
                if isinstance(out, tuple):
                    pl.when(z < 2)(functools.partial(start, at, out[0], z & 1))
                    pl.when(z >= 2)(functools.partial(start, at, out[1], z & 1))
                else:
                    start(at, out, z)


def wait_all(buffer, sem):
    pltpu.make_async_copy(buffer, buffer, sem).wait()


def own_kernel(place, a, b, out, lhs, rhs, lhs_sems, rhs_sem):
    m = pl.program_id(0)
    half = rhs.shape[1]

    @pl.when(m == 0)
    def _():
        at = pl.ds(pl.multiple_of((place[1] ^ place[0]) * half, half), half)
        pltpu.make_async_copy(b.at[:, at], rhs, rhs_sem).start()
        for k in range(2):
            at = pl.ds(pl.multiple_of(place[1] * half + k * TILE, TILE), TILE)
            pltpu.make_async_copy(a.at[:, at], lhs.at[k], lhs_sems.at[k]).start()
        wait_all(rhs, rhs_sem)

    wait_all(lhs.at[m], lhs_sems.at[m])
    out[...] = contract(lhs[m], rhs[...])


def cross_kernel(place, a, b, partial, own, ahead1, ahead2, ahead3, held, buffer, held_sems, sem):
    m = pl.program_id(0)

    @pl.when(m == 0)
    def _():
        for k in range(2):
            rows = partial.at[pl.ds(k * TILE, TILE)]
            pltpu.make_async_copy(rows, held.at[k], held_sems.at[k]).start()

    tile = contract(a[...], b[...])
    wait_all(held.at[m], held_sems.at[m])
    buffer[m] = (held[m] + tile).astype(BF)
    place_tile(place, buffer, sem, [own, ahead1, ahead2, ahead3], m, 2)
    pl.when(m == 1)(lambda: wait_all(buffer, sem))


def cross_own(place, grads, acts):
    tokens, half = grads.shape[0], grads.shape[1] // 2
    return pl.pallas_call(
        own_kernel,
        out_shape=jax.ShapeDtypeStruct((half, half), F32),
        grid_spec=pltpu.PrefetchScalarGridSpec(
            num_scalar_prefetch=1,
            grid=(2,),
            in_specs=[pl.BlockSpec(memory_space=pltpu.HBM)] * 2,
            out_specs=pl.BlockSpec((TILE, half), lambda m, p: (m, 0)),
            scratch_shapes=[
                pltpu.VMEM((2, tokens, TILE), BF),
                pltpu.VMEM((tokens, half), BF),
                pltpu.SemaphoreType.DMA((2,)),
                pltpu.SemaphoreType.DMA,
            ],
        ),
        compiler_params=pltpu.CompilerParams(vmem_limit_bytes=28 * 2**20),
        cost_estimate=pl.CostEstimate(
            flops=2 * tokens * half * half, bytes_accessed=8 * tokens * half, transcendentals=0
        ),
        name="cross_own",
    )(place, grads, acts)


def cross_term(place, grads_next, acts_next, partial):
    tokens, half = grads_next.shape[0], grads_next.shape[1] // 2
    out = pltpu.HBM((4, half // 16, half), BF)
    return pl.pallas_call(
        cross_kernel,
        out_shape=[out] * 4,
        grid_spec=pltpu.PrefetchScalarGridSpec(
            num_scalar_prefetch=1,
            grid=(2,),
            in_specs=[
                pl.BlockSpec((tokens, TILE), lambda m, p: (0, p[1] * 2 + m)),
                pl.BlockSpec((tokens, half), lambda m, p: (0, p[1] ^ p[0])),
                ANY,
            ],
            out_specs=[pl.BlockSpec(memory_space=pltpu.HBM)] * 4,
            scratch_shapes=[
                pltpu.VMEM((2, TILE, half), F32),
                pltpu.VMEM((2, TILE, half), BF),
                pltpu.SemaphoreType.DMA((2,)),
                pltpu.SemaphoreType.DMA,
            ],
        ),
        compiler_params=pltpu.CompilerParams(vmem_limit_bytes=28 * 2**20),
        cost_estimate=pl.CostEstimate(
            flops=2 * tokens * half * half, bytes_accessed=10 * tokens * half, transcendentals=0
        ),
        name="cross_term",
    )(place, grads_next, acts_next, partial)


def factor_kernel(place, h_own, g_own, h_next, g_next, after, *rest):
    del after
    own, right, far_a, far_b, left, lhs, rhs, buffer, lhs_sems, rhs_sem, sem = rest
    m = pl.program_id(0)
    half = rhs.shape[2]

    def fetch(step, with_rhs):
        slot = step & 1
        at = pl.ds(pl.multiple_of(step * TILE, TILE), TILE)
        columns = pl.ds(pl.multiple_of(place[1] * half, half), half)
        for owner, refs in enumerate(((h_own, h_next), (g_own, g_next))):

            @pl.when(place[0] == owner)
            def _():
                for k, ref in enumerate(refs):
                    pltpu.make_async_copy(ref.at[:, at], lhs.at[slot, k], lhs_sems.at[slot]).start()
                    if with_rhs:
                        pltpu.make_async_copy(ref.at[:, columns], rhs.at[k], rhs_sem).start()

    pl.when(m == 0)(lambda: fetch(0, True))
    pl.when(m < 3)(lambda: fetch(m + 1, False))
    slot = m & 1
    wait_all(lhs.at[slot], lhs_sems.at[slot])
    pl.when(m == 0)(lambda: wait_all(rhs, rhs_sem))

    buffer[m] = (contract(lhs[slot, 0], rhs[0]) + contract(lhs[slot, 1], rhs[1])).astype(BF)
    place_tile(place, buffer, sem, [own, right, (far_a, far_b), left], m, 1)
    pl.when(m == 3)(lambda: wait_all(buffer, sem))


def factor_term(place, acts, grads, acts_next, grads_next, after):
    tokens, width = acts.shape
    half = width // 2
    hbm = pl.BlockSpec(memory_space=pltpu.HBM)
    out = pltpu.HBM((4, width // 16, half), BF)
    side = pltpu.HBM((2, width // 16, half), BF)
    return pl.pallas_call(
        factor_kernel,
        out_shape=[out, out, side, side, out],
        grid_spec=pltpu.PrefetchScalarGridSpec(
            num_scalar_prefetch=1,
            grid=(4,),
            in_specs=[hbm] * 2 + [ANY] * 3,
            out_specs=[hbm] * 5,
            scratch_shapes=[
                pltpu.VMEM((2, 2, tokens, TILE), BF),
                pltpu.VMEM((2, tokens, half), BF),
                pltpu.VMEM((4, TILE, half), BF),
                pltpu.SemaphoreType.DMA((2,)),
                pltpu.SemaphoreType.DMA,
                pltpu.SemaphoreType.DMA,
            ],
        ),
        compiler_params=pltpu.CompilerParams(vmem_limit_bytes=30 * 2**20),
        cost_estimate=pl.CostEstimate(
            flops=4 * tokens * width * half, bytes_accessed=16 * tokens * half, transcendentals=0
        ),
        name="factor_term",
    )(place, acts, grads, acts_next, grads_next, after)


def add(first, *rest):
    total = first.astype(F32)
    for x in rest:
        total = total + x.astype(F32)
    return total


def fold_kernel(count, me, *refs):
    own, *others = refs[-6:-2]
    held, sems = refs[-2:]
    steps = [(1, others[0]), (2, others[1]), (3, others[2]), (0, own)]
    for r, _ in steps:
        pltpu.make_async_copy(refs[0].at[(me[0] + r) & 3], held.at[r], sems.at[r]).start()
    for r, out in steps:
        wait_all(held.at[r], sems.at[r])
        at = (me[0] + r) & 3
        out[...] = add(held[r], *[part[at] for part in refs[1:count]]).astype(out.dtype)


def fold(me, parts, *after):
    _, rows, width = parts[0].shape
    whole = pl.BlockSpec((rows, width), lambda s, m: (0, 0))
    return pl.pallas_call(
        functools.partial(fold_kernel, len(parts)),
        out_shape=[pltpu.HBM((rows, width), F32)]
        + [pltpu.VMEM((rows, width), BF)] * 3,
        grid_spec=pltpu.PrefetchScalarGridSpec(
            num_scalar_prefetch=1,
            grid=(1,),
            in_specs=[pl.BlockSpec(memory_space=pltpu.HBM)]
            + [VMEM] * (len(parts) - 1)
            + [ANY] * len(after),
            out_specs=[whole] + [VMEM] * 3,
            scratch_shapes=[pltpu.VMEM((4, rows, width), BF), pltpu.SemaphoreType.DMA((4,))],
        ),
        compiler_params=pltpu.CompilerParams(vmem_limit_bytes=12 * 2**20),
        cost_estimate=pl.CostEstimate(flops=0, bytes_accessed=0, transcendentals=0),
        name="fold",
    )(me, in_hbm(parts[0]), *parts[1:], *after)


def settle_kernel(count, xl, *refs):
    mine, theirs, total = refs[-3:]
    rows = mine.shape[0]
    value = None
    for ref in refs[:count]:
        for part in [ref[...]] if len(ref.shape) == 2 else [ref[k] for k in range(ref.shape[0])]:
            value = part.astype(F32) if value is None else value + part.astype(F32)
    total[...] = value
    for out, index in ((mine, xl[0]), (theirs, 1 - xl[0])):
        out[...] = total[pl.ds(pl.multiple_of(index * rows, 8), rows)].astype(out.dtype)


def settle(xl, parts, dtype, *after):
    rows, width = parts[0].shape[-2:]
    half = pl.BlockSpec((rows // 2, width), lambda s, x: (0, 0))
    return pl.pallas_call(
        functools.partial(settle_kernel, len(parts)),
        out_shape=[jax.ShapeDtypeStruct((rows // 2, width), t) for t in (F32, dtype)],
        grid_spec=pltpu.PrefetchScalarGridSpec(
            num_scalar_prefetch=1,
            grid=(1,),
            in_specs=[pl.BlockSpec((rows, width), lambda s, x: (0, 0))]
            + [VMEM] * (len(parts) - 1)
            + [ANY] * len(after),
            out_specs=[half] * 2,
            scratch_shapes=[pltpu.VMEM((rows, width), F32)],
        ),
        compiler_params=pltpu.CompilerParams(vmem_limit_bytes=8 * 2**20),
        cost_estimate=pl.CostEstimate(flops=0, bytes_accessed=0, transcendentals=0),
        name="settle",
    )(xl, *parts, *after)


def grow_kernel(right, left, from_left, from_right, *refs):
    out_right, out_left, held, sems, out_sem = refs[-5:]
    jobs = [(right, 0, from_left, 0, out_right), (left, 2, from_right, 0, out_left)]
    jobs += [(right, 1, from_left, 1, out_right), (left, 3, from_right, 1, out_left)]
    for n, (x, at, _, _, _) in enumerate(jobs):
        pltpu.make_async_copy(x.at[at], held.at[n], sems.at[n]).start()
    for n, (_, at, received, k, out) in enumerate(jobs):
        wait_all(held.at[n], sems.at[n])
        held[n] = add(held[n], received[k]).astype(BF)
        pltpu.make_async_copy(held.at[n], out.at[at], out_sem).start()
    wait_all(held, out_sem)


def grow(right, left, from_left, from_right, *after):
    hbm = pl.BlockSpec(memory_space=pltpu.HBM)
    return pl.pallas_call(
        grow_kernel,
        out_shape=[pltpu.HBM(x.shape, x.dtype) for x in (right, left)],
        grid=(1,),
        in_specs=[hbm, hbm, VMEM, VMEM] + [ANY] * len(after),
        out_specs=[hbm, hbm],
        scratch_shapes=[
            pltpu.VMEM(right.shape, right.dtype),
            pltpu.SemaphoreType.DMA((4,)),
            pltpu.SemaphoreType.DMA,
        ],
        input_output_aliases={0: 0, 1: 1},
        compiler_params=pltpu.CompilerParams(vmem_limit_bytes=8 * 2**20),
        cost_estimate=pl.CostEstimate(flops=0, bytes_accessed=0, transcendentals=0),
        name="grow",
    )(in_hbm(right), in_hbm(left), from_left, from_right, *after)


def fetch_tiles(step, source, held, sems):
    @pl.when(step == 0)
    def _():
        for k in range(4):
            rows = source.at[pl.ds(k * TILE, TILE)]
            pltpu.make_async_copy(rows, held.at[k], sems.at[k]).start()

    wait_all(held.at[step], sems.at[step])


def left_kernel(own, place, a, b, left, *rest):
    before = None if own else rest[0]
    out, total, held, sems = rest[-4:] if own else (rest[1], rest[2], *rest[4:])
    step = pl.program_id(0)
    rows = a.shape[0]
    at = pl.ds(pl.multiple_of(step * TILE, TILE), TILE)
    part = place[1] ^ place[0] if own else 1 - (place[1] ^ place[0])

    @pl.when(step == 0)
    def _():
        for k in range(2):
            tile = left.at[pl.ds(pl.multiple_of((part * 2 + k) * TILE, TILE), TILE)]
            pltpu.make_async_copy(tile, held.at[k], sems.at[k]).start()

    stacked = jnp.concatenate(split_pair(a[:, at] + b[:, at]), axis=0)
    wait_all(held.at[step], sems.at[step])
    value = jnp.dot(stacked, held[step], preferred_element_type=F32)
    pl.when(step == 0)(lambda: total.__setitem__(..., value if own else before[...] + value))
    pl.when(step == 1)(lambda: total.__setitem__(..., total[...] + value))
    if own:
        pl.when(step == 1)(lambda: out.__setitem__(..., total[...]))
        return
    packed = rest[3]

    @pl.when(step == 1)
    def _():
        result = total[:rows] + total[rows:]
        for z in range(2):
            for y in range(4):
                for xl in range(2):
                    for c in range(2):
                        n = ((z * 4 + y) * 2 + xl) * 2 + c
                        block = result[:, n * rows : (n + 1) * rows]
                        packed[n, 0:16, 0:rows] = block[0:16]
                        packed[n, 0:16, rows : 2 * rows] = block[16:32]
                        packed[n, 0:8, 2 * rows : 3 * rows] = block[32:40]
                        ready = packed[n].astype(BF)
                        for there in (0, 2):
                            d = c * 32 + (there + z) * 8 + y * 2 + xl
                            out[d] = ready
                            out[64 + d] = ready


def left_product(place, a, b, left, before=None):
    rows, half = a.shape
    own = before is None
    total = pltpu.VMEM((2 * rows, half), F32)
    return pl.pallas_call(
        functools.partial(left_kernel, own),
        out_shape=total if own else pltpu.HBM((128, 16, 128), BF),
        grid_spec=pltpu.PrefetchScalarGridSpec(
            num_scalar_prefetch=1,
            grid=(2,),
            in_specs=[VMEM, VMEM, pl.BlockSpec(memory_space=pltpu.HBM)] + [VMEM] * (not own),
            out_specs=VMEM if own else pl.BlockSpec((128, 16, 128), lambda k, p: (0, 0, 0)),
            scratch_shapes=[total]
            + [pltpu.VMEM((32, 16, 128), F32)] * (not own)
            + [pltpu.VMEM((2, TILE, half), BF), pltpu.SemaphoreType.DMA((2,))],
        ),
        compiler_params=pltpu.CompilerParams(vmem_limit_bytes=16 * 2**20),
        cost_estimate=pl.CostEstimate(
            flops=0 if own else 256 * rows * half * half, bytes_accessed=0, transcendentals=0
        ),
        name="left_own" if own else "left_product",
    )(place, a, b, left, *([] if own else [before]))


def right_kernel(place, blocks, right, late, out, rows_in, held, sems):
    del late
    step = pl.program_id(0)
    fetch_tiles(step, right, held, sems)
    rows = out.shape[0]
    for near in range(2):
        for y in range(4):
            for xl in range(2):
                core = (step >> 1) ^ ((near + y) & 1)
                block = blocks[core * 32 + ((step & 1) * 2 + near) * 8 + y * 2 + xl].astype(F32)
                at = ((near * 4 + y) * 2 + xl) * rows
                rows_in[at : at + 16, :] = block[:, 0:rows]
                rows_in[at + 16 : at + 32, :] = block[:, rows : 2 * rows]
                rows_in[at + 32 : at + 40, :] = block[0:8, 2 * rows : 3 * rows]
    value = contract(rows_in[...].astype(BF), held[step])
    pl.when(step == 0)(lambda: out.__setitem__(..., value))
    pl.when(step > 0)(lambda: out.__setitem__(..., out[...] + value))


def right_product(place, blocks, right, late):
    width, half = right.shape
    rows = width // 64
    return pl.pallas_call(
        right_kernel,
        out_shape=jax.ShapeDtypeStruct((rows, half), F32),
        grid_spec=pltpu.PrefetchScalarGridSpec(
            num_scalar_prefetch=1,
            grid=(4,),
            in_specs=[
                pl.BlockSpec((64, 16, 128), lambda k, p: (p[2] >> 1, 0, 0)),
                pl.BlockSpec(memory_space=pltpu.HBM),
                ANY,
            ],
            out_specs=pl.BlockSpec((rows, half), lambda k, p: (0, 0)),
            scratch_shapes=[
                pltpu.VMEM((TILE, rows), F32),
                pltpu.VMEM((4, TILE, half), BF),
                pltpu.SemaphoreType.DMA((4,)),
            ],
        ),
        compiler_params=pltpu.CompilerParams(vmem_limit_bytes=20 * 2**20),
        cost_estimate=pl.CostEstimate(
            flops=640 * rows * half * half, bytes_accessed=4 * half * half, transcendentals=0
        ),
        name="right_product",
    )(place, blocks, right, late)


def per_device(hidden, out_grad, left_inverse, right_inverse):
    z, y, xl, c, o = (lax.axis_index(n) for n in ("z", "y", "xl", "c", "o"))
    tokens, width = hidden.shape
    half = width // 2
    token_total = tokens * 64
    first = o == 0
    h = c ^ ((z + y) & 1)
    hidden, out_grad = in_hbm(hidden), in_hbm(out_grad)
    left_inverse, right_inverse = in_hbm(left_inverse), in_hbm(right_inverse)
    place = jnp.stack([o, h, z, y]).astype(jnp.int32)
    second_me = jnp.where(h == 0, y, z).astype(jnp.int32)[None]

    grads_next, acts_next = in_hbm(shift(out_grad, "c", 1)), in_hbm(shift(hidden, "c", 1))
    partial = cross_own(place, out_grad, hidden)

    own, m1, m2, m3 = cross_term(place, grads_next, acts_next, partial)
    m_parts = [own, turn(m1, 1, 0), turn(m3, 3, 0), turn(m2, 2, 0)]

    f_own, right, far_a, far_b, left = factor_term(
        place, hidden, out_grad, acts_next, grads_next, in_hbm(m1)
    )
    from_left, from_right = turn(far_a, 1, 0), turn(far_b, -1, 0)

    my_xl = xl.astype(jnp.int32)[None]

    def second_sends(pieces):
        return [turn(pieces[s - 1], s, 1) for s in (1, 3, 2)]

    m, *m_pieces = fold(second_me, m_parts, in_hbm(f_own))
    m_received = second_sends(m_pieces)
    right, left = grow(right, left, from_left, from_right, *m_received)
    f_parts = [f_own, turn(right, 1, 0), turn(left, -1, 0)]

    mine, theirs = settle(my_xl, [in_hbm(m), *m_received], F32)
    across = lax.ppermute(theirs, ("xl", "o"), [(i, 3 - i) for i in range(4)])
    products = left_product(place, mine, shift(theirs, "xl", 1), left_inverse)
    products = left_product(place, across, shift(mine, "o", 1), left_inverse, products)
    blocks = lax.all_to_all(products, ("o", "c", "z", "y", "xl"), 0, 0, tiled=True)
    f, *f_pieces = fold(second_me, f_parts, in_hbm(products))
    update = right_product(place, blocks, right_inverse, f_pieces[0])
    f_mine, f_theirs = settle(my_xl, [in_hbm(f), *second_sends(f_pieces)], BF, in_hbm(update))

    f = add(f_mine, shift(f_theirs, "xl", 1))
    f = f * jnp.where(first, 1.0 / token_total, 1.0).astype(F32)
    f = f.reshape(2, width // 64, half)
    mine = pick(f, 0, c)
    theirs = shift(pick(f, 0, 1 - c), "c", 1)
    factors = jnp.concatenate(
        [jnp.where(h == 0, mine, theirs), jnp.where(h == 0, theirs, mine)], axis=1
    )[None]
    return factors, update


def solution(mesh):
    fine = Mesh(mesh.devices.reshape(4, 4, 2, 2, 2), ("z", "y", "xl", "c", "o"))
    dp = ("z", "y", "xl", "c")
    in_specs = (P(dp, None), P(dp, None), P(None, "o"), P(None, "o"))
    out_specs = (P("o", dp, None), P(dp, "o"))
    return jax.shard_map(
        per_device, mesh=fine, in_specs=in_specs, out_specs=out_specs, check_vma=False
    )
```

```python
import functools

import jax
import jax.numpy as jnp
from jax import lax
from jax.experimental import pallas as pl
from jax.experimental.pallas import tpu as pltpu
from jax.sharding import Mesh, PartitionSpec as P

BF = jnp.bfloat16
F32 = jnp.float32
TILE = 640
ANY = pl.BlockSpec(memory_space=pl.ANY)
VMEM = pl.BlockSpec(memory_space=pltpu.VMEM)


def contract(first_rows, second_rows):
    return lax.dot_general(
        first_rows, second_rows, (((0,), (0,)), ((), ())), preferred_element_type=F32
    )


def shift(x, axis, step):
    size = lax.axis_size(axis)
    return lax.ppermute(x, axis, [(i, (i + step) % size) for i in range(size)])


def turn(x, step, stage):
    pairs = []
    for z in range(4):
        for y in range(4):
            for h in range(2):
                along_z = (h == 0) == (stage == 0)
                z2, y2 = ((z + step) % 4, y) if along_z else (z, (y + step) % 4)
                core, core2 = h ^ ((z + y) & 1), h ^ ((z2 + y2) & 1)
                pairs.append(((z * 4 + y) * 2 + core, (z2 * 4 + y2) * 2 + core2))
    return lax.ppermute(x, ("z", "y", "c"), pairs)


def in_hbm(x):
    return pltpu.with_memory_space_constraint(x, pltpu.HBM)


def pick(x, dim, index):
    return lax.dynamic_index_in_dim(x, index, dim, keepdims=False)


def split_pair(x):
    high = x.astype(BF)
    return high, (x - high.astype(F32)).astype(BF)


def place_tile(place, buffer, sem, outs, m, zs):
    rows = TILE // (zs * 4)

    def start(at, out, slot):
        block = buffer.at[m, pl.ds(at, rows)]
        pltpu.make_async_copy(block, out.at[slot], sem).start()

    for a in range(zs):
        z = m * zs + a

        @pl.when(place[1] == 0)
        def _():
            for r, out in enumerate(outs):

                @pl.when(((z - place[2] + 4) & 3) == r)
                def _():
                    for k in range(4):
                        if isinstance(out, tuple):
                            start((a * 4 + k) * rows, out[k // 2], k % 2)
                        else:
                            start((a * 4 + k) * rows, out, k)

        @pl.when(place[1] == 1)
        def _():
            for r, out in enumerate(outs):
                at = pl.multiple_of((a * 4 + ((place[3] + r) & 3)) * rows, 16)
                if isinstance(out, tuple):
                    pl.when(z < 2)(functools.partial(start, at, out[0], z & 1))
                    pl.when(z >= 2)(functools.partial(start, at, out[1], z & 1))
                else:
                    start(at, out, z)


def wait_all(buffer, sem):
    pltpu.make_async_copy(buffer, buffer, sem).wait()


def own_kernel(place, a, b, out, lhs, rhs, lhs_sems, rhs_sem):
    m = pl.program_id(0)
    half = rhs.shape[1]

    @pl.when(m == 0)
    def _():
        at = pl.ds(pl.multiple_of((place[1] ^ place[0]) * half, half), half)
        pltpu.make_async_copy(b.at[:, at], rhs, rhs_sem).start()
        for k in range(2):
            at = pl.ds(pl.multiple_of(place[1] * half + k * TILE, TILE), TILE)
            pltpu.make_async_copy(a.at[:, at], lhs.at[k], lhs_sems.at[k]).start()
        wait_all(rhs, rhs_sem)

    wait_all(lhs.at[m], lhs_sems.at[m])
    out[...] = contract(lhs[m], rhs[...])


def cross_kernel(place, a, b, partial, own, ahead1, ahead2, ahead3, held, buffer, held_sems, sem):
    m = pl.program_id(0)

    @pl.when(m == 0)
    def _():
        for k in range(2):
            rows = partial.at[pl.ds(k * TILE, TILE)]
            pltpu.make_async_copy(rows, held.at[k], held_sems.at[k]).start()

    tile = contract(a[...], b[...])
    wait_all(held.at[m], held_sems.at[m])
    buffer[m] = (held[m] + tile).astype(BF)
    place_tile(place, buffer, sem, [own, ahead1, ahead2, ahead3], m, 2)
    pl.when(m == 1)(lambda: wait_all(buffer, sem))


def cross_own(place, grads, acts):
    tokens, half = grads.shape[0], grads.shape[1] // 2
    return pl.pallas_call(
        own_kernel,
        out_shape=jax.ShapeDtypeStruct((half, half), F32),
        grid_spec=pltpu.PrefetchScalarGridSpec(
            num_scalar_prefetch=1,
            grid=(2,),
            in_specs=[pl.BlockSpec(memory_space=pltpu.HBM)] * 2,
            out_specs=pl.BlockSpec((TILE, half), lambda m, p: (m, 0)),
            scratch_shapes=[
                pltpu.VMEM((2, tokens, TILE), BF),
                pltpu.VMEM((tokens, half), BF),
                pltpu.SemaphoreType.DMA((2,)),
                pltpu.SemaphoreType.DMA,
            ],
        ),
        compiler_params=pltpu.CompilerParams(vmem_limit_bytes=28 * 2**20),
        cost_estimate=pl.CostEstimate(
            flops=2 * tokens * half * half, bytes_accessed=8 * tokens * half, transcendentals=0
        ),
        name="cross_own",
    )(place, grads, acts)


def cross_term(place, grads_next, acts_next, partial):
    tokens, half = grads_next.shape[0], grads_next.shape[1] // 2
    out = pltpu.HBM((4, half // 16, half), BF)
    return pl.pallas_call(
        cross_kernel,
        out_shape=[out] * 4,
        grid_spec=pltpu.PrefetchScalarGridSpec(
            num_scalar_prefetch=1,
            grid=(2,),
            in_specs=[
                pl.BlockSpec((tokens, TILE), lambda m, p: (0, p[1] * 2 + m)),
                pl.BlockSpec((tokens, half), lambda m, p: (0, p[1] ^ p[0])),
                ANY,
            ],
            out_specs=[pl.BlockSpec(memory_space=pltpu.HBM)] * 4,
            scratch_shapes=[
                pltpu.VMEM((2, TILE, half), F32),
                pltpu.VMEM((2, TILE, half), BF),
                pltpu.SemaphoreType.DMA((2,)),
                pltpu.SemaphoreType.DMA,
            ],
        ),
        compiler_params=pltpu.CompilerParams(vmem_limit_bytes=28 * 2**20),
        cost_estimate=pl.CostEstimate(
            flops=2 * tokens * half * half, bytes_accessed=10 * tokens * half, transcendentals=0
        ),
        name="cross_term",
    )(place, grads_next, acts_next, partial)


def factor_kernel(place, h_own, g_own, h_next, g_next, after, *rest):
    del after
    own, right, far_a, far_b, left, lhs, rhs, buffer, lhs_sems, rhs_sem, sem = rest
    m = pl.program_id(0)
    half = rhs.shape[2]

    def fetch(step, with_rhs):
        slot = step & 1
        at = pl.ds(pl.multiple_of(step * TILE, TILE), TILE)
        columns = pl.ds(pl.multiple_of(place[1] * half, half), half)
        for owner, refs in enumerate(((h_own, h_next), (g_own, g_next))):

            @pl.when(place[0] == owner)
            def _():
                for k, ref in enumerate(refs):
                    pltpu.make_async_copy(ref.at[:, at], lhs.at[slot, k], lhs_sems.at[slot]).start()
                    if with_rhs:
                        pltpu.make_async_copy(ref.at[:, columns], rhs.at[k], rhs_sem).start()

    pl.when(m == 0)(lambda: fetch(0, True))
    pl.when(m < 3)(lambda: fetch(m + 1, False))
    slot = m & 1
    wait_all(lhs.at[slot], lhs_sems.at[slot])
    pl.when(m == 0)(lambda: wait_all(rhs, rhs_sem))

    buffer[m] = (contract(lhs[slot, 0], rhs[0]) + contract(lhs[slot, 1], rhs[1])).astype(BF)
    place_tile(place, buffer, sem, [own, right, (far_a, far_b), left], m, 1)
    pl.when(m == 3)(lambda: wait_all(buffer, sem))


def factor_term(place, acts, grads, acts_next, grads_next, after):
    tokens, width = acts.shape
    half = width // 2
    hbm = pl.BlockSpec(memory_space=pltpu.HBM)
    out = pltpu.HBM((4, width // 16, half), BF)
    side = pltpu.HBM((2, width // 16, half), BF)
    return pl.pallas_call(
        factor_kernel,
        out_shape=[out, out, side, side, out],
        grid_spec=pltpu.PrefetchScalarGridSpec(
            num_scalar_prefetch=1,
            grid=(4,),
            in_specs=[hbm] * 2 + [ANY] * 3,
            out_specs=[hbm] * 5,
            scratch_shapes=[
                pltpu.VMEM((2, 2, tokens, TILE), BF),
                pltpu.VMEM((2, tokens, half), BF),
                pltpu.VMEM((4, TILE, half), BF),
                pltpu.SemaphoreType.DMA((2,)),
                pltpu.SemaphoreType.DMA,
                pltpu.SemaphoreType.DMA,
            ],
        ),
        compiler_params=pltpu.CompilerParams(vmem_limit_bytes=30 * 2**20),
        cost_estimate=pl.CostEstimate(
            flops=4 * tokens * width * half, bytes_accessed=16 * tokens * half, transcendentals=0
        ),
        name="factor_term",
    )(place, acts, grads, acts_next, grads_next, after)


def add(first, *rest):
    total = first.astype(F32)
    for x in rest:
        total = total + x.astype(F32)
    return total


def fold_kernel(count, ahead, me, *refs):
    outs, (held, sems) = refs[-2 - len(ahead) : -2], refs[-2:]
    for n, r in enumerate(ahead):
        pltpu.make_async_copy(refs[0].at[(me[0] + r) & 3], held.at[n], sems.at[n]).start()
    for n, r in enumerate(ahead):
        wait_all(held.at[n], sems.at[n])
        at = (me[0] + r) & 3
        outs[n][...] = add(held[n], *[part[at] for part in refs[1:count]]).astype(outs[n].dtype)


def fold(me, parts, ahead, dtype, *after):
    _, rows, width = parts[0].shape
    n = len(ahead)
    return pl.pallas_call(
        functools.partial(fold_kernel, len(parts), ahead),
        out_shape=[pltpu.VMEM((rows, width), dtype)] * n,
        grid_spec=pltpu.PrefetchScalarGridSpec(
            num_scalar_prefetch=1,
            grid=(1,),
            in_specs=[pl.BlockSpec(memory_space=pltpu.HBM)]
            + [VMEM] * (len(parts) - 1)
            + [ANY] * len(after),
            out_specs=[VMEM] * n,
            scratch_shapes=[pltpu.VMEM((n, rows, width), BF), pltpu.SemaphoreType.DMA((n,))],
        ),
        compiler_params=pltpu.CompilerParams(vmem_limit_bytes=8 * 2**20),
        cost_estimate=pl.CostEstimate(flops=0, bytes_accessed=0, transcendentals=0),
        name="fold",
    )(me, in_hbm(parts[0]), *parts[1:], *after)


def settle_kernel(count, xl, *refs):
    mine, theirs, total = refs[-3:]
    rows = mine.shape[0]
    value = None
    for ref in refs[:count]:
        for part in [ref[...]] if len(ref.shape) == 2 else [ref[k] for k in range(ref.shape[0])]:
            value = part.astype(F32) if value is None else value + part.astype(F32)
    total[...] = value
    for out, index in ((mine, xl[0]), (theirs, 1 - xl[0])):
        out[...] = total[pl.ds(pl.multiple_of(index * rows, 8), rows)].astype(out.dtype)


def settle(xl, parts, dtype, *after):
    rows, width = parts[0].shape[-2:]
    half = pl.BlockSpec((rows // 2, width), lambda s, x: (0, 0))
    return pl.pallas_call(
        functools.partial(settle_kernel, len(parts)),
        out_shape=[jax.ShapeDtypeStruct((rows // 2, width), t) for t in (F32, dtype)],
        grid_spec=pltpu.PrefetchScalarGridSpec(
            num_scalar_prefetch=1,
            grid=(1,),
            in_specs=[VMEM] * len(parts)
            + [ANY] * len(after),
            out_specs=[half] * 2,
            scratch_shapes=[pltpu.VMEM((rows, width), F32)],
        ),
        compiler_params=pltpu.CompilerParams(vmem_limit_bytes=8 * 2**20),
        cost_estimate=pl.CostEstimate(flops=0, bytes_accessed=0, transcendentals=0),
        name="settle",
    )(xl, *parts, *after)


def grow_kernel(right, left, from_left, from_right, *refs):
    out_right, out_left, held, sems, out_sem = refs[-5:]
    jobs = [(right, 0, from_left, 0, out_right), (left, 2, from_right, 0, out_left)]
    jobs += [(right, 1, from_left, 1, out_right), (left, 3, from_right, 1, out_left)]
    for n, (x, at, _, _, _) in enumerate(jobs):
        pltpu.make_async_copy(x.at[at], held.at[n], sems.at[n]).start()
    for n, (_, at, received, k, out) in enumerate(jobs):
        wait_all(held.at[n], sems.at[n])
        held[n] = add(held[n], received[k]).astype(BF)
        pltpu.make_async_copy(held.at[n], out.at[at], out_sem).start()
    wait_all(held, out_sem)


def grow(right, left, from_left, from_right, *after):
    hbm = pl.BlockSpec(memory_space=pltpu.HBM)
    return pl.pallas_call(
        grow_kernel,
        out_shape=[pltpu.HBM(x.shape, x.dtype) for x in (right, left)],
        grid=(1,),
        in_specs=[hbm, hbm, VMEM, VMEM] + [ANY] * len(after),
        out_specs=[hbm, hbm],
        scratch_shapes=[
            pltpu.VMEM(right.shape, right.dtype),
            pltpu.SemaphoreType.DMA((4,)),
            pltpu.SemaphoreType.DMA,
        ],
        input_output_aliases={0: 0, 1: 1},
        compiler_params=pltpu.CompilerParams(vmem_limit_bytes=8 * 2**20),
        cost_estimate=pl.CostEstimate(flops=0, bytes_accessed=0, transcendentals=0),
        name="grow",
    )(in_hbm(right), in_hbm(left), from_left, from_right, *after)


def fetch_tiles(step, source, held, sems):
    @pl.when(step == 0)
    def _():
        for k in range(4):
            rows = source.at[pl.ds(k * TILE, TILE)]
            pltpu.make_async_copy(rows, held.at[k], sems.at[k]).start()

    wait_all(held.at[step], sems.at[step])


def left_kernel(own, place, a, b, left, *rest):
    before = None if own else rest[0]
    out, total, held, sems = rest[-4:] if own else (rest[1], rest[2], *rest[4:])
    step = pl.program_id(0)
    rows = a.shape[0]
    at = pl.ds(pl.multiple_of(step * TILE, TILE), TILE)
    part = place[1] ^ place[0] if own else 1 - (place[1] ^ place[0])

    @pl.when(step == 0)
    def _():
        for k in range(2):
            tile = left.at[pl.ds(pl.multiple_of((part * 2 + k) * TILE, TILE), TILE)]
            pltpu.make_async_copy(tile, held.at[k], sems.at[k]).start()

    stacked = jnp.concatenate(split_pair(a[:, at] + b[:, at]), axis=0)
    wait_all(held.at[step], sems.at[step])
    value = jnp.dot(stacked, held[step], preferred_element_type=F32)
    pl.when(step == 0)(lambda: total.__setitem__(..., value if own else before[...] + value))
    pl.when(step == 1)(lambda: total.__setitem__(..., total[...] + value))
    if own:
        pl.when(step == 1)(lambda: out.__setitem__(..., total[...]))
        return
    packed = rest[3]

    @pl.when(step == 1)
    def _():
        result = total[:rows] + total[rows:]
        for z in range(2):
            for y in range(4):
                for xl in range(2):
                    for c in range(2):
                        n = ((z * 4 + y) * 2 + xl) * 2 + c
                        block = result[:, n * rows : (n + 1) * rows]
                        packed[n, 0:16, 0:rows] = block[0:16]
                        packed[n, 0:16, rows : 2 * rows] = block[16:32]
                        packed[n, 0:8, 2 * rows : 3 * rows] = block[32:40]
                        ready = packed[n].astype(BF)
                        for there in (0, 2):
                            d = c * 32 + (there + z) * 8 + y * 2 + xl
                            out[d] = ready
                            out[64 + d] = ready


def left_product(place, a, b, left, before=None):
    rows, half = a.shape
    own = before is None
    total = pltpu.VMEM((2 * rows, half), F32)
    return pl.pallas_call(
        functools.partial(left_kernel, own),
        out_shape=total if own else pltpu.HBM((128, 16, 128), BF),
        grid_spec=pltpu.PrefetchScalarGridSpec(
            num_scalar_prefetch=1,
            grid=(2,),
            in_specs=[VMEM, VMEM, pl.BlockSpec(memory_space=pltpu.HBM)] + [VMEM] * (not own),
            out_specs=VMEM if own else pl.BlockSpec((128, 16, 128), lambda k, p: (0, 0, 0)),
            scratch_shapes=[total]
            + [pltpu.VMEM((32, 16, 128), F32)] * (not own)
            + [pltpu.VMEM((2, TILE, half), BF), pltpu.SemaphoreType.DMA((2,))],
        ),
        compiler_params=pltpu.CompilerParams(vmem_limit_bytes=16 * 2**20),
        cost_estimate=pl.CostEstimate(
            flops=0 if own else 256 * rows * half * half, bytes_accessed=0, transcendentals=0
        ),
        name="left_own" if own else "left_product",
    )(place, a, b, left, *([] if own else [before]))


def right_kernel(place, blocks, right, late, out, rows_in, held, sems):
    del late
    step = pl.program_id(0)
    fetch_tiles(step, right, held, sems)
    rows = out.shape[0]
    for near in range(2):
        for y in range(4):
            for xl in range(2):
                core = (step >> 1) ^ ((near + y) & 1)
                block = blocks[core * 32 + ((step & 1) * 2 + near) * 8 + y * 2 + xl].astype(F32)
                at = ((near * 4 + y) * 2 + xl) * rows
                rows_in[at : at + 16, :] = block[:, 0:rows]
                rows_in[at + 16 : at + 32, :] = block[:, rows : 2 * rows]
                rows_in[at + 32 : at + 40, :] = block[0:8, 2 * rows : 3 * rows]
    value = contract(rows_in[...].astype(BF), held[step])
    pl.when(step == 0)(lambda: out.__setitem__(..., value))
    pl.when(step > 0)(lambda: out.__setitem__(..., out[...] + value))


def right_product(place, blocks, right, late):
    width, half = right.shape
    rows = width // 64
    return pl.pallas_call(
        right_kernel,
        out_shape=jax.ShapeDtypeStruct((rows, half), F32),
        grid_spec=pltpu.PrefetchScalarGridSpec(
            num_scalar_prefetch=1,
            grid=(4,),
            in_specs=[
                pl.BlockSpec((64, 16, 128), lambda k, p: (p[2] >> 1, 0, 0)),
                pl.BlockSpec(memory_space=pltpu.HBM),
                ANY,
            ],
            out_specs=pl.BlockSpec((rows, half), lambda k, p: (0, 0)),
            scratch_shapes=[
                pltpu.VMEM((TILE, rows), F32),
                pltpu.VMEM((4, TILE, half), BF),
                pltpu.SemaphoreType.DMA((4,)),
            ],
        ),
        compiler_params=pltpu.CompilerParams(vmem_limit_bytes=20 * 2**20),
        cost_estimate=pl.CostEstimate(
            flops=640 * rows * half * half, bytes_accessed=4 * half * half, transcendentals=0
        ),
        name="right_product",
    )(place, blocks, right, late)


def per_device(hidden, out_grad, left_inverse, right_inverse):
    z, y, xl, c, o = (lax.axis_index(n) for n in ("z", "y", "xl", "c", "o"))
    tokens, width = hidden.shape
    half = width // 2
    token_total = tokens * 64
    first = o == 0
    h = c ^ ((z + y) & 1)
    hidden, out_grad = in_hbm(hidden), in_hbm(out_grad)
    left_inverse, right_inverse = in_hbm(left_inverse), in_hbm(right_inverse)
    place = jnp.stack([o, h, z, y]).astype(jnp.int32)
    second_me = jnp.where(h == 0, y, z).astype(jnp.int32)[None]

    grads_next, acts_next = in_hbm(shift(out_grad, "c", 1)), in_hbm(shift(hidden, "c", 1))
    partial = cross_own(place, out_grad, hidden)

    own, m1, m2, m3 = cross_term(place, grads_next, acts_next, partial)
    m_parts = [own, turn(m1, 1, 0), turn(m3, 3, 0), turn(m2, 2, 0)]

    f_own, right, far_a, far_b, left = factor_term(
        place, hidden, out_grad, acts_next, grads_next, in_hbm(m1)
    )
    from_left, from_right = turn(far_a, 1, 0), turn(far_b, -1, 0)

    my_xl = xl.astype(jnp.int32)[None]

    def second_sends(pieces):
        return [turn(pieces[s - 1], s, 1) for s in (1, 3, 2)]

    m_pieces = fold(second_me, m_parts, (1, 2, 3), BF, in_hbm(f_own))
    (m,) = fold(second_me, m_parts, (0,), F32, m_pieces[0])
    m_received = second_sends(m_pieces)
    right, left = grow(right, left, from_left, from_right, *m_received)
    f_parts = [f_own, turn(right, 1, 0), turn(left, -1, 0)]

    mine, theirs = settle(my_xl, [m, *m_received], F32)
    across = lax.ppermute(theirs, ("xl", "o"), [(i, 3 - i) for i in range(4)])
    products = left_product(place, mine, shift(theirs, "xl", 1), left_inverse)
    products = left_product(place, across, shift(mine, "o", 1), left_inverse, products)
    blocks = lax.all_to_all(products, ("o", "c", "z", "y", "xl"), 0, 0, tiled=True)
    f_pieces = fold(second_me, f_parts, (1, 2, 3), BF, in_hbm(products))
    (f,) = fold(second_me, f_parts, (0,), F32, f_pieces[0])
    update = right_product(place, blocks, right_inverse, f_pieces[0])
    f_mine, f_theirs = settle(my_xl, [f, *second_sends(f_pieces)], BF, in_hbm(update))

    f = add(f_mine, shift(f_theirs, "xl", 1))
    f = f * jnp.where(first, 1.0 / token_total, 1.0).astype(F32)
    f = f.reshape(2, width // 64, half)
    mine = pick(f, 0, c)
    theirs = shift(pick(f, 0, 1 - c), "c", 1)
    factors = jnp.concatenate(
        [jnp.where(h == 0, mine, theirs), jnp.where(h == 0, theirs, mine)], axis=1
    )[None]
    return factors, update


def solution(mesh):
    fine = Mesh(mesh.devices.reshape(4, 4, 2, 2, 2), ("z", "y", "xl", "c", "o"))
    dp = ("z", "y", "xl", "c")
    in_specs = (P(dp, None), P(dp, None), P(None, "o"), P(None, "o"))
    out_specs = (P("o", dp, None), P(dp, "o"))
    return jax.shard_map(
        per_device, mesh=fine, in_specs=in_specs, out_specs=out_specs, check_vma=False
    )
```

```python
import functools

import jax
import jax.numpy as jnp
from jax import lax
from jax.experimental import pallas as pl
from jax.experimental.pallas import tpu as pltpu
from jax.sharding import Mesh, PartitionSpec as P

BF = jnp.bfloat16
F32 = jnp.float32
TILE = 640
ANY = pl.BlockSpec(memory_space=pl.ANY)
VMEM = pl.BlockSpec(memory_space=pltpu.VMEM)


def contract(first_rows, second_rows):
    return lax.dot_general(
        first_rows, second_rows, (((0,), (0,)), ((), ())), preferred_element_type=F32
    )


def shift(x, axis, step):
    size = lax.axis_size(axis)
    return lax.ppermute(x, axis, [(i, (i + step) % size) for i in range(size)])


def turn(x, step, stage):
    pairs = []
    for z in range(4):
        for y in range(4):
            for h in range(2):
                along_z = (h == 0) == (stage == 0)
                z2, y2 = ((z + step) % 4, y) if along_z else (z, (y + step) % 4)
                core, core2 = h ^ ((z + y) & 1), h ^ ((z2 + y2) & 1)
                pairs.append(((z * 4 + y) * 2 + core, (z2 * 4 + y2) * 2 + core2))
    return lax.ppermute(x, ("z", "y", "c"), pairs)


def in_hbm(x):
    return pltpu.with_memory_space_constraint(x, pltpu.HBM)


def pick(x, dim, index):
    return lax.dynamic_index_in_dim(x, index, dim, keepdims=False)


def split_pair(x):
    high = x.astype(BF)
    return high, (x - high.astype(F32)).astype(BF)


def place_tile(place, buffer, sem, outs, m, zs):
    rows = TILE // (zs * 4)

    def start(at, out, slot):
        block = buffer.at[m, pl.ds(at, rows)]
        pltpu.make_async_copy(block, out.at[slot], sem).start()

    for a in range(zs):
        z = m * zs + a

        @pl.when(place[1] == 0)
        def _():
            for r, out in enumerate(outs):

                @pl.when(((z - place[2] + 4) & 3) == r)
                def _():
                    for k in range(4):
                        if isinstance(out, tuple):
                            start((a * 4 + k) * rows, out[k // 2], k % 2)
                        else:
                            start((a * 4 + k) * rows, out, k)

        @pl.when(place[1] == 1)
        def _():
            for r, out in enumerate(outs):
                at = pl.multiple_of((a * 4 + ((place[3] + r) & 3)) * rows, 16)
                if isinstance(out, tuple):
                    pl.when(z < 2)(functools.partial(start, at, out[0], z & 1))
                    pl.when(z >= 2)(functools.partial(start, at, out[1], z & 1))
                else:
                    start(at, out, z)


def wait_all(buffer, sem):
    pltpu.make_async_copy(buffer, buffer, sem).wait()


def own_kernel(place, a, b, out, lhs, rhs, lhs_sems, rhs_sem):
    m = pl.program_id(0)
    half = rhs.shape[1]

    @pl.when(m == 0)
    def _():
        at = pl.ds(pl.multiple_of((place[1] ^ place[0]) * half, half), half)
        pltpu.make_async_copy(b.at[:, at], rhs, rhs_sem).start()
        for k in range(2):
            at = pl.ds(pl.multiple_of(place[1] * half + k * TILE, TILE), TILE)
            pltpu.make_async_copy(a.at[:, at], lhs.at[k], lhs_sems.at[k]).start()
        wait_all(rhs, rhs_sem)

    wait_all(lhs.at[m], lhs_sems.at[m])
    out[...] = contract(lhs[m], rhs[...])


def cross_kernel(place, a, b, partial, own, ahead1, ahead2, ahead3, held, buffer, held_sems, sem):
    m = pl.program_id(0)

    @pl.when(m == 0)
    def _():
        for k in range(2):
            rows = partial.at[pl.ds(k * TILE, TILE)]
            pltpu.make_async_copy(rows, held.at[k], held_sems.at[k]).start()

    tile = contract(a[...], b[...])
    wait_all(held.at[m], held_sems.at[m])
    buffer[m] = (held[m] + tile).astype(BF)
    place_tile(place, buffer, sem, [own, ahead1, ahead2, ahead3], m, 2)
    pl.when(m == 1)(lambda: wait_all(buffer, sem))


def cross_own(place, grads, acts):
    tokens, half = grads.shape[0], grads.shape[1] // 2
    return pl.pallas_call(
        own_kernel,
        out_shape=jax.ShapeDtypeStruct((half, half), F32),
        grid_spec=pltpu.PrefetchScalarGridSpec(
            num_scalar_prefetch=1,
            grid=(2,),
            in_specs=[pl.BlockSpec(memory_space=pltpu.HBM)] * 2,
            out_specs=pl.BlockSpec((TILE, half), lambda m, p: (m, 0)),
            scratch_shapes=[
                pltpu.VMEM((2, tokens, TILE), BF),
                pltpu.VMEM((tokens, half), BF),
                pltpu.SemaphoreType.DMA((2,)),
                pltpu.SemaphoreType.DMA,
            ],
        ),
        compiler_params=pltpu.CompilerParams(vmem_limit_bytes=28 * 2**20),
        cost_estimate=pl.CostEstimate(
            flops=2 * tokens * half * half, bytes_accessed=8 * tokens * half, transcendentals=0
        ),
        name="cross_own",
    )(place, grads, acts)


def cross_term(place, grads_next, acts_next, partial):
    tokens, half = grads_next.shape[0], grads_next.shape[1] // 2
    out = pltpu.HBM((4, half // 16, half), BF)
    return pl.pallas_call(
        cross_kernel,
        out_shape=[out] * 4,
        grid_spec=pltpu.PrefetchScalarGridSpec(
            num_scalar_prefetch=1,
            grid=(2,),
            in_specs=[
                pl.BlockSpec((tokens, TILE), lambda m, p: (0, p[1] * 2 + m)),
                pl.BlockSpec((tokens, half), lambda m, p: (0, p[1] ^ p[0])),
                ANY,
            ],
            out_specs=[pl.BlockSpec(memory_space=pltpu.HBM)] * 4,
            scratch_shapes=[
                pltpu.VMEM((2, TILE, half), F32),
                pltpu.VMEM((2, TILE, half), BF),
                pltpu.SemaphoreType.DMA((2,)),
                pltpu.SemaphoreType.DMA,
            ],
        ),
        compiler_params=pltpu.CompilerParams(vmem_limit_bytes=28 * 2**20),
        cost_estimate=pl.CostEstimate(
            flops=2 * tokens * half * half, bytes_accessed=10 * tokens * half, transcendentals=0
        ),
        name="cross_term",
    )(place, grads_next, acts_next, partial)


def factor_kernel(place, h_own, g_own, h_next, g_next, after, *rest):
    del after
    own, right, far_a, far_b, left, lhs, rhs, buffer, lhs_sems, rhs_sem, sem = rest
    m = pl.program_id(0)
    half = rhs.shape[2]

    def fetch(step, with_rhs):
        slot = step & 1
        at = pl.ds(pl.multiple_of(step * TILE, TILE), TILE)
        columns = pl.ds(pl.multiple_of(place[1] * half, half), half)
        for owner, refs in enumerate(((h_own, h_next), (g_own, g_next))):

            @pl.when(place[0] == owner)
            def _():
                for k, ref in enumerate(refs):
                    pltpu.make_async_copy(ref.at[:, at], lhs.at[slot, k], lhs_sems.at[slot, k]).start()
                    if with_rhs:
                        pltpu.make_async_copy(ref.at[:, columns], rhs.at[k], rhs_sem.at[k]).start()

    pl.when(m == 0)(lambda: fetch(0, True))
    pl.when(m < 3)(lambda: fetch(m + 1, False))
    slot = m & 1
    terms = []
    for k in range(2):
        wait_all(lhs.at[slot, k], lhs_sems.at[slot, k])
        pl.when(m == 0)(functools.partial(wait_all, rhs.at[k], rhs_sem.at[k]))
        terms.append(contract(lhs[slot, k], rhs[k]))
    buffer[m] = (terms[0] + terms[1]).astype(BF)
    place_tile(place, buffer, sem, [own, right, (far_a, far_b), left], m, 1)
    pl.when(m == 3)(lambda: wait_all(buffer, sem))


def factor_term(place, acts, grads, acts_next, grads_next, after):
    tokens, width = acts.shape
    half = width // 2
    hbm = pl.BlockSpec(memory_space=pltpu.HBM)
    out = pltpu.HBM((4, width // 16, half), BF)
    side = pltpu.HBM((2, width // 16, half), BF)
    return pl.pallas_call(
        factor_kernel,
        out_shape=[out, out, side, side, out],
        grid_spec=pltpu.PrefetchScalarGridSpec(
            num_scalar_prefetch=1,
            grid=(4,),
            in_specs=[hbm] * 2 + [ANY] * 3,
            out_specs=[hbm] * 5,
            scratch_shapes=[
                pltpu.VMEM((2, 2, tokens, TILE), BF),
                pltpu.VMEM((2, tokens, half), BF),
                pltpu.VMEM((4, TILE, half), BF),
                pltpu.SemaphoreType.DMA((2, 2)),
                pltpu.SemaphoreType.DMA((2,)),
                pltpu.SemaphoreType.DMA,
            ],
        ),
        compiler_params=pltpu.CompilerParams(vmem_limit_bytes=30 * 2**20),
        cost_estimate=pl.CostEstimate(
            flops=4 * tokens * width * half, bytes_accessed=16 * tokens * half, transcendentals=0
        ),
        name="factor_term",
    )(place, acts, grads, acts_next, grads_next, after)


def add(first, *rest):
    total = first.astype(F32)
    for x in rest:
        total = total + x.astype(F32)
    return total


def fold_kernel(count, me, *refs):
    own, *others = refs[-6:-2]
    held, sems = refs[-2:]
    steps = [(1, others[0]), (2, others[1]), (3, others[2]), (0, own)]
    for r, _ in steps:
        pltpu.make_async_copy(refs[0].at[(me[0] + r) & 3], held.at[r], sems.at[r]).start()
    for r, out in steps:
        wait_all(held.at[r], sems.at[r])
        at = (me[0] + r) & 3
        out[...] = add(held[r], *[part[at] for part in refs[1:count]]).astype(out.dtype)


def fold(me, parts, *after):
    _, rows, width = parts[0].shape
    whole = pl.BlockSpec((rows, width), lambda s, m: (0, 0))
    return pl.pallas_call(
        functools.partial(fold_kernel, len(parts)),
        out_shape=[pltpu.HBM((rows, width), F32)]
        + [pltpu.VMEM((rows, width), BF)] * 3,
        grid_spec=pltpu.PrefetchScalarGridSpec(
            num_scalar_prefetch=1,
            grid=(1,),
            in_specs=[pl.BlockSpec(memory_space=pltpu.HBM)]
            + [VMEM] * (len(parts) - 1)
            + [ANY] * len(after),
            out_specs=[whole] + [VMEM] * 3,
            scratch_shapes=[pltpu.VMEM((4, rows, width), BF), pltpu.SemaphoreType.DMA((4,))],
        ),
        compiler_params=pltpu.CompilerParams(vmem_limit_bytes=12 * 2**20),
        cost_estimate=pl.CostEstimate(flops=0, bytes_accessed=0, transcendentals=0),
        name="fold",
    )(me, in_hbm(parts[0]), *parts[1:], *after)


def settle_kernel(count, xl, *refs):
    mine, theirs, total = refs[-3:]
    rows = mine.shape[0]
    value = None
    for ref in refs[:count]:
        for part in [ref[...]] if len(ref.shape) == 2 else [ref[k] for k in range(ref.shape[0])]:
            value = part.astype(F32) if value is None else value + part.astype(F32)
    total[...] = value
    for out, index in ((mine, xl[0]), (theirs, 1 - xl[0])):
        out[...] = total[pl.ds(pl.multiple_of(index * rows, 8), rows)].astype(out.dtype)


def settle(xl, parts, dtype, *after):
    rows, width = parts[0].shape[-2:]
    half = pl.BlockSpec((rows // 2, width), lambda s, x: (0, 0))
    return pl.pallas_call(
        functools.partial(settle_kernel, len(parts)),
        out_shape=[jax.ShapeDtypeStruct((rows // 2, width), t) for t in (F32, dtype)],
        grid_spec=pltpu.PrefetchScalarGridSpec(
            num_scalar_prefetch=1,
            grid=(1,),
            in_specs=[pl.BlockSpec((rows, width), lambda s, x: (0, 0))]
            + [VMEM] * (len(parts) - 1)
            + [ANY] * len(after),
            out_specs=[half] * 2,
            scratch_shapes=[pltpu.VMEM((rows, width), F32)],
        ),
        compiler_params=pltpu.CompilerParams(vmem_limit_bytes=8 * 2**20),
        cost_estimate=pl.CostEstimate(flops=0, bytes_accessed=0, transcendentals=0),
        name="settle",
    )(xl, *parts, *after)


def grow_kernel(right, left, from_left, from_right, *refs):
    out_right, out_left, held, sems, out_sem = refs[-5:]
    jobs = [(right, 0, from_left, 0, out_right), (left, 2, from_right, 0, out_left)]
    jobs += [(right, 1, from_left, 1, out_right), (left, 3, from_right, 1, out_left)]
    for n, (x, at, _, _, _) in enumerate(jobs):
        pltpu.make_async_copy(x.at[at], held.at[n], sems.at[n]).start()
    for n, (_, at, received, k, out) in enumerate(jobs):
        wait_all(held.at[n], sems.at[n])
        held[n] = add(held[n], received[k]).astype(BF)
        pltpu.make_async_copy(held.at[n], out.at[at], out_sem).start()
    wait_all(held, out_sem)


def grow(right, left, from_left, from_right, *after):
    hbm = pl.BlockSpec(memory_space=pltpu.HBM)
    return pl.pallas_call(
        grow_kernel,
        out_shape=[pltpu.HBM(x.shape, x.dtype) for x in (right, left)],
        grid=(1,),
        in_specs=[hbm, hbm, VMEM, VMEM] + [ANY] * len(after),
        out_specs=[hbm, hbm],
        scratch_shapes=[
            pltpu.VMEM(right.shape, right.dtype),
            pltpu.SemaphoreType.DMA((4,)),
            pltpu.SemaphoreType.DMA,
        ],
        input_output_aliases={0: 0, 1: 1},
        compiler_params=pltpu.CompilerParams(vmem_limit_bytes=8 * 2**20),
        cost_estimate=pl.CostEstimate(flops=0, bytes_accessed=0, transcendentals=0),
        name="grow",
    )(in_hbm(right), in_hbm(left), from_left, from_right, *after)


def fetch_tiles(step, source, held, sems):
    @pl.when(step == 0)
    def _():
        for k in range(4):
            rows = source.at[pl.ds(k * TILE, TILE)]
            pltpu.make_async_copy(rows, held.at[k], sems.at[k]).start()

    wait_all(held.at[step], sems.at[step])


def left_kernel(own, place, a, b, left, *rest):
    before = None if own else rest[0]
    out, total, held, sems = rest[-4:] if own else (rest[1], rest[2], *rest[4:])
    step = pl.program_id(0)
    rows = a.shape[0]
    at = pl.ds(pl.multiple_of(step * TILE, TILE), TILE)
    part = place[1] ^ place[0] if own else 1 - (place[1] ^ place[0])

    @pl.when(step == 0)
    def _():
        for k in range(2):
            tile = left.at[pl.ds(pl.multiple_of((part * 2 + k) * TILE, TILE), TILE)]
            pltpu.make_async_copy(tile, held.at[k], sems.at[k]).start()

    stacked = jnp.concatenate(split_pair(a[:, at] + b[:, at]), axis=0)
    wait_all(held.at[step], sems.at[step])
    value = jnp.dot(stacked, held[step], preferred_element_type=F32)
    pl.when(step == 0)(lambda: total.__setitem__(..., value if own else before[...] + value))
    pl.when(step == 1)(lambda: total.__setitem__(..., total[...] + value))
    if own:
        pl.when(step == 1)(lambda: out.__setitem__(..., total[...]))
        return
    packed = rest[3]

    @pl.when(step == 1)
    def _():
        result = total[:rows] + total[rows:]
        for z in range(2):
            for y in range(4):
                for xl in range(2):
                    for c in range(2):
                        n = ((z * 4 + y) * 2 + xl) * 2 + c
                        block = result[:, n * rows : (n + 1) * rows]
                        packed[n, 0:16, 0:rows] = block[0:16]
                        packed[n, 0:16, rows : 2 * rows] = block[16:32]
                        packed[n, 0:8, 2 * rows : 3 * rows] = block[32:40]
                        ready = packed[n].astype(BF)
                        for there in (0, 2):
                            d = c * 32 + (there + z) * 8 + y * 2 + xl
                            out[d] = ready
                            out[64 + d] = ready


def left_product(place, a, b, left, before=None):
    rows, half = a.shape
    own = before is None
    total = pltpu.VMEM((2 * rows, half), F32)
    return pl.pallas_call(
        functools.partial(left_kernel, own),
        out_shape=total if own else pltpu.HBM((128, 16, 128), BF),
        grid_spec=pltpu.PrefetchScalarGridSpec(
            num_scalar_prefetch=1,
            grid=(2,),
            in_specs=[VMEM, VMEM, pl.BlockSpec(memory_space=pltpu.HBM)] + [VMEM] * (not own),
            out_specs=VMEM if own else pl.BlockSpec((128, 16, 128), lambda k, p: (0, 0, 0)),
            scratch_shapes=[total]
            + [pltpu.VMEM((32, 16, 128), F32)] * (not own)
            + [pltpu.VMEM((2, TILE, half), BF), pltpu.SemaphoreType.DMA((2,))],
        ),
        compiler_params=pltpu.CompilerParams(vmem_limit_bytes=16 * 2**20),
        cost_estimate=pl.CostEstimate(
            flops=0 if own else 256 * rows * half * half, bytes_accessed=0, transcendentals=0
        ),
        name="left_own" if own else "left_product",
    )(place, a, b, left, *([] if own else [before]))


def right_kernel(place, blocks, right, late, out, rows_in, held, sems):
    del late
    step = pl.program_id(0)
    fetch_tiles(step, right, held, sems)
    rows = out.shape[0]
    for near in range(2):
        for y in range(4):
            for xl in range(2):
                core = (step >> 1) ^ ((near + y) & 1)
                block = blocks[core * 32 + ((step & 1) * 2 + near) * 8 + y * 2 + xl].astype(F32)
                at = ((near * 4 + y) * 2 + xl) * rows
                rows_in[at : at + 16, :] = block[:, 0:rows]
                rows_in[at + 16 : at + 32, :] = block[:, rows : 2 * rows]
                rows_in[at + 32 : at + 40, :] = block[0:8, 2 * rows : 3 * rows]
    value = contract(rows_in[...].astype(BF), held[step])
    pl.when(step == 0)(lambda: out.__setitem__(..., value))
    pl.when(step > 0)(lambda: out.__setitem__(..., out[...] + value))


def right_product(place, blocks, right, late):
    width, half = right.shape
    rows = width // 64
    return pl.pallas_call(
        right_kernel,
        out_shape=jax.ShapeDtypeStruct((rows, half), F32),
        grid_spec=pltpu.PrefetchScalarGridSpec(
            num_scalar_prefetch=1,
            grid=(4,),
            in_specs=[
                pl.BlockSpec((64, 16, 128), lambda k, p: (p[2] >> 1, 0, 0)),
                pl.BlockSpec(memory_space=pltpu.HBM),
                ANY,
            ],
            out_specs=pl.BlockSpec((rows, half), lambda k, p: (0, 0)),
            scratch_shapes=[
                pltpu.VMEM((TILE, rows), F32),
                pltpu.VMEM((4, TILE, half), BF),
                pltpu.SemaphoreType.DMA((4,)),
            ],
        ),
        compiler_params=pltpu.CompilerParams(vmem_limit_bytes=20 * 2**20),
        cost_estimate=pl.CostEstimate(
            flops=640 * rows * half * half, bytes_accessed=4 * half * half, transcendentals=0
        ),
        name="right_product",
    )(place, blocks, right, late)


def per_device(hidden, out_grad, left_inverse, right_inverse):
    z, y, xl, c, o = (lax.axis_index(n) for n in ("z", "y", "xl", "c", "o"))
    tokens, width = hidden.shape
    half = width // 2
    token_total = tokens * 64
    first = o == 0
    h = c ^ ((z + y) & 1)
    hidden, out_grad = in_hbm(hidden), in_hbm(out_grad)
    left_inverse, right_inverse = in_hbm(left_inverse), in_hbm(right_inverse)
    place = jnp.stack([o, h, z, y]).astype(jnp.int32)
    second_me = jnp.where(h == 0, y, z).astype(jnp.int32)[None]

    grads_next, acts_next = in_hbm(shift(out_grad, "c", 1)), in_hbm(shift(hidden, "c", 1))
    partial = cross_own(place, out_grad, hidden)

    own, m1, m2, m3 = cross_term(place, grads_next, acts_next, partial)
    m_parts = [own, turn(m1, 1, 0), turn(m3, 3, 0), turn(m2, 2, 0)]

    f_own, right, far_a, far_b, left = factor_term(
        place, hidden, out_grad, acts_next, grads_next, in_hbm(m1)
    )
    from_left, from_right = turn(far_a, 1, 0), turn(far_b, -1, 0)

    my_xl = xl.astype(jnp.int32)[None]

    def second_sends(pieces):
        return [turn(pieces[s - 1], s, 1) for s in (1, 3, 2)]

    m, *m_pieces = fold(second_me, m_parts, in_hbm(f_own))
    m_received = second_sends(m_pieces)
    right, left = grow(right, left, from_left, from_right, *m_received)
    f_parts = [f_own, turn(right, 1, 0), turn(left, -1, 0)]

    mine, theirs = settle(my_xl, [in_hbm(m), *m_received], F32)
    across = lax.ppermute(theirs, ("xl", "o"), [(i, 3 - i) for i in range(4)])
    products = left_product(place, mine, shift(theirs, "xl", 1), left_inverse)
    products = left_product(place, across, shift(mine, "o", 1), left_inverse, products)
    blocks = lax.all_to_all(products, ("o", "c", "z", "y", "xl"), 0, 0, tiled=True)
    f, *f_pieces = fold(second_me, f_parts, in_hbm(products))
    update = right_product(place, blocks, right_inverse, f_pieces[0])
    f_mine, f_theirs = settle(my_xl, [in_hbm(f), *second_sends(f_pieces)], BF, in_hbm(update))

    f = add(f_mine, shift(f_theirs, "xl", 1))
    f = f * jnp.where(first, 1.0 / token_total, 1.0).astype(F32)
    f = f.reshape(2, width // 64, half)
    mine = pick(f, 0, c)
    theirs = shift(pick(f, 0, 1 - c), "c", 1)
    factors = jnp.concatenate(
        [jnp.where(h == 0, mine, theirs), jnp.where(h == 0, theirs, mine)], axis=1
    )[None]
    return factors, update


def solution(mesh):
    fine = Mesh(mesh.devices.reshape(4, 4, 2, 2, 2), ("z", "y", "xl", "c", "o"))
    dp = ("z", "y", "xl", "c")
    in_specs = (P(dp, None), P(dp, None), P(None, "o"), P(None, "o"))
    out_specs = (P("o", dp, None), P(dp, "o"))
    return jax.shard_map(
        per_device, mesh=fine, in_specs=in_specs, out_specs=out_specs, check_vma=False
    )
```
